32 devices in a mesh: seqhi: 4 (over x, core), seqlo: 8 (over z, y).
Axes of the slice: x: 2, y: 2, z: 4, core: 2. Of those that a mesh axis runs over, the one named last changes fastest.
Arguments:
- queries: float32 [4096, 768], P(('seqhi', 'seqlo')), may hold values from -6 to 6
- keys: float32 [4096, 768], P(('seqhi', 'seqlo')), may hold values from -6 to 6
- values: float32 [4096, 768], P(('seqhi', 'seqlo')), may hold values from -6 to 6
- cotangent: float32 [4096, 768], P(('seqhi', 'seqlo')), may hold values from -6 to 6
Outputs:
- attended: float32 [4096, 768], P(('seqhi', 'seqlo'))
- query_grad: float32 [4096, 768], P(('seqhi', 'seqlo'))
- key_grad: float32 [4096, 768], P(('seqhi', 'seqlo'))
- value_grad: float32 [4096, 768], P(('seqhi', 'seqlo'))
The draws below stay inside these ranges and needn't reach their ends.
All inputs are finite; a program needn't handle non-finite values.
Results may differ from the reference program's by a relative error of at most 0.0003.
Values sent between devices are 32-bit elements; how exact they have to be, the bound alone decides.
No kernel may reach another device: no remote copies, remote signals or barrier semaphores. Data moves between devices by JAX's collectives and lax.ppermute only.
A program may use at most 128 MiB of HBM per device.

```python
import math
import jax
import jax.numpy as jnp
from jax import lax

HEADS = 12
D = 768
BLOCK = 128
TOKENS = 4096


def draw_queries(key, part):
    key = jax.random.fold_in(key, 1)
    return jnp.clip(jax.random.normal(key, (TOKENS, D), jnp.float32), -6.0, 6.0)


def draw_keys(key, part):
    key = jax.random.fold_in(key, 2)
    return jnp.clip(jax.random.normal(key, (TOKENS, D), jnp.float32), -6.0, 6.0)


def block_levels(own_key, dims, cuts, low, high):
    factor_of = 1.0
    for dim, blocks in cuts:
        heights = jax.random.uniform(jax.random.fold_in(jax.random.fold_in(own_key, 6), dim), (blocks,), jnp.float32, low / len(cuts), high / len(cuts))
        factor_of = factor_of * jnp.repeat(jnp.exp(heights), dims[dim] // blocks).reshape((-1,) + (1,) * (len(dims) - 1 - dim))
    return factor_of


def centred(rng, dims, width, bound, pieces=(), held_as=jnp.bfloat16):
    entries = width * jax.random.normal(rng, dims, jnp.float32)
    if pieces:
        entries = entries * block_levels(rng, dims, pieces, -0.22, 0.18)
    return jnp.clip(entries, -bound, bound).astype(held_as)


def setup_inputs(seed: int = 0) -> dict:
    seeds = jax.random.split(jax.random.key(seed), 5)
    return {
        "queries": draw_queries(jax.random.fold_in(seeds[4], 71), 0),
        "keys": draw_keys(jax.random.fold_in(seeds[4], 71), 0),
        "values": centred(seeds[2], (TOKENS, D), 1.0, 6.0, ((0, 32),), jnp.float32),
        "cotangent": centred(seeds[3], (TOKENS, D), 1.0, 6.0, ((0, 32),), jnp.float32),
    }


LOG_TWO = math.log(2.0)
HIGHEST_PRECISION = lax.Precision.HIGHEST

def halve_rows(matrix):
    paired = matrix.reshape(matrix.shape[0] // 2, 2, matrix.shape[1])
    return 0.5 * (paired[:, 0] + paired[:, 1])

def reference(queries, keys, values, cotangent):
    total_tokens = queries.shape[0]
    features = queries.shape[1]
    head_dim = features // HEADS
    blocks = total_tokens // BLOCK
    depth = blocks.bit_length() - 1
    score_scale = 1.0 / math.sqrt(head_dim)
    paired_rows = jnp.concatenate([keys, values], axis=1)
    coarse = [paired_rows]
    for height in range(1, depth):
        coarse.append(halve_rows(coarse[-1]))
    offsets = jnp.array([0.0] + [height * LOG_TWO for height in range(depth)], queries.dtype)
    pending_start = tuple((jnp.zeros_like(matrix) for matrix in coarse))

    def advance(pending, number):
        first_row = (number * BLOCK).astype(jnp.int32)
        query_block = lax.dynamic_slice_in_dim(queries, first_row, BLOCK, 0).reshape(BLOCK, HEADS, head_dim)
        grad_block = lax.dynamic_slice_in_dim(cotangent, first_row, BLOCK, 0).reshape(BLOCK, HEADS, head_dim)
        key_sets = [lax.dynamic_slice_in_dim(paired_rows, first_row, BLOCK, 0)]
        starts = []
        for height in range(depth):
            segment = number // 2 ** height
            sibling = segment + 1 - 2 * (segment % 2)
            sibling_row = (sibling * BLOCK).astype(jnp.int32)
            starts.append(sibling_row)
            key_sets.append(lax.dynamic_slice_in_dim(coarse[height], sibling_row, BLOCK, 0))
        stacked = jnp.stack(key_sets).reshape(depth + 1, BLOCK, 2, HEADS, head_dim)
        key_part = stacked[:, :, 0]
        value_part = stacked[:, :, 1]
        scores = jnp.einsum('qhd,jkhd->hqjk', query_block, key_part, precision=HIGHEST_PRECISION) * score_scale
        scores = scores + offsets[None, None, :, None]
        highest = lax.optimization_barrier(jnp.max(scores, axis=(2, 3), keepdims=True))
        exponent = jnp.exp(scores - highest)
        weights = exponent / lax.optimization_barrier(jnp.sum(exponent, axis=(2, 3), keepdims=True))
        attended = jnp.einsum('hqjk,jkhd->qhd', weights, value_part, precision=HIGHEST_PRECISION)
        row_dot = lax.optimization_barrier(jnp.sum(attended * grad_block, axis=2))
        prob_grad = jnp.einsum('qhd,jkhd->hqjk', grad_block, value_part, precision=HIGHEST_PRECISION)
        score_grad = weights * (prob_grad - row_dot.T[:, :, None, None])
        query_grad = jnp.einsum('hqjk,jkhd->qhd', score_grad, key_part, precision=HIGHEST_PRECISION) * score_scale
        key_grad = jnp.einsum('hqjk,qhd->jkhd', score_grad, query_block, precision=HIGHEST_PRECISION) * score_scale
        value_grad = jnp.einsum('hqjk,qhd->jkhd', weights, grad_block, precision=HIGHEST_PRECISION)
        pair_grad = jnp.stack([key_grad, value_grad], axis=2).reshape(depth + 1, BLOCK, 2 * features)
        updated = []
        for height in range(depth):
            present = lax.dynamic_slice_in_dim(pending[height], starts[height], BLOCK, 0)
            updated.append(lax.dynamic_update_slice_in_dim(pending[height], present + pair_grad[height + 1], starts[height], 0))
        return (tuple(updated), (attended.reshape(BLOCK, features), query_grad.reshape(BLOCK, features), pair_grad[0]))
    pending, (attended_rows, query_rows, own_rows) = lax.scan(advance, pending_start, jnp.arange(blocks, dtype=jnp.int32))
    token_grad = own_rows.reshape(total_tokens, 2 * features)
    for height in range(depth):
        token_grad = token_grad + jnp.repeat(pending[height] / 2 ** height, 2 ** height, axis=0)
    attended = attended_rows.reshape(total_tokens, features)
    query_grad = query_rows.reshape(total_tokens, features)
    return (attended, query_grad, token_grad[:, :features], token_grad[:, features:])
```

```python
import math

import jax
import jax.numpy as jnp
from jax import lax
from jax.experimental import pallas as pl
from jax.experimental.pallas import tpu as pltpu
from jax.sharding import PartitionSpec as P

HEADS = 12
BLOCK = 128
HEAD_DIM = 64
LANES = 2 * HEAD_DIM
AXES = ("seqhi", "seqlo")
CHUNKS = (3,)
VMEM_LIMIT = 48 * 1024 * 1024
F32 = jnp.float32
BF16 = jnp.bfloat16
LOG2_E = 1.0 / math.log(2.0)


def struct(*shape):
    return jax.ShapeDtypeStruct(shape, F32)


def call(kernel, operands, outs, scratch=(), scalar=None, flops=0, exps=0):
    vmem = pl.BlockSpec(memory_space=pltpu.VMEM)
    smem = pl.BlockSpec(memory_space=pltpu.SMEM)
    in_specs = [vmem] * len(operands)
    if scalar is not None:
        operands = [scalar, *operands]
        in_specs = [smem, *in_specs]
    moved = sum(4 * math.prod(a.shape) for a in [*operands, *outs])
    return pl.pallas_call(
        kernel,
        out_shape=list(outs),
        in_specs=in_specs,
        out_specs=[vmem] * len(outs),
        scratch_shapes=list(scratch),
        compiler_params=pltpu.CompilerParams(vmem_limit_bytes=VMEM_LIMIT),
        cost_estimate=pl.CostEstimate(
            flops=flops, bytes_accessed=moved, transcendentals=exps
        ),
    )(*operands)


def exchange(value, offset):
    count = lax.axis_size(AXES)
    return lax.ppermute(value, AXES, [(i, i ^ offset) for i in range(count)])


def mean_rows(ref, lead, first, count, factor):
    total = None
    for step in range(factor):
        rows = pl.ds(first + step, count, stride=factor)
        part = ref[(*lead, rows, slice(None))]
        total = part if total is None else total + part
    return total * (1.0 / factor)


def add_spread(ref, lead, first, value, factor):
    count = value.shape[0]
    value = value * (1.0 / factor)
    for step in range(factor):
        rows = pl.ds(first + step, count, stride=factor)
        place = (*lead, rows, slice(None))
        ref[place] = ref[place] + value


class Plan:
    def __init__(self, lo_bits, hi_bits):
        self.lo_bits = lo_bits
        self.hi_bits = hi_bits
        self.partners = list(range(1, 2 ** (lo_bits - 1)))
        self.own_rows = BLOCK >> (lo_bits - 1)
        self.held = {}
        self.payload = {}
        for step in range(hi_bits - 1, -1, -1):
            rows = BLOCK >> step
            payload = [(None, 0, rows)]
            fresh = {step: [(step, 0, rows)]}
            for level in range(step + 1, hi_bits):
                for piece in self.held[level]:
                    payload.append(piece)
                    fresh.setdefault(level, []).append((step, rows, piece[2]))
                    rows += piece[2]
            self.payload[step] = payload
            for level, pieces in fresh.items():
                self.held[level] = self.held.get(level, []) + pieces

    def level(self, partner):
        return partner.bit_length()

    def rows(self, partner):
        return BLOCK >> (self.level(partner) - 1)

    def step_rows(self, step):
        return sum(piece[2] for piece in self.payload[step])


def split(value):
    high = value.astype(BF16).astype(F32)
    return high, value - high


def halves_by_head(value):
    high, low = split(value)
    first = lax.broadcasted_iota(jnp.int32, value.shape, 1) < HEAD_DIM
    one = jnp.where(first, high, pltpu.roll(low, HEAD_DIM, 1))
    two = jnp.where(first, pltpu.roll(high, HEAD_DIM, 1), low)
    return one.astype(BF16), two.astype(BF16)


def dot(lhs, rhs, dims):
    return lax.dot_general(lhs, rhs, (dims, ((), ())), preferred_element_type=F32)


NN = ((1,), (0,))
NT = ((1,), (1,))
TN = ((0,), (0,))


def attention(plan, first_pair, pairs, operands, scalar):
    queries, keys, values, cotangent, key_value, query_grad, *rest = operands
    zs = rest[: len(plan.partners)]
    rs = rest[len(plan.partners) :]
    sets = []
    for index, partner in enumerate(plan.partners):
        sets.append((plan.level(partner), index, 0, plan.rows(partner)))
    for level in range(plan.hi_bits):
        for step, row, rows in plan.held[level]:
            sets.append((plan.lo_bits + level, len(zs) + step, row, rows))
    total = 2 * BLOCK + sum(s[3] for s in sets)
    segment = BLOCK
    segments = total // segment
    levels = [0, 0]
    filled = 0
    for level, _, _, rows in sets:
        if filled == 0:
            levels.append(level)
        filled = (filled + rows) % segment
    queries_count = 2 * BLOCK
    scale = 1.0 / math.sqrt(HEAD_DIM)

    def kernel(*refs):
        bit = refs[0]
        q, k, v, g, kv_in, qg_in = refs[1:7]
        rest_in = refs[7 : 7 + len(rest)]
        outs = refs[7 + len(rest) :]
        og_keep, og_send, kv_keep, kv_send = outs[:4]
        rest_out = outs[4 : 4 + len(rest)]
        s_ref, eh_ref, el_ref, dh_ref, dl_ref, kc_ref, vc_ref = outs[4 + len(rest) :]

        def one_pair(pair):
            own = pl.multiple_of(
                bit[0] * (q.shape[1] // 2) + (first_pair + pair) * LANES, LANES
            )
            own = pl.ds(own, LANES)

            def gathered(which, mine):
                tile = which * pairs + pair
                parts = [mine[:, own], kv_in[tile]]
                for _, index, row, rows in sets:
                    parts.append(rest_in[index][tile, pl.ds(row, rows), :])
                return jnp.concatenate(parts, axis=0)

            key_halves = halves_by_head(gathered(0, k))
            value_halves = halves_by_head(gathered(1, v))
            for head in range(2):
                kc_ref[head] = key_halves[head]
                vc_ref[head] = value_halves[head]
            query_t = jnp.concatenate([q[:, own], qg_in[pair]], axis=0).T
            query_t = query_t * (scale * LOG2_E)
            grad_t = jnp.concatenate([g[:, own], qg_in[pairs + pair]], axis=0).T
            out_t = []
            query_grad_t = []
            key_grads = [[], []]
            for head in range(2):
                part = slice(head * HEAD_DIM, (head + 1) * HEAD_DIM)
                qh, ql = split(query_t[part])
                q_rows = jnp.concatenate([qh, ql], axis=0).astype(BF16)
                q_four = jnp.concatenate([qh, qh, ql, ql], axis=0).astype(BF16)
                highest = None
                for index in range(segments):
                    rows = pl.ds(index * segment, segment)
                    half = kc_ref[head, rows, :]
                    s = dot(jnp.concatenate([half, half], axis=1), q_four, NN)
                    s = s + float(levels[index]) if levels[index] else s
                    s_ref[rows, :] = s
                    top = jnp.max(s.reshape(segment // 8, 8, queries_count), axis=0)
                    highest = top if highest is None else jnp.maximum(highest, top)
                highest = jnp.max(highest, axis=0, keepdims=True)
                sums = None
                for index in range(segments):
                    rows = pl.ds(index * segment, segment)
                    e = jnp.exp2(s_ref[rows, :] - highest)
                    s_ref[rows, :] = e
                    eh = e.astype(BF16)
                    eh_ref[rows, :] = eh
                    el_ref[rows, :] = (e - eh.astype(F32)).astype(BF16)
                    part_sum = jnp.sum(e.reshape(segment // 8, 8, queries_count), axis=0)
                    sums = part_sum if sums is None else sums + part_sum
                inverse = 1.0 / jnp.sum(sums, axis=0, keepdims=True)
                vc = vc_ref[head]
                o = dot(vc, eh_ref[...], TN) + dot(vc, el_ref[...], TN)
                o = (o[:HEAD_DIM] + o[HEAD_DIM:]) * inverse
                out_t.append(o)
                g_scaled = grad_t[part] * inverse
                gh, gl = split(g_scaled)
                g_rows = jnp.concatenate([gh, gl], axis=0).astype(BF16)
                g_four = jnp.concatenate([gh, gh, gl, gl], axis=0).astype(BF16)
                row_dot = jnp.sum(o * g_scaled, axis=0, keepdims=True)
                for index in range(segments):
                    rows = pl.ds(index * segment, segment)
                    half = vc_ref[head, rows, :]
                    dp = dot(jnp.concatenate([half, half], axis=1), g_four, NN)
                    ds = s_ref[rows, :] * (dp - row_dot)
                    dh = ds.astype(BF16)
                    dh_ref[rows, :] = dh
                    dl_ref[rows, :] = (ds - dh.astype(F32)).astype(BF16)
                kc = kc_ref[head]
                dq = dot(kc, dh_ref[...], TN) + dot(kc, dl_ref[...], TN)
                query_grad_t.append((dq[:HEAD_DIM] + dq[HEAD_DIM:]) * scale)
                dk = dot(dh_ref[...], q_rows, NT) + dot(dl_ref[...], q_rows, NT)
                key_grads[0].append(dk)
                dv = dot(eh_ref[...], g_rows, NT) + dot(el_ref[...], g_rows, NT)
                key_grads[1].append(dv)
            for which, parts in enumerate((out_t, query_grad_t)):
                both = jnp.concatenate(parts, axis=0).T
                og_keep[which * pairs + pair] = both[:BLOCK]
                og_send[which * pairs + pair] = both[BLOCK:]
            for which in range(2):
                one, two = key_grads[which]
                first = lax.broadcasted_iota(jnp.int32, one.shape, 1) < HEAD_DIM
                both = jnp.where(
                    first,
                    one + pltpu.roll(one, HEAD_DIM, 1),
                    two + pltpu.roll(two, HEAD_DIM, 1),
                )
                if which == 0:
                    both = both * (1.0 / LOG2_E)
                tile = which * pairs + pair
                kv_keep[tile] = both[:BLOCK]
                kv_send[tile] = both[BLOCK : 2 * BLOCK]
                filled = 2 * BLOCK
                for _, index, row, rows in sets:
                    rest_out[index][tile, pl.ds(row, rows), :] = both[
                        filled : filled + rows
                    ]
                    filled += rows

        if pairs == 1:
            one_pair(0)
        else:
            pl.loop(0, pairs)(one_pair)

    block = struct(2 * pairs, BLOCK, LANES)
    outs = [block] * 4 + [struct(*a.shape) for a in rest]
    flops = 2 * 6 * 4 * pairs * 2 * total * queries_count * HEAD_DIM
    return call(
        kernel,
        operands,
        outs,
        scratch=[
            pltpu.VMEM((total, queries_count), F32),
            pltpu.VMEM((total, queries_count), BF16),
            pltpu.VMEM((total, queries_count), BF16),
            pltpu.VMEM((total, queries_count), BF16),
            pltpu.VMEM((total, queries_count), BF16),
            pltpu.VMEM((2, total, LANES), BF16),
            pltpu.VMEM((2, total, LANES), BF16),
        ],
        scalar=scalar,
        flops=flops,
        exps=pairs * 2 * total * queries_count,
    )


def pack(first_pairs, counts, operands, scalar):
    chunks = len(counts)

    def kernel(bit, q, k, v, g, *outs):
        for index, (first, pairs) in enumerate(zip(first_pairs, counts)):
            for pair in range(pairs):
                theirs = (1 - bit[0]) * (q.shape[1] // 2) + (first + pair) * LANES
                theirs = pl.ds(pl.multiple_of(theirs, LANES), LANES)
                outs[index][pair] = k[:, theirs]
                outs[index][pairs + pair] = v[:, theirs]
                outs[chunks + index][pair] = q[:, theirs]
                outs[chunks + index][pairs + pair] = g[:, theirs]

    outs = [struct(2 * pairs, BLOCK, LANES) for pairs in counts] * 2
    outs = call(kernel, operands, outs, scalar=scalar)
    return outs[:chunks], outs[chunks:]


def coarsen_pair(plan, first_pair, pairs, keys, values, received, scalar):
    top = plan.lo_bits - 1

    def kernel(bit, k, v, got, *refs):
        outs = refs[:top]
        mine = refs[top]
        half = BLOCK // 2
        for tile in range(2 * pairs):
            own = bit[0] * (k.shape[1] // 2) + (first_pair + tile % pairs) * LANES
            own = pl.ds(pl.multiple_of(own, LANES), LANES)
            mine[tile] = (k, v)[tile // pairs][:, own]
            outs[0][tile, :half] = mean_rows(mine, (tile,), 0, half, 2)
            outs[0][tile, half:] = mean_rows(got, (tile,), 0, half, 2)
            for index in range(1, top):
                outs[index][tile] = mean_rows(
                    outs[index - 1], (tile,), 0, BLOCK >> index, 2
                )

    outs = [struct(2 * pairs, BLOCK >> index, LANES) for index in range(top)]
    return call(
        kernel,
        [keys, values, received],
        outs,
        scratch=[pltpu.VMEM((2 * pairs, BLOCK, LANES), F32)],
        scalar=scalar,
    )


def coarsen_group(plan, pairs, finest, zs):
    rows = plan.own_rows

    def kernel(own, *refs):
        ins = refs[: len(zs)]
        outs = refs[len(zs) :]
        for tile in range(2 * pairs):
            outs[0][tile, pl.ds(0, rows)] = mean_rows(own, (tile,), 0, rows, 2)
            for index, partner in enumerate(plan.partners):
                outs[0][tile, pl.ds((index + 1) * rows, rows)] = mean_rows(
                    ins[index], (tile,), 0, rows, plan.rows(partner) // rows
                )
            for step in range(1, plan.hi_bits):
                outs[step][tile] = mean_rows(
                    outs[step - 1], (tile,), 0, BLOCK >> step, 2
                )

    outs = [struct(2 * pairs, BLOCK >> step, LANES) for step in range(plan.hi_bits)]
    return call(kernel, [finest, *zs], outs)


def spread_group(plan, pairs, group_grads, zs_grad):
    rows = plan.own_rows

    def kernel(*refs):
        steps = refs[: plan.hi_bits]
        ins = refs[plan.hi_bits : plan.hi_bits + len(zs_grad)]
        own_out, *outs = refs[plan.hi_bits + len(zs_grad) : -1]
        total = refs[-1]
        for tile in range(2 * pairs):
            total[tile] = steps[0][tile]
            for step in range(1, plan.hi_bits):
                add_spread(total, (tile,), 0, steps[step][tile], 1 << step)
            own_out[tile] = total[tile, pl.ds(0, rows)]
            for index, partner in enumerate(plan.partners):
                outs[index][tile] = ins[index][tile]
                part = total[tile, pl.ds((index + 1) * rows, rows)]
                add_spread(outs[index], (tile,), 0, part, plan.rows(partner) // rows)

    outs = [struct(2 * pairs, rows, LANES)] + [struct(*a.shape) for a in zs_grad]
    own, *zs_out = call(
        kernel,
        [*group_grads, *zs_grad],
        outs,
        scratch=[pltpu.VMEM((2 * pairs, BLOCK, LANES), F32)],
    )
    return own, zs_out


def spread_pair(plan, pairs, own_grad, returned, keep, send):
    top = plan.lo_bits - 1

    def kernel(own, *refs):
        back = refs[: len(returned)]
        keep_in, send_in, keep_out, send_out, *totals = refs[len(returned) :]
        half = BLOCK // 2
        for tile in range(2 * pairs):
            above = own[tile]
            for level in range(top, 0, -1):
                total = totals[level - 1]
                parts = [
                    back[index][tile]
                    for index, partner in enumerate(plan.partners)
                    if plan.level(partner) == level
                ]
                total[tile] = sum(parts[1:], parts[0])
                add_spread(total, (tile,), 0, above, 2)
                above = total[tile]
            keep_out[tile] = keep_in[tile]
            add_spread(keep_out, (tile,), 0, above[:half], 2)
            send_out[tile] = send_in[tile]
            add_spread(send_out, (tile,), 0, above[half:], 2)

    return call(
        kernel,
        [own_grad, *returned, keep, send],
        [struct(2 * pairs, BLOCK, LANES)] * 2,
        scratch=[
            pltpu.VMEM((2 * pairs, BLOCK >> index, LANES), F32) for index in range(top)
        ],
    )


def unpack(first_pairs, counts, kept, features, scalar):
    chunks = len(counts)

    def kernel(bit, *refs):
        ins = refs[: 4 * chunks]
        outs = refs[4 * chunks :]
        for index, (first, pairs) in enumerate(zip(first_pairs, counts)):
            for pair in range(pairs):
                column = (first + pair) * LANES
                mine = bit[0] * (features // 2) + column
                theirs = (1 - bit[0]) * (features // 2) + column
                for group in range(2):
                    for which in range(2):
                        out = outs[2 * group + which]
                        for source, place in ((0, mine), (1, theirs)):
                            array = ins[4 * index + 2 * group + source]
                            place = pl.ds(pl.multiple_of(place, LANES), LANES)
                            out[:, place] = array[which * pairs + pair]

    flat = [array for chunk in kept for array in chunk]
    return call(kernel, flat, [struct(BLOCK, features)] * 4, scalar=scalar)


def on_device(queries, keys, values, cotangent):
    features = queries.shape[1]
    assert queries.shape[0] == BLOCK
    plan = Plan(
        lax.axis_size("seqlo").bit_length() - 1, lax.axis_size("seqhi").bit_length() - 1
    )
    scalar = (lax.axis_index("seqlo") % 2).astype(jnp.int32).reshape(1)
    counts = CHUNKS
    firsts = [sum(counts[:index]) for index in range(len(counts))]
    sends_kv, sends_qg = pack(
        firsts, counts, [queries, keys, values, cotangent], scalar
    )
    kept = []
    for first, pairs, send_kv, send_qg in zip(firsts, counts, sends_kv, sends_qg):
        kv = exchange(send_kv, 1)
        qg = exchange(send_qg, 1)
        coarse = coarsen_pair(plan, first, pairs, keys, values, kv, scalar)
        zs = [
            exchange(coarse[plan.level(partner) - 1], 2 * partner)
            for partner in plan.partners
        ]
        group = coarsen_group(plan, pairs, coarse[-1], zs)
        rs = [None] * plan.hi_bits
        for step in range(plan.hi_bits - 1, -1, -1):
            parts = [group[step]]
            for source, row, rows in plan.payload[step][1:]:
                parts.append(rs[source][:, row : row + rows])
            rs[step] = exchange(jnp.concatenate(parts, axis=1), 1 << plan.lo_bits + step)
        og_keep, og_send, kv_keep, kv_send, *grads = attention(
            plan,
            first,
            pairs,
            [queries, keys, values, cotangent, kv, qg, *zs, *rs],
            scalar,
        )
        og_back = exchange(og_send, 1)
        zs_grad = grads[: len(zs)]
        rs_grad = grads[len(zs) :]
        group_grads = []
        for step in range(plan.hi_bits):
            back = exchange(rs_grad[step], 1 << plan.lo_bits + step)
            filled = BLOCK >> step
            group_grads.append(back[:, :filled])
            for source, row, rows in plan.payload[step][1:]:
                rs_grad[source] = (
                    rs_grad[source].at[:, row : row + rows].add(back[:, filled : filled + rows])
                )
                filled += rows
        own_grad, zs_grad = spread_group(plan, pairs, group_grads, zs_grad)
        returned = [
            exchange(grad, 2 * partner) for partner, grad in zip(plan.partners, zs_grad)
        ]
        kv_keep, kv_send = spread_pair(plan, pairs, own_grad, returned, kv_keep, kv_send)
        kv_back = exchange(kv_send, 1)
        kept.append((og_keep, og_back, kv_keep, kv_back))
    return tuple(unpack(firsts, counts, kept, features, scalar))


def solution(mesh):
    spec = P(AXES, None)
    return jax.shard_map(
        on_device,
        mesh=mesh,
        in_specs=(spec,) * 4,
        out_specs=(spec,) * 4,
        check_vma=False,
    )
```

```python
import math

import jax
import jax.numpy as jnp
from jax import lax
from jax.experimental import pallas as pl
from jax.experimental.pallas import tpu as pltpu
from jax.sharding import PartitionSpec as P

HEADS = 12
BLOCK = 128
HEAD_DIM = 64
LANES = 2 * HEAD_DIM
AXES = ("seqhi", "seqlo")
CHUNKS = (1, 1, 1)
VMEM_LIMIT = 20 * 1024 * 1024
F32 = jnp.float32
BF16 = jnp.bfloat16
LOG2_E = 1.0 / math.log(2.0)
SCALE = 1.0 / math.sqrt(HEAD_DIM)


def struct(*shape):
    return jax.ShapeDtypeStruct(shape, F32)


def call(kernel, operands, outs, scratch=(), scalar=None, flops=0, exps=0, where=None):
    vmem = pl.BlockSpec(memory_space=pltpu.VMEM)
    smem = pl.BlockSpec(memory_space=pltpu.SMEM)
    in_specs = [pl.BlockSpec(memory_space=where) if where else vmem] * len(operands)
    if scalar is not None:
        operands = [scalar, *operands]
        in_specs = [smem, *in_specs]
    moved = sum(4 * math.prod(a.shape) for a in [*operands, *outs])
    return pl.pallas_call(
        kernel,
        out_shape=list(outs),
        in_specs=in_specs,
        out_specs=[vmem] * len(outs),
        scratch_shapes=list(scratch),
        compiler_params=pltpu.CompilerParams(vmem_limit_bytes=VMEM_LIMIT),
        cost_estimate=pl.CostEstimate(
            flops=flops, bytes_accessed=moved, transcendentals=exps
        ),
    )(*operands)


def exchange(value, offset):
    count = lax.axis_size(AXES)
    return lax.ppermute(value, AXES, [(i, i ^ offset) for i in range(count)])


def mean_rows(ref, lead, first, count, factor):
    total = None
    for step in range(factor):
        rows = pl.ds(first + step, count, stride=factor)
        part = ref[(*lead, rows, slice(None))]
        total = part if total is None else total + part
    return total * (1.0 / factor)


def add_spread(ref, lead, first, value, factor):
    count = value.shape[0]
    value = value * (1.0 / factor)
    for step in range(factor):
        rows = pl.ds(first + step, count, stride=factor)
        place = (*lead, rows, slice(None))
        ref[place] = ref[place] + value


class Plan:
    def __init__(self, lo_bits, hi_bits):
        self.lo_bits = lo_bits
        self.hi_bits = hi_bits
        self.partners = list(range(1, 2 ** (lo_bits - 1)))
        self.own_rows = BLOCK >> (lo_bits - 1)
        self.held = {}
        self.payload = {}
        for step in range(hi_bits - 1, -1, -1):
            rows = BLOCK >> step
            payload = [(None, 0, rows)]
            fresh = {step: [(step, 0, rows)]}
            for level in range(step + 1, hi_bits):
                for piece in self.held[level]:
                    payload.append(piece)
                    fresh.setdefault(level, []).append((step, rows, piece[2]))
                    rows += piece[2]
            self.payload[step] = payload
            for level, pieces in fresh.items():
                self.held[level] = self.held.get(level, []) + pieces

    def level(self, partner):
        return partner.bit_length()

    def rows(self, partner):
        return BLOCK >> (self.level(partner) - 1)

    def step_rows(self, step):
        return sum(piece[2] for piece in self.payload[step])


def split(value):
    high = value.astype(BF16).astype(F32)
    return high, value - high


def halves_by_head(value):
    high, low = split(value)
    first = lax.broadcasted_iota(jnp.int32, value.shape, 1) < HEAD_DIM
    one = jnp.where(first, high, pltpu.roll(low, HEAD_DIM, 1))
    two = jnp.where(first, pltpu.roll(high, HEAD_DIM, 1), low)
    return one.astype(BF16), two.astype(BF16)


def dot(lhs, rhs, dims):
    return lax.dot_general(lhs, rhs, (dims, ((), ())), preferred_element_type=F32)


NN = ((1,), (0,))
NT = ((1,), (1,))
TN = ((0,), (0,))


def attention(plan, pairs, operands):
    mine, key_value, turned, *rest = operands
    zs = rest[: len(plan.partners)]
    rs = rest[len(plan.partners) :]
    sets = []
    for index, partner in enumerate(plan.partners):
        sets.append((plan.level(partner), index, 0, plan.rows(partner)))
    for level in range(plan.hi_bits):
        for step, row, rows in plan.held[level]:
            sets.append((plan.lo_bits + level, len(zs) + step, row, rows))
    total = 2 * BLOCK + sum(s[3] for s in sets)
    segment = BLOCK
    segments = total // segment
    levels = [0, 0]
    filled = 0
    for level, _, _, rows in sets:
        if filled == 0:
            levels.append(level)
        filled = (filled + rows) % segment
    queries_count = 2 * BLOCK

    def kernel(mine_in, kv_in, qg_in, *refs):
        rest_in = refs[: len(rest)]
        outs = refs[len(rest) :]
        og_keep, og_send, kv_keep, kv_send = outs[:4]
        rest_out = outs[4 : 4 + len(rest)]
        s_ref, eh_ref, el_ref, dh_ref, dl_ref, kc_ref, vc_ref = outs[4 + len(rest) :]

        def one_pair(pair):
            def gathered(which):
                tile = which * pairs + pair
                parts = [mine_in[tile], kv_in[tile]]
                for _, index, row, rows in sets:
                    parts.append(rest_in[index][tile, pl.ds(row, rows), :])
                return jnp.concatenate(parts, axis=0)

            key_halves = halves_by_head(gathered(0))
            value_halves = halves_by_head(gathered(1))
            for head in range(2):
                kc_ref[head] = key_halves[head]
                vc_ref[head] = value_halves[head]
            query_t = qg_in[pair]
            grad_t = qg_in[pairs + pair]
            out_t = []
            query_grad_t = []
            key_grads = [[], []]
            for head in range(2):
                part = slice(head * HEAD_DIM, (head + 1) * HEAD_DIM)
                qh, ql = split(query_t[part])
                q_rows = jnp.concatenate([qh, ql], axis=0).astype(BF16)
                q_four = jnp.concatenate([qh, qh, ql, ql], axis=0).astype(BF16)
                highest = None
                for index in range(segments):
                    rows = pl.ds(index * segment, segment)
                    half = kc_ref[head, rows, :]
                    s = dot(jnp.concatenate([half, half], axis=1), q_four, NN)
                    s = s + float(levels[index]) if levels[index] else s
                    s_ref[rows, :] = s
                    top = jnp.max(s.reshape(segment // 8, 8, queries_count), axis=0)
                    highest = top if highest is None else jnp.maximum(highest, top)
                highest = jnp.max(highest, axis=0, keepdims=True)
                sums = None
                for index in range(segments):
                    rows = pl.ds(index * segment, segment)
                    e = jnp.exp2(s_ref[rows, :] - highest)
                    s_ref[rows, :] = e
                    eh = e.astype(BF16)
                    eh_ref[rows, :] = eh
                    el_ref[rows, :] = (e - eh.astype(F32)).astype(BF16)
                    part_sum = jnp.sum(e.reshape(segment // 8, 8, queries_count), axis=0)
                    sums = part_sum if sums is None else sums + part_sum
                inverse = 1.0 / jnp.sum(sums, axis=0, keepdims=True)
                vc = vc_ref[head]
                o = dot(vc, eh_ref[...], TN) + dot(vc, el_ref[...], TN)
                o = (o[:HEAD_DIM] + o[HEAD_DIM:]) * inverse
                out_t.append(o)
                g_scaled = grad_t[part] * inverse
                gh, gl = split(g_scaled)
                g_rows = jnp.concatenate([gh, gl], axis=0).astype(BF16)
                g_four = jnp.concatenate([gh, gh, gl, gl], axis=0).astype(BF16)
                row_dot = jnp.sum(o * g_scaled, axis=0, keepdims=True)
                for index in range(segments):
                    rows = pl.ds(index * segment, segment)
                    half = vc_ref[head, rows, :]
                    dp = dot(jnp.concatenate([half, half], axis=1), g_four, NN)
                    ds = s_ref[rows, :] * (dp - row_dot)
                    dh = ds.astype(BF16)
                    dh_ref[rows, :] = dh
                    dl_ref[rows, :] = (ds - dh.astype(F32)).astype(BF16)
                kc = kc_ref[head]
                dq = dot(kc, dh_ref[...], TN) + dot(kc, dl_ref[...], TN)
                query_grad_t.append((dq[:HEAD_DIM] + dq[HEAD_DIM:]) * SCALE)
                dk = dot(dh_ref[...], q_rows, NT) + dot(dl_ref[...], q_rows, NT)
                key_grads[0].append(dk)
                dv = dot(eh_ref[...], g_rows, NT) + dot(el_ref[...], g_rows, NT)
                key_grads[1].append(dv)
            for which, parts in enumerate((out_t, query_grad_t)):
                both = jnp.concatenate(parts, axis=0).T
                og_keep[which * pairs + pair] = both[:BLOCK]
                og_send[which * pairs + pair] = both[BLOCK:]
            for which in range(2):
                one, two = key_grads[which]
                first = lax.broadcasted_iota(jnp.int32, one.shape, 1) < HEAD_DIM
                both = jnp.where(
                    first,
                    one + pltpu.roll(one, HEAD_DIM, 1),
                    two + pltpu.roll(two, HEAD_DIM, 1),
                )
                if which == 0:
                    both = both * (1.0 / LOG2_E)
                tile = which * pairs + pair
                kv_keep[tile] = both[:BLOCK]
                kv_send[tile] = both[BLOCK : 2 * BLOCK]
                filled = 2 * BLOCK
                for _, index, row, rows in sets:
                    rest_out[index][tile, pl.ds(row, rows), :] = both[
                        filled : filled + rows
                    ]
                    filled += rows

        if pairs == 1:
            one_pair(0)
        else:
            pl.loop(0, pairs)(one_pair)

    block = struct(2 * pairs, BLOCK, LANES)
    outs = [block] * 4 + [struct(*a.shape) for a in rest]
    flops = 2 * 6 * 4 * pairs * 2 * total * queries_count * HEAD_DIM
    return call(
        kernel,
        operands,
        outs,
        scratch=[
            pltpu.VMEM((total, queries_count), F32),
            pltpu.VMEM((total, queries_count), BF16),
            pltpu.VMEM((total, queries_count), BF16),
            pltpu.VMEM((total, queries_count), BF16),
            pltpu.VMEM((total, queries_count), BF16),
            pltpu.VMEM((2, total, LANES), BF16),
            pltpu.VMEM((2, total, LANES), BF16),
        ],
        flops=flops,
        exps=pairs * 2 * total * queries_count,
    )


def pack(firsts, counts, operands, scalar):
    chunks = len(counts)
    copies = 4 * 2 * sum(counts)

    def kernel(bit, q, k, v, g, *refs):
        outs, sems = refs[:-1], refs[-1]
        started = []
        for group, arrays in enumerate(((k, v), (q, g)) * 2):
            side = bit[0] if group >= 2 else 1 - bit[0]
            for index, (first, pairs) in enumerate(zip(firsts, counts)):
                out = outs[group * chunks + index]
                for tile in range(2 * pairs):
                    column = side * (q.shape[1] // 2) + (first + tile % pairs) * LANES
                    column = pl.ds(pl.multiple_of(column, LANES), LANES)
                    copy = pltpu.make_async_copy(
                        arrays[tile // pairs].at[:, column],
                        out.at[tile],
                        sems.at[len(started)],
                    )
                    copy.start()
                    started.append(copy)
        for copy in started:
            copy.wait()

    outs = [struct(2 * pairs, BLOCK, LANES) for pairs in counts] * 4
    outs = call(
        kernel,
        operands,
        outs,
        scratch=[pltpu.SemaphoreType.DMA((copies,))],
        scalar=scalar,
        where=pltpu.HBM,
    )
    return [outs[group * chunks : (group + 1) * chunks] for group in range(4)]


def coarsen_pair(plan, pairs, mine, received):
    top = plan.lo_bits - 1

    def kernel(own, got, *outs):
        half = BLOCK // 2
        for tile in range(2 * pairs):
            outs[0][tile, :half] = mean_rows(own, (tile,), 0, half, 2)
            outs[0][tile, half:] = mean_rows(got, (tile,), 0, half, 2)
            for index in range(1, top):
                outs[index][tile] = mean_rows(
                    outs[index - 1], (tile,), 0, BLOCK >> index, 2
                )

    outs = [struct(2 * pairs, BLOCK >> index, LANES) for index in range(top)]
    return call(kernel, [mine, received], outs)


def coarsen_group(plan, pairs, finest, zs, mine, received):
    rows = plan.own_rows

    def kernel(own, mine_in, got, *refs):
        ins = refs[: len(zs)]
        *outs, turned = refs[len(zs) :]
        for tile in range(2 * pairs):
            outs[0][tile, pl.ds(0, rows)] = mean_rows(own, (tile,), 0, rows, 2)
            for index, partner in enumerate(plan.partners):
                outs[0][tile, pl.ds((index + 1) * rows, rows)] = mean_rows(
                    ins[index], (tile,), 0, rows, plan.rows(partner) // rows
                )
            for step in range(1, plan.hi_bits):
                outs[step][tile] = mean_rows(
                    outs[step - 1], (tile,), 0, BLOCK >> step, 2
                )
        for tile in range(2 * pairs):
            both = jnp.concatenate([mine_in[tile], got[tile]], axis=0).T
            turned[tile] = both * (SCALE * LOG2_E) if tile < pairs else both

    outs = [struct(2 * pairs, BLOCK >> step, LANES) for step in range(plan.hi_bits)]
    outs.append(struct(2 * pairs, LANES, 2 * BLOCK))
    *group, turned = call(kernel, [finest, mine, received, *zs], outs)
    return group, turned


def spread_group(plan, pairs, group_grads, zs_grad):
    rows = plan.own_rows

    def kernel(*refs):
        steps = refs[: plan.hi_bits]
        ins = refs[plan.hi_bits : plan.hi_bits + len(zs_grad)]
        own_out, *outs = refs[plan.hi_bits + len(zs_grad) : -1]
        total = refs[-1]
        for tile in range(2 * pairs):
            total[tile] = steps[0][tile]
            for step in range(1, plan.hi_bits):
                add_spread(total, (tile,), 0, steps[step][tile], 1 << step)
            own_out[tile] = total[tile, pl.ds(0, rows)]
            for index, partner in enumerate(plan.partners):
                outs[index][tile] = ins[index][tile]
                part = total[tile, pl.ds((index + 1) * rows, rows)]
                add_spread(outs[index], (tile,), 0, part, plan.rows(partner) // rows)

    outs = [struct(2 * pairs, rows, LANES)] + [struct(*a.shape) for a in zs_grad]
    own, *zs_out = call(
        kernel,
        [*group_grads, *zs_grad],
        outs,
        scratch=[pltpu.VMEM((2 * pairs, BLOCK, LANES), F32)],
    )
    return own, zs_out


def spread_pair(plan, pairs, own_grad, returned, keep, send):
    top = plan.lo_bits - 1

    def kernel(own, *refs):
        back = refs[: len(returned)]
        keep_in, send_in, keep_out, send_out, *totals = refs[len(returned) :]
        half = BLOCK // 2
        for tile in range(2 * pairs):
            above = own[tile]
            for level in range(top, 0, -1):
                total = totals[level - 1]
                parts = [
                    back[index][tile]
                    for index, partner in enumerate(plan.partners)
                    if plan.level(partner) == level
                ]
                total[tile] = sum(parts[1:], parts[0])
                add_spread(total, (tile,), 0, above, 2)
                above = total[tile]
            keep_out[tile] = keep_in[tile]
            add_spread(keep_out, (tile,), 0, above[:half], 2)
            send_out[tile] = send_in[tile]
            add_spread(send_out, (tile,), 0, above[half:], 2)

    return call(
        kernel,
        [own_grad, *returned, keep, send],
        [struct(2 * pairs, BLOCK, LANES)] * 2,
        scratch=[
            pltpu.VMEM((2 * pairs, BLOCK >> index, LANES), F32) for index in range(top)
        ],
    )


def unpack(first_pairs, counts, kept, features, scalar):
    chunks = len(counts)

    def kernel(bit, *refs):
        ins = refs[: 4 * chunks]
        outs = refs[4 * chunks :]
        for index, (first, pairs) in enumerate(zip(first_pairs, counts)):
            for pair in range(pairs):
                column = (first + pair) * LANES
                mine = bit[0] * (features // 2) + column
                theirs = (1 - bit[0]) * (features // 2) + column
                for group in range(2):
                    for which in range(2):
                        out = outs[2 * group + which]
                        for source, place in ((0, mine), (1, theirs)):
                            array = ins[4 * index + 2 * group + source]
                            place = pl.ds(pl.multiple_of(place, LANES), LANES)
                            out[:, place] = array[which * pairs + pair]

    flat = [array for chunk in kept for array in chunk]
    return call(kernel, flat, [struct(BLOCK, features)] * 4, scalar=scalar)


def on_device(queries, keys, values, cotangent):
    features = queries.shape[1]
    assert queries.shape[0] == BLOCK
    plan = Plan(
        lax.axis_size("seqlo").bit_length() - 1, lax.axis_size("seqhi").bit_length() - 1
    )
    scalar = (lax.axis_index("seqlo") % 2).astype(jnp.int32).reshape(1)
    counts = CHUNKS
    firsts = [sum(counts[:index]) for index in range(len(counts))]
    packed = pack(firsts, counts, [queries, keys, values, cotangent], scalar)
    kept = []
    for pairs, send_kv, send_qg, mine_kv, mine_qg in zip(counts, *packed):
        kv = exchange(send_kv, 1)
        send_qg, kv = lax.optimization_barrier((send_qg, kv))
        qg = exchange(send_qg, 1)
        coarse = coarsen_pair(plan, pairs, mine_kv, kv)
        zs = [
            exchange(coarse[plan.level(partner) - 1], 2 * partner)
            for partner in plan.partners
        ]
        group, turned = coarsen_group(plan, pairs, coarse[-1], zs, mine_qg, qg)
        rs = [None] * plan.hi_bits
        for step in range(plan.hi_bits - 1, -1, -1):
            parts = [group[step]]
            for source, row, rows in plan.payload[step][1:]:
                parts.append(rs[source][:, row : row + rows])
            rs[step] = exchange(jnp.concatenate(parts, axis=1), 1 << plan.lo_bits + step)
        og_keep, og_send, kv_keep, kv_send, *grads = attention(
            plan, pairs, [mine_kv, kv, turned, *zs, *rs]
        )
        og_back = exchange(og_send, 1)
        zs_grad = grads[: len(zs)]
        rs_grad = grads[len(zs) :]
        group_grads = []
        for step in range(plan.hi_bits):
            back = exchange(rs_grad[step], 1 << plan.lo_bits + step)
            filled = BLOCK >> step
            group_grads.append(back[:, :filled])
            for source, row, rows in plan.payload[step][1:]:
                rs_grad[source] = (
                    rs_grad[source].at[:, row : row + rows].add(back[:, filled : filled + rows])
                )
                filled += rows
        own_grad, zs_grad = spread_group(plan, pairs, group_grads, zs_grad)
        returned = [
            exchange(grad, 2 * partner) for partner, grad in zip(plan.partners, zs_grad)
        ]
        kv_keep, kv_send = spread_pair(plan, pairs, own_grad, returned, kv_keep, kv_send)
        kv_back = exchange(kv_send, 1)
        kept.append((og_keep, og_back, kv_keep, kv_back))
    return tuple(unpack(firsts, counts, kept, features, scalar))


def solution(mesh):
    spec = P(AXES, None)
    return jax.shard_map(
        on_device,
        mesh=mesh,
        in_specs=(spec,) * 4,
        out_specs=(spec,) * 4,
        check_vma=False,
    )
```

```python
import math

import jax
import jax.numpy as jnp
from jax import lax
from jax.experimental import pallas as pl
from jax.experimental.pallas import tpu as pltpu
from jax.sharding import PartitionSpec as P

HEADS = 12
BLOCK = 128
HEAD_DIM = 64
LANES = 2 * HEAD_DIM
AXES = ("seqhi", "seqlo")
CHUNKS = (1, 1, 1)
VMEM_LIMIT = 20 * 1024 * 1024
F32 = jnp.float32
BF16 = jnp.bfloat16
LOG2_E = 1.0 / math.log(2.0)
SCALE = 1.0 / math.sqrt(HEAD_DIM)


def struct(*shape):
    return jax.ShapeDtypeStruct(shape, F32)


def call(kernel, operands, outs, scratch=(), scalar=None, flops=0, exps=0, where=None):
    vmem = pl.BlockSpec(memory_space=pltpu.VMEM)
    smem = pl.BlockSpec(memory_space=pltpu.SMEM)
    in_specs = [pl.BlockSpec(memory_space=where) if where else vmem] * len(operands)
    if scalar is not None:
        operands = [scalar, *operands]
        in_specs = [smem, *in_specs]
    moved = sum(4 * math.prod(a.shape) for a in [*operands, *outs])
    return pl.pallas_call(
        kernel,
        out_shape=list(outs),
        in_specs=in_specs,
        out_specs=[vmem] * len(outs),
        scratch_shapes=list(scratch),
        compiler_params=pltpu.CompilerParams(vmem_limit_bytes=VMEM_LIMIT),
        cost_estimate=pl.CostEstimate(
            flops=flops, bytes_accessed=moved, transcendentals=exps
        ),
    )(*operands)


def exchange(value, offset):
    count = lax.axis_size(AXES)
    return lax.ppermute(value, AXES, [(i, i ^ offset) for i in range(count)])


def mean_rows(ref, lead, first, count, factor):
    total = None
    for step in range(factor):
        rows = pl.ds(first + step, count, stride=factor)
        part = ref[(*lead, rows, slice(None))]
        total = part if total is None else total + part
    return total * (1.0 / factor)


def add_spread(ref, lead, first, value, factor):
    count = value.shape[0]
    value = value * (1.0 / factor)
    for step in range(factor):
        rows = pl.ds(first + step, count, stride=factor)
        place = (*lead, rows, slice(None))
        ref[place] = ref[place] + value


class Tree:
    def __init__(self, bits, first_bit):
        self.bits = bits
        self.first_bit = first_bit
        self.held = {}
        self.payload = {}
        for step in range(bits - 1, -1, -1):
            rows = BLOCK >> step
            payload = []
            fresh = {step: [(step, 0, rows)]}
            for level in range(step + 1, bits):
                for piece in self.held[level]:
                    payload.append(piece)
                    fresh.setdefault(level, []).append((step, rows, piece[2]))
                    rows += piece[2]
            self.payload[step] = payload
            for level, pieces in fresh.items():
                self.held[level] = self.held.get(level, []) + pieces

    def gather(self, own):
        arrived = [None] * self.bits
        for step in range(self.bits - 1, -1, -1):
            parts = [own[step]]
            for source, row, rows in self.payload[step]:
                parts.append(arrived[source][:, row : row + rows])
            sent = jnp.concatenate(parts, axis=1) if len(parts) > 1 else own[step]
            arrived[step] = exchange(sent, 1 << self.first_bit + step)
        return arrived

    def scatter(self, grads):
        grads = list(grads)
        returned = []
        for step in range(self.bits):
            back = exchange(grads[step], 1 << self.first_bit + step)
            returned.append(back)
            filled = BLOCK >> step
            for source, row, rows in self.payload[step]:
                grads[source] = (
                    grads[source].at[:, row : row + rows].add(back[:, filled : filled + rows])
                )
                filled += rows
        return returned


def split(value):
    high = value.astype(BF16).astype(F32)
    return high, value - high


def halves_by_head(value):
    high, low = split(value)
    first = lax.broadcasted_iota(jnp.int32, value.shape, 1) < HEAD_DIM
    one = jnp.where(first, high, pltpu.roll(low, HEAD_DIM, 1))
    two = jnp.where(first, pltpu.roll(high, HEAD_DIM, 1), low)
    return one.astype(BF16), two.astype(BF16)


def dot(lhs, rhs, dims):
    return lax.dot_general(lhs, rhs, (dims, ((), ())), preferred_element_type=F32)


NN = ((1,), (0,))
NT = ((1,), (1,))
TN = ((0,), (0,))


def attention(lo, hi, pairs, operands):
    mine, key_value, turned, *rest = operands
    sets = []
    for tree, first in ((lo, 0), (hi, lo.bits)):
        for level in range(tree.bits):
            for step, row, rows in tree.held[level]:
                sets.append((tree.first_bit + level, first + step, row, rows))
    total = 2 * BLOCK + sum(s[3] for s in sets)
    segment = BLOCK
    segments = total // segment
    levels = [0, 0]
    filled = 0
    for level, _, _, rows in sets:
        if filled == 0:
            levels.append(level)
        filled = (filled + rows) % segment
    queries_count = 2 * BLOCK

    def kernel(mine_in, kv_in, qg_in, *refs):
        rest_in = refs[: len(rest)]
        outs = refs[len(rest) :]
        og_keep, og_send, kv_keep, kv_send = outs[:4]
        rest_out = outs[4 : 4 + len(rest)]
        s_ref, eh_ref, el_ref, dh_ref, dl_ref, kc_ref, vc_ref = outs[4 + len(rest) :]

        def one_pair(pair):
            def gathered(which):
                tile = which * pairs + pair
                parts = [mine_in[tile], kv_in[tile]]
                for _, index, row, rows in sets:
                    parts.append(rest_in[index][tile, pl.ds(row, rows), :])
                return jnp.concatenate(parts, axis=0)

            key_halves = halves_by_head(gathered(0))
            value_halves = halves_by_head(gathered(1))
            for head in range(2):
                kc_ref[head] = key_halves[head]
                vc_ref[head] = value_halves[head]
            query_t = qg_in[pair]
            grad_t = qg_in[pairs + pair]
            out_t = []
            query_grad_t = []
            key_grads = [[], []]
            for head in range(2):
                part = slice(head * HEAD_DIM, (head + 1) * HEAD_DIM)
                qh, ql = split(query_t[part])
                q_rows = jnp.concatenate([qh, ql], axis=0).astype(BF16)
                q_four = jnp.concatenate([qh, qh, ql, ql], axis=0).astype(BF16)
                highest = None
                for index in range(segments):
                    rows = pl.ds(index * segment, segment)
                    half = kc_ref[head, rows, :]
                    s = dot(jnp.concatenate([half, half], axis=1), q_four, NN)
                    s = s + float(levels[index]) if levels[index] else s
                    s_ref[rows, :] = s
                    top = jnp.max(s.reshape(segment // 8, 8, queries_count), axis=0)
                    highest = top if highest is None else jnp.maximum(highest, top)
                highest = jnp.max(highest, axis=0, keepdims=True)
                sums = None
                for index in range(segments):
                    rows = pl.ds(index * segment, segment)
                    e = jnp.exp2(s_ref[rows, :] - highest)
                    s_ref[rows, :] = e
                    eh = e.astype(BF16)
                    eh_ref[rows, :] = eh
                    el_ref[rows, :] = (e - eh.astype(F32)).astype(BF16)
                    part_sum = jnp.sum(e.reshape(segment // 8, 8, queries_count), axis=0)
                    sums = part_sum if sums is None else sums + part_sum
                inverse = 1.0 / jnp.sum(sums, axis=0, keepdims=True)
                vc = vc_ref[head]
                o = dot(vc, eh_ref[...], TN) + dot(vc, el_ref[...], TN)
                o = (o[:HEAD_DIM] + o[HEAD_DIM:]) * inverse
                out_t.append(o)
                g_scaled = grad_t[part] * inverse
                gh, gl = split(g_scaled)
                g_rows = jnp.concatenate([gh, gl], axis=0).astype(BF16)
                g_four = jnp.concatenate([gh, gh, gl, gl], axis=0).astype(BF16)
                row_dot = jnp.sum(o * g_scaled, axis=0, keepdims=True)
                for index in range(segments):
                    rows = pl.ds(index * segment, segment)
                    half = vc_ref[head, rows, :]
                    dp = dot(jnp.concatenate([half, half], axis=1), g_four, NN)
                    ds = s_ref[rows, :] * (dp - row_dot)
                    dh = ds.astype(BF16)
                    dh_ref[rows, :] = dh
                    dl_ref[rows, :] = (ds - dh.astype(F32)).astype(BF16)
                kc = kc_ref[head]
                dq = dot(kc, dh_ref[...], TN) + dot(kc, dl_ref[...], TN)
                query_grad_t.append((dq[:HEAD_DIM] + dq[HEAD_DIM:]) * SCALE)
                dk = dot(dh_ref[...], q_rows, NT) + dot(dl_ref[...], q_rows, NT)
                key_grads[0].append(dk)
                dv = dot(eh_ref[...], g_rows, NT) + dot(el_ref[...], g_rows, NT)
                key_grads[1].append(dv)
            for which, parts in enumerate((out_t, query_grad_t)):
                both = jnp.concatenate(parts, axis=0).T
                og_keep[which * pairs + pair] = both[:BLOCK]
                og_send[which * pairs + pair] = both[BLOCK:]
            for which in range(2):
                one, two = key_grads[which]
                first = lax.broadcasted_iota(jnp.int32, one.shape, 1) < HEAD_DIM
                both = jnp.where(
                    first,
                    one + pltpu.roll(one, HEAD_DIM, 1),
                    two + pltpu.roll(two, HEAD_DIM, 1),
                )
                if which == 0:
                    both = both * (1.0 / LOG2_E)
                tile = which * pairs + pair
                kv_keep[tile] = both[:BLOCK]
                kv_send[tile] = both[BLOCK : 2 * BLOCK]
                filled = 2 * BLOCK
                for _, index, row, rows in sets:
                    rest_out[index][tile, pl.ds(row, rows), :] = both[
                        filled : filled + rows
                    ]
                    filled += rows

        if pairs == 1:
            one_pair(0)
        else:
            pl.loop(0, pairs)(one_pair)

    block = struct(2 * pairs, BLOCK, LANES)
    outs = [block] * 4 + [struct(*a.shape) for a in rest]
    flops = 2 * 6 * 4 * pairs * 2 * total * queries_count * HEAD_DIM
    return call(
        kernel,
        operands,
        outs,
        scratch=[
            pltpu.VMEM((total, queries_count), F32),
            pltpu.VMEM((total, queries_count), BF16),
            pltpu.VMEM((total, queries_count), BF16),
            pltpu.VMEM((total, queries_count), BF16),
            pltpu.VMEM((total, queries_count), BF16),
            pltpu.VMEM((2, total, LANES), BF16),
            pltpu.VMEM((2, total, LANES), BF16),
        ],
        flops=flops,
        exps=pairs * 2 * total * queries_count,
    )


def pack(firsts, counts, operands, scalar):
    chunks = len(counts)
    shapes = [struct(2 * pairs, BLOCK, LANES) for pairs in counts]
    outs = shapes + [struct(2 * sum(counts), BLOCK, LANES)] + shapes * 2
    moves = []
    for group, arrays, theirs, out in (
        (0, (1, 2), True, 0),
        (1, (0, 3), True, chunks),
        (2, (1, 2), False, chunks + 1),
        (3, (0, 3), False, 2 * chunks + 1),
    ):
        for index, (first, pairs) in enumerate(zip(firsts, counts)):
            for tile in range(2 * pairs):
                column = (first + tile % pairs) * LANES
                place = (out, 2 * first + tile) if group == 1 else (out + index, tile)
                moves.append((arrays[tile // pairs], theirs, column, *place))

    def kernel(bit, *refs):
        ins, sems = refs[: len(operands)], refs[-1]
        results = refs[len(operands) : -1]
        started = []
        for operand, theirs, column, out, tile in moves:
            side = 1 - bit[0] if theirs else bit[0]
            column = side * (ins[operand].shape[1] // 2) + column
            column = pl.ds(pl.multiple_of(column, LANES), LANES)
            copy = pltpu.make_async_copy(
                ins[operand].at[:, column], results[out].at[tile], sems.at[len(started)]
            )
            copy.start()
            started.append(copy)
        for copy in started:
            copy.wait()

    outs = call(
        kernel,
        operands,
        outs,
        scratch=[pltpu.SemaphoreType.DMA((len(moves),))],
        scalar=scalar,
        where=pl.ANY,
    )
    return outs[:chunks], outs[chunks], outs[chunks + 1 : 2 * chunks + 1], outs[2 * chunks + 1 :]


def coarsen_pair(lo, pairs, mine, received):
    def kernel(own, got, *outs):
        half = BLOCK // 2
        for tile in range(2 * pairs):
            outs[0][tile, :half] = mean_rows(own, (tile,), 0, half, 2)
            outs[0][tile, half:] = mean_rows(got, (tile,), 0, half, 2)
            for index in range(1, lo.bits + 1):
                outs[index][tile] = mean_rows(
                    outs[index - 1], (tile,), 0, BLOCK >> index, 2
                )

    outs = [struct(2 * pairs, BLOCK >> index, LANES) for index in range(lo.bits + 1)]
    return call(kernel, [mine, received], outs)


def group_pieces(lo):
    pieces = []
    filled = BLOCK >> lo.bits
    for level in range(lo.bits):
        factor = 1 << lo.bits - level
        for step, row, rows in lo.held[level]:
            pieces.append((step, row, rows, factor, filled))
            filled += rows // factor
    return pieces


def coarsen_group(lo, hi, pairs, own, arrived):
    pieces = group_pieces(lo)

    def kernel(own_in, *refs):
        ins = refs[: lo.bits]
        outs = refs[lo.bits :]
        for tile in range(2 * pairs):
            outs[0][tile, pl.ds(0, BLOCK >> lo.bits)] = own_in[tile]
            for step, row, rows, factor, place in pieces:
                count = rows // factor
                outs[0][tile, pl.ds(place, count)] = mean_rows(
                    ins[step], (tile,), row, count, factor
                )
            for step in range(1, hi.bits):
                outs[step][tile] = mean_rows(
                    outs[step - 1], (tile,), 0, BLOCK >> step, 2
                )

    outs = [struct(2 * pairs, BLOCK >> step, LANES) for step in range(hi.bits)]
    return call(kernel, [own, *arrived], outs)


def turn(pairs, mine, received):
    def kernel(own, got, turned):
        for tile in range(2 * pairs):
            both = jnp.concatenate([own[tile], got[tile]], axis=0).T
            turned[tile] = both * (SCALE * LOG2_E) if tile < pairs else both

    return call(kernel, [mine, received], [struct(2 * pairs, LANES, 2 * BLOCK)])[0]


def spread_group(lo, hi, pairs, group_grads, grads):
    pieces = group_pieces(lo)
    own_rows = BLOCK >> lo.bits

    def kernel(*refs):
        steps = refs[: hi.bits]
        ins = refs[hi.bits : hi.bits + lo.bits]
        own_out, *outs = refs[hi.bits + lo.bits : -1]
        total = refs[-1]
        for tile in range(2 * pairs):
            total[tile] = steps[0][tile, pl.ds(0, BLOCK)]
            for step in range(1, hi.bits):
                above = steps[step][tile, pl.ds(0, BLOCK >> step)]
                add_spread(total, (tile,), 0, above, 1 << step)
            own_out[tile] = total[tile, pl.ds(0, own_rows)]
            for out, value in zip(outs, ins):
                out[tile] = value[tile]
            for step, row, rows, factor, place in pieces:
                part = total[tile, pl.ds(place, rows // factor)]
                add_spread(outs[step], (tile,), row, part, factor)

    outs = [struct(2 * pairs, own_rows, LANES)] + [struct(*a.shape) for a in grads]
    own, *grads = call(
        kernel,
        [*group_grads, *grads],
        outs,
        scratch=[pltpu.VMEM((2 * pairs, BLOCK, LANES), F32)],
    )
    return own, grads


def spread_pair(lo, pairs, own_grad, returned, keep, send):
    def kernel(own, *refs):
        back = refs[: lo.bits]
        keep_in, send_in, keep_out, send_out, *totals = refs[lo.bits :]
        half = BLOCK // 2
        for tile in range(2 * pairs):
            above = own[tile]
            for step in range(lo.bits - 1, -1, -1):
                total = totals[step]
                total[tile] = back[step][tile, pl.ds(0, BLOCK >> step)]
                add_spread(total, (tile,), 0, above, 2)
                above = total[tile]
            keep_out[tile] = keep_in[tile]
            add_spread(keep_out, (tile,), 0, above[:half], 2)
            send_out[tile] = send_in[tile]
            add_spread(send_out, (tile,), 0, above[half:], 2)

    return call(
        kernel,
        [own_grad, *returned, keep, send],
        [struct(2 * pairs, BLOCK, LANES)] * 2,
        scratch=[
            pltpu.VMEM((2 * pairs, BLOCK >> step, LANES), F32) for step in range(lo.bits)
        ],
    )


def unpack(firsts, counts, forward, kept, features, scalar):
    ins = [forward]
    places = []
    for index, (first, pairs) in enumerate(zip(firsts, counts)):
        for array, group, mine in zip(kept[index], (0, 2, 2), (True, True, False)):
            for tile in range(2 * pairs):
                column = (first + tile % pairs) * LANES
                places.append((len(ins), tile, group + tile // pairs, column, mine))
            ins.append(array)
        for tile in range(2 * pairs):
            column = (first + tile % pairs) * LANES
            places.append((0, 2 * first + tile, tile // pairs, column, False))

    def kernel(bit, *refs):
        outs = refs[len(ins) :]
        for index, tile, out, column, mine in places:
            side = bit[0] if mine else 1 - bit[0]
            column = pl.multiple_of(side * (features // 2) + column, LANES)
            outs[out][:, pl.ds(column, LANES)] = refs[index][tile]

    return call(kernel, ins, [struct(BLOCK, features)] * 4, scalar=scalar)


def on_device(queries, keys, values, cotangent):
    features = queries.shape[1]
    assert queries.shape[0] == BLOCK
    lo_bits = lax.axis_size("seqlo").bit_length() - 1
    lo = Tree(lo_bits - 1, 1)
    hi = Tree(lax.axis_size("seqhi").bit_length() - 1, lo_bits)
    scalar = (lax.axis_index("seqlo") % 2).astype(jnp.int32).reshape(1)
    counts = CHUNKS
    firsts = [sum(counts[:index]) for index in range(len(counts))]
    arrays = [
        pltpu.with_memory_space_constraint(array, pltpu.HBM)
        for array in (queries, keys, values, cotangent)
    ]
    send_kv, send_qg, mine_kv, mine_qg = pack(firsts, counts, arrays, scalar)
    chunks = range(len(counts))
    kv = [exchange(array, 1) for array in send_kv]
    send_qg, kv[-1] = lax.optimization_barrier((send_qg, kv[-1]))
    qg = exchange(send_qg, 1)
    coarse = [coarsen_pair(lo, counts[i], mine_kv[i], kv[i]) for i in chunks]
    gathered = [lo.gather(coarse[i][:-1]) for i in chunks]
    qg, gathered[-1] = lax.optimization_barrier((qg, gathered[-1]))
    forward = []
    kept = []
    for index in chunks:
        pairs = counts[index]
        first = 2 * firsts[index]
        turned = turn(pairs, mine_qg[index], qg[first : first + 2 * pairs])
        zs = gathered[index]
        group = coarsen_group(lo, hi, pairs, coarse[index][-1], zs)
        rs = hi.gather(group)
        og_keep, og_send, kv_keep, kv_send, *grads = attention(
            lo, hi, pairs, [mine_kv[index], kv[index], turned, *zs, *rs]
        )
        forward.append(og_send)
        group_grads = hi.scatter(grads[lo.bits :])
        own_grad, grads = spread_group(lo, hi, pairs, group_grads, grads[: lo.bits])
        returned = lo.scatter(grads)
        kv_keep, kv_send = spread_pair(lo, pairs, own_grad, returned, kv_keep, kv_send)
        kept.append((og_keep, kv_keep, exchange(kv_send, 1)))
    og_back = exchange(jnp.concatenate(forward, axis=0), 1)
    return tuple(unpack(firsts, counts, og_back, kept, features, scalar))


def solution(mesh):
    spec = P(AXES, None)
    return jax.shard_map(
        on_device,
        mesh=mesh,
        in_specs=(spec,) * 4,
        out_specs=(spec,) * 4,
        check_vma=False,
    )
```

```python
import math

import jax
import jax.numpy as jnp
from jax import lax
from jax.experimental import pallas as pl
from jax.experimental.pallas import tpu as pltpu
from jax.sharding import PartitionSpec as P

HEADS = 12
BLOCK = 128
HEAD_DIM = 64
LANES = 2 * HEAD_DIM
AXES = ("seqhi", "seqlo")
CHUNKS = (1, 1, 1)
VMEM_LIMIT = 20 * 1024 * 1024
F32 = jnp.float32
BF16 = jnp.bfloat16
LOG2_E = 1.0 / math.log(2.0)
SCALE = 1.0 / math.sqrt(HEAD_DIM)


def struct(*shape):
    return jax.ShapeDtypeStruct(shape, F32)


def call(kernel, operands, outs, scratch=(), scalar=None, flops=0, exps=0, where=None):
    vmem = pl.BlockSpec(memory_space=pltpu.VMEM)
    smem = pl.BlockSpec(memory_space=pltpu.SMEM)
    in_specs = [pl.BlockSpec(memory_space=where) if where else vmem] * len(operands)
    if scalar is not None:
        operands = [scalar, *operands]
        in_specs = [smem, *in_specs]
    moved = sum(4 * math.prod(a.shape) for a in [*operands, *outs])
    return pl.pallas_call(
        kernel,
        out_shape=list(outs),
        in_specs=in_specs,
        out_specs=[vmem] * len(outs),
        scratch_shapes=list(scratch),
        compiler_params=pltpu.CompilerParams(vmem_limit_bytes=VMEM_LIMIT),
        cost_estimate=pl.CostEstimate(
            flops=flops, bytes_accessed=moved, transcendentals=exps
        ),
    )(*operands)


def exchange(value, offset):
    count = lax.axis_size(AXES)
    return lax.ppermute(value, AXES, [(i, i ^ offset) for i in range(count)])


def ordered(value, after):
    return value if after is None else lax.optimization_barrier((value, after))[0]


def mean_rows(ref, lead, first, count, factor):
    total = None
    for step in range(factor):
        rows = pl.ds(first + step, count, stride=factor)
        part = ref[(*lead, rows, slice(None))]
        total = part if total is None else total + part
    return total * (1.0 / factor)


def add_spread(ref, lead, first, value, factor):
    count = value.shape[0]
    value = value * (1.0 / factor)
    for step in range(factor):
        rows = pl.ds(first + step, count, stride=factor)
        place = (*lead, rows, slice(None))
        ref[place] = ref[place] + value


class Tree:
    def __init__(self, bits, first_bit):
        self.bits = bits
        self.first_bit = first_bit
        self.held = {}
        self.payload = {}
        for step in range(bits - 1, -1, -1):
            rows = BLOCK >> step
            payload = []
            fresh = {step: [(step, 0, rows)]}
            for level in range(step + 1, bits):
                for piece in self.held[level]:
                    payload.append(piece)
                    fresh.setdefault(level, []).append((step, rows, piece[2]))
                    rows += piece[2]
            self.payload[step] = payload
            for level, pieces in fresh.items():
                self.held[level] = self.held.get(level, []) + pieces

    def gather(self, own, after=None):
        arrived = [None] * self.bits
        for step in range(self.bits - 1, -1, -1):
            parts = [own[step]]
            for source, row, rows in self.payload[step]:
                parts.append(arrived[source][:, row : row + rows])
            sent = jnp.concatenate(parts, axis=1) if len(parts) > 1 else own[step]
            if step == 0:
                sent = ordered(sent, after)
            arrived[step] = exchange(sent, 1 << self.first_bit + step)
        return arrived

    def scatter(self, grads, after=None):
        grads = list(grads)
        grads[0] = ordered(grads[0], after)
        returned = []
        for step in range(self.bits):
            back = exchange(grads[step], 1 << self.first_bit + step)
            returned.append(back)
            filled = BLOCK >> step
            for source, row, rows in self.payload[step]:
                grads[source] = (
                    grads[source].at[:, row : row + rows].add(back[:, filled : filled + rows])
                )
                filled += rows
        return returned


def split(value):
    high = value.astype(BF16).astype(F32)
    return high, value - high


def halves_by_head(value):
    high, low = split(value)
    first = lax.broadcasted_iota(jnp.int32, value.shape, 1) < HEAD_DIM
    one = jnp.where(first, high, pltpu.roll(low, HEAD_DIM, 1))
    two = jnp.where(first, pltpu.roll(high, HEAD_DIM, 1), low)
    return one.astype(BF16), two.astype(BF16)


def dot(lhs, rhs, dims):
    return lax.dot_general(lhs, rhs, (dims, ((), ())), preferred_element_type=F32)


NN = ((1,), (0,))
NT = ((1,), (1,))
TN = ((0,), (0,))


def attention(lo, hi, pairs, operands):
    mine, key_value, turned, *rest = operands
    sets = []
    for tree, first in ((lo, 0), (hi, lo.bits)):
        for level in range(tree.bits):
            for step, row, rows in tree.held[level]:
                sets.append((tree.first_bit + level, first + step, row, rows))
    total = 2 * BLOCK + sum(s[3] for s in sets)
    segment = BLOCK
    segments = total // segment
    levels = [0, 0]
    filled = 0
    for level, _, _, rows in sets:
        if filled == 0:
            levels.append(level)
        filled = (filled + rows) % segment
    queries_count = 2 * BLOCK

    def kernel(mine_in, kv_in, qg_in, *refs):
        rest_in = refs[: len(rest)]
        outs = refs[len(rest) :]
        og_keep, og_send, kv_keep, kv_send = outs[:4]
        rest_out = outs[4 : 4 + len(rest)]
        s_ref, eh_ref, el_ref, dh_ref, dl_ref, kc_ref, vc_ref = outs[4 + len(rest) :]

        def one_pair(pair):
            def gathered(which):
                tile = which * pairs + pair
                parts = [mine_in[tile], kv_in[tile]]
                for _, index, row, rows in sets:
                    parts.append(rest_in[index][tile, pl.ds(row, rows), :])
                return jnp.concatenate(parts, axis=0)

            key_halves = halves_by_head(gathered(0))
            value_halves = halves_by_head(gathered(1))
            for head in range(2):
                kc_ref[head] = key_halves[head]
                vc_ref[head] = value_halves[head]
            query_t = qg_in[pair]
            grad_t = qg_in[pairs + pair]
            out_t = []
            query_grad_t = []
            key_grads = [[], []]
            for head in range(2):
                part = slice(head * HEAD_DIM, (head + 1) * HEAD_DIM)
                qh, ql = split(query_t[part])
                q_rows = jnp.concatenate([qh, ql], axis=0).astype(BF16)
                q_four = jnp.concatenate([qh, qh, ql, ql], axis=0).astype(BF16)
                highest = None
                for index in range(segments):
                    rows = pl.ds(index * segment, segment)
                    half = kc_ref[head, rows, :]
                    s = dot(jnp.concatenate([half, half], axis=1), q_four, NN)
                    s = s + float(levels[index]) if levels[index] else s
                    s_ref[rows, :] = s
                    top = jnp.max(s.reshape(segment // 8, 8, queries_count), axis=0)
                    highest = top if highest is None else jnp.maximum(highest, top)
                highest = jnp.max(highest, axis=0, keepdims=True)
                sums = None
                for index in range(segments):
                    rows = pl.ds(index * segment, segment)
                    e = jnp.exp2(s_ref[rows, :] - highest)
                    s_ref[rows, :] = e
                    eh = e.astype(BF16)
                    eh_ref[rows, :] = eh
                    el_ref[rows, :] = (e - eh.astype(F32)).astype(BF16)
                    part_sum = jnp.sum(e.reshape(segment // 8, 8, queries_count), axis=0)
                    sums = part_sum if sums is None else sums + part_sum
                inverse = 1.0 / jnp.sum(sums, axis=0, keepdims=True)
                vc = vc_ref[head]
                o = dot(vc, eh_ref[...], TN) + dot(vc, el_ref[...], TN)
                o = (o[:HEAD_DIM] + o[HEAD_DIM:]) * inverse
                out_t.append(o)
                g_scaled = grad_t[part] * inverse
                gh, gl = split(g_scaled)
                g_rows = jnp.concatenate([gh, gl], axis=0).astype(BF16)
                g_four = jnp.concatenate([gh, gh, gl, gl], axis=0).astype(BF16)
                row_dot = jnp.sum(o * g_scaled, axis=0, keepdims=True)
                for index in range(segments):
                    rows = pl.ds(index * segment, segment)
                    half = vc_ref[head, rows, :]
                    dp = dot(jnp.concatenate([half, half], axis=1), g_four, NN)
                    ds = s_ref[rows, :] * (dp - row_dot)
                    dh = ds.astype(BF16)
                    dh_ref[rows, :] = dh
                    dl_ref[rows, :] = (ds - dh.astype(F32)).astype(BF16)
                kc = kc_ref[head]
                dq = dot(kc, dh_ref[...], TN) + dot(kc, dl_ref[...], TN)
                query_grad_t.append((dq[:HEAD_DIM] + dq[HEAD_DIM:]) * SCALE)
                dk = dot(dh_ref[...], q_rows, NT) + dot(dl_ref[...], q_rows, NT)
                key_grads[0].append(dk)
                dv = dot(eh_ref[...], g_rows, NT) + dot(el_ref[...], g_rows, NT)
                key_grads[1].append(dv)
            for which, parts in enumerate((out_t, query_grad_t)):
                both = jnp.concatenate(parts, axis=0).T
                og_keep[which * pairs + pair] = both[:BLOCK]
                og_send[which * pairs + pair] = both[BLOCK:]
            for which in range(2):
                one, two = key_grads[which]
                first = lax.broadcasted_iota(jnp.int32, one.shape, 1) < HEAD_DIM
                both = jnp.where(
                    first,
                    one + pltpu.roll(one, HEAD_DIM, 1),
                    two + pltpu.roll(two, HEAD_DIM, 1),
                )
                if which == 0:
                    both = both * (1.0 / LOG2_E)
                tile = which * pairs + pair
                kv_keep[tile] = both[:BLOCK]
                kv_send[tile] = both[BLOCK : 2 * BLOCK]
                filled = 2 * BLOCK
                for _, index, row, rows in sets:
                    rest_out[index][tile, pl.ds(row, rows), :] = both[
                        filled : filled + rows
                    ]
                    filled += rows

        if pairs == 1:
            one_pair(0)
        else:
            pl.loop(0, pairs)(one_pair)

    block = struct(2 * pairs, BLOCK, LANES)
    outs = [block] * 4 + [struct(*a.shape) for a in rest]
    flops = 2 * 6 * 4 * pairs * 2 * total * queries_count * HEAD_DIM
    return call(
        kernel,
        operands,
        outs,
        scratch=[
            pltpu.VMEM((total, queries_count), F32),
            pltpu.VMEM((total, queries_count), BF16),
            pltpu.VMEM((total, queries_count), BF16),
            pltpu.VMEM((total, queries_count), BF16),
            pltpu.VMEM((total, queries_count), BF16),
            pltpu.VMEM((2, total, LANES), BF16),
            pltpu.VMEM((2, total, LANES), BF16),
        ],
        flops=flops,
        exps=pairs * 2 * total * queries_count,
    )


def pack(firsts, counts, operands, scalar):
    chunks = len(counts)
    shapes = [struct(2 * pairs, BLOCK, LANES) for pairs in counts]
    outs = shapes + [struct(2 * sum(counts), BLOCK, LANES)] + shapes * 2
    moves = []
    for group, arrays, theirs, out in (
        (0, (1, 2), True, 0),
        (1, (0, 3), True, chunks),
        (2, (1, 2), False, chunks + 1),
        (3, (0, 3), False, 2 * chunks + 1),
    ):
        for index, (first, pairs) in enumerate(zip(firsts, counts)):
            for tile in range(2 * pairs):
                column = (first + tile % pairs) * LANES
                place = (out, 2 * first + tile) if group == 1 else (out + index, tile)
                moves.append((arrays[tile // pairs], theirs, column, *place))

    def kernel(bit, *refs):
        ins, sems = refs[: len(operands)], refs[-1]
        results = refs[len(operands) : -1]
        started = []
        for operand, theirs, column, out, tile in moves:
            side = 1 - bit[0] if theirs else bit[0]
            column = side * (ins[operand].shape[1] // 2) + column
            column = pl.ds(pl.multiple_of(column, LANES), LANES)
            copy = pltpu.make_async_copy(
                ins[operand].at[:, column], results[out].at[tile], sems.at[len(started)]
            )
            copy.start()
            started.append(copy)
        for copy in started:
            copy.wait()

    outs = call(
        kernel,
        operands,
        outs,
        scratch=[pltpu.SemaphoreType.DMA((len(moves),))],
        scalar=scalar,
        where=pl.ANY,
    )
    return outs[:chunks], outs[chunks], outs[chunks + 1 : 2 * chunks + 1], outs[2 * chunks + 1 :]


def coarsen_pair(lo, pairs, mine, received):
    def kernel(own, got, *outs):
        half = BLOCK // 2
        for tile in range(2 * pairs):
            outs[0][tile, :half] = mean_rows(own, (tile,), 0, half, 2)
            outs[0][tile, half:] = mean_rows(got, (tile,), 0, half, 2)
            for index in range(1, lo.bits + 1):
                outs[index][tile] = mean_rows(
                    outs[index - 1], (tile,), 0, BLOCK >> index, 2
                )

    outs = [struct(2 * pairs, BLOCK >> index, LANES) for index in range(lo.bits + 1)]
    return call(kernel, [mine, received], outs)


def group_pieces(lo):
    pieces = []
    filled = BLOCK >> lo.bits
    for level in range(lo.bits):
        factor = 1 << lo.bits - level
        for step, row, rows in lo.held[level]:
            pieces.append((step, row, rows, factor, filled))
            filled += rows // factor
    return pieces


def coarsen_group(lo, hi, pairs, own, arrived):
    pieces = group_pieces(lo)

    def kernel(own_in, *refs):
        ins = refs[: lo.bits]
        outs = refs[lo.bits :]
        for tile in range(2 * pairs):
            outs[0][tile, pl.ds(0, BLOCK >> lo.bits)] = own_in[tile]
            for step, row, rows, factor, place in pieces:
                count = rows // factor
                outs[0][tile, pl.ds(place, count)] = mean_rows(
                    ins[step], (tile,), row, count, factor
                )
            for step in range(1, hi.bits):
                outs[step][tile] = mean_rows(
                    outs[step - 1], (tile,), 0, BLOCK >> step, 2
                )

    outs = [struct(2 * pairs, BLOCK >> step, LANES) for step in range(hi.bits)]
    return call(kernel, [own, *arrived], outs)


def turn(pairs, mine, received):
    def kernel(own, got, turned):
        for tile in range(2 * pairs):
            both = jnp.concatenate([own[tile], got[tile]], axis=0).T
            turned[tile] = both * (SCALE * LOG2_E) if tile < pairs else both

    return call(kernel, [mine, received], [struct(2 * pairs, LANES, 2 * BLOCK)])[0]


def spread_group(lo, hi, pairs, group_grads, grads):
    pieces = group_pieces(lo)
    own_rows = BLOCK >> lo.bits

    def kernel(*refs):
        steps = refs[: hi.bits]
        ins = refs[hi.bits : hi.bits + lo.bits]
        own_out, *outs = refs[hi.bits + lo.bits : -1]
        total = refs[-1]
        for tile in range(2 * pairs):
            total[tile] = steps[0][tile, pl.ds(0, BLOCK)]
            for step in range(1, hi.bits):
                above = steps[step][tile, pl.ds(0, BLOCK >> step)]
                add_spread(total, (tile,), 0, above, 1 << step)
            own_out[tile] = total[tile, pl.ds(0, own_rows)]
            for out, value in zip(outs, ins):
                out[tile] = value[tile]
            for step, row, rows, factor, place in pieces:
                part = total[tile, pl.ds(place, rows // factor)]
                add_spread(outs[step], (tile,), row, part, factor)

    outs = [struct(2 * pairs, own_rows, LANES)] + [struct(*a.shape) for a in grads]
    own, *grads = call(
        kernel,
        [*group_grads, *grads],
        outs,
        scratch=[pltpu.VMEM((2 * pairs, BLOCK, LANES), F32)],
    )
    return own, grads


def spread_pair(lo, pairs, own_grad, returned, keep, send):
    def kernel(own, *refs):
        back = refs[: lo.bits]
        keep_in, send_in, keep_out, send_out, *totals = refs[lo.bits :]
        half = BLOCK // 2
        for tile in range(2 * pairs):
            above = own[tile]
            for step in range(lo.bits - 1, -1, -1):
                total = totals[step]
                total[tile] = back[step][tile, pl.ds(0, BLOCK >> step)]
                add_spread(total, (tile,), 0, above, 2)
                above = total[tile]
            keep_out[tile] = keep_in[tile]
            add_spread(keep_out, (tile,), 0, above[:half], 2)
            send_out[tile] = send_in[tile]
            add_spread(send_out, (tile,), 0, above[half:], 2)

    return call(
        kernel,
        [own_grad, *returned, keep, send],
        [struct(2 * pairs, BLOCK, LANES)] * 2,
        scratch=[
            pltpu.VMEM((2 * pairs, BLOCK >> step, LANES), F32) for step in range(lo.bits)
        ],
    )


def unpack(firsts, counts, forward, kept, features, scalar):
    ins = [forward]
    places = []
    for index, (first, pairs) in enumerate(zip(firsts, counts)):
        for array, group, mine in zip(kept[index], (0, 2, 2), (True, True, False)):
            for tile in range(2 * pairs):
                column = (first + tile % pairs) * LANES
                places.append((len(ins), tile, group + tile // pairs, column, mine))
            ins.append(array)
        for tile in range(2 * pairs):
            column = (first + tile % pairs) * LANES
            places.append((0, 2 * first + tile, tile // pairs, column, False))

    def kernel(bit, *refs):
        outs = refs[len(ins) :]
        for index, tile, out, column, mine in places:
            side = bit[0] if mine else 1 - bit[0]
            column = pl.multiple_of(side * (features // 2) + column, LANES)
            outs[out][:, pl.ds(column, LANES)] = refs[index][tile]

    return call(kernel, ins, [struct(BLOCK, features)] * 4, scalar=scalar)


def on_device(queries, keys, values, cotangent):
    features = queries.shape[1]
    assert queries.shape[0] == BLOCK
    lo_bits = lax.axis_size("seqlo").bit_length() - 1
    lo = Tree(lo_bits - 1, 1)
    hi = Tree(lax.axis_size("seqhi").bit_length() - 1, lo_bits)
    scalar = (lax.axis_index("seqlo") % 2).astype(jnp.int32).reshape(1)
    counts = CHUNKS
    firsts = [sum(counts[:index]) for index in range(len(counts))]
    arrays = [
        pltpu.with_memory_space_constraint(array, pltpu.HBM)
        for array in (queries, keys, values, cotangent)
    ]
    send_kv, send_qg, mine_kv, mine_qg = pack(firsts, counts, arrays, scalar)
    chunks = range(len(counts))
    kv = [exchange(array, 1) for array in send_kv]
    send_qg, kv[-1] = lax.optimization_barrier((send_qg, kv[-1]))
    qg = exchange(send_qg, 1)
    forward = []
    kept = []
    arrived, attended, spread, first_back = [], [], [], [None]
    for index in chunks:
        pairs = counts[index]
        first = 2 * firsts[index]
        earlier = index - 2
        turned = turn(pairs, mine_qg[index], qg[first : first + 2 * pairs])
        coarse = coarsen_pair(lo, pairs, mine_kv[index], kv[index])
        zs = lo.gather(coarse[:-1], arrived[earlier] if earlier >= 0 else None)
        if earlier >= 0:
            zs[0] = ordered(zs[0], attended[earlier])
        group = coarsen_group(lo, hi, pairs, coarse[-1], zs)
        rs = hi.gather(group)
        arrived.append(rs[-1])
        if earlier >= 0:
            turned = ordered(turned, spread[earlier])
        og_keep, og_send, kv_keep, kv_send, *grads = attention(
            lo, hi, pairs, [mine_kv[index], kv[index], turned, *zs, *rs]
        )
        attended.append(og_keep)
        forward.append(og_send)
        group_grads = hi.scatter(grads[lo.bits :])
        own_grad, grads = spread_group(lo, hi, pairs, group_grads, grads[: lo.bits])
        spread.append(own_grad)
        returned = lo.scatter(grads, first_back[-1])
        first_back.append(returned[0])
        kv_keep, kv_send = spread_pair(lo, pairs, own_grad, returned, kv_keep, kv_send)
        kept.append((og_keep, kv_keep, exchange(kv_send, 1)))
    og_back = exchange(jnp.concatenate(forward, axis=0), 1)
    return tuple(unpack(firsts, counts, og_back, kept, features, scalar))


def solution(mesh):
    spec = P(AXES, None)
    return jax.shard_map(
        on_device,
        mesh=mesh,
        in_specs=(spec,) * 4,
        out_specs=(spec,) * 4,
        check_vma=False,
    )
```

```python
import math

import jax
import jax.numpy as jnp
from jax import lax
from jax.experimental import pallas as pl
from jax.experimental.pallas import tpu as pltpu
from jax.sharding import PartitionSpec as P

HEADS = 12
BLOCK = 128
HEAD_DIM = 64
LANES = 2 * HEAD_DIM
AXES = ("seqhi", "seqlo")
CHUNKS = (1, 1, 1)
VMEM_LIMIT = 20 * 1024 * 1024
F32 = jnp.float32
BF16 = jnp.bfloat16
LOG2_E = 1.0 / math.log(2.0)
SCALE = 1.0 / math.sqrt(HEAD_DIM)


def struct(*shape):
    return jax.ShapeDtypeStruct(shape, F32)


def call(kernel, operands, outs, scratch=(), scalar=None, flops=0, exps=0, where=None):
    vmem = pl.BlockSpec(memory_space=pltpu.VMEM)
    smem = pl.BlockSpec(memory_space=pltpu.SMEM)
    in_specs = [pl.BlockSpec(memory_space=where) if where else vmem] * len(operands)
    if scalar is not None:
        operands = [scalar, *operands]
        in_specs = [smem, *in_specs]
    moved = sum(4 * math.prod(a.shape) for a in [*operands, *outs])
    return pl.pallas_call(
        kernel,
        out_shape=list(outs),
        in_specs=in_specs,
        out_specs=[vmem] * len(outs),
        scratch_shapes=list(scratch),
        compiler_params=pltpu.CompilerParams(vmem_limit_bytes=VMEM_LIMIT),
        cost_estimate=pl.CostEstimate(
            flops=flops, bytes_accessed=moved, transcendentals=exps
        ),
    )(*operands)


def exchange(value, offset):
    lo = lax.axis_size("seqlo")
    if offset < lo:
        axis, count = "seqlo", lo
    else:
        axis, count, offset = "seqhi", lax.axis_size("seqhi"), offset // lo
    groups = [[i, i ^ offset] for i in range(count) if not i & offset]
    both = lax.all_gather(value, axis, axis_index_groups=groups)
    bit = (lax.axis_index(axis) // offset) % 2
    return lax.dynamic_index_in_dim(both, 1 - bit, 0, keepdims=False)


def ordered(value, after):
    return value if after is None else lax.optimization_barrier((value, after))[0]


def mean_rows(ref, lead, first, count, factor):
    total = None
    for step in range(factor):
        rows = pl.ds(first + step, count, stride=factor)
        part = ref[(*lead, rows, slice(None))]
        total = part if total is None else total + part
    return total * (1.0 / factor)


def add_spread(ref, lead, first, value, factor):
    count = value.shape[0]
    value = value * (1.0 / factor)
    for step in range(factor):
        rows = pl.ds(first + step, count, stride=factor)
        place = (*lead, rows, slice(None))
        ref[place] = ref[place] + value


class Tree:
    def __init__(self, bits, first_bit):
        self.bits = bits
        self.first_bit = first_bit
        self.held = {}
        self.payload = {}
        for step in range(bits - 1, -1, -1):
            rows = BLOCK >> step
            payload = []
            fresh = {step: [(step, 0, rows)]}
            for level in range(step + 1, bits):
                for piece in self.held[level]:
                    payload.append(piece)
                    fresh.setdefault(level, []).append((step, rows, piece[2]))
                    rows += piece[2]
            self.payload[step] = payload
            for level, pieces in fresh.items():
                self.held[level] = self.held.get(level, []) + pieces

    def gather(self, own, after=None):
        arrived = [None] * self.bits
        for step in range(self.bits - 1, -1, -1):
            parts = [own[step]]
            for source, row, rows in self.payload[step]:
                parts.append(arrived[source][:, row : row + rows])
            sent = jnp.concatenate(parts, axis=1) if len(parts) > 1 else own[step]
            if step == 0:
                sent = ordered(sent, after)
            arrived[step] = exchange(sent, 1 << self.first_bit + step)
        return arrived

    def scatter(self, grads, after=None):
        grads = list(grads)
        grads[0] = ordered(grads[0], after)
        returned = []
        for step in range(self.bits):
            back = exchange(grads[step], 1 << self.first_bit + step)
            returned.append(back)
            filled = BLOCK >> step
            for source, row, rows in self.payload[step]:
                grads[source] = (
                    grads[source].at[:, row : row + rows].add(back[:, filled : filled + rows])
                )
                filled += rows
        return returned


def split(value):
    high = value.astype(BF16).astype(F32)
    return high, value - high


def halves_by_head(value):
    high, low = split(value)
    first = lax.broadcasted_iota(jnp.int32, value.shape, 1) < HEAD_DIM
    one = jnp.where(first, high, pltpu.roll(low, HEAD_DIM, 1))
    two = jnp.where(first, pltpu.roll(high, HEAD_DIM, 1), low)
    return one.astype(BF16), two.astype(BF16)


def dot(lhs, rhs, dims):
    return lax.dot_general(lhs, rhs, (dims, ((), ())), preferred_element_type=F32)


NN = ((1,), (0,))
NT = ((1,), (1,))
TN = ((0,), (0,))


def attention(lo, hi, pairs, operands):
    mine, key_value, turned, *rest = operands
    sets = []
    for tree, first in ((lo, 0), (hi, lo.bits)):
        for level in range(tree.bits):
            for step, row, rows in tree.held[level]:
                sets.append((tree.first_bit + level, first + step, row, rows))
    total = 2 * BLOCK + sum(s[3] for s in sets)
    segment = BLOCK
    segments = total // segment
    levels = [0, 0]
    filled = 0
    for level, _, _, rows in sets:
        if filled == 0:
            levels.append(level)
        filled = (filled + rows) % segment
    queries_count = 2 * BLOCK

    def kernel(mine_in, kv_in, qg_in, *refs):
        rest_in = refs[: len(rest)]
        outs = refs[len(rest) :]
        og_keep, og_send, kv_keep, kv_send = outs[:4]
        rest_out = outs[4 : 4 + len(rest)]
        s_ref, eh_ref, el_ref, dh_ref, dl_ref, kc_ref, vc_ref = outs[4 + len(rest) :]

        def one_pair(pair):
            def gathered(which):
                tile = which * pairs + pair
                parts = [mine_in[tile], kv_in[tile]]
                for _, index, row, rows in sets:
                    parts.append(rest_in[index][tile, pl.ds(row, rows), :])
                return jnp.concatenate(parts, axis=0)

            key_halves = halves_by_head(gathered(0))
            value_halves = halves_by_head(gathered(1))
            for head in range(2):
                kc_ref[head] = key_halves[head]
                vc_ref[head] = value_halves[head]
            query_t = qg_in[pair]
            grad_t = qg_in[pairs + pair]
            out_t = []
            query_grad_t = []
            key_grads = [[], []]
            for head in range(2):
                part = slice(head * HEAD_DIM, (head + 1) * HEAD_DIM)
                qh, ql = split(query_t[part])
                q_rows = jnp.concatenate([qh, ql], axis=0).astype(BF16)
                q_four = jnp.concatenate([qh, qh, ql, ql], axis=0).astype(BF16)
                highest = None
                for index in range(segments):
                    rows = pl.ds(index * segment, segment)
                    half = kc_ref[head, rows, :]
                    s = dot(jnp.concatenate([half, half], axis=1), q_four, NN)
                    s = s + float(levels[index]) if levels[index] else s
                    s_ref[rows, :] = s
                    top = jnp.max(s.reshape(segment // 8, 8, queries_count), axis=0)
                    highest = top if highest is None else jnp.maximum(highest, top)
                highest = jnp.max(highest, axis=0, keepdims=True)
                sums = None
                for index in range(segments):
                    rows = pl.ds(index * segment, segment)
                    e = jnp.exp2(s_ref[rows, :] - highest)
                    s_ref[rows, :] = e
                    eh = e.astype(BF16)
                    eh_ref[rows, :] = eh
                    el_ref[rows, :] = (e - eh.astype(F32)).astype(BF16)
                    part_sum = jnp.sum(e.reshape(segment // 8, 8, queries_count), axis=0)
                    sums = part_sum if sums is None else sums + part_sum
                inverse = 1.0 / jnp.sum(sums, axis=0, keepdims=True)
                vc = vc_ref[head]
                o = dot(vc, eh_ref[...], TN) + dot(vc, el_ref[...], TN)
                o = (o[:HEAD_DIM] + o[HEAD_DIM:]) * inverse
                out_t.append(o)
                g_scaled = grad_t[part] * inverse
                gh, gl = split(g_scaled)
                g_rows = jnp.concatenate([gh, gl], axis=0).astype(BF16)
                g_four = jnp.concatenate([gh, gh, gl, gl], axis=0).astype(BF16)
                row_dot = jnp.sum(o * g_scaled, axis=0, keepdims=True)
                for index in range(segments):
                    rows = pl.ds(index * segment, segment)
                    half = vc_ref[head, rows, :]
                    dp = dot(jnp.concatenate([half, half], axis=1), g_four, NN)
                    ds = s_ref[rows, :] * (dp - row_dot)
                    dh = ds.astype(BF16)
                    dh_ref[rows, :] = dh
                    dl_ref[rows, :] = (ds - dh.astype(F32)).astype(BF16)
                kc = kc_ref[head]
                dq = dot(kc, dh_ref[...], TN) + dot(kc, dl_ref[...], TN)
                query_grad_t.append((dq[:HEAD_DIM] + dq[HEAD_DIM:]) * SCALE)
                dk = dot(dh_ref[...], q_rows, NT) + dot(dl_ref[...], q_rows, NT)
                key_grads[0].append(dk)
                dv = dot(eh_ref[...], g_rows, NT) + dot(el_ref[...], g_rows, NT)
                key_grads[1].append(dv)
            for which, parts in enumerate((out_t, query_grad_t)):
                both = jnp.concatenate(parts, axis=0).T
                og_keep[which * pairs + pair] = both[:BLOCK]
                og_send[which * pairs + pair] = both[BLOCK:]
            for which in range(2):
                one, two = key_grads[which]
                first = lax.broadcasted_iota(jnp.int32, one.shape, 1) < HEAD_DIM
                both = jnp.where(
                    first,
                    one + pltpu.roll(one, HEAD_DIM, 1),
                    two + pltpu.roll(two, HEAD_DIM, 1),
                )
                if which == 0:
                    both = both * (1.0 / LOG2_E)
                tile = which * pairs + pair
                kv_keep[tile] = both[:BLOCK]
                kv_send[tile] = both[BLOCK : 2 * BLOCK]
                filled = 2 * BLOCK
                for _, index, row, rows in sets:
                    rest_out[index][tile, pl.ds(row, rows), :] = both[
                        filled : filled + rows
                    ]
                    filled += rows

        if pairs == 1:
            one_pair(0)
        else:
            pl.loop(0, pairs)(one_pair)

    block = struct(2 * pairs, BLOCK, LANES)
    outs = [block] * 4 + [struct(*a.shape) for a in rest]
    flops = 2 * 6 * 4 * pairs * 2 * total * queries_count * HEAD_DIM
    return call(
        kernel,
        operands,
        outs,
        scratch=[
            pltpu.VMEM((total, queries_count), F32),
            pltpu.VMEM((total, queries_count), BF16),
            pltpu.VMEM((total, queries_count), BF16),
            pltpu.VMEM((total, queries_count), BF16),
            pltpu.VMEM((total, queries_count), BF16),
            pltpu.VMEM((2, total, LANES), BF16),
            pltpu.VMEM((2, total, LANES), BF16),
        ],
        flops=flops,
        exps=pairs * 2 * total * queries_count,
    )


def pack(firsts, counts, operands, scalar):
    chunks = len(counts)
    shapes = [struct(2 * pairs, BLOCK, LANES) for pairs in counts]
    outs = shapes + [struct(2 * sum(counts), BLOCK, LANES)] + shapes * 2
    moves = []
    for group, arrays, theirs, out in (
        (0, (1, 2), True, 0),
        (1, (0, 3), True, chunks),
        (2, (1, 2), False, chunks + 1),
        (3, (0, 3), False, 2 * chunks + 1),
    ):
        for index, (first, pairs) in enumerate(zip(firsts, counts)):
            for tile in range(2 * pairs):
                column = (first + tile % pairs) * LANES
                place = (out, 2 * first + tile) if group == 1 else (out + index, tile)
                moves.append((arrays[tile // pairs], theirs, column, *place))

    def kernel(bit, *refs):
        ins, sems = refs[: len(operands)], refs[-1]
        results = refs[len(operands) : -1]
        started = []
        for operand, theirs, column, out, tile in moves:
            side = 1 - bit[0] if theirs else bit[0]
            column = side * (ins[operand].shape[1] // 2) + column
            column = pl.ds(pl.multiple_of(column, LANES), LANES)
            copy = pltpu.make_async_copy(
                ins[operand].at[:, column], results[out].at[tile], sems.at[len(started)]
            )
            copy.start()
            started.append(copy)
        for copy in started:
            copy.wait()

    outs = call(
        kernel,
        operands,
        outs,
        scratch=[pltpu.SemaphoreType.DMA((len(moves),))],
        scalar=scalar,
        where=pl.ANY,
    )
    return outs[:chunks], outs[chunks], outs[chunks + 1 : 2 * chunks + 1], outs[2 * chunks + 1 :]


def coarsen_pair(lo, pairs, mine, received):
    def kernel(own, got, *outs):
        half = BLOCK // 2
        for tile in range(2 * pairs):
            outs[0][tile, :half] = mean_rows(own, (tile,), 0, half, 2)
            outs[0][tile, half:] = mean_rows(got, (tile,), 0, half, 2)
            for index in range(1, lo.bits + 1):
                outs[index][tile] = mean_rows(
                    outs[index - 1], (tile,), 0, BLOCK >> index, 2
                )

    outs = [struct(2 * pairs, BLOCK >> index, LANES) for index in range(lo.bits + 1)]
    return call(kernel, [mine, received], outs)


def group_pieces(lo):
    pieces = []
    filled = BLOCK >> lo.bits
    for level in range(lo.bits):
        factor = 1 << lo.bits - level
        for step, row, rows in lo.held[level]:
            pieces.append((step, row, rows, factor, filled))
            filled += rows // factor
    return pieces


def coarsen_group(lo, hi, pairs, own, arrived):
    pieces = group_pieces(lo)

    def kernel(own_in, *refs):
        ins = refs[: lo.bits]
        outs = refs[lo.bits :]
        for tile in range(2 * pairs):
            outs[0][tile, pl.ds(0, BLOCK >> lo.bits)] = own_in[tile]
            for step, row, rows, factor, place in pieces:
                count = rows // factor
                outs[0][tile, pl.ds(place, count)] = mean_rows(
                    ins[step], (tile,), row, count, factor
                )
            for step in range(1, hi.bits):
                outs[step][tile] = mean_rows(
                    outs[step - 1], (tile,), 0, BLOCK >> step, 2
                )

    outs = [struct(2 * pairs, BLOCK >> step, LANES) for step in range(hi.bits)]
    return call(kernel, [own, *arrived], outs)


def turn(pairs, mine, received):
    def kernel(own, got, turned):
        for tile in range(2 * pairs):
            both = jnp.concatenate([own[tile], got[tile]], axis=0).T
            turned[tile] = both * (SCALE * LOG2_E) if tile < pairs else both

    return call(kernel, [mine, received], [struct(2 * pairs, LANES, 2 * BLOCK)])[0]


def spread_group(lo, hi, pairs, group_grads, grads):
    pieces = group_pieces(lo)
    own_rows = BLOCK >> lo.bits

    def kernel(*refs):
        steps = refs[: hi.bits]
        ins = refs[hi.bits : hi.bits + lo.bits]
        own_out, *outs = refs[hi.bits + lo.bits : -1]
        total = refs[-1]
        for tile in range(2 * pairs):
            total[tile] = steps[0][tile, pl.ds(0, BLOCK)]
            for step in range(1, hi.bits):
                above = steps[step][tile, pl.ds(0, BLOCK >> step)]
                add_spread(total, (tile,), 0, above, 1 << step)
            own_out[tile] = total[tile, pl.ds(0, own_rows)]
            for out, value in zip(outs, ins):
                out[tile] = value[tile]
            for step, row, rows, factor, place in pieces:
                part = total[tile, pl.ds(place, rows // factor)]
                add_spread(outs[step], (tile,), row, part, factor)

    outs = [struct(2 * pairs, own_rows, LANES)] + [struct(*a.shape) for a in grads]
    own, *grads = call(
        kernel,
        [*group_grads, *grads],
        outs,
        scratch=[pltpu.VMEM((2 * pairs, BLOCK, LANES), F32)],
    )
    return own, grads


def spread_pair(lo, pairs, own_grad, returned, keep, send):
    def kernel(own, *refs):
        back = refs[: lo.bits]
        keep_in, send_in, keep_out, send_out, *totals = refs[lo.bits :]
        half = BLOCK // 2
        for tile in range(2 * pairs):
            above = own[tile]
            for step in range(lo.bits - 1, -1, -1):
                total = totals[step]
                total[tile] = back[step][tile, pl.ds(0, BLOCK >> step)]
                add_spread(total, (tile,), 0, above, 2)
                above = total[tile]
            keep_out[tile] = keep_in[tile]
            add_spread(keep_out, (tile,), 0, above[:half], 2)
            send_out[tile] = send_in[tile]
            add_spread(send_out, (tile,), 0, above[half:], 2)

    return call(
        kernel,
        [own_grad, *returned, keep, send],
        [struct(2 * pairs, BLOCK, LANES)] * 2,
        scratch=[
            pltpu.VMEM((2 * pairs, BLOCK >> step, LANES), F32) for step in range(lo.bits)
        ],
    )


def unpack(firsts, counts, forward, kept, features, scalar):
    ins = [forward]
    places = []
    for index, (first, pairs) in enumerate(zip(firsts, counts)):
        for array, group, mine in zip(kept[index], (0, 2, 2), (True, True, False)):
            for tile in range(2 * pairs):
                column = (first + tile % pairs) * LANES
                places.append((len(ins), tile, group + tile // pairs, column, mine))
            ins.append(array)
        for tile in range(2 * pairs):
            column = (first + tile % pairs) * LANES
            places.append((0, 2 * first + tile, tile // pairs, column, False))

    def kernel(bit, *refs):
        outs = refs[len(ins) :]
        for index, tile, out, column, mine in places:
            side = bit[0] if mine else 1 - bit[0]
            column = pl.multiple_of(side * (features // 2) + column, LANES)
            outs[out][:, pl.ds(column, LANES)] = refs[index][tile]

    return call(kernel, ins, [struct(BLOCK, features)] * 4, scalar=scalar)


def on_device(queries, keys, values, cotangent):
    features = queries.shape[1]
    assert queries.shape[0] == BLOCK
    lo_bits = lax.axis_size("seqlo").bit_length() - 1
    lo = Tree(lo_bits - 1, 1)
    hi = Tree(lax.axis_size("seqhi").bit_length() - 1, lo_bits)
    scalar = (lax.axis_index("seqlo") % 2).astype(jnp.int32).reshape(1)
    counts = CHUNKS
    firsts = [sum(counts[:index]) for index in range(len(counts))]
    arrays = [
        pltpu.with_memory_space_constraint(array, pltpu.HBM)
        for array in (queries, keys, values, cotangent)
    ]
    send_kv, send_qg, mine_kv, mine_qg = pack(firsts, counts, arrays, scalar)
    chunks = range(len(counts))
    kv = [exchange(array, 1) for array in send_kv]
    send_qg, kv[-1] = lax.optimization_barrier((send_qg, kv[-1]))
    qg = exchange(send_qg, 1)
    forward = []
    kept = []
    arrived, attended, spread, first_back = [], [], [], [None]
    for index in chunks:
        pairs = counts[index]
        first = 2 * firsts[index]
        earlier = index - 2
        turned = turn(pairs, mine_qg[index], qg[first : first + 2 * pairs])
        coarse = coarsen_pair(lo, pairs, mine_kv[index], kv[index])
        zs = lo.gather(coarse[:-1], arrived[earlier] if earlier >= 0 else None)
        if earlier >= 0:
            zs[0] = ordered(zs[0], attended[earlier])
        group = coarsen_group(lo, hi, pairs, coarse[-1], zs)
        rs = hi.gather(group)
        arrived.append(rs[-1])
        if earlier >= 0:
            turned = ordered(turned, spread[earlier])
        og_keep, og_send, kv_keep, kv_send, *grads = attention(
            lo, hi, pairs, [mine_kv[index], kv[index], turned, *zs, *rs]
        )
        attended.append(og_keep)
        forward.append(og_send)
        group_grads = hi.scatter(grads[lo.bits :])
        own_grad, grads = spread_group(lo, hi, pairs, group_grads, grads[: lo.bits])
        spread.append(own_grad)
        returned = lo.scatter(grads, first_back[-1])
        first_back.append(returned[0])
        kv_keep, kv_send = spread_pair(lo, pairs, own_grad, returned, kv_keep, kv_send)
        kept.append((og_keep, kv_keep, exchange(kv_send, 1)))
    og_back = exchange(jnp.concatenate(forward, axis=0), 1)
    return tuple(unpack(firsts, counts, og_back, kept, features, scalar))


def solution(mesh):
    spec = P(AXES, None)
    return jax.shard_map(
        on_device,
        mesh=mesh,
        in_specs=(spec,) * 4,
        out_specs=(spec,) * 4,
        check_vma=False,
    )
```

```python
import math

import jax
import jax.numpy as jnp
from jax import lax
from jax.experimental import pallas as pl
from jax.experimental.pallas import tpu as pltpu
from jax.sharding import PartitionSpec as P

HEADS = 12
BLOCK = 128
HEAD_DIM = 64
LANES = 2 * HEAD_DIM
AXES = ("seqhi", "seqlo")
VMEM_LIMIT = 20 * 1024 * 1024
F32 = jnp.float32
BF16 = jnp.bfloat16
LOG2_E = 1.0 / math.log(2.0)
SCALE = 1.0 / math.sqrt(HEAD_DIM)


def struct(*shape):
    return jax.ShapeDtypeStruct(shape, F32)


def call(kernel, operands, outs, scratch=(), scalar=None, flops=0, exps=0, where=None):
    vmem = pl.BlockSpec(memory_space=pltpu.VMEM)
    smem = pl.BlockSpec(memory_space=pltpu.SMEM)
    in_specs = [pl.BlockSpec(memory_space=where) if where else vmem] * len(operands)
    if scalar is not None:
        operands = [scalar, *operands]
        in_specs = [smem, *in_specs]
    moved = sum(4 * math.prod(a.shape) for a in [*operands, *outs])
    return pl.pallas_call(
        kernel,
        out_shape=list(outs),
        in_specs=in_specs,
        out_specs=[vmem] * len(outs),
        scratch_shapes=list(scratch),
        compiler_params=pltpu.CompilerParams(vmem_limit_bytes=VMEM_LIMIT),
        cost_estimate=pl.CostEstimate(
            flops=flops, bytes_accessed=moved, transcendentals=exps
        ),
    )(*operands)


def exchange(value, offset):
    count = lax.axis_size(AXES)
    return lax.ppermute(value, AXES, [(i, i ^ offset) for i in range(count)])


def ordered(value, after):
    return value if after is None else lax.optimization_barrier((value, after))[0]


def mean_rows(ref, lead, first, count, factor):
    total = None
    for step in range(factor):
        rows = pl.ds(first + step, count, stride=factor)
        part = ref[(*lead, rows, slice(None))]
        total = part if total is None else total + part
    return total * (1.0 / factor)


def add_spread(ref, lead, first, value, factor):
    count = value.shape[0]
    value = value * (1.0 / factor)
    for step in range(factor):
        rows = pl.ds(first + step, count, stride=factor)
        place = (*lead, rows, slice(None))
        ref[place] = ref[place] + value


class Tree:
    def __init__(self, bits, first_bit, lowest=True):
        self.bits = bits
        self.first_bit = first_bit
        self.own_rows = [BLOCK >> step for step in range(bits)]
        if not lowest:
            self.own_rows[0] = 0
        self.held = {}
        self.payload = {}
        for step in range(bits - 1, -1, -1):
            rows = self.own_rows[step]
            payload = []
            fresh = {step: [(step, 0, rows)] if rows else []}
            for level in range(step + 1, bits):
                for piece in self.held[level]:
                    payload.append(piece)
                    fresh.setdefault(level, []).append((step, rows, piece[2]))
                    rows += piece[2]
            self.payload[step] = payload
            for level, pieces in fresh.items():
                self.held[level] = self.held.get(level, []) + pieces

    def partner(self, value, step):
        return exchange(value, 1 << self.first_bit + step)

    def gather(self, own, after=None):
        arrived = [None] * self.bits
        for step in range(self.bits - 1, -1, -1):
            parts = [own[step]] if self.own_rows[step] else []
            for source, row, rows in self.payload[step]:
                part = arrived[source]
                whole = rows == part.shape[1]
                parts.append(part if whole else part[:, row : row + rows])
            sent = jnp.concatenate(parts, axis=1) if len(parts) > 1 else parts[0]
            if step == 0:
                sent = ordered(sent, after)
            arrived[step] = self.partner(sent, step)
        return arrived

    def scatter(self, grads):
        grads = list(grads)
        returned = []
        for step in range(self.bits):
            back = self.partner(grads[step], step)
            returned.append(back)
            filled = self.own_rows[step]
            for source, row, rows in self.payload[step]:
                part = back[:, filled : filled + rows]
                grads[source] = grads[source].at[:, row : row + rows].add(part)
                filled += rows
        return returned


def split(value):
    high = value.astype(BF16).astype(F32)
    return high, value - high


def halves_by_head(value):
    high, low = split(value)
    first = lax.broadcasted_iota(jnp.int32, value.shape, 1) < HEAD_DIM
    one = jnp.where(first, high, pltpu.roll(low, HEAD_DIM, 1))
    two = jnp.where(first, pltpu.roll(high, HEAD_DIM, 1), low)
    return one.astype(BF16), two.astype(BF16)


def dot(lhs, rhs, dims):
    return lax.dot_general(lhs, rhs, (dims, ((), ())), preferred_element_type=F32)


NN = ((1,), (0,))
NT = ((1,), (1,))
TN = ((0,), (0,))


def attention(lo, hi, pairs, operands):
    mine, key_value, turned, *rest = operands
    sets = [(1, 0, 0, BLOCK // 2), (1, 1, 0, BLOCK // 2)]
    for tree, first in ((lo, 2), (hi, 2 + lo.bits)):
        for level in range(tree.bits):
            for step, row, rows in tree.held[level]:
                sets.append((tree.first_bit + level, first + step, row, rows))
    total = 2 * BLOCK + sum(s[3] for s in sets)
    segment = BLOCK
    segments = total // segment
    levels = [0, 0]
    filled = 0
    for level, _, _, rows in sets:
        if filled == 0:
            levels.append(level)
        filled = (filled + rows) % segment
    queries_count = 2 * BLOCK

    def kernel(mine_in, kv_in, qg_in, *refs):
        rest_in = refs[: len(rest)]
        outs = refs[len(rest) :]
        og_keep, og_send, kv_keep, kv_send = outs[:4]
        rest_out = outs[4 : 4 + len(rest)]
        s_ref, eh_ref, el_ref, dh_ref, dl_ref, kc_ref, vc_ref = outs[4 + len(rest) :]

        def one_pair(pair):
            def gathered(which):
                tile = which * pairs + pair
                parts = [mine_in[tile], kv_in[tile]]
                for _, index, row, rows in sets:
                    parts.append(rest_in[index][tile, pl.ds(row, rows), :])
                return jnp.concatenate(parts, axis=0)

            key_halves = halves_by_head(gathered(0))
            value_halves = halves_by_head(gathered(1))
            for head in range(2):
                kc_ref[head] = key_halves[head]
                vc_ref[head] = value_halves[head]
            query_t = qg_in[pair]
            grad_t = qg_in[pairs + pair]
            out_t = []
            query_grad_t = []
            key_grads = [[], []]
            for head in range(2):
                part = slice(head * HEAD_DIM, (head + 1) * HEAD_DIM)
                qh, ql = split(query_t[part])
                q_rows = jnp.concatenate([qh, ql], axis=0).astype(BF16)
                q_four = jnp.concatenate([qh, qh, ql, ql], axis=0).astype(BF16)
                highest = None
                for index in range(segments):
                    rows = pl.ds(index * segment, segment)
                    half = kc_ref[head, rows, :]
                    s = dot(jnp.concatenate([half, half], axis=1), q_four, NN)
                    s = s + float(levels[index]) if levels[index] else s
                    s_ref[rows, :] = s
                    top = jnp.max(s.reshape(segment // 8, 8, queries_count), axis=0)
                    highest = top if highest is None else jnp.maximum(highest, top)
                highest = jnp.max(highest, axis=0, keepdims=True)
                sums = None
                for index in range(segments):
                    rows = pl.ds(index * segment, segment)
                    e = jnp.exp2(s_ref[rows, :] - highest)
                    s_ref[rows, :] = e
                    eh = e.astype(BF16)
                    eh_ref[rows, :] = eh
                    el_ref[rows, :] = (e - eh.astype(F32)).astype(BF16)
                    part_sum = jnp.sum(e.reshape(segment // 8, 8, queries_count), axis=0)
                    sums = part_sum if sums is None else sums + part_sum
                inverse = 1.0 / jnp.sum(sums, axis=0, keepdims=True)
                vc = vc_ref[head]
                o = dot(vc, eh_ref[...], TN) + dot(vc, el_ref[...], TN)
                o = (o[:HEAD_DIM] + o[HEAD_DIM:]) * inverse
                out_t.append(o)
                g_scaled = grad_t[part] * inverse
                gh, gl = split(g_scaled)
                g_rows = jnp.concatenate([gh, gl], axis=0).astype(BF16)
                g_four = jnp.concatenate([gh, gh, gl, gl], axis=0).astype(BF16)
                row_dot = jnp.sum(o * g_scaled, axis=0, keepdims=True)
                for index in range(segments):
                    rows = pl.ds(index * segment, segment)
                    half = vc_ref[head, rows, :]
                    dp = dot(jnp.concatenate([half, half], axis=1), g_four, NN)
                    ds = s_ref[rows, :] * (dp - row_dot)
                    dh = ds.astype(BF16)
                    dh_ref[rows, :] = dh
                    dl_ref[rows, :] = (ds - dh.astype(F32)).astype(BF16)
                kc = kc_ref[head]
                dq = dot(kc, dh_ref[...], TN) + dot(kc, dl_ref[...], TN)
                query_grad_t.append((dq[:HEAD_DIM] + dq[HEAD_DIM:]) * SCALE)
                dk = dot(dh_ref[...], q_rows, NT) + dot(dl_ref[...], q_rows, NT)
                key_grads[0].append(dk)
                dv = dot(eh_ref[...], g_rows, NT) + dot(el_ref[...], g_rows, NT)
                key_grads[1].append(dv)
            for which, parts in enumerate((out_t, query_grad_t)):
                both = jnp.concatenate(parts, axis=0).T
                og_keep[which * pairs + pair] = both[:BLOCK]
                og_send[which * pairs + pair] = both[BLOCK:]
            for which in range(2):
                one, two = key_grads[which]
                first = lax.broadcasted_iota(jnp.int32, one.shape, 1) < HEAD_DIM
                both = jnp.where(
                    first,
                    one + pltpu.roll(one, HEAD_DIM, 1),
                    two + pltpu.roll(two, HEAD_DIM, 1),
                )
                if which == 0:
                    both = both * (1.0 / LOG2_E)
                tile = which * pairs + pair
                kv_keep[tile] = both[:BLOCK]
                kv_send[tile] = both[BLOCK : 2 * BLOCK]
                filled = 2 * BLOCK
                for _, index, row, rows in sets:
                    rest_out[index][tile, pl.ds(row, rows), :] = both[
                        filled : filled + rows
                    ]
                    filled += rows

        if pairs == 1:
            one_pair(0)
        else:
            pl.loop(0, pairs)(one_pair)

    block = struct(2 * pairs, BLOCK, LANES)
    outs = [block] * 4 + [struct(2 * pairs, *a.shape[1:]) for a in rest]
    flops = 2 * 6 * 4 * pairs * 2 * total * queries_count * HEAD_DIM
    return call(
        kernel,
        operands,
        outs,
        scratch=[
            pltpu.VMEM((total, queries_count), F32),
            pltpu.VMEM((total, queries_count), BF16),
            pltpu.VMEM((total, queries_count), BF16),
            pltpu.VMEM((total, queries_count), BF16),
            pltpu.VMEM((total, queries_count), BF16),
            pltpu.VMEM((2, total, LANES), BF16),
            pltpu.VMEM((2, total, LANES), BF16),
        ],
        flops=flops,
        exps=pairs * 2 * total * queries_count,
    )


def copy_columns(moves, ins, sems, bit):
    started = []
    for operand, theirs, column, place in moves:
        side = 1 - bit if theirs else bit
        column = side * (ins[operand].shape[1] // 2) + column
        column = pl.ds(pl.multiple_of(column, LANES), LANES)
        copy = pltpu.make_async_copy(
            ins[operand].at[:, column], place, sems.at[len(started)]
        )
        copy.start()
        started.append(copy)
    return started


def pack(pairs, first, second, scalar):
    def kernel(bit, one, two, theirs, mine, sems):
        moves = []
        for tile in range(2 * pairs):
            for out, other in ((theirs, True), (mine, False)):
                column = tile % pairs * LANES
                moves.append((tile // pairs, other, column, out.at[tile]))
        for copy in copy_columns(moves, (one, two), sems, bit[0]):
            copy.wait()

    return call(
        kernel,
        [first, second],
        [struct(2 * pairs, BLOCK, LANES)] * 2,
        scratch=[pltpu.SemaphoreType.DMA((4 * pairs,))],
        scalar=scalar,
        where=pl.ANY,
    )


def pack_coarse(pairs, keys, values, scalar):
    def kernel(bit, k, v, theirs, mine, finest, c_theirs, c_mine, sems):
        moves = []
        for out, other in ((theirs, True), (mine, False)):
            for tile in range(2 * pairs):
                column = tile % pairs * LANES
                moves.append((tile // pairs, other, column, out.at[tile]))
        copies = copy_columns(moves, (k, v), sems, bit[0])
        for index, copy in enumerate(copies):
            copy.wait()
            tile = index % (2 * pairs)
            source, place, coarse = (
                (theirs, 2 * pairs + tile, c_theirs)
                if index < 2 * pairs
                else (mine, tile, c_mine)
            )
            finest[place] = mean_rows(source, (tile,), 0, BLOCK // 2, 2)
            coarse[tile] = mean_rows(finest, (place,), 0, BLOCK // 4, 2)

    return call(
        kernel,
        [keys, values],
        [struct(2 * pairs, BLOCK, LANES)] * 2
        + [struct(4 * pairs, BLOCK // 2, LANES)]
        + [struct(2 * pairs, BLOCK // 4, LANES)] * 2,
        scratch=[pltpu.SemaphoreType.DMA((4 * pairs,))],
        scalar=scalar,
        where=pl.ANY,
    )


def coarsen_pair(lo, pairs, mine, received):
    def kernel(own, got, *outs):
        for tile in range(2 * pairs):
            outs[0][tile, : BLOCK // 4] = own[tile]
            outs[0][tile, BLOCK // 4 :] = got[tile]
            for index in range(1, lo.bits):
                outs[index][tile] = mean_rows(
                    outs[index - 1], (tile,), 0, BLOCK >> index + 1, 2
                )

    outs = [struct(2 * pairs, BLOCK >> step, LANES) for step in range(1, lo.bits + 1)]
    return call(kernel, [mine, received], outs)


def group_pieces(lo):
    own = BLOCK >> lo.bits
    factor = 1 << lo.bits
    pieces = [
        (-2, 0, BLOCK // 2, factor, own),
        (-1, 0, BLOCK // 2, factor, own + own // 2),
    ]
    filled = 2 * own
    for level in range(1, lo.bits):
        factor = 1 << lo.bits - level
        for step, row, rows in lo.held[level]:
            pieces.append((step, row, rows, factor, filled))
            filled += rows // factor
    return pieces


def coarsen_group(lo, hi, pairs, own, halves, arrived):
    pieces = group_pieces(lo)

    def kernel(own_in, *refs):
        ins = refs[: 2 + lo.bits]
        outs = refs[2 + lo.bits :]
        for tile in range(2 * pairs):
            outs[0][tile, pl.ds(0, BLOCK >> lo.bits)] = own_in[tile]
            for step, row, rows, factor, place in pieces:
                count = rows // factor
                outs[0][tile, pl.ds(place, count)] = mean_rows(
                    ins[2 + step], (tile,), row, count, factor
                )
            for step in range(1, hi.bits):
                outs[step][tile] = mean_rows(
                    outs[step - 1], (tile,), 0, BLOCK >> step, 2
                )

    outs = [struct(2 * pairs, BLOCK >> step, LANES) for step in range(hi.bits)]
    return call(kernel, [own, *halves, *arrived], outs)


def turn(pairs, mine, received):
    def kernel(own, got, turned):
        for tile in range(2 * pairs):
            both = jnp.concatenate([own[tile], got[tile]], axis=0).T
            turned[tile] = both * (SCALE * LOG2_E) if tile < pairs else both

    return call(kernel, [mine, received], [struct(2 * pairs, LANES, 2 * BLOCK)])[0]


def spread_group(lo, hi, pairs, group_grads, grads):
    pieces = group_pieces(lo)
    own_rows = BLOCK >> lo.bits

    def kernel(*refs):
        steps = refs[: hi.bits]
        ins = refs[hi.bits : hi.bits + lo.bits]
        own_out, *outs = refs[hi.bits + lo.bits : -1]
        total = refs[-1]
        for tile in range(2 * pairs):
            total[tile] = steps[0][tile, pl.ds(0, BLOCK)]
            for step in range(1, hi.bits):
                above = steps[step][tile, pl.ds(0, BLOCK >> step)]
                add_spread(total, (tile,), 0, above, 1 << step)
            own_out[tile] = total[tile, pl.ds(0, own_rows)]
            for out, value in zip(outs, ins):
                out[tile, pl.ds(0, value.shape[1])] = value[tile]
            outs[0][tile, pl.ds(ins[0].shape[1], own_rows)] = total[
                tile, pl.ds(own_rows, own_rows)
            ]
            for step, row, rows, factor, place in pieces:
                if step >= 0:
                    part = total[tile, pl.ds(place, rows // factor)]
                    add_spread(outs[step], (tile,), row, part, factor)

    shapes = [list(a.shape) for a in grads]
    shapes[0][1] += own_rows
    outs = [struct(2 * pairs, own_rows, LANES)] + [struct(*shape) for shape in shapes]
    own, *grads = call(
        kernel,
        [*group_grads, *grads],
        outs,
        scratch=[pltpu.VMEM((2 * pairs, BLOCK, LANES), F32)],
    )
    return own, grads


def spread_pair(lo, pairs, own_grad, returned):
    own_rows = BLOCK >> lo.bits

    def kernel(own, *refs):
        back = refs[: lo.bits]
        mine, theirs, *totals = refs[lo.bits :]
        last = pl.ds(back[0].shape[1] - own_rows, own_rows)
        for tile in range(2 * pairs):
            above = own[tile] + back[0][tile, last]
            for step in range(lo.bits - 1, 0, -1):
                total = totals[step - 1]
                total[tile] = back[step][tile, pl.ds(0, BLOCK >> step)]
                add_spread(total, (tile,), 0, above, 2)
                above = total[tile]
            mine[tile] = above[: BLOCK // 4]
            theirs[tile] = above[BLOCK // 4 :]

    return call(
        kernel,
        [own_grad, *returned],
        [struct(2 * pairs, BLOCK // 4, LANES)] * 2,
        scratch=[
            pltpu.VMEM((2 * pairs, BLOCK >> step, LANES), F32)
            for step in range(1, lo.bits)
        ],
    )


def unpack(pairs, kept, arrived, features, scalar):
    def kernel(bit, mine, theirs, *outs):
        for tile in range(2 * pairs):
            for side, array in ((bit[0], mine), (1 - bit[0], theirs)):
                column = side * (features // 2) + tile % pairs * LANES
                column = pl.ds(pl.multiple_of(column, LANES), LANES)
                outs[tile // pairs][:, column] = array[tile]

    return call(kernel, [kept, arrived], [struct(BLOCK, features)] * 2, scalar=scalar)


def finish(pairs, blocks, finest, seconds, features, scalar):
    def kernel(bit, *refs):
        outs, total = refs[6:8], refs[8]
        for tile in range(2 * pairs):
            for source, side in ((0, bit[0]), (1, 1 - bit[0])):
                place = (source * 2 * pairs + tile,)
                total[(*place, slice(None), slice(None))] = refs[source][tile]
                add_spread(total, place, 0, refs[2 + source][tile], 2)
                add_spread(total, place, 0, refs[4 + source][tile], 4)
                column = side * (features // 2) + tile % pairs * LANES
                column = pl.ds(pl.multiple_of(column, LANES), LANES)
                outs[tile // pairs][:, column] = total[(*place, slice(None), slice(None))]

    return call(
        kernel,
        [*blocks, *finest, *seconds],
        [struct(BLOCK, features)] * 2,
        scratch=[pltpu.VMEM((4 * pairs, BLOCK, LANES), F32)],
        scalar=scalar,
    )


def on_device(queries, keys, values, cotangent):
    features = queries.shape[1]
    assert queries.shape[0] == BLOCK
    pairs = features // LANES // 2
    lo_bits = lax.axis_size("seqlo").bit_length() - 1
    lo = Tree(lo_bits - 1, 1, lowest=False)
    hi = Tree(lax.axis_size("seqhi").bit_length() - 1, lo_bits)
    scalar = (lax.axis_index("seqlo") % 2).astype(jnp.int32).reshape(1)
    queries, keys, values, cotangent = [
        pltpu.with_memory_space_constraint(array, pltpu.HBM)
        for array in (queries, keys, values, cotangent)
    ]
    send_kv, mine_kv, finest, c_send, c_mine = pack_coarse(pairs, keys, values, scalar)
    second = exchange(c_send, 1)
    finest = exchange(finest, 2)
    kv = exchange(ordered(send_kv, second), 1)
    half = exchange(ordered(finest[2 * pairs :], kv), 1)
    send_qg, mine_qg = pack(pairs, queries, cotangent, scalar)
    qg = exchange(ordered(send_qg, half), 1)
    coarse = coarsen_pair(lo, pairs, c_mine, second)
    zs = lo.gather([None, *coarse])
    group = coarsen_group(lo, hi, pairs, coarse[-1], [finest, half], zs)
    turned = turn(pairs, mine_qg, qg)
    rs = hi.gather(group, turned)
    og_keep, og_send, kv_keep, kv_send, *grads = attention(
        lo, hi, pairs, [mine_kv, kv, turned, finest, half, *zs, *rs]
    )
    finest_grad, half_grad, *grads = grads
    finest_mine = exchange(finest_grad, 2)
    half_back = exchange(half_grad, 1)
    kv_back = exchange(ordered(kv_send, half_back), 1)
    og_back = exchange(ordered(og_send, half_back), 1)
    group_grads = hi.scatter(grads[lo.bits :])
    group_grads[-1] = ordered(group_grads[-1], (finest_mine, half_back))
    own_grad, grads = spread_group(lo, hi, pairs, group_grads, grads[: lo.bits])
    returned = lo.scatter(grads)
    finest_theirs = exchange(ordered(half_back, returned[0]), 2)
    own_grad = ordered(own_grad, (kv_back, og_back))
    second_mine, second_send = spread_pair(lo, pairs, own_grad, returned)
    second_theirs = exchange(second_send, 1)
    attended, query_grad = unpack(pairs, og_keep, og_back, features, scalar)
    key_grad, value_grad = finish(
        pairs,
        (kv_keep, kv_back),
        (finest_mine, finest_theirs),
        (second_mine, second_theirs),
        features,
        scalar,
    )
    return attended, query_grad, key_grad, value_grad


def solution(mesh):
    spec = P(AXES, None)
    return jax.shard_map(
        on_device,
        mesh=mesh,
        in_specs=(spec,) * 4,
        out_specs=(spec,) * 4,
        check_vma=False,
    )
```

```python
import math

import jax
import jax.numpy as jnp
from jax import lax
from jax.experimental import pallas as pl
from jax.experimental.pallas import tpu as pltpu
from jax.sharding import PartitionSpec as P

HEADS = 12
BLOCK = 128
HEAD_DIM = 64
LANES = 2 * HEAD_DIM
AXES = ("seqhi", "seqlo")
VMEM_LIMIT = 20 * 1024 * 1024
F32 = jnp.float32
BF16 = jnp.bfloat16
LOG2_E = 1.0 / math.log(2.0)
SCALE = 1.0 / math.sqrt(HEAD_DIM)


def struct(*shape):
    return jax.ShapeDtypeStruct(shape, F32)


def call(kernel, operands, outs, scratch=(), scalar=None, flops=0, exps=0, where=None):
    vmem = pl.BlockSpec(memory_space=pltpu.VMEM)
    smem = pl.BlockSpec(memory_space=pltpu.SMEM)
    in_specs = [pl.BlockSpec(memory_space=where) if where else vmem] * len(operands)
    if scalar is not None:
        operands = [scalar, *operands]
        in_specs = [smem, *in_specs]
    moved = sum(4 * math.prod(a.shape) for a in [*operands, *outs])
    return pl.pallas_call(
        kernel,
        out_shape=list(outs),
        in_specs=in_specs,
        out_specs=[vmem] * len(outs),
        scratch_shapes=list(scratch),
        compiler_params=pltpu.CompilerParams(vmem_limit_bytes=VMEM_LIMIT),
        cost_estimate=pl.CostEstimate(
            flops=flops, bytes_accessed=moved, transcendentals=exps
        ),
    )(*operands)


def exchange(value, offset):
    count = lax.axis_size(AXES)
    return lax.ppermute(value, AXES, [(i, i ^ offset) for i in range(count)])


def ordered(value, after):
    return value if after is None else lax.optimization_barrier((value, after))[0]


def half_difference(ref, lead, first, count):
    even = ref[(*lead, pl.ds(first, count, stride=2), slice(None))]
    odd = ref[(*lead, pl.ds(first + 1, count, stride=2), slice(None))]
    return 0.5 * (even - odd)


def put_pairs(ref, lead, total, difference):
    count = total.shape[0]
    ref[(*lead, pl.ds(0, count, stride=2), slice(None))] = total + difference
    ref[(*lead, pl.ds(1, count, stride=2), slice(None))] = total - difference


def mean_rows(ref, lead, first, count, factor):
    total = None
    for step in range(factor):
        rows = pl.ds(first + step, count, stride=factor)
        part = ref[(*lead, rows, slice(None))]
        total = part if total is None else total + part
    return total * (1.0 / factor)


def add_spread(ref, lead, first, value, factor):
    count = value.shape[0]
    value = value * (1.0 / factor)
    for step in range(factor):
        rows = pl.ds(first + step, count, stride=factor)
        place = (*lead, rows, slice(None))
        ref[place] = ref[place] + value


class Tree:
    def __init__(self, bits, first_bit, lowest=True):
        self.bits = bits
        self.first_bit = first_bit
        self.own_rows = [BLOCK >> step for step in range(bits)]
        if not lowest:
            self.own_rows[0] = 0
        self.held = {}
        self.payload = {}
        for step in range(bits - 1, -1, -1):
            rows = self.own_rows[step]
            payload = []
            fresh = {step: [(step, 0, rows)] if rows else []}
            for level in range(step + 1, bits):
                for piece in self.held[level]:
                    payload.append(piece)
                    fresh.setdefault(level, []).append((step, rows, piece[2]))
                    rows += piece[2]
            self.payload[step] = payload
            for level, pieces in fresh.items():
                self.held[level] = self.held.get(level, []) + pieces

    def partner(self, value, step):
        return exchange(value, 1 << self.first_bit + step)

    def gather(self, own, after=None):
        arrived = [None] * self.bits
        for step in range(self.bits - 1, -1, -1):
            parts = [own[step]] if self.own_rows[step] else []
            for source, row, rows in self.payload[step]:
                part = arrived[source]
                whole = rows == part.shape[1]
                parts.append(part if whole else part[:, row : row + rows])
            sent = jnp.concatenate(parts, axis=1) if len(parts) > 1 else parts[0]
            if step == 0:
                sent = ordered(sent, after)
            arrived[step] = self.partner(sent, step)
        return arrived

    def scatter(self, grads):
        grads = list(grads)
        returned = []
        for step in range(self.bits):
            back = self.partner(grads[step], step)
            returned.append(back)
            filled = self.own_rows[step]
            for source, row, rows in self.payload[step]:
                part = back[:, filled : filled + rows]
                grads[source] = grads[source].at[:, row : row + rows].add(part)
                filled += rows
        return returned


def split(value):
    high = value.astype(BF16).astype(F32)
    return high, value - high


def halves_by_head(value):
    high, low = split(value)
    first = lax.broadcasted_iota(jnp.int32, value.shape, 1) < HEAD_DIM
    one = jnp.where(first, high, pltpu.roll(low, HEAD_DIM, 1))
    two = jnp.where(first, pltpu.roll(high, HEAD_DIM, 1), low)
    return one.astype(BF16), two.astype(BF16)


def dot(lhs, rhs, dims):
    return lax.dot_general(lhs, rhs, (dims, ((), ())), preferred_element_type=F32)


NN = ((1,), (0,))
NT = ((1,), (1,))
TN = ((0,), (0,))


BOTH = 2 * BLOCK


def halves_of(sets, ins, which, pairs, pair):
    tile = which * pairs + pair
    parts = [ins[index][tile, pl.ds(row, rows), :] for _, index, row, rows in sets]
    return halves_by_head(jnp.concatenate(parts, axis=0))


def segment_levels(sets):
    levels, filled = [], 0
    for level, _, _, rows in sets:
        if filled % BLOCK == 0:
            levels.append(level)
        filled += rows
    return levels


def four_rows(value):
    high, low = split(value)
    four = jnp.concatenate([high, high, low, low], axis=0).astype(BF16)
    return four, jnp.concatenate([high, low], axis=0).astype(BF16)


def store_split(high_ref, low_ref, place, value):
    high = value.astype(BF16)
    high_ref[place] = high
    low_ref[place] = (value - high.astype(F32)).astype(BF16)


def fold_rows(value):
    return value[:HEAD_DIM] + value[HEAD_DIM:]


def fold_heads(one, two):
    first = lax.broadcasted_iota(jnp.int32, one.shape, 1) < HEAD_DIM
    return jnp.where(
        first, one + pltpu.roll(one, HEAD_DIM, 1), two + pltpu.roll(two, HEAD_DIM, 1)
    )


def column_scores(levels, keys_of, q_four, s_ref, highest):
    for index, level in enumerate(levels):
        rows = pl.ds(index * BLOCK, BLOCK)
        half = keys_of(rows)
        s = dot(jnp.concatenate([half, half], axis=1), q_four, NN)
        s = s + float(level) if level else s
        s_ref[rows, :] = s
        top = jnp.max(s.reshape(BLOCK // 8, 8, BOTH), axis=0)
        highest = top if highest is None else jnp.maximum(highest, top)
    return highest


def each_pair(pairs, body):
    if pairs == 1:
        body(0)
    else:
        pl.loop(0, pairs)(body)


def costs(pairs, rows, products, exps=0):
    return dict(
        flops=2 * 4 * products * pairs * 2 * rows * BOTH * HEAD_DIM,
        exps=exps * pairs * 2 * rows * BOTH,
    )


def attend_first(pairs, sets, operands, turned):
    total = sum(s[3] for s in sets)
    levels = segment_levels(sets)

    def kernel(turn_in, *refs):
        ins = refs[: len(operands)]
        kc, vc, eh, el, tops, sums, out, s_ref = refs[len(operands) :]

        def one_pair(pair):
            keys = halves_of(sets, ins, 0, pairs, pair)
            values = halves_of(sets, ins, 1, pairs, pair)
            for head in range(2):
                at = 2 * pair + head
                kc[at] = keys[head]
                vc[at] = values[head]
                part = slice(head * HEAD_DIM, (head + 1) * HEAD_DIM)
                q_four, _ = four_rows(turn_in[pair][part])
                top = column_scores(levels, lambda r: kc[at, r, :], q_four, s_ref, None)
                top = jnp.max(top, axis=0, keepdims=True)
                tops[at] = top
                summed = None
                for index in range(len(levels)):
                    rows = pl.ds(index * BLOCK, BLOCK)
                    e = jnp.exp2(s_ref[rows, :] - top)
                    store_split(eh, el, (at, rows, slice(None)), e)
                    part_sum = jnp.sum(e.reshape(BLOCK // 8, 8, BOTH), axis=0)
                    summed = part_sum if summed is None else summed + part_sum
                sums[at] = jnp.sum(summed, axis=0, keepdims=True)
                o = dot(vc[at], eh[at], TN) + dot(vc[at], el[at], TN)
                out[at] = fold_rows(o)

        each_pair(pairs, one_pair)

    heads = 2 * pairs
    half = jax.ShapeDtypeStruct((heads, total, LANES), BF16)
    exponents = jax.ShapeDtypeStruct((heads, total, BOTH), BF16)
    outs = [half, half, exponents, exponents]
    outs += [struct(heads, 1, BOTH)] * 2 + [struct(heads, HEAD_DIM, BOTH)]
    return call(
        kernel,
        [turned, *operands],
        outs,
        scratch=[pltpu.VMEM((total, BOTH), F32)],
        **costs(pairs, total, 2, 1),
    )


def attend_last(pairs, sets, operands, turned, tops, sums, partial):
    total = sum(s[3] for s in sets)
    levels = segment_levels(sets)

    def kernel(turn_in, top_in, sum_in, part_in, *refs):
        ins = refs[: len(operands)]
        grads = refs[len(operands) : 2 * len(operands)]
        o_keep, o_send, g_out, r_out, dq_out = refs[2 * len(operands) : -7]
        s_ref, eh, el, dh, dl, kc, vc = refs[-7:]

        def one_pair(pair):
            keys = halves_of(sets, ins, 0, pairs, pair)
            values = halves_of(sets, ins, 1, pairs, pair)
            out_t, key_grads, value_grads = [], [], []
            for head in range(2):
                kc[head] = keys[head]
                vc[head] = values[head]
                at = 2 * pair + head
                part = slice(head * HEAD_DIM, (head + 1) * HEAD_DIM)
                q_four, q_rows = four_rows(turn_in[pair][part])
                grad = turn_in[pairs + pair][part]
                top = column_scores(levels, lambda r: kc[head, r, :], q_four, s_ref, None)
                first_top = top_in[at]
                top = jnp.maximum(jnp.max(top, axis=0, keepdims=True), first_top)
                rescale = jnp.exp2(first_top - top)
                summed = None
                for index in range(len(levels)):
                    rows = pl.ds(index * BLOCK, BLOCK)
                    e = jnp.exp2(s_ref[rows, :] - top)
                    s_ref[rows, :] = e
                    store_split(eh, el, (rows, slice(None)), e)
                    part_sum = jnp.sum(e.reshape(BLOCK // 8, 8, BOTH), axis=0)
                    summed = part_sum if summed is None else summed + part_sum
                summed = jnp.sum(summed, axis=0, keepdims=True) + sum_in[at] * rescale
                inverse = 1.0 / summed
                o = dot(vc[head], eh[...], TN) + dot(vc[head], el[...], TN)
                o = (fold_rows(o) + part_in[at] * rescale) * inverse
                out_t.append(o)
                g_scaled = grad * inverse
                g_four, g_rows = four_rows(g_scaled)
                row_dot = jnp.sum(o * g_scaled, axis=0, keepdims=True)
                g_out[at] = g_scaled * rescale
                r_out[at] = row_dot * rescale
                for index in range(len(levels)):
                    rows = pl.ds(index * BLOCK, BLOCK)
                    half = vc[head, rows, :]
                    dp = dot(jnp.concatenate([half, half], axis=1), g_four, NN)
                    ds = s_ref[rows, :] * (dp - row_dot)
                    store_split(dh, dl, (rows, slice(None)), ds)
                dq = dot(kc[head], dh[...], TN) + dot(kc[head], dl[...], TN)
                dq_out[at] = fold_rows(dq)
                key_grads.append(dot(dh[...], q_rows, NT) + dot(dl[...], q_rows, NT))
                value_grads.append(dot(eh[...], g_rows, NT) + dot(el[...], g_rows, NT))
            both = jnp.concatenate(out_t, axis=0).T
            o_keep[pair] = both[:BLOCK]
            o_send[pair] = both[BLOCK:]
            put_grads(pairs, pair, sets, grads, key_grads, value_grads)

        each_pair(pairs, one_pair)

    heads = 2 * pairs
    outs = [struct(*a.shape) for a in operands]
    outs += [struct(pairs, BLOCK, LANES)] * 2
    outs += [struct(heads, HEAD_DIM, BOTH), struct(heads, 1, BOTH)]
    outs.append(struct(heads, HEAD_DIM, BOTH))
    wide = [pltpu.VMEM((total, BOTH), BF16)] * 4
    return call(
        kernel,
        [turned, tops, sums, partial, *operands],
        outs,
        scratch=[pltpu.VMEM((total, BOTH), F32)]
        + wide
        + [pltpu.VMEM((2, total, LANES), BF16)] * 2,
        **costs(pairs, total, 6, 1),
    )


def put_grads(pairs, pair, sets, grads, key_grads, value_grads):
    for which, parts in enumerate((key_grads, value_grads)):
        both = fold_heads(*parts)
        if which == 0:
            both = both * (1.0 / LOG2_E)
        filled = 0
        for _, index, row, rows in sets:
            piece = both[filled : filled + rows]
            grads[index][which * pairs + pair, pl.ds(row, rows), :] = piece
            filled += rows


def attend_back(pairs, sets, shapes, first, kept, turned, g_scaled, row_dot, dq, last):
    total = sum(s[3] for s in sets)
    segments = total // BLOCK

    def kernel(turn_in, kc, vc, eh, el, g_in, r_in, dq_in, *refs):
        grads = refs[: len(shapes)]
        dq_out = refs[len(shapes) : -2]
        dh, dl = refs[-2:]
        span = pl.ds(first, total)

        def one_pair(pair):
            dq_t, key_grads, value_grads = [], [], []
            for head in range(2):
                at = 2 * pair + head
                part = slice(head * HEAD_DIM, (head + 1) * HEAD_DIM)
                _, q_rows = four_rows(turn_in[pair][part])
                g_four, g_rows = four_rows(g_in[at])
                dots = r_in[at]
                for index in range(segments):
                    rows = pl.ds(first + index * BLOCK, BLOCK)
                    half = vc[at, rows, :]
                    dp = dot(jnp.concatenate([half, half], axis=1), g_four, NN)
                    e = eh[at, rows, :].astype(F32) + el[at, rows, :].astype(F32)
                    place = (pl.ds(index * BLOCK, BLOCK), slice(None))
                    store_split(dh, dl, place, e * (dp - dots))
                keys = kc[at, span, :]
                part_dq = dot(keys, dh[...], TN) + dot(keys, dl[...], TN)
                dq_t.append(fold_rows(part_dq) + dq_in[at])
                key_grads.append(dot(dh[...], q_rows, NT) + dot(dl[...], q_rows, NT))
                value_grads.append(
                    dot(eh[at, span, :], g_rows, NT) + dot(el[at, span, :], g_rows, NT)
                )
            put_grads(pairs, pair, sets, grads, key_grads, value_grads)
            if last:
                both = jnp.concatenate(dq_t, axis=0).T * SCALE
                dq_out[0][pair] = both[:BLOCK]
                dq_out[1][pair] = both[BLOCK:]
            else:
                for head in range(2):
                    dq_out[0][2 * pair + head] = dq_t[head]

        each_pair(pairs, one_pair)

    outs = [struct(*shape) for shape in shapes]
    if last:
        outs += [struct(pairs, BLOCK, LANES)] * 2
    else:
        outs.append(struct(*dq.shape))
    return call(
        kernel,
        [turned, *kept, g_scaled, row_dot, dq],
        outs,
        scratch=[pltpu.VMEM((total, BOTH), BF16)] * 2,
        **costs(pairs, total, 4),
    )


def copy_columns(moves, ins, sems, bit):
    started = []
    for operand, theirs, column, place in moves:
        side = 1 - bit if theirs else bit
        column = side * (ins[operand].shape[1] // 2) + column
        column = pl.ds(pl.multiple_of(column, LANES), LANES)
        copy = pltpu.make_async_copy(
            ins[operand].at[:, column], place, sems.at[len(started)]
        )
        copy.start()
        started.append(copy)
    return started


def pack(pairs, first, second, scalar):
    def kernel(bit, one, two, theirs, mine, sems):
        moves = []
        for tile in range(2 * pairs):
            for out, other in ((theirs, True), (mine, False)):
                column = tile % pairs * LANES
                moves.append((tile // pairs, other, column, out.at[tile]))
        for copy in copy_columns(moves, (one, two), sems, bit[0]):
            copy.wait()

    return call(
        kernel,
        [first, second],
        [struct(2 * pairs, BLOCK, LANES)] * 2,
        scratch=[pltpu.SemaphoreType.DMA((4 * pairs,))],
        scalar=scalar,
        where=pl.ANY,
    )


QUARTER = BLOCK // 4
HALF = BLOCK // 2


def pack_coarse(pairs, keys, values, scalar):
    def kernel(bit, k, v, mine, finest, c_theirs, c_mine, rest, theirs, sems):
        moves = []
        for out, other in ((theirs, True), (mine, False)):
            for tile in range(2 * pairs):
                column = tile % pairs * LANES
                moves.append((tile // pairs, other, column, out.at[tile]))
        copies = copy_columns(moves, (k, v), sems, bit[0])
        for index, copy in enumerate(copies):
            copy.wait()
            tile = index % (2 * pairs)
            other = index < 2 * pairs
            source, place = (theirs, 2 * pairs + tile) if other else (mine, tile)
            coarse = c_theirs if other else c_mine
            finest[place] = mean_rows(source, (tile,), 0, HALF, 2)
            coarse[tile] = mean_rows(finest, (place,), 0, QUARTER, 2)
            if other:
                rest[tile, :QUARTER] = half_difference(finest, (place,), 0, QUARTER)
                rest[tile, QUARTER:] = half_difference(source, (tile,), 0, HALF)

    return call(
        kernel,
        [keys, values],
        [struct(2 * pairs, BLOCK, LANES), struct(4 * pairs, HALF, LANES)]
        + [struct(2 * pairs, QUARTER, LANES)] * 2
        + [struct(2 * pairs, QUARTER + HALF, LANES)],
        scratch=[
            pltpu.VMEM((2 * pairs, BLOCK, LANES), F32),
            pltpu.SemaphoreType.DMA((4 * pairs,)),
        ],
        scalar=scalar,
        where=pl.ANY,
    )


def rebuild(pairs, second, rest):
    def kernel(second_in, rest_in, out, finest):
        for tile in range(2 * pairs):
            put_pairs(finest, (tile,), second_in[tile], rest_in[tile, :QUARTER])
            put_pairs(out, (tile,), finest[tile], rest_in[tile, QUARTER:])

    return call(
        kernel,
        [second, rest],
        [struct(2 * pairs, BLOCK, LANES)],
        scratch=[pltpu.VMEM((2 * pairs, HALF, LANES), F32)],
    )[0]


def take_apart(pairs, block_grad):
    def kernel(block, second, rest, finest):
        for tile in range(2 * pairs):
            finest[tile] = 2.0 * mean_rows(block, (tile,), 0, HALF, 2)
            rest[tile, QUARTER:] = 2.0 * half_difference(block, (tile,), 0, HALF)
            second[tile] = 2.0 * mean_rows(finest, (tile,), 0, QUARTER, 2)
            rest[tile, :QUARTER] = 2.0 * half_difference(finest, (tile,), 0, QUARTER)

    return call(
        kernel,
        [block_grad],
        [
            struct(2 * pairs, QUARTER, LANES),
            struct(2 * pairs, QUARTER + HALF, LANES),
        ],
        scratch=[pltpu.VMEM((2 * pairs, HALF, LANES), F32)],
    )


def coarsen_pair(lo, pairs, mine, received):
    def kernel(own, got, *outs):
        for tile in range(2 * pairs):
            outs[0][tile, : BLOCK // 4] = own[tile]
            outs[0][tile, BLOCK // 4 :] = got[tile]
            for index in range(1, lo.bits):
                outs[index][tile] = mean_rows(
                    outs[index - 1], (tile,), 0, BLOCK >> index + 1, 2
                )

    outs = [struct(2 * pairs, BLOCK >> step, LANES) for step in range(1, lo.bits + 1)]
    return call(kernel, [mine, received], outs)


def group_pieces(lo):
    own = BLOCK >> lo.bits
    factor = 1 << lo.bits
    pieces = [
        (-2, 0, BLOCK // 2, factor, own),
        (-1, 0, BLOCK // 2, factor, own + own // 2),
    ]
    filled = 2 * own
    for level in range(1, lo.bits):
        factor = 1 << lo.bits - level
        for step, row, rows in lo.held[level]:
            pieces.append((step, row, rows, factor, filled))
            filled += rows // factor
    return pieces


def coarsen_group(lo, hi, pairs, own, halves, arrived):
    pieces = group_pieces(lo)

    def kernel(own_in, *refs):
        ins = refs[: 2 + lo.bits]
        outs = refs[2 + lo.bits :]
        for tile in range(2 * pairs):
            outs[0][tile, pl.ds(0, BLOCK >> lo.bits)] = own_in[tile]
            for step, row, rows, factor, place in pieces:
                count = rows // factor
                outs[0][tile, pl.ds(place, count)] = mean_rows(
                    ins[2 + step], (tile,), row, count, factor
                )
            for step in range(1, hi.bits):
                outs[step][tile] = mean_rows(
                    outs[step - 1], (tile,), 0, BLOCK >> step, 2
                )

    outs = [struct(2 * pairs, BLOCK >> step, LANES) for step in range(hi.bits)]
    return call(kernel, [own, *halves, *arrived], outs)


def turn(pairs, mine, received):
    def kernel(own, got, turned):
        for tile in range(2 * pairs):
            both = jnp.concatenate([own[tile], got[tile]], axis=0).T
            turned[tile] = both * (SCALE * LOG2_E) if tile < pairs else both

    return call(kernel, [mine, received], [struct(2 * pairs, LANES, 2 * BLOCK)])[0]


def spread_group(lo, hi, pairs, group_grads, grads):
    pieces = group_pieces(lo)
    own_rows = BLOCK >> lo.bits

    def kernel(*refs):
        steps = refs[: hi.bits]
        ins = refs[hi.bits : hi.bits + lo.bits]
        own_out, *outs = refs[hi.bits + lo.bits : -1]
        total = refs[-1]
        for tile in range(2 * pairs):
            total[tile] = steps[0][tile, pl.ds(0, BLOCK)]
            for step in range(1, hi.bits):
                above = steps[step][tile, pl.ds(0, BLOCK >> step)]
                add_spread(total, (tile,), 0, above, 1 << step)
            own_out[tile] = total[tile, pl.ds(0, own_rows)]
            for out, value in zip(outs, ins):
                out[tile, pl.ds(0, value.shape[1])] = value[tile]
            outs[0][tile, pl.ds(ins[0].shape[1], own_rows)] = total[
                tile, pl.ds(own_rows, own_rows)
            ]
            for step, row, rows, factor, place in pieces:
                if step >= 0:
                    part = total[tile, pl.ds(place, rows // factor)]
                    add_spread(outs[step], (tile,), row, part, factor)

    shapes = [list(a.shape) for a in grads]
    shapes[0][1] += own_rows
    outs = [struct(2 * pairs, own_rows, LANES)] + [struct(*shape) for shape in shapes]
    own, *grads = call(
        kernel,
        [*group_grads, *grads],
        outs,
        scratch=[pltpu.VMEM((2 * pairs, BLOCK, LANES), F32)],
    )
    return own, grads


def spread_pair(lo, pairs, own_grad, returned, block_second):
    own_rows = BLOCK >> lo.bits

    def kernel(own, block, *refs):
        back = refs[: lo.bits]
        mine, theirs, *totals = refs[lo.bits :]
        last = pl.ds(back[0].shape[1] - own_rows, own_rows)
        for tile in range(2 * pairs):
            above = own[tile] + back[0][tile, last]
            for step in range(lo.bits - 1, 0, -1):
                total = totals[step - 1]
                total[tile] = back[step][tile, pl.ds(0, BLOCK >> step)]
                add_spread(total, (tile,), 0, above, 2)
                above = total[tile]
            mine[tile] = above[: BLOCK // 4]
            theirs[tile] = above[BLOCK // 4 :] + block[tile]

    return call(
        kernel,
        [own_grad, block_second, *returned],
        [struct(2 * pairs, BLOCK // 4, LANES)] * 2,
        scratch=[
            pltpu.VMEM((2 * pairs, BLOCK >> step, LANES), F32)
            for step in range(1, lo.bits)
        ],
    )


def unpack(pairs, kept, arrived, features, scalar):
    def kernel(bit, mine, theirs, *outs):
        for tile in range(2 * pairs):
            for side, array in ((bit[0], mine), (1 - bit[0], theirs)):
                column = side * (features // 2) + tile % pairs * LANES
                column = pl.ds(pl.multiple_of(column, LANES), LANES)
                outs[tile // pairs][:, column] = array[tile]

    return call(kernel, [kept, arrived], [struct(BLOCK, features)] * 2, scalar=scalar)


def finish(pairs, kept, rest, finest, seconds, features, scalar):
    def kernel(bit, kept_in, rest_in, f_mine, f_theirs, s_mine, s_theirs, *refs):
        outs, total, middle = refs[:2], refs[2], refs[3]
        for tile in range(2 * pairs):
            out = outs[tile // pairs]
            column = tile % pairs * LANES
            at = (tile,)
            total[tile] = kept_in[tile]
            add_spread(total, at, 0, f_mine[tile], 2)
            add_spread(total, at, 0, s_mine[tile], 4)
            place = bit[0] * (features // 2) + column
            out[:, pl.ds(pl.multiple_of(place, LANES), LANES)] = total[tile]
            put_pairs(middle, at, 0.5 * s_theirs[tile], 0.5 * rest_in[tile, :QUARTER])
            first = 0.5 * (middle[tile] + f_theirs[tile])
            put_pairs(total, at, first, 0.5 * rest_in[tile, QUARTER:])
            place = (1 - bit[0]) * (features // 2) + column
            out[:, pl.ds(pl.multiple_of(place, LANES), LANES)] = total[tile]

    return call(
        kernel,
        [kept, rest, *finest, *seconds],
        [struct(BLOCK, features)] * 2,
        scratch=[
            pltpu.VMEM((2 * pairs, BLOCK, LANES), F32),
            pltpu.VMEM((2 * pairs, HALF, LANES), F32),
        ],
        scalar=scalar,
    )


def on_device(queries, keys, values, cotangent):
    features = queries.shape[1]
    assert queries.shape[0] == BLOCK
    pairs = features // LANES // 2
    lo_bits = lax.axis_size("seqlo").bit_length() - 1
    lo = Tree(lo_bits - 1, 1, lowest=False)
    hi = Tree(lax.axis_size("seqhi").bit_length() - 1, lo_bits)
    scalar = (lax.axis_index("seqlo") % 2).astype(jnp.int32).reshape(1)
    queries, keys, values, cotangent = [
        pltpu.with_memory_space_constraint(array, pltpu.HBM)
        for array in (queries, keys, values, cotangent)
    ]
    mine_kv, finest, c_send, c_mine, rest = pack_coarse(pairs, keys, values, scalar)
    second = exchange(c_send, 1)
    finest = exchange(finest, 2)
    coarse = coarsen_pair(lo, pairs, c_mine, second)
    rest = exchange(ordered(rest, coarse[0]), 1)
    half = exchange(ordered(finest[2 * pairs :], rest), 1)
    kv = rebuild(pairs, second, rest)
    send_qg, mine_qg = pack(pairs, queries, cotangent, scalar)
    qg = exchange(ordered(send_qg, half), 1)
    zs = lo.gather([None, *coarse])
    group = coarsen_group(lo, hi, pairs, coarse[-1], [finest, half], zs)
    turned = turn(pairs, mine_qg, qg)
    rs = hi.gather(group, turned)
    block_sets = [(0, 0, 0, BLOCK), (0, 1, 0, BLOCK)]
    lo_sets = [(1, 2, 0, BLOCK // 2), (1, 3, 0, BLOCK // 2)]
    for level in range(lo.bits):
        for step, row, rows in lo.held[level]:
            lo_sets.append((1 + level, 4 + step, row, rows))
    hi_sets = []
    for level in range(hi.bits):
        for step, row, rows in hi.held[level]:
            hi_sets.append((lo_bits + level, step, row, rows))
    first_in = [mine_kv, kv, finest, half, *zs]
    *kept, tops, sums, partial = attend_first(
        pairs, block_sets + lo_sets, first_in, turned
    )
    *rs_grads, o_keep, o_send, g_scaled, row_dot, dq = attend_last(
        pairs, hi_sets, rs, turned, tops, sums, partial
    )
    shapes = [(2 * pairs, *a.shape[1:]) for a in first_in]
    finest_grad, half_grad, *zs_grads, dq = attend_back(
        pairs,
        [(level, index - 2, row, rows) for level, index, row, rows in lo_sets],
        shapes[2:],
        BOTH,
        kept,
        turned,
        g_scaled,
        row_dot,
        dq,
        False,
    )
    kv_keep, kv_send, dq_keep, dq_send = attend_back(
        pairs, block_sets, shapes[:2], 0, kept, turned, g_scaled, row_dot, dq, True
    )
    og_keep = jnp.concatenate([o_keep, dq_keep], axis=0)
    og_send = jnp.concatenate([o_send, dq_send], axis=0)
    finest_mine = exchange(finest_grad, 2)
    half_back = exchange(half_grad, 1)
    block_second, rest_grad = take_apart(pairs, kv_send)
    rest_back = exchange(ordered(rest_grad, half_back), 1)
    og_back = exchange(ordered(og_send, half_back), 1)
    group_grads = hi.scatter(rs_grads)
    group_grads[-1] = ordered(group_grads[-1], (finest_mine, half_back, kv_send))
    own_grad, grads = spread_group(lo, hi, pairs, group_grads, zs_grads)
    returned = lo.scatter(grads)
    finest_theirs = exchange(ordered(half_back, returned[0]), 2)
    own_grad = ordered(own_grad, (rest_back, og_back))
    second_mine, second_send = spread_pair(lo, pairs, own_grad, returned, block_second)
    second_theirs = exchange(second_send, 1)
    attended, query_grad = unpack(pairs, og_keep, og_back, features, scalar)
    key_grad, value_grad = finish(
        pairs,
        kv_keep,
        rest_back,
        (finest_mine, finest_theirs),
        (second_mine, second_theirs),
        features,
        scalar,
    )
    return attended, query_grad, key_grad, value_grad


def solution(mesh):
    spec = P(AXES, None)
    return jax.shard_map(
        on_device,
        mesh=mesh,
        in_specs=(spec,) * 4,
        out_specs=(spec,) * 4,
        check_vma=False,
    )
```

```python
import math

import jax
import jax.numpy as jnp
from jax import lax
from jax.experimental import pallas as pl
from jax.experimental.pallas import tpu as pltpu
from jax.sharding import PartitionSpec as P

HEADS = 12
BLOCK = 128
HEAD_DIM = 64
LANES = 2 * HEAD_DIM
AXES = ("seqhi", "seqlo")
VMEM_LIMIT = 20 * 1024 * 1024
F32 = jnp.float32
BF16 = jnp.bfloat16
LOG2_E = 1.0 / math.log(2.0)
SCALE = 1.0 / math.sqrt(HEAD_DIM)


def struct(*shape):
    return jax.ShapeDtypeStruct(shape, F32)


def call(kernel, operands, outs, scratch=(), scalar=None, flops=0, exps=0, where=None):
    vmem = pl.BlockSpec(memory_space=pltpu.VMEM)
    smem = pl.BlockSpec(memory_space=pltpu.SMEM)
    in_specs = [pl.BlockSpec(memory_space=where) if where else vmem] * len(operands)
    if scalar is not None:
        operands = [scalar, *operands]
        in_specs = [smem, *in_specs]
    moved = sum(4 * math.prod(a.shape) for a in [*operands, *outs])
    return pl.pallas_call(
        kernel,
        out_shape=list(outs),
        in_specs=in_specs,
        out_specs=[vmem] * len(outs),
        scratch_shapes=list(scratch),
        compiler_params=pltpu.CompilerParams(vmem_limit_bytes=VMEM_LIMIT),
        cost_estimate=pl.CostEstimate(
            flops=flops, bytes_accessed=moved, transcendentals=exps
        ),
    )(*operands)


def exchange(value, offset):
    count = lax.axis_size(AXES)
    return lax.ppermute(value, AXES, [(i, i ^ offset) for i in range(count)])


def ordered(value, after):
    return value if after is None else lax.optimization_barrier((value, after))[0]


def half_difference(ref, lead, first, count):
    even = ref[(*lead, pl.ds(first, count, stride=2), slice(None))]
    odd = ref[(*lead, pl.ds(first + 1, count, stride=2), slice(None))]
    return 0.5 * (even - odd)


def put_pairs(ref, lead, total, difference):
    count = total.shape[0]
    ref[(*lead, pl.ds(0, count, stride=2), slice(None))] = total + difference
    ref[(*lead, pl.ds(1, count, stride=2), slice(None))] = total - difference


def mean_rows(ref, lead, first, count, factor):
    total = None
    for step in range(factor):
        rows = pl.ds(first + step, count, stride=factor)
        part = ref[(*lead, rows, slice(None))]
        total = part if total is None else total + part
    return total * (1.0 / factor)


def add_spread(ref, lead, first, value, factor):
    count = value.shape[0]
    value = value * (1.0 / factor)
    for step in range(factor):
        rows = pl.ds(first + step, count, stride=factor)
        place = (*lead, rows, slice(None))
        ref[place] = ref[place] + value


class Tree:
    def __init__(self, first_bit, own_rows):
        self.bits = bits = len(own_rows)
        self.first_bit = first_bit
        self.own_rows = own_rows
        self.held = {}
        self.payload = {}
        for step in range(bits - 1, -1, -1):
            rows = self.own_rows[step]
            payload = []
            fresh = {step: [(step, 0, rows)] if rows else []}
            for level in range(step + 1, bits):
                for piece in self.held[level]:
                    payload.append(piece)
                    fresh.setdefault(level, []).append((step, rows, piece[2]))
                    rows += piece[2]
            self.payload[step] = payload
            for level, pieces in fresh.items():
                self.held[level] = self.held.get(level, []) + pieces

    def partner(self, value, step):
        return exchange(value, 1 << self.first_bit + step)

    def gather(self, own, after=None):
        arrived = [None] * self.bits
        for step in range(self.bits - 1, -1, -1):
            parts = [own[step]] if self.own_rows[step] else []
            for source, row, rows in self.payload[step]:
                part = arrived[source]
                whole = rows == part.shape[1]
                parts.append(part if whole else part[:, row : row + rows])
            sent = jnp.concatenate(parts, axis=1) if len(parts) > 1 else parts[0]
            if step == 0:
                sent = ordered(sent, after)
            arrived[step] = self.partner(sent, step)
        return arrived

    def scatter(self, grads):
        grads = list(grads)
        returned = []
        for step in range(self.bits):
            back = self.partner(grads[step], step)
            returned.append(back)
            filled = self.own_rows[step]
            for source, row, rows in self.payload[step]:
                part = back[:, filled : filled + rows]
                grads[source] = grads[source].at[:, row : row + rows].add(part)
                filled += rows
        return returned


def split(value):
    high = value.astype(BF16).astype(F32)
    return high, value - high


def halves_by_head(value):
    high, low = split(value)
    first = lax.broadcasted_iota(jnp.int32, value.shape, 1) < HEAD_DIM
    one = jnp.where(first, high, pltpu.roll(low, HEAD_DIM, 1))
    two = jnp.where(first, pltpu.roll(high, HEAD_DIM, 1), low)
    return one.astype(BF16), two.astype(BF16)


def dot(lhs, rhs, dims):
    return lax.dot_general(lhs, rhs, (dims, ((), ())), preferred_element_type=F32)


NN = ((1,), (0,))
NT = ((1,), (1,))
TN = ((0,), (0,))


BOTH = 2 * BLOCK


def halves_of(sets, ins, which, pairs, pair):
    tile = which * pairs + pair
    parts = [ins[index][tile, pl.ds(row, rows), :] for _, index, row, rows in sets]
    return halves_by_head(jnp.concatenate(parts, axis=0))


def segment_levels(sets):
    levels, filled = [], 0
    for level, _, _, rows in sets:
        if filled % BLOCK == 0:
            levels.append(level)
        filled += rows
    return levels


def four_rows(value):
    high, low = split(value)
    four = jnp.concatenate([high, high, low, low], axis=0).astype(BF16)
    return four, jnp.concatenate([high, low], axis=0).astype(BF16)


def store_split(high_ref, low_ref, place, value):
    high = value.astype(BF16)
    high_ref[place] = high
    low_ref[place] = (value - high.astype(F32)).astype(BF16)


def fold_rows(value):
    return value[:HEAD_DIM] + value[HEAD_DIM:]


def fold_heads(one, two):
    first = lax.broadcasted_iota(jnp.int32, one.shape, 1) < HEAD_DIM
    return jnp.where(
        first, one + pltpu.roll(one, HEAD_DIM, 1), two + pltpu.roll(two, HEAD_DIM, 1)
    )


def column_scores(levels, keys_of, q_four, s_ref, highest):
    for index, level in enumerate(levels):
        rows = pl.ds(index * BLOCK, BLOCK)
        half = keys_of(rows)
        s = dot(jnp.concatenate([half, half], axis=1), q_four, NN)
        s = s + float(level) if level else s
        s_ref[rows, :] = s
        top = jnp.max(s.reshape(BLOCK // 8, 8, BOTH), axis=0)
        highest = top if highest is None else jnp.maximum(highest, top)
    return highest


def each_pair(pairs, body):
    if pairs == 1:
        body(0)
    else:
        pl.loop(0, pairs)(body)


def costs(pairs, rows, products, exps=0):
    return dict(
        flops=2 * 4 * products * pairs * 2 * rows * BOTH * HEAD_DIM,
        exps=exps * pairs * 2 * rows * BOTH,
    )


def attend_first(pairs, sets, operands, turned):
    total = sum(s[3] for s in sets)
    levels = segment_levels(sets)

    def kernel(turn_in, *refs):
        ins = refs[: len(operands)]
        kc, vc, eh, el, tops, sums, out, s_ref = refs[len(operands) :]

        def one_pair(pair):
            keys = halves_of(sets, ins, 0, pairs, pair)
            values = halves_of(sets, ins, 1, pairs, pair)
            for head in range(2):
                at = 2 * pair + head
                kc[at] = keys[head]
                vc[at] = values[head]
                part = slice(head * HEAD_DIM, (head + 1) * HEAD_DIM)
                q_four, _ = four_rows(turn_in[pair][part])
                top = column_scores(levels, lambda r: kc[at, r, :], q_four, s_ref, None)
                top = jnp.max(top, axis=0, keepdims=True)
                tops[at] = top
                summed = None
                for index in range(len(levels)):
                    rows = pl.ds(index * BLOCK, BLOCK)
                    e = jnp.exp2(s_ref[rows, :] - top)
                    store_split(eh, el, (at, rows, slice(None)), e)
                    part_sum = jnp.sum(e.reshape(BLOCK // 8, 8, BOTH), axis=0)
                    summed = part_sum if summed is None else summed + part_sum
                sums[at] = jnp.sum(summed, axis=0, keepdims=True)
                o = dot(vc[at], eh[at], TN) + dot(vc[at], el[at], TN)
                out[at] = fold_rows(o)

        each_pair(pairs, one_pair)

    heads = 2 * pairs
    half = jax.ShapeDtypeStruct((heads, total, LANES), BF16)
    exponents = jax.ShapeDtypeStruct((heads, total, BOTH), BF16)
    outs = [half, half, exponents, exponents]
    outs += [struct(heads, 1, BOTH)] * 2 + [struct(heads, HEAD_DIM, BOTH)]
    return call(
        kernel,
        [turned, *operands],
        outs,
        scratch=[pltpu.VMEM((total, BOTH), F32)],
        **costs(pairs, total, 2, 1),
    )


def attend_last(pairs, sets, operands, turned, tops, sums, partial):
    total = sum(s[3] for s in sets)
    levels = segment_levels(sets)

    def kernel(turn_in, top_in, sum_in, part_in, *refs):
        ins = refs[: len(operands)]
        grads = refs[len(operands) : 2 * len(operands)]
        o_keep, o_send, g_out, r_out, dq_out = refs[2 * len(operands) : -7]
        s_ref, eh, el, dh, dl, kc, vc = refs[-7:]

        def one_pair(pair):
            keys = halves_of(sets, ins, 0, pairs, pair)
            values = halves_of(sets, ins, 1, pairs, pair)
            out_t, key_grads, value_grads = [], [], []
            for head in range(2):
                kc[head] = keys[head]
                vc[head] = values[head]
                at = 2 * pair + head
                part = slice(head * HEAD_DIM, (head + 1) * HEAD_DIM)
                q_four, q_rows = four_rows(turn_in[pair][part])
                grad = turn_in[pairs + pair][part]
                top = column_scores(levels, lambda r: kc[head, r, :], q_four, s_ref, None)
                first_top = top_in[at]
                top = jnp.maximum(jnp.max(top, axis=0, keepdims=True), first_top)
                rescale = jnp.exp2(first_top - top)
                summed = None
                for index in range(len(levels)):
                    rows = pl.ds(index * BLOCK, BLOCK)
                    e = jnp.exp2(s_ref[rows, :] - top)
                    s_ref[rows, :] = e
                    store_split(eh, el, (rows, slice(None)), e)
                    part_sum = jnp.sum(e.reshape(BLOCK // 8, 8, BOTH), axis=0)
                    summed = part_sum if summed is None else summed + part_sum
                summed = jnp.sum(summed, axis=0, keepdims=True) + sum_in[at] * rescale
                inverse = 1.0 / summed
                o = dot(vc[head], eh[...], TN) + dot(vc[head], el[...], TN)
                o = (fold_rows(o) + part_in[at] * rescale) * inverse
                out_t.append(o)
                g_scaled = grad * inverse
                g_four, g_rows = four_rows(g_scaled)
                row_dot = jnp.sum(o * g_scaled, axis=0, keepdims=True)
                g_out[at] = g_scaled * rescale
                r_out[at] = row_dot * rescale
                for index in range(len(levels)):
                    rows = pl.ds(index * BLOCK, BLOCK)
                    half = vc[head, rows, :]
                    dp = dot(jnp.concatenate([half, half], axis=1), g_four, NN)
                    ds = s_ref[rows, :] * (dp - row_dot)
                    store_split(dh, dl, (rows, slice(None)), ds)
                dq = dot(kc[head], dh[...], TN) + dot(kc[head], dl[...], TN)
                dq_out[at] = fold_rows(dq)
                key_grads.append(dot(dh[...], q_rows, NT) + dot(dl[...], q_rows, NT))
                value_grads.append(dot(eh[...], g_rows, NT) + dot(el[...], g_rows, NT))
            both = jnp.concatenate(out_t, axis=0).T
            o_keep[pair] = both[:BLOCK]
            o_send[pair] = both[BLOCK:]
            put_grads(pairs, pair, sets, grads, key_grads, value_grads)

        each_pair(pairs, one_pair)

    heads = 2 * pairs
    outs = [struct(*a.shape) for a in operands]
    outs += [struct(pairs, BLOCK, LANES)] * 2
    outs += [struct(heads, HEAD_DIM, BOTH), struct(heads, 1, BOTH)]
    outs.append(struct(heads, HEAD_DIM, BOTH))
    wide = [pltpu.VMEM((total, BOTH), BF16)] * 4
    return call(
        kernel,
        [turned, tops, sums, partial, *operands],
        outs,
        scratch=[pltpu.VMEM((total, BOTH), F32)]
        + wide
        + [pltpu.VMEM((2, total, LANES), BF16)] * 2,
        **costs(pairs, total, 6, 1),
    )


def put_grads(pairs, pair, sets, grads, key_grads, value_grads):
    for which, parts in enumerate((key_grads, value_grads)):
        both = fold_heads(*parts)
        if which == 0:
            both = both * (1.0 / LOG2_E)
        filled = 0
        for _, index, row, rows in sets:
            piece = both[filled : filled + rows]
            grads[index][which * pairs + pair, pl.ds(row, rows), :] = piece
            filled += rows


def attend_back(pairs, sets, shapes, first, kept, turned, g_scaled, row_dot, dq, last):
    total = sum(s[3] for s in sets)
    segments = total // BLOCK

    def kernel(turn_in, kc, vc, eh, el, g_in, r_in, dq_in, *refs):
        grads = refs[: len(shapes)]
        dq_out = refs[len(shapes) : -2]
        dh, dl = refs[-2:]
        span = pl.ds(first, total)

        def one_pair(pair):
            dq_t, key_grads, value_grads = [], [], []
            for head in range(2):
                at = 2 * pair + head
                part = slice(head * HEAD_DIM, (head + 1) * HEAD_DIM)
                _, q_rows = four_rows(turn_in[pair][part])
                g_four, g_rows = four_rows(g_in[at])
                dots = r_in[at]
                for index in range(segments):
                    rows = pl.ds(first + index * BLOCK, BLOCK)
                    half = vc[at, rows, :]
                    dp = dot(jnp.concatenate([half, half], axis=1), g_four, NN)
                    e = eh[at, rows, :].astype(F32) + el[at, rows, :].astype(F32)
                    place = (pl.ds(index * BLOCK, BLOCK), slice(None))
                    store_split(dh, dl, place, e * (dp - dots))
                keys = kc[at, span, :]
                part_dq = dot(keys, dh[...], TN) + dot(keys, dl[...], TN)
                dq_t.append(fold_rows(part_dq) + dq_in[at])
                key_grads.append(dot(dh[...], q_rows, NT) + dot(dl[...], q_rows, NT))
                value_grads.append(
                    dot(eh[at, span, :], g_rows, NT) + dot(el[at, span, :], g_rows, NT)
                )
            put_grads(pairs, pair, sets, grads, key_grads, value_grads)
            if last:
                both = jnp.concatenate(dq_t, axis=0).T * SCALE
                dq_out[0][pair] = both[:BLOCK]
                dq_out[1][pair] = both[BLOCK:]
            else:
                for head in range(2):
                    dq_out[0][2 * pair + head] = dq_t[head]

        each_pair(pairs, one_pair)

    outs = [struct(*shape) for shape in shapes]
    if last:
        outs += [struct(pairs, BLOCK, LANES)] * 2
    else:
        outs.append(struct(*dq.shape))
    return call(
        kernel,
        [turned, *kept, g_scaled, row_dot, dq],
        outs,
        scratch=[pltpu.VMEM((total, BOTH), BF16)] * 2,
        **costs(pairs, total, 4),
    )


def copy_columns(moves, ins, sems, bit):
    started = []
    for operand, theirs, column, place in moves:
        side = 1 - bit if theirs else bit
        column = side * (ins[operand].shape[1] // 2) + column
        column = pl.ds(pl.multiple_of(column, LANES), LANES)
        copy = pltpu.make_async_copy(
            ins[operand].at[:, column], place, sems.at[len(started)]
        )
        copy.start()
        started.append(copy)
    return started


def pack(pairs, first, second, scalar):
    def kernel(bit, one, two, theirs, mine, sems):
        moves = []
        for tile in range(2 * pairs):
            for out, other in ((theirs, True), (mine, False)):
                column = tile % pairs * LANES
                moves.append((tile // pairs, other, column, out.at[tile]))
        for copy in copy_columns(moves, (one, two), sems, bit[0]):
            copy.wait()

    return call(
        kernel,
        [first, second],
        [struct(2 * pairs, BLOCK, LANES)] * 2,
        scratch=[pltpu.SemaphoreType.DMA((4 * pairs,))],
        scalar=scalar,
        where=pl.ANY,
    )


QUARTER = BLOCK // 4
HALF = BLOCK // 2


def pack_coarse(pairs, keys, values, scalar):
    def kernel(bit, k, v, mine, f_theirs, f_mine, c_theirs, c_mine, rest, theirs, sems):
        moves = []
        for out, other in ((theirs, True), (mine, False)):
            for tile in range(2 * pairs):
                column = tile % pairs * LANES
                moves.append((tile // pairs, other, column, out.at[tile]))
        copies = copy_columns(moves, (k, v), sems, bit[0])
        for index, copy in enumerate(copies):
            copy.wait()
            tile = index % (2 * pairs)
            other = index < 2 * pairs
            source, finest, coarse = (
                (theirs, f_theirs, c_theirs) if other else (mine, f_mine, c_mine)
            )
            finest[tile] = mean_rows(source, (tile,), 0, HALF, 2)
            coarse[tile] = mean_rows(finest, (tile,), 0, QUARTER, 2)
            if other:
                rest[tile, :QUARTER] = half_difference(finest, (tile,), 0, QUARTER)
                rest[tile, QUARTER:] = half_difference(source, (tile,), 0, HALF)

    return call(
        kernel,
        [keys, values],
        [struct(2 * pairs, BLOCK, LANES)]
        + [struct(2 * pairs, HALF, LANES)] * 2
        + [struct(2 * pairs, QUARTER, LANES)] * 2
        + [struct(2 * pairs, QUARTER + HALF, LANES)],
        scratch=[
            pltpu.VMEM((2 * pairs, BLOCK, LANES), F32),
            pltpu.SemaphoreType.DMA((4 * pairs,)),
        ],
        scalar=scalar,
        where=pl.ANY,
    )


def rebuild(pairs, second, rest):
    def kernel(second_in, rest_in, out, finest):
        for tile in range(2 * pairs):
            put_pairs(finest, (tile,), second_in[tile], rest_in[tile, :QUARTER])
            put_pairs(out, (tile,), finest[tile], rest_in[tile, QUARTER:])

    return call(
        kernel,
        [second, rest],
        [struct(2 * pairs, BLOCK, LANES)],
        scratch=[pltpu.VMEM((2 * pairs, HALF, LANES), F32)],
    )[0]


def take_apart(pairs, block_grad):
    def kernel(block, second, rest, finest):
        for tile in range(2 * pairs):
            finest[tile] = 2.0 * mean_rows(block, (tile,), 0, HALF, 2)
            rest[tile, QUARTER:] = 2.0 * half_difference(block, (tile,), 0, HALF)
            second[tile] = 2.0 * mean_rows(finest, (tile,), 0, QUARTER, 2)
            rest[tile, :QUARTER] = 2.0 * half_difference(finest, (tile,), 0, QUARTER)

    return call(
        kernel,
        [block_grad],
        [
            struct(2 * pairs, QUARTER, LANES),
            struct(2 * pairs, QUARTER + HALF, LANES),
        ],
        scratch=[pltpu.VMEM((2 * pairs, HALF, LANES), F32)],
    )


class Levels:
    def __init__(self, bits):
        self.bits = bits
        self.rows = BLOCK >> bits
        self.differences = [
            [(m, BLOCK >> m) for m in range(bits, step, -1)] for step in range(bits)
        ]
        sums = [0] + [(BLOCK >> step) - self.rows for step in range(1, bits)]
        self.rough = Tree(1, [0] + [self.rows] * (bits - 1))
        self.fine = Tree(1, sums)
        self.pieces = []
        for level in range(1, bits):
            place = 0
            for rough, fine in zip(self.rough.held[level], self.fine.held[level]):
                self.pieces.append((level, rough[0], rough[1], fine[1], place))
                place += BLOCK >> level

    def scratch(self):
        shapes = [(BLOCK >> m, LANES) for m in range(1, self.bits + 1)]
        return [pltpu.VMEM(shape, F32) for shape in shapes]


def coarsen_pair(levels, pairs, mine, received):
    def kernel(own, got, rough, *refs):
        outs = refs[: levels.bits - 1]
        ladder = refs[levels.bits - 1 :]
        for tile in range(2 * pairs):
            ladder[0][:QUARTER, :] = own[tile]
            ladder[0][QUARTER:, :] = got[tile]
            for m in range(2, levels.bits + 1):
                ladder[m - 1][...] = mean_rows(ladder[m - 2], (), 0, BLOCK >> m, 2)
            rough[tile] = ladder[levels.bits - 1][...]
            for step in range(1, levels.bits):
                filled = 0
                for m, rows in levels.differences[step]:
                    outs[step - 1][tile, pl.ds(filled, rows)] = half_difference(
                        ladder[m - 2], (), 0, rows
                    )
                    filled += rows

    outs = [struct(2 * pairs, levels.rows, LANES)]
    outs += [struct(2 * pairs, rows, LANES) for rows in levels.fine.own_rows[1:]]
    rough, *fine = call(kernel, [mine, received], outs, scratch=levels.scratch())
    return rough, fine


def rebuild_levels(levels, pairs, rough, fine):
    def kernel(*refs):
        rough_in = refs[: levels.bits]
        fine_in = refs[levels.bits : 2 * levels.bits]
        outs = refs[2 * levels.bits : 3 * levels.bits - 1]
        ladder = refs[3 * levels.bits - 1 :]
        for tile in range(2 * pairs):
            for level, step, rough_row, fine_row, place in levels.pieces:
                current = rough_in[step][tile, pl.ds(rough_row, levels.rows)]
                for m, rows in levels.differences[level]:
                    part = fine_in[step][tile, pl.ds(fine_row, rows)]
                    fine_row += rows
                    put_pairs(ladder[m - 2], (), current, part)
                    current = ladder[m - 2][...]
                outs[level - 1][tile, pl.ds(place, BLOCK >> level)] = current

    outs = [struct(2 * pairs, BLOCK, LANES)] * (levels.bits - 1)
    return call(kernel, [*rough, *fine], outs, scratch=levels.scratch())


def take_levels(levels, pairs, grads, rough_shapes, fine_shapes):
    def kernel(*refs):
        ins = refs[: levels.bits - 1]
        rough = refs[levels.bits - 1 : 2 * levels.bits - 1]
        fine = refs[2 * levels.bits - 1 : 3 * levels.bits - 1]
        ladder = refs[3 * levels.bits - 1 :]
        for tile in range(2 * pairs):
            for level, step, rough_row, fine_row, place in levels.pieces:
                source = ladder[level - 1]
                source[...] = ins[level - 1][tile, pl.ds(place, BLOCK >> level)]
                fine_row += sum(rows for _, rows in levels.differences[level])
                for m, rows in reversed(levels.differences[level]):
                    fine_row -= rows
                    part = 2.0 * half_difference(source, (), 0, rows)
                    fine[step][tile, pl.ds(fine_row, rows)] = part
                    ladder[m - 1][...] = 2.0 * mean_rows(source, (), 0, rows, 2)
                    source = ladder[m - 1]
                rough[step][tile, pl.ds(rough_row, levels.rows)] = source[...]

    outs = [struct(*shape) for shape in [*rough_shapes, *fine_shapes]]
    outs = call(kernel, grads, outs, scratch=levels.scratch())
    return outs[: levels.bits], outs[levels.bits :]


def group_pieces(levels):
    pieces = []
    for index, (_, step, row, _, _) in enumerate(levels.pieces):
        pieces.append((step, row, (2 + index) * levels.rows))
    return pieces


def coarsen_group(levels, hi, pairs, own, halves, rough):
    rows = levels.rows
    factor = 1 << levels.bits

    def kernel(own_in, one, two, *refs):
        ins = refs[: levels.bits]
        outs = refs[levels.bits :]
        for tile in range(2 * pairs):
            outs[0][tile, pl.ds(0, rows)] = own_in[tile]
            for index, half in enumerate((one, two)):
                outs[0][tile, pl.ds(rows + index * rows // 2, rows // 2)] = mean_rows(
                    half, (tile,), 0, rows // 2, factor
                )
            for step, row, place in group_pieces(levels):
                outs[0][tile, pl.ds(place, rows)] = ins[step][tile, pl.ds(row, rows)]
            for step in range(1, hi.bits):
                outs[step][tile] = mean_rows(
                    outs[step - 1], (tile,), 0, BLOCK >> step, 2
                )

    outs = [struct(2 * pairs, BLOCK >> step, LANES) for step in range(hi.bits)]
    return call(kernel, [own, *halves, *rough], outs)


def turn(pairs, mine, received):
    def kernel(own, got, turned):
        for tile in range(2 * pairs):
            both = jnp.concatenate([own[tile], got[tile]], axis=0).T
            turned[tile] = both * (SCALE * LOG2_E) if tile < pairs else both

    return call(kernel, [mine, received], [struct(2 * pairs, LANES, 2 * BLOCK)])[0]


def spread_group(levels, hi, pairs, group_grads, grads):
    own_rows = levels.rows

    def kernel(*refs):
        steps = refs[: hi.bits]
        ins = refs[hi.bits : hi.bits + levels.bits]
        own_out, *outs = refs[hi.bits + levels.bits : -1]
        total = refs[-1]
        for tile in range(2 * pairs):
            total[tile] = steps[0][tile, pl.ds(0, BLOCK)]
            for step in range(1, hi.bits):
                above = steps[step][tile, pl.ds(0, BLOCK >> step)]
                add_spread(total, (tile,), 0, above, 1 << step)
            own_out[tile] = total[tile, pl.ds(0, own_rows)]
            for step, row, place in group_pieces(levels):
                rows = pl.ds(row, own_rows)
                part = total[tile, pl.ds(place, own_rows)]
                outs[step][tile, rows] = ins[step][tile, rows] + part
            outs[0][tile, pl.ds(ins[0].shape[1], own_rows)] = total[
                tile, pl.ds(own_rows, own_rows)
            ]

    shapes = [list(a.shape) for a in grads]
    shapes[0][1] += own_rows
    outs = [struct(2 * pairs, own_rows, LANES)] + [struct(*shape) for shape in shapes]
    own, *grads = call(
        kernel,
        [*group_grads, *grads],
        outs,
        scratch=[pltpu.VMEM((2 * pairs, BLOCK, LANES), F32)],
    )
    return own, grads


def spread_pair(levels, pairs, own_grad, rough, fine, block_second):
    own_rows = levels.rows

    def kernel(own, block, *refs):
        rough_in = refs[: levels.bits]
        fine_in = refs[levels.bits : 2 * levels.bits]
        mine, theirs, *ladder = refs[2 * levels.bits :]
        last = pl.ds(rough_in[0].shape[1] - own_rows, own_rows)
        for tile in range(2 * pairs):
            above = own[tile] + rough_in[0][tile, last]
            for step in range(1, levels.bits):
                above = above + rough_in[step][tile, pl.ds(0, own_rows)]
            filled = 0
            for m, rows in levels.differences[1]:
                part = fine_in[1][tile, pl.ds(filled, rows)]
                for step in range(2, min(m, levels.bits)):
                    part = part + fine_in[step][tile, pl.ds(filled, rows)]
                filled += rows
                put_pairs(ladder[m - 2], (), 0.5 * above, 0.5 * part)
                above = ladder[m - 2][...]
            mine[tile] = above[:QUARTER]
            theirs[tile] = above[QUARTER:] + block[tile]

    return call(
        kernel,
        [own_grad, block_second, *rough, *fine],
        [struct(2 * pairs, QUARTER, LANES)] * 2,
        scratch=levels.scratch(),
    )


def unpack(pairs, kept, arrived, features, scalar):
    def kernel(bit, mine, theirs, *outs):
        for tile in range(2 * pairs):
            for side, array in ((bit[0], mine), (1 - bit[0], theirs)):
                column = side * (features // 2) + tile % pairs * LANES
                column = pl.ds(pl.multiple_of(column, LANES), LANES)
                outs[tile // pairs][:, column] = array[tile]

    return call(kernel, [kept, arrived], [struct(BLOCK, features)] * 2, scalar=scalar)


def finish(pairs, kept, rest, finest, seconds, features, scalar):
    def kernel(bit, kept_in, rest_in, f_mine, f_theirs, s_mine, s_theirs, *refs):
        outs, total, middle = refs[:2], refs[2], refs[3]
        for tile in range(2 * pairs):
            out = outs[tile // pairs]
            column = tile % pairs * LANES
            at = (tile,)
            total[tile] = kept_in[tile]
            add_spread(total, at, 0, f_mine[tile], 2)
            add_spread(total, at, 0, s_mine[tile], 4)
            place = bit[0] * (features // 2) + column
            out[:, pl.ds(pl.multiple_of(place, LANES), LANES)] = total[tile]
            put_pairs(middle, at, 0.5 * s_theirs[tile], 0.5 * rest_in[tile, :QUARTER])
            first = 0.5 * (middle[tile] + f_theirs[tile])
            put_pairs(total, at, first, 0.5 * rest_in[tile, QUARTER:])
            place = (1 - bit[0]) * (features // 2) + column
            out[:, pl.ds(pl.multiple_of(place, LANES), LANES)] = total[tile]

    return call(
        kernel,
        [kept, rest, *finest, *seconds],
        [struct(BLOCK, features)] * 2,
        scratch=[
            pltpu.VMEM((2 * pairs, BLOCK, LANES), F32),
            pltpu.VMEM((2 * pairs, HALF, LANES), F32),
        ],
        scalar=scalar,
    )


def on_device(queries, keys, values, cotangent):
    features = queries.shape[1]
    assert queries.shape[0] == BLOCK
    pairs = features // LANES // 2
    lo_bits = lax.axis_size("seqlo").bit_length() - 1
    levels = Levels(lo_bits - 1)
    hi_bits = lax.axis_size("seqhi").bit_length() - 1
    hi = Tree(lo_bits, [BLOCK >> step for step in range(hi_bits)])
    scalar = (lax.axis_index("seqlo") % 2).astype(jnp.int32).reshape(1)
    queries, keys, values, cotangent = [
        pltpu.with_memory_space_constraint(array, pltpu.HBM)
        for array in (queries, keys, values, cotangent)
    ]
    mine_kv, f_theirs, f_mine, c_send, c_mine, rest = pack_coarse(
        pairs, keys, values, scalar
    )
    second = exchange(c_send, 1)
    finest_theirs = exchange(f_theirs, 2)
    own_rough, own_fine = coarsen_pair(levels, pairs, c_mine, second)
    rough = levels.rough.gather([None] + [own_rough] * (levels.bits - 1))
    finest = exchange(f_mine, 2)
    rest = exchange(ordered(rest, own_rough), 1)
    half = exchange(ordered(finest_theirs, (rest, rough[-1])), 1)
    kv = rebuild(pairs, second, rest)
    send_qg, mine_qg = pack(pairs, queries, cotangent, scalar)
    qg = exchange(ordered(send_qg, half), 1)
    own_fine = ordered(own_fine, rough[-1])
    fine = levels.fine.gather([None, *own_fine])
    own_rough = ordered(own_rough, fine[-1])
    group = coarsen_group(levels, hi, pairs, own_rough, [finest, half], rough)
    turned = turn(pairs, mine_qg, ordered(qg, fine[0]))
    rs = hi.gather(group, turned)
    lo_levels = rebuild_levels(levels, pairs, rough, fine)
    block_sets = [(0, 0, 0, BLOCK), (0, 1, 0, BLOCK)]
    lo_sets = [(1, 2, 0, HALF), (1, 3, 0, HALF)]
    for level in range(1, levels.bits):
        lo_sets.append((1 + level, 3 + level, 0, BLOCK))
    hi_sets = []
    for level in range(hi.bits):
        for step, row, rows in hi.held[level]:
            hi_sets.append((lo_bits + level, step, row, rows))
    first_in = [mine_kv, kv, finest, half, *lo_levels]
    *kept, tops, sums, partial = attend_first(
        pairs, block_sets + lo_sets, first_in, turned
    )
    *rs_grads, o_keep, o_send, g_scaled, row_dot, dq = attend_last(
        pairs, hi_sets, rs, turned, tops, sums, partial
    )
    shapes = [a.shape for a in first_in]
    finest_grad, half_grad, *level_grads, dq = attend_back(
        pairs,
        [(level, index - 2, row, rows) for level, index, row, rows in lo_sets],
        shapes[2:],
        BOTH,
        kept,
        turned,
        g_scaled,
        row_dot,
        dq,
        False,
    )
    kv_keep, kv_send, dq_keep, dq_send = attend_back(
        pairs, block_sets, shapes[:2], 0, kept, turned, g_scaled, row_dot, dq, True
    )
    og_keep = jnp.concatenate([o_keep, dq_keep], axis=0)
    og_send = jnp.concatenate([o_send, dq_send], axis=0)
    rough_grads, fine_grads = take_levels(
        levels, pairs, level_grads, [a.shape for a in rough], [a.shape for a in fine]
    )
    finest_mine = exchange(finest_grad, 2)
    half_back = exchange(half_grad, 1)
    fine_back = levels.fine.scatter(fine_grads)
    block_second, rest_grad = take_apart(pairs, kv_send)
    rest_back = exchange(ordered(rest_grad, half_back), 1)
    og_back = exchange(ordered(og_send, half_back), 1)
    group_grads = hi.scatter(rs_grads)
    group_grads[-1] = ordered(
        group_grads[-1], (finest_mine, half_back, fine_back[0], kv_send)
    )
    own_grad, rough_grads = spread_group(levels, hi, pairs, group_grads, rough_grads)
    rough_back = levels.rough.scatter(rough_grads)
    finest_theirs = exchange(ordered(half_back, rough_back[0]), 2)
    own_grad = ordered(own_grad, (rest_back, og_back))
    second_mine, second_send = spread_pair(
        levels, pairs, own_grad, rough_back, fine_back, block_second
    )
    second_theirs = exchange(second_send, 1)
    attended, query_grad = unpack(pairs, og_keep, og_back, features, scalar)
    key_grad, value_grad = finish(
        pairs,
        kv_keep,
        rest_back,
        (finest_mine, finest_theirs),
        (second_mine, second_theirs),
        features,
        scalar,
    )
    return attended, query_grad, key_grad, value_grad


def solution(mesh):
    spec = P(AXES, None)
    return jax.shard_map(
        on_device,
        mesh=mesh,
        in_specs=(spec,) * 4,
        out_specs=(spec,) * 4,
        check_vma=False,
    )
```

```python
import math

import jax
import jax.numpy as jnp
from jax import lax
from jax.experimental import pallas as pl
from jax.experimental.pallas import tpu as pltpu
from jax.sharding import PartitionSpec as P

HEADS = 12
BLOCK = 128
HEAD_DIM = 64
LANES = 2 * HEAD_DIM
AXES = ("seqhi", "seqlo")
VMEM_LIMIT = 20 * 1024 * 1024
F32 = jnp.float32
BF16 = jnp.bfloat16
LOG2_E = 1.0 / math.log(2.0)
SCALE = 1.0 / math.sqrt(HEAD_DIM)


def struct(*shape):
    return jax.ShapeDtypeStruct(shape, F32)


def call(kernel, operands, outs, scratch=(), scalar=None, flops=0, exps=0, where=None):
    vmem = pl.BlockSpec(memory_space=pltpu.VMEM)
    smem = pl.BlockSpec(memory_space=pltpu.SMEM)
    in_specs = [pl.BlockSpec(memory_space=where) if where else vmem] * len(operands)
    if scalar is not None:
        operands = [scalar, *operands]
        in_specs = [smem, *in_specs]
    moved = sum(4 * math.prod(a.shape) for a in [*operands, *outs])
    return pl.pallas_call(
        kernel,
        out_shape=list(outs),
        in_specs=in_specs,
        out_specs=[vmem] * len(outs),
        scratch_shapes=list(scratch),
        compiler_params=pltpu.CompilerParams(vmem_limit_bytes=VMEM_LIMIT),
        cost_estimate=pl.CostEstimate(
            flops=flops, bytes_accessed=moved, transcendentals=exps
        ),
    )(*operands)


def exchange(value, offset):
    count = lax.axis_size(AXES)
    return lax.ppermute(value, AXES, [(i, i ^ offset) for i in range(count)])


def ordered(value, after):
    return value if after is None else lax.optimization_barrier((value, after))[0]


def half_difference(ref, lead, first, count):
    even = ref[(*lead, pl.ds(first, count, stride=2), slice(None))]
    odd = ref[(*lead, pl.ds(first + 1, count, stride=2), slice(None))]
    return 0.5 * (even - odd)


def put_pairs(ref, lead, total, difference):
    count = total.shape[0]
    ref[(*lead, pl.ds(0, count, stride=2), slice(None))] = total + difference
    ref[(*lead, pl.ds(1, count, stride=2), slice(None))] = total - difference


def mean_rows(ref, lead, first, count, factor):
    total = None
    for step in range(factor):
        rows = pl.ds(first + step, count, stride=factor)
        part = ref[(*lead, rows, slice(None))]
        total = part if total is None else total + part
    return total * (1.0 / factor)


def add_spread(ref, lead, first, value, factor):
    count = value.shape[0]
    value = value * (1.0 / factor)
    for step in range(factor):
        rows = pl.ds(first + step, count, stride=factor)
        place = (*lead, rows, slice(None))
        ref[place] = ref[place] + value


class Tree:
    def __init__(self, bits, first_bit, lowest=True):
        self.bits = bits
        self.first_bit = first_bit
        self.own_rows = [BLOCK >> step for step in range(bits)]
        if not lowest:
            self.own_rows[0] = 0
        self.held = {}
        self.payload = {}
        for step in range(bits - 1, -1, -1):
            rows = self.own_rows[step]
            payload = []
            fresh = {step: [(step, 0, rows)] if rows else []}
            for level in range(step + 1, bits):
                for piece in self.held[level]:
                    payload.append(piece)
                    fresh.setdefault(level, []).append((step, rows, piece[2]))
                    rows += piece[2]
            self.payload[step] = payload
            for level, pieces in fresh.items():
                self.held[level] = self.held.get(level, []) + pieces

    def partner(self, value, step):
        return exchange(value, 1 << self.first_bit + step)

    def gather(self, own, after=None):
        arrived = [None] * self.bits
        for step in range(self.bits - 1, -1, -1):
            parts = [own[step]] if self.own_rows[step] else []
            for source, row, rows in self.payload[step]:
                part = arrived[source]
                whole = rows == part.shape[1]
                parts.append(part if whole else part[:, row : row + rows])
            sent = jnp.concatenate(parts, axis=1) if len(parts) > 1 else parts[0]
            if step == 0:
                sent = ordered(sent, after)
            arrived[step] = self.partner(sent, step)
        return arrived

    def scatter(self, grads):
        grads = list(grads)
        returned = []
        for step in range(self.bits):
            back = self.partner(grads[step], step)
            returned.append(back)
            filled = self.own_rows[step]
            for source, row, rows in self.payload[step]:
                part = back[:, filled : filled + rows]
                grads[source] = grads[source].at[:, row : row + rows].add(part)
                filled += rows
        return returned


def split(value):
    high = value.astype(BF16).astype(F32)
    return high, value - high


def halves_by_head(value):
    high, low = split(value)
    first = lax.broadcasted_iota(jnp.int32, value.shape, 1) < HEAD_DIM
    one = jnp.where(first, high, pltpu.roll(low, HEAD_DIM, 1))
    two = jnp.where(first, pltpu.roll(high, HEAD_DIM, 1), low)
    return one.astype(BF16), two.astype(BF16)


def dot(lhs, rhs, dims):
    return lax.dot_general(lhs, rhs, (dims, ((), ())), preferred_element_type=F32)


NN = ((1,), (0,))
NT = ((1,), (1,))
TN = ((0,), (0,))


BOTH = 2 * BLOCK


def halves_of(sets, ins, which, pairs, pair):
    tile = which * pairs + pair
    parts = [ins[index][tile, pl.ds(row, rows), :] for _, index, row, rows in sets]
    return halves_by_head(jnp.concatenate(parts, axis=0))


def segment_levels(sets):
    levels, filled = [], 0
    for level, _, _, rows in sets:
        if filled % BLOCK == 0:
            levels.append(level)
        filled += rows
    return levels


def four_rows(value):
    high, low = split(value)
    four = jnp.concatenate([high, high, low, low], axis=0).astype(BF16)
    return four, jnp.concatenate([high, low], axis=0).astype(BF16)


def store_split(high_ref, low_ref, place, value):
    high = value.astype(BF16)
    high_ref[place] = high
    low_ref[place] = (value - high.astype(F32)).astype(BF16)


def fold_rows(value):
    return value[:HEAD_DIM] + value[HEAD_DIM:]


def fold_heads(one, two):
    first = lax.broadcasted_iota(jnp.int32, one.shape, 1) < HEAD_DIM
    return jnp.where(
        first, one + pltpu.roll(one, HEAD_DIM, 1), two + pltpu.roll(two, HEAD_DIM, 1)
    )


def column_scores(levels, keys_of, q_four, s_ref, highest):
    for index, level in enumerate(levels):
        rows = pl.ds(index * BLOCK, BLOCK)
        half = keys_of(rows)
        s = dot(jnp.concatenate([half, half], axis=1), q_four, NN)
        s = s + float(level) if level else s
        s_ref[rows, :] = s
        top = jnp.max(s.reshape(BLOCK // 8, 8, BOTH), axis=0)
        highest = top if highest is None else jnp.maximum(highest, top)
    return highest


def each_pair(pairs, body):
    if pairs == 1:
        body(0)
    else:
        pl.loop(0, pairs)(body)


def costs(pairs, rows, products, exps=0):
    return dict(
        flops=2 * 4 * products * pairs * 2 * rows * BOTH * HEAD_DIM,
        exps=exps * pairs * 2 * rows * BOTH,
    )


def attend_first(pairs, sets, operands, turned):
    total = sum(s[3] for s in sets)
    levels = segment_levels(sets)

    def kernel(turn_in, *refs):
        ins = refs[: len(operands)]
        kc, vc, eh, el, tops, sums, out, s_ref = refs[len(operands) :]

        def one_pair(pair):
            keys = halves_of(sets, ins, 0, pairs, pair)
            values = halves_of(sets, ins, 1, pairs, pair)
            for head in range(2):
                at = 2 * pair + head
                kc[at] = keys[head]
                vc[at] = values[head]
                part = slice(head * HEAD_DIM, (head + 1) * HEAD_DIM)
                q_four, _ = four_rows(turn_in[pair][part])
                top = column_scores(levels, lambda r: kc[at, r, :], q_four, s_ref, None)
                top = jnp.max(top, axis=0, keepdims=True)
                tops[at] = top
                summed = None
                for index in range(len(levels)):
                    rows = pl.ds(index * BLOCK, BLOCK)
                    e = jnp.exp2(s_ref[rows, :] - top)
                    store_split(eh, el, (at, rows, slice(None)), e)
                    part_sum = jnp.sum(e.reshape(BLOCK // 8, 8, BOTH), axis=0)
                    summed = part_sum if summed is None else summed + part_sum
                sums[at] = jnp.sum(summed, axis=0, keepdims=True)
                o = dot(vc[at], eh[at], TN) + dot(vc[at], el[at], TN)
                out[at] = fold_rows(o)

        each_pair(pairs, one_pair)

    heads = 2 * pairs
    half = jax.ShapeDtypeStruct((heads, total, LANES), BF16)
    exponents = jax.ShapeDtypeStruct((heads, total, BOTH), BF16)
    outs = [half, half, exponents, exponents]
    outs += [struct(heads, 1, BOTH)] * 2 + [struct(heads, HEAD_DIM, BOTH)]
    return call(
        kernel,
        [turned, *operands],
        outs,
        scratch=[pltpu.VMEM((total, BOTH), F32)],
        **costs(pairs, total, 2, 1),
    )


def attend_last(pairs, sets, operands, turned, tops, sums, partial):
    total = sum(s[3] for s in sets)
    levels = segment_levels(sets)

    def kernel(turn_in, top_in, sum_in, part_in, *refs):
        ins = refs[: len(operands)]
        grads = refs[len(operands) : 2 * len(operands)]
        o_keep, o_send, g_out, r_out, dq_out = refs[2 * len(operands) : -7]
        s_ref, eh, el, dh, dl, kc, vc = refs[-7:]

        def one_pair(pair):
            keys = halves_of(sets, ins, 0, pairs, pair)
            values = halves_of(sets, ins, 1, pairs, pair)
            out_t, key_grads, value_grads = [], [], []
            for head in range(2):
                kc[head] = keys[head]
                vc[head] = values[head]
                at = 2 * pair + head
                part = slice(head * HEAD_DIM, (head + 1) * HEAD_DIM)
                q_four, q_rows = four_rows(turn_in[pair][part])
                grad = turn_in[pairs + pair][part]
                top = column_scores(levels, lambda r: kc[head, r, :], q_four, s_ref, None)
                first_top = top_in[at]
                top = jnp.maximum(jnp.max(top, axis=0, keepdims=True), first_top)
                rescale = jnp.exp2(first_top - top)
                summed = None
                for index in range(len(levels)):
                    rows = pl.ds(index * BLOCK, BLOCK)
                    e = jnp.exp2(s_ref[rows, :] - top)
                    s_ref[rows, :] = e
                    store_split(eh, el, (rows, slice(None)), e)
                    part_sum = jnp.sum(e.reshape(BLOCK // 8, 8, BOTH), axis=0)
                    summed = part_sum if summed is None else summed + part_sum
                summed = jnp.sum(summed, axis=0, keepdims=True) + sum_in[at] * rescale
                inverse = 1.0 / summed
                o = dot(vc[head], eh[...], TN) + dot(vc[head], el[...], TN)
                o = (fold_rows(o) + part_in[at] * rescale) * inverse
                out_t.append(o)
                g_scaled = grad * inverse
                g_four, g_rows = four_rows(g_scaled)
                row_dot = jnp.sum(o * g_scaled, axis=0, keepdims=True)
                g_out[at] = g_scaled * rescale
                r_out[at] = row_dot * rescale
                for index in range(len(levels)):
                    rows = pl.ds(index * BLOCK, BLOCK)
                    half = vc[head, rows, :]
                    dp = dot(jnp.concatenate([half, half], axis=1), g_four, NN)
                    ds = s_ref[rows, :] * (dp - row_dot)
                    store_split(dh, dl, (rows, slice(None)), ds)
                dq = dot(kc[head], dh[...], TN) + dot(kc[head], dl[...], TN)
                dq_out[at] = fold_rows(dq)
                key_grads.append(dot(dh[...], q_rows, NT) + dot(dl[...], q_rows, NT))
                value_grads.append(dot(eh[...], g_rows, NT) + dot(el[...], g_rows, NT))
            both = jnp.concatenate(out_t, axis=0).T
            o_keep[pair] = both[:BLOCK]
            o_send[pair] = both[BLOCK:]
            put_grads(pairs, pair, sets, grads, key_grads, value_grads)

        each_pair(pairs, one_pair)

    heads = 2 * pairs
    outs = [struct(*a.shape) for a in operands]
    outs += [struct(pairs, BLOCK, LANES)] * 2
    outs += [struct(heads, HEAD_DIM, BOTH), struct(heads, 1, BOTH)]
    outs.append(struct(heads, HEAD_DIM, BOTH))
    wide = [pltpu.VMEM((total, BOTH), BF16)] * 4
    return call(
        kernel,
        [turned, tops, sums, partial, *operands],
        outs,
        scratch=[pltpu.VMEM((total, BOTH), F32)]
        + wide
        + [pltpu.VMEM((2, total, LANES), BF16)] * 2,
        **costs(pairs, total, 6, 1),
    )


def put_grads(pairs, pair, sets, grads, key_grads, value_grads):
    for which, parts in enumerate((key_grads, value_grads)):
        both = fold_heads(*parts)
        if which == 0:
            both = both * (1.0 / LOG2_E)
        filled = 0
        for _, index, row, rows in sets:
            piece = both[filled : filled + rows]
            grads[index][which * pairs + pair, pl.ds(row, rows), :] = piece
            filled += rows


def attend_back(pairs, sets, shapes, first, kept, turned, g_scaled, row_dot, dq, last):
    total = sum(s[3] for s in sets)
    segments = total // BLOCK

    def kernel(turn_in, kc, vc, eh, el, g_in, r_in, dq_in, *refs):
        grads = refs[: len(shapes)]
        dq_out = refs[len(shapes) : -2]
        dh, dl = refs[-2:]
        span = pl.ds(first, total)

        def one_pair(pair):
            dq_t, key_grads, value_grads = [], [], []
            for head in range(2):
                at = 2 * pair + head
                part = slice(head * HEAD_DIM, (head + 1) * HEAD_DIM)
                _, q_rows = four_rows(turn_in[pair][part])
                g_four, g_rows = four_rows(g_in[at])
                dots = r_in[at]
                for index in range(segments):
                    rows = pl.ds(first + index * BLOCK, BLOCK)
                    half = vc[at, rows, :]
                    dp = dot(jnp.concatenate([half, half], axis=1), g_four, NN)
                    e = eh[at, rows, :].astype(F32) + el[at, rows, :].astype(F32)
                    place = (pl.ds(index * BLOCK, BLOCK), slice(None))
                    store_split(dh, dl, place, e * (dp - dots))
                keys = kc[at, span, :]
                part_dq = dot(keys, dh[...], TN) + dot(keys, dl[...], TN)
                dq_t.append(fold_rows(part_dq) + dq_in[at])
                key_grads.append(dot(dh[...], q_rows, NT) + dot(dl[...], q_rows, NT))
                value_grads.append(
                    dot(eh[at, span, :], g_rows, NT) + dot(el[at, span, :], g_rows, NT)
                )
            put_grads(pairs, pair, sets, grads, key_grads, value_grads)
            if last:
                both = jnp.concatenate(dq_t, axis=0).T * SCALE
                dq_out[0][pair] = both[:BLOCK]
                dq_out[1][pair] = both[BLOCK:]
            else:
                for head in range(2):
                    dq_out[0][2 * pair + head] = dq_t[head]

        each_pair(pairs, one_pair)

    outs = [struct(*shape) for shape in shapes]
    if last:
        outs += [struct(pairs, BLOCK, LANES)] * 2
    else:
        outs.append(struct(*dq.shape))
    return call(
        kernel,
        [turned, *kept, g_scaled, row_dot, dq],
        outs,
        scratch=[pltpu.VMEM((total, BOTH), BF16)] * 2,
        **costs(pairs, total, 4),
    )


def copy_columns(moves, ins, sems, bit):
    started = []
    for operand, theirs, column, place in moves:
        side = 1 - bit if theirs else bit
        column = side * (ins[operand].shape[1] // 2) + column
        column = pl.ds(pl.multiple_of(column, LANES), LANES)
        copy = pltpu.make_async_copy(
            ins[operand].at[:, column], place, sems.at[len(started)]
        )
        copy.start()
        started.append(copy)
    return started


def pack(pairs, first, second, scalar):
    def kernel(bit, one, two, theirs, mine, sems):
        moves = []
        for tile in range(2 * pairs):
            for out, other in ((theirs, True), (mine, False)):
                column = tile % pairs * LANES
                moves.append((tile // pairs, other, column, out.at[tile]))
        for copy in copy_columns(moves, (one, two), sems, bit[0]):
            copy.wait()

    return call(
        kernel,
        [first, second],
        [struct(2 * pairs, BLOCK, LANES)] * 2,
        scratch=[pltpu.SemaphoreType.DMA((4 * pairs,))],
        scalar=scalar,
        where=pl.ANY,
    )


QUARTER = BLOCK // 4
HALF = BLOCK // 2


def pack_coarse(pairs, keys, values, scalar):
    def kernel(bit, k, v, mine, f_theirs, f_mine, c_theirs, c_mine, rest, theirs, sems):
        moves = []
        for out, other in ((theirs, True), (mine, False)):
            for tile in range(2 * pairs):
                column = tile % pairs * LANES
                moves.append((tile // pairs, other, column, out.at[tile]))
        copies = copy_columns(moves, (k, v), sems, bit[0])
        for index, copy in enumerate(copies):
            copy.wait()
            tile = index % (2 * pairs)
            other = index < 2 * pairs
            source, finest, coarse = (
                (theirs, f_theirs, c_theirs) if other else (mine, f_mine, c_mine)
            )
            finest[tile] = mean_rows(source, (tile,), 0, HALF, 2)
            coarse[tile] = mean_rows(finest, (tile,), 0, QUARTER, 2)
            if other:
                rest[tile, :QUARTER] = half_difference(finest, (tile,), 0, QUARTER)
                rest[tile, QUARTER:] = half_difference(source, (tile,), 0, HALF)

    return call(
        kernel,
        [keys, values],
        [struct(2 * pairs, BLOCK, LANES)]
        + [struct(2 * pairs, HALF, LANES)] * 2
        + [struct(2 * pairs, QUARTER, LANES)] * 2
        + [struct(2 * pairs, QUARTER + HALF, LANES)],
        scratch=[
            pltpu.VMEM((2 * pairs, BLOCK, LANES), F32),
            pltpu.SemaphoreType.DMA((4 * pairs,)),
        ],
        scalar=scalar,
        where=pl.ANY,
    )


def rebuild(pairs, second, rest):
    def kernel(second_in, rest_in, out, finest):
        for tile in range(2 * pairs):
            put_pairs(finest, (tile,), second_in[tile], rest_in[tile, :QUARTER])
            put_pairs(out, (tile,), finest[tile], rest_in[tile, QUARTER:])

    return call(
        kernel,
        [second, rest],
        [struct(2 * pairs, BLOCK, LANES)],
        scratch=[pltpu.VMEM((2 * pairs, HALF, LANES), F32)],
    )[0]


def take_apart(pairs, block_grad):
    def kernel(block, second, rest, finest):
        for tile in range(2 * pairs):
            finest[tile] = 2.0 * mean_rows(block, (tile,), 0, HALF, 2)
            rest[tile, QUARTER:] = 2.0 * half_difference(block, (tile,), 0, HALF)
            second[tile] = 2.0 * mean_rows(finest, (tile,), 0, QUARTER, 2)
            rest[tile, :QUARTER] = 2.0 * half_difference(finest, (tile,), 0, QUARTER)

    return call(
        kernel,
        [block_grad],
        [
            struct(2 * pairs, QUARTER, LANES),
            struct(2 * pairs, QUARTER + HALF, LANES),
        ],
        scratch=[pltpu.VMEM((2 * pairs, HALF, LANES), F32)],
    )


def coarsen_pair(lo, pairs, mine, received):
    def kernel(own, got, *outs):
        for tile in range(2 * pairs):
            outs[0][tile, : BLOCK // 4] = own[tile]
            outs[0][tile, BLOCK // 4 :] = got[tile]
            for index in range(1, lo.bits):
                outs[index][tile] = mean_rows(
                    outs[index - 1], (tile,), 0, BLOCK >> index + 1, 2
                )

    outs = [struct(2 * pairs, BLOCK >> step, LANES) for step in range(1, lo.bits + 1)]
    return call(kernel, [mine, received], outs)


def group_pieces(lo):
    own = BLOCK >> lo.bits
    factor = 1 << lo.bits
    pieces = [
        (-2, 0, BLOCK // 2, factor, own),
        (-1, 0, BLOCK // 2, factor, own + own // 2),
    ]
    filled = 2 * own
    for level in range(1, lo.bits):
        factor = 1 << lo.bits - level
        for step, row, rows in lo.held[level]:
            pieces.append((step, row, rows, factor, filled))
            filled += rows // factor
    return pieces


def coarsen_group(lo, hi, pairs, own, halves, arrived):
    pieces = group_pieces(lo)

    def kernel(own_in, *refs):
        ins = refs[: 2 + lo.bits]
        outs = refs[2 + lo.bits :]
        for tile in range(2 * pairs):
            outs[0][tile, pl.ds(0, BLOCK >> lo.bits)] = own_in[tile]
            for step, row, rows, factor, place in pieces:
                count = rows // factor
                outs[0][tile, pl.ds(place, count)] = mean_rows(
                    ins[2 + step], (tile,), row, count, factor
                )
            for step in range(1, hi.bits):
                outs[step][tile] = mean_rows(
                    outs[step - 1], (tile,), 0, BLOCK >> step, 2
                )

    outs = [struct(2 * pairs, BLOCK >> step, LANES) for step in range(hi.bits)]
    return call(kernel, [own, *halves, *arrived], outs)


def turn(pairs, mine, received):
    def kernel(own, got, turned):
        for tile in range(2 * pairs):
            both = jnp.concatenate([own[tile], got[tile]], axis=0).T
            turned[tile] = both * (SCALE * LOG2_E) if tile < pairs else both

    return call(kernel, [mine, received], [struct(2 * pairs, LANES, 2 * BLOCK)])[0]


def spread_group(lo, hi, pairs, group_grads, grads):
    pieces = group_pieces(lo)
    own_rows = BLOCK >> lo.bits

    def kernel(*refs):
        steps = refs[: hi.bits]
        ins = refs[hi.bits : hi.bits + lo.bits]
        own_out, *outs = refs[hi.bits + lo.bits : -1]
        total = refs[-1]
        for tile in range(2 * pairs):
            total[tile] = steps[0][tile, pl.ds(0, BLOCK)]
            for step in range(1, hi.bits):
                above = steps[step][tile, pl.ds(0, BLOCK >> step)]
                add_spread(total, (tile,), 0, above, 1 << step)
            own_out[tile] = total[tile, pl.ds(0, own_rows)]
            for out, value in zip(outs, ins):
                out[tile, pl.ds(0, value.shape[1])] = value[tile]
            outs[0][tile, pl.ds(ins[0].shape[1], own_rows)] = total[
                tile, pl.ds(own_rows, own_rows)
            ]
            for step, row, rows, factor, place in pieces:
                if step >= 0:
                    part = total[tile, pl.ds(place, rows // factor)]
                    add_spread(outs[step], (tile,), row, part, factor)

    shapes = [list(a.shape) for a in grads]
    shapes[0][1] += own_rows
    outs = [struct(2 * pairs, own_rows, LANES)] + [struct(*shape) for shape in shapes]
    own, *grads = call(
        kernel,
        [*group_grads, *grads],
        outs,
        scratch=[pltpu.VMEM((2 * pairs, BLOCK, LANES), F32)],
    )
    return own, grads


def spread_pair(lo, pairs, own_grad, returned, block_second):
    own_rows = BLOCK >> lo.bits

    def kernel(own, block, *refs):
        back = refs[: lo.bits]
        mine, theirs, *totals = refs[lo.bits :]
        last = pl.ds(back[0].shape[1] - own_rows, own_rows)
        for tile in range(2 * pairs):
            above = own[tile] + back[0][tile, last]
            for step in range(lo.bits - 1, 0, -1):
                total = totals[step - 1]
                total[tile] = back[step][tile, pl.ds(0, BLOCK >> step)]
                add_spread(total, (tile,), 0, above, 2)
                above = total[tile]
            mine[tile] = above[: BLOCK // 4]
            theirs[tile] = above[BLOCK // 4 :] + block[tile]

    return call(
        kernel,
        [own_grad, block_second, *returned],
        [struct(2 * pairs, BLOCK // 4, LANES)] * 2,
        scratch=[
            pltpu.VMEM((2 * pairs, BLOCK >> step, LANES), F32)
            for step in range(1, lo.bits)
        ],
    )


def unpack(pairs, kept, arrived, features, scalar):
    def kernel(bit, mine, theirs, *outs):
        for tile in range(2 * pairs):
            for side, array in ((bit[0], mine), (1 - bit[0], theirs)):
                column = side * (features // 2) + tile % pairs * LANES
                column = pl.ds(pl.multiple_of(column, LANES), LANES)
                outs[tile // pairs][:, column] = array[tile]

    return call(kernel, [kept, arrived], [struct(BLOCK, features)] * 2, scalar=scalar)


def finish(pairs, kept, rest, finest, seconds, features, scalar):
    def kernel(bit, kept_in, rest_in, f_mine, f_theirs, s_mine, s_theirs, *refs):
        outs, total, middle = refs[:2], refs[2], refs[3]
        for tile in range(2 * pairs):
            out = outs[tile // pairs]
            column = tile % pairs * LANES
            at = (tile,)
            total[tile] = kept_in[tile]
            add_spread(total, at, 0, f_mine[tile], 2)
            add_spread(total, at, 0, s_mine[tile], 4)
            place = bit[0] * (features // 2) + column
            out[:, pl.ds(pl.multiple_of(place, LANES), LANES)] = total[tile]
            put_pairs(middle, at, 0.5 * s_theirs[tile], 0.5 * rest_in[tile, :QUARTER])
            first = 0.5 * (middle[tile] + f_theirs[tile])
            put_pairs(total, at, first, 0.5 * rest_in[tile, QUARTER:])
            place = (1 - bit[0]) * (features // 2) + column
            out[:, pl.ds(pl.multiple_of(place, LANES), LANES)] = total[tile]

    return call(
        kernel,
        [kept, rest, *finest, *seconds],
        [struct(BLOCK, features)] * 2,
        scratch=[
            pltpu.VMEM((2 * pairs, BLOCK, LANES), F32),
            pltpu.VMEM((2 * pairs, HALF, LANES), F32),
        ],
        scalar=scalar,
    )


def on_device(queries, keys, values, cotangent):
    features = queries.shape[1]
    assert queries.shape[0] == BLOCK
    pairs = features // LANES // 2
    lo_bits = lax.axis_size("seqlo").bit_length() - 1
    lo = Tree(lo_bits - 1, 1, lowest=False)
    hi = Tree(lax.axis_size("seqhi").bit_length() - 1, lo_bits)
    scalar = (lax.axis_index("seqlo") % 2).astype(jnp.int32).reshape(1)
    queries, keys, values, cotangent = [
        pltpu.with_memory_space_constraint(array, pltpu.HBM)
        for array in (queries, keys, values, cotangent)
    ]
    mine_kv, f_theirs, f_mine, c_send, c_mine, rest = pack_coarse(
        pairs, keys, values, scalar
    )
    second = exchange(c_send, 1)
    finest_theirs = exchange(f_theirs, 2)
    coarse = coarsen_pair(lo, pairs, c_mine, second)
    finest = exchange(f_mine, 2)
    half = exchange(finest_theirs, 1)
    rest = exchange(ordered(rest, finest_theirs), 1)
    kv = rebuild(pairs, second, rest)
    send_qg, mine_qg = pack(pairs, queries, cotangent, scalar)
    qg = exchange(ordered(send_qg, finest_theirs), 1)
    zs = lo.gather([None, *coarse])
    group = coarsen_group(
        lo, hi, pairs, ordered(coarse[-1], rest), [finest, half], zs
    )
    turned = turn(pairs, mine_qg, qg)
    rs = hi.gather(group, turned)
    block_sets = [(0, 0, 0, BLOCK), (0, 1, 0, BLOCK)]
    lo_sets = [(1, 2, 0, BLOCK // 2), (1, 3, 0, BLOCK // 2)]
    for level in range(lo.bits):
        for step, row, rows in lo.held[level]:
            lo_sets.append((1 + level, 4 + step, row, rows))
    hi_sets = []
    for level in range(hi.bits):
        for step, row, rows in hi.held[level]:
            hi_sets.append((lo_bits + level, step, row, rows))
    first_in = [mine_kv, kv, finest, half, *zs]
    *kept, tops, sums, partial = attend_first(
        pairs, block_sets + lo_sets, first_in, turned
    )
    *rs_grads, o_keep, o_send, g_scaled, row_dot, dq = attend_last(
        pairs, hi_sets, rs, turned, tops, sums, partial
    )
    shapes = [(2 * pairs, *a.shape[1:]) for a in first_in]
    finest_grad, half_grad, *zs_grads, dq = attend_back(
        pairs,
        [(level, index - 2, row, rows) for level, index, row, rows in lo_sets],
        shapes[2:],
        BOTH,
        kept,
        turned,
        g_scaled,
        row_dot,
        dq,
        False,
    )
    kv_keep, kv_send, dq_keep, dq_send = attend_back(
        pairs, block_sets, shapes[:2], 0, kept, turned, g_scaled, row_dot, dq, True
    )
    og_keep = jnp.concatenate([o_keep, dq_keep], axis=0)
    og_send = jnp.concatenate([o_send, dq_send], axis=0)
    finest_mine = exchange(finest_grad, 2)
    half_back = exchange(half_grad, 1)
    block_second, rest_grad = take_apart(pairs, kv_send)
    rest_back = exchange(ordered(rest_grad, half_back), 1)
    og_back = exchange(ordered(og_send, half_back), 1)
    group_grads = hi.scatter(rs_grads)
    group_grads[-1] = ordered(group_grads[-1], (finest_mine, half_back, kv_send))
    own_grad, grads = spread_group(lo, hi, pairs, group_grads, zs_grads)
    returned = lo.scatter(grads)
    finest_theirs = exchange(ordered(half_back, returned[0]), 2)
    own_grad = ordered(own_grad, (rest_back, og_back))
    second_mine, second_send = spread_pair(lo, pairs, own_grad, returned, block_second)
    second_theirs = exchange(second_send, 1)
    attended, query_grad = unpack(pairs, og_keep, og_back, features, scalar)
    key_grad, value_grad = finish(
        pairs,
        kv_keep,
        rest_back,
        (finest_mine, finest_theirs),
        (second_mine, second_theirs),
        features,
        scalar,
    )
    return attended, query_grad, key_grad, value_grad


def solution(mesh):
    spec = P(AXES, None)
    return jax.shard_map(
        on_device,
        mesh=mesh,
        in_specs=(spec,) * 4,
        out_specs=(spec,) * 4,
        check_vma=False,
    )
```

```python
import math

import jax
import jax.numpy as jnp
from jax import lax
from jax.experimental import pallas as pl
from jax.experimental.pallas import tpu as pltpu
from jax.sharding import PartitionSpec as P

HEADS = 12
BLOCK = 128
HEAD_DIM = 64
LANES = 2 * HEAD_DIM
AXES = ("seqhi", "seqlo")
VMEM_LIMIT = 20 * 1024 * 1024
F32 = jnp.float32
BF16 = jnp.bfloat16
LOG2_E = 1.0 / math.log(2.0)
SCALE = 1.0 / math.sqrt(HEAD_DIM)


def struct(*shape):
    return jax.ShapeDtypeStruct(shape, F32)


def call(kernel, operands, outs, scratch=(), scalar=None, flops=0, exps=0, where=None):
    vmem = pl.BlockSpec(memory_space=pltpu.VMEM)
    smem = pl.BlockSpec(memory_space=pltpu.SMEM)
    in_specs = [pl.BlockSpec(memory_space=where) if where else vmem] * len(operands)
    if scalar is not None:
        operands = [scalar, *operands]
        in_specs = [smem, *in_specs]
    moved = sum(4 * math.prod(a.shape) for a in [*operands, *outs])
    return pl.pallas_call(
        kernel,
        out_shape=list(outs),
        in_specs=in_specs,
        out_specs=[vmem] * len(outs),
        scratch_shapes=list(scratch),
        compiler_params=pltpu.CompilerParams(vmem_limit_bytes=VMEM_LIMIT),
        cost_estimate=pl.CostEstimate(
            flops=flops, bytes_accessed=moved, transcendentals=exps
        ),
    )(*operands)


def exchange(value, offset):
    count = lax.axis_size(AXES)
    return lax.ppermute(value, AXES, [(i, i ^ offset) for i in range(count)])


def ordered(value, after):
    return value if after is None else lax.optimization_barrier((value, after))[0]


def half_difference(ref, lead, first, count):
    even = ref[(*lead, pl.ds(first, count, stride=2), slice(None))]
    odd = ref[(*lead, pl.ds(first + 1, count, stride=2), slice(None))]
    return 0.5 * (even - odd)


def put_pairs(ref, lead, total, difference):
    count = total.shape[0]
    ref[(*lead, pl.ds(0, count, stride=2), slice(None))] = total + difference
    ref[(*lead, pl.ds(1, count, stride=2), slice(None))] = total - difference


def mean_rows(ref, lead, first, count, factor):
    total = None
    for step in range(factor):
        rows = pl.ds(first + step, count, stride=factor)
        part = ref[(*lead, rows, slice(None))]
        total = part if total is None else total + part
    return total * (1.0 / factor)


def add_spread(ref, lead, first, value, factor):
    count = value.shape[0]
    value = value * (1.0 / factor)
    for step in range(factor):
        rows = pl.ds(first + step, count, stride=factor)
        place = (*lead, rows, slice(None))
        ref[place] = ref[place] + value


class Tree:
    def __init__(self, bits, first_bit, lowest=True):
        self.bits = bits
        self.first_bit = first_bit
        self.own_rows = [BLOCK >> step for step in range(bits)]
        if not lowest:
            self.own_rows[0] = 0
        self.held = {}
        self.payload = {}
        for step in range(bits - 1, -1, -1):
            rows = self.own_rows[step]
            payload = []
            fresh = {step: [(step, 0, rows)] if rows else []}
            for level in range(step + 1, bits):
                for piece in self.held[level]:
                    payload.append(piece)
                    fresh.setdefault(level, []).append((step, rows, piece[2]))
                    rows += piece[2]
            self.payload[step] = payload
            for level, pieces in fresh.items():
                self.held[level] = self.held.get(level, []) + pieces

    def partner(self, value, step):
        return exchange(value, 1 << self.first_bit + step)

    def gather(self, own, after=None):
        arrived = [None] * self.bits
        for step in range(self.bits - 1, -1, -1):
            parts = [own[step]] if self.own_rows[step] else []
            for source, row, rows in self.payload[step]:
                part = arrived[source]
                whole = rows == part.shape[1]
                parts.append(part if whole else part[:, row : row + rows])
            sent = jnp.concatenate(parts, axis=1) if len(parts) > 1 else parts[0]
            if step == 0:
                sent = ordered(sent, after)
            arrived[step] = self.partner(sent, step)
        return arrived

    def scatter(self, grads):
        grads = list(grads)
        returned = []
        for step in range(self.bits):
            back = self.partner(grads[step], step)
            returned.append(back)
            filled = self.own_rows[step]
            for source, row, rows in self.payload[step]:
                part = back[:, filled : filled + rows]
                grads[source] = grads[source].at[:, row : row + rows].add(part)
                filled += rows
        return returned


def split(value):
    high = value.astype(BF16).astype(F32)
    return high, value - high


def halves_by_head(value):
    high, low = split(value)
    first = lax.broadcasted_iota(jnp.int32, value.shape, 1) < HEAD_DIM
    one = jnp.where(first, high, pltpu.roll(low, HEAD_DIM, 1))
    two = jnp.where(first, pltpu.roll(high, HEAD_DIM, 1), low)
    return one, two


def dot(lhs, rhs, dims):
    return lax.dot_general(lhs, rhs, (dims, ((), ())), preferred_element_type=F32)


NN = ((1,), (0,))
NT = ((1,), (1,))


BOTH = 2 * BLOCK
GROUP = 3


def halves_of(sets, ins, which, pairs, pair):
    tile = which * pairs + pair
    parts = [ins[index][tile, pl.ds(row, rows), :] for _, index, row, rows in sets]
    return halves_by_head(jnp.concatenate(parts, axis=0))


def segment_levels(sets):
    levels, filled = [], 0
    for level, _, _, rows in sets:
        if filled % BLOCK == 0:
            levels.append(level)
        filled += rows
    return levels


def four_rows(value):
    high, low = split(value)
    four = jnp.concatenate([high, high, low, low], axis=0).astype(BF16)
    return four, jnp.concatenate([high, low], axis=0).astype(BF16)


def store_split(ref, lead, rows, value):
    high = value.astype(BF16)
    ref[(lead, 0, rows)] = high
    ref[(lead, 1, rows)] = (value - high.astype(F32)).astype(BF16)


def fold_rows(value):
    return value[:HEAD_DIM] + value[HEAD_DIM:]


def fold_heads(one, two):
    first = lax.broadcasted_iota(jnp.int32, one.shape, 1) < HEAD_DIM
    return jnp.where(
        first, one + pltpu.roll(one, HEAD_DIM, 1), two + pltpu.roll(two, HEAD_DIM, 1)
    )


def twice(value):
    return jnp.concatenate([value, value], axis=1)


def stacked(ref, at, rows=slice(None)):
    return jnp.concatenate([ref[at, 0, rows], ref[at, 1, rows]], axis=0)


def abreast(ref, at, rows=slice(None)):
    return jnp.concatenate([ref[at, 0, rows], ref[at, 1, rows]], axis=1)


def column_scores(levels, keys, at, q_four, s_ref):
    highest = None
    for index, level in enumerate(levels):
        rows = pl.ds(index * BLOCK, BLOCK)
        s = dot(twice(keys[at, rows]), q_four, NN)
        s = s + float(level) if level else s
        s_ref[at, rows] = s
        top = jnp.max(s.reshape(BLOCK // 8, 8, BOTH), axis=0)
        highest = top if highest is None else jnp.maximum(highest, top)
    return jnp.max(highest, axis=0, keepdims=True)


def exponents(levels, at, top, s_ref, e_ref, keep):
    summed = None
    for index in range(len(levels)):
        rows = pl.ds(index * BLOCK, BLOCK)
        e = jnp.exp2(s_ref[at, rows] - top)
        if keep:
            s_ref[at, rows] = e
        store_split(e_ref, at, rows, e)
        part = jnp.sum(e.reshape(BLOCK // 8, 8, BOTH), axis=0)
        summed = part if summed is None else summed + part
    return jnp.sum(summed, axis=0, keepdims=True)


def head_rows(ref, pair, head):
    return ref[pair, pl.ds(head * HEAD_DIM, HEAD_DIM)]


def each_group(pairs, body):
    for first in range(0, pairs, GROUP):
        group = range(first, min(first + GROUP, pairs))
        body(group, [(pair, head, 2 * pair + head) for pair in group for head in (0, 1)])


def costs(pairs, rows, products, exps=0):
    return dict(
        flops=2 * 4 * products * pairs * 2 * rows * BOTH * HEAD_DIM,
        exps=exps * pairs * 2 * rows * BOTH,
    )


def put_halves(pairs, sets, ins, group, plain, turned):
    for which in range(2):
        for pair in group:
            for head, value in enumerate(halves_of(sets, ins, which, pairs, pair)):
                plain[which][2 * pair + head] = value.astype(BF16)
                turned[which][2 * pair + head] = value.T.astype(BF16)


def attend_first(pairs, sets, operands, turned):
    total = sum(s[3] for s in sets)
    levels = segment_levels(sets)

    def kernel(turn_in, *refs):
        ins = refs[: len(operands)]
        kt, vc, e_ref, tops, sums, out, s_ref, kc, vt = refs[len(operands) :]

        def body(group, heads):
            put_halves(pairs, sets, ins, group, (kc, vc), (kt, vt))
            for pair, head, at in heads:
                q_four, _ = four_rows(head_rows(turn_in, pair, head))
                tops[at] = column_scores(levels, kc, at, q_four, s_ref)
            for _, _, at in heads:
                sums[at] = exponents(levels, at, tops[at], s_ref, e_ref, False)
            for _, _, at in heads:
                out[at] = fold_rows(dot(twice(vt[at]), stacked(e_ref, at), NN))

        each_group(pairs, body)

    heads = 2 * pairs
    outs = [
        jax.ShapeDtypeStruct((heads, LANES, total), BF16),
        jax.ShapeDtypeStruct((heads, total, LANES), BF16),
        jax.ShapeDtypeStruct((heads, 2, total, BOTH), BF16),
    ]
    outs += [struct(heads, 1, BOTH)] * 2 + [struct(heads, HEAD_DIM, BOTH)]
    return call(
        kernel,
        [turned, *operands],
        outs,
        scratch=[
            pltpu.VMEM((heads, total, BOTH), F32),
            pltpu.VMEM((heads, total, LANES), BF16),
            pltpu.VMEM((heads, LANES, total), BF16),
        ],
        **costs(pairs, total, 2, 1),
    )


def attend_last(pairs, sets, operands, turned, tops, sums, partial):
    total = sum(s[3] for s in sets)
    levels = segment_levels(sets)

    def kernel(turn_in, top_in, sum_in, part_in, *refs):
        ins = refs[: len(operands)]
        grads = refs[len(operands) : 2 * len(operands)]
        o_keep, o_send, g_out, r_out, dq_out = refs[2 * len(operands) : -7]
        s_ref, e_ref, d_ref, kc, vc, kt, vt = refs[-7:]

        def body(group, heads):
            put_halves(pairs, sets, ins, group, (kc, vc), (kt, vt))
            queries = {}
            top = {}
            for pair, head, at in heads:
                q_four, queries[at] = four_rows(head_rows(turn_in, pair, head))
                top[at] = column_scores(levels, kc, at, q_four, s_ref)
            inverse = {}
            rescale = {}
            for _, _, at in heads:
                first_top = top_in[at]
                highest = jnp.maximum(top[at], first_top)
                rescale[at] = jnp.exp2(first_top - highest)
                summed = exponents(levels, at, highest, s_ref, e_ref, True)
                inverse[at] = 1.0 / (summed + sum_in[at] * rescale[at])
            output = {}
            cotangents = {}
            row_dot = {}
            for pair, head, at in heads:
                o = fold_rows(dot(twice(vt[at]), stacked(e_ref, at), NN))
                o = (o + part_in[at] * rescale[at]) * inverse[at]
                output[at] = o
                scaled = head_rows(turn_in, pairs + pair, head) * inverse[at]
                cotangents[at] = four_rows(scaled)
                row_dot[at] = jnp.sum(o * scaled, axis=0, keepdims=True)
                g_out[at] = scaled * rescale[at]
                r_out[at] = row_dot[at] * rescale[at]
            for _, _, at in heads:
                for index in range(len(levels)):
                    rows = pl.ds(index * BLOCK, BLOCK)
                    dp = dot(twice(vc[at, rows]), cotangents[at][0], NN)
                    store_split(d_ref, at, rows, s_ref[at, rows] * (dp - row_dot[at]))
            key_grads = {}
            value_grads = {}
            for _, _, at in heads:
                value_grads[at] = dot(abreast(e_ref, at), twice(cotangents[at][1]), NT)
                key_grads[at] = dot(abreast(d_ref, at), twice(queries[at]), NT)
                dq_out[at] = fold_rows(dot(twice(kt[at]), stacked(d_ref, at), NN))
            for pair in group:
                put_grads(pairs, pair, sets, grads, key_grads, value_grads)
                both = [output[2 * pair], output[2 * pair + 1]]
                both = jnp.concatenate(both, axis=0).T
                o_keep[pair] = both[:BLOCK]
                o_send[pair] = both[BLOCK:]

        each_group(pairs, body)

    heads = 2 * pairs
    outs = [struct(*a.shape) for a in operands]
    outs += [struct(pairs, BLOCK, LANES)] * 2
    outs += [struct(heads, HEAD_DIM, BOTH), struct(heads, 1, BOTH)]
    outs.append(struct(heads, HEAD_DIM, BOTH))
    return call(
        kernel,
        [turned, tops, sums, partial, *operands],
        outs,
        scratch=[pltpu.VMEM((heads, total, BOTH), F32)]
        + [pltpu.VMEM((heads, 2, total, BOTH), BF16)] * 2
        + [pltpu.VMEM((heads, total, LANES), BF16)] * 2
        + [pltpu.VMEM((heads, LANES, total), BF16)] * 2,
        **costs(pairs, total, 6, 1),
    )


def put_grads(pairs, pair, sets, grads, key_grads, value_grads):
    for which, parts in enumerate((key_grads, value_grads)):
        both = fold_heads(parts[2 * pair], parts[2 * pair + 1])
        if which == 0:
            both = both * (1.0 / LOG2_E)
        filled = 0
        for _, index, row, rows in sets:
            piece = both[filled : filled + rows]
            grads[index][which * pairs + pair, pl.ds(row, rows), :] = piece
            filled += rows


def attend_back(pairs, sets, shapes, first, kept, turned, g_scaled, row_dot, dq, last):
    total = sum(s[3] for s in sets)
    segments = total // BLOCK

    def kernel(turn_in, kt, vc, e_ref, g_in, r_in, dq_in, *refs):
        grads = refs[: len(shapes)]
        dq_out = refs[len(shapes) : -1]
        d_ref = refs[-1]
        span = pl.ds(first, total)

        def body(group, heads):
            cotangents = {}
            for _, _, at in heads:
                g_four, cotangents[at] = four_rows(g_in[at])
                for index in range(segments):
                    rows = pl.ds(first + index * BLOCK, BLOCK)
                    dp = dot(twice(vc[at, rows]), g_four, NN)
                    e = e_ref[at, 0, rows].astype(F32) + e_ref[at, 1, rows].astype(F32)
                    place = pl.ds(index * BLOCK, BLOCK)
                    store_split(d_ref, at, place, e * (dp - r_in[at]))
            queries_grad = {}
            key_grads = {}
            value_grads = {}
            for pair, head, at in heads:
                _, q_rows = four_rows(head_rows(turn_in, pair, head))
                g_rows = cotangents[at]
                value_grads[at] = dot(abreast(e_ref, at, span), twice(g_rows), NT)
                key_grads[at] = dot(abreast(d_ref, at), twice(q_rows), NT)
                part = dot(twice(kt[at, :, span]), stacked(d_ref, at), NN)
                queries_grad[at] = fold_rows(part) + dq_in[at]
            for pair in group:
                put_grads(pairs, pair, sets, grads, key_grads, value_grads)
                both = [queries_grad[2 * pair], queries_grad[2 * pair + 1]]
                if last:
                    both = jnp.concatenate(both, axis=0).T * SCALE
                    dq_out[0][pair] = both[:BLOCK]
                    dq_out[1][pair] = both[BLOCK:]
                else:
                    for head in range(2):
                        dq_out[0][2 * pair + head] = both[head]

        each_group(pairs, body)

    outs = [struct(*shape) for shape in shapes]
    if last:
        outs += [struct(pairs, BLOCK, LANES)] * 2
    else:
        outs.append(struct(*dq.shape))
    return call(
        kernel,
        [turned, *kept, g_scaled, row_dot, dq],
        outs,
        scratch=[pltpu.VMEM((2 * pairs, 2, total, BOTH), BF16)],
        **costs(pairs, total, 4),
    )


def copy_columns(moves, ins, sems, bit):
    started = []
    for operand, theirs, column, place in moves:
        side = 1 - bit if theirs else bit
        column = side * (ins[operand].shape[1] // 2) + column
        column = pl.ds(pl.multiple_of(column, LANES), LANES)
        copy = pltpu.make_async_copy(
            ins[operand].at[:, column], place, sems.at[len(started)]
        )
        copy.start()
        started.append(copy)
    return started


def pack(pairs, first, second, scalar):
    def kernel(bit, one, two, theirs, mine, sems):
        moves = []
        for tile in range(2 * pairs):
            for out, other in ((theirs, True), (mine, False)):
                column = tile % pairs * LANES
                moves.append((tile // pairs, other, column, out.at[tile]))
        for copy in copy_columns(moves, (one, two), sems, bit[0]):
            copy.wait()

    return call(
        kernel,
        [first, second],
        [struct(2 * pairs, BLOCK, LANES)] * 2,
        scratch=[pltpu.SemaphoreType.DMA((4 * pairs,))],
        scalar=scalar,
        where=pl.ANY,
    )


QUARTER = BLOCK // 4
HALF = BLOCK // 2


def pack_coarse(pairs, keys, values, scalar):
    def kernel(bit, k, v, mine, f_theirs, f_mine, c_theirs, c_mine, rest, theirs, sems):
        moves = []
        for out, other in ((theirs, True), (mine, False)):
            for tile in range(2 * pairs):
                column = tile % pairs * LANES
                moves.append((tile // pairs, other, column, out.at[tile]))
        copies = copy_columns(moves, (k, v), sems, bit[0])
        for index, copy in enumerate(copies):
            copy.wait()
            tile = index % (2 * pairs)
            other = index < 2 * pairs
            source, finest, coarse = (
                (theirs, f_theirs, c_theirs) if other else (mine, f_mine, c_mine)
            )
            finest[tile] = mean_rows(source, (tile,), 0, HALF, 2)
            coarse[tile] = mean_rows(finest, (tile,), 0, QUARTER, 2)
            if other:
                rest[tile, :QUARTER] = half_difference(finest, (tile,), 0, QUARTER)
                rest[tile, QUARTER:] = half_difference(source, (tile,), 0, HALF)

    return call(
        kernel,
        [keys, values],
        [struct(2 * pairs, BLOCK, LANES)]
        + [struct(2 * pairs, HALF, LANES)] * 2
        + [struct(2 * pairs, QUARTER, LANES)] * 2
        + [struct(2 * pairs, QUARTER + HALF, LANES)],
        scratch=[
            pltpu.VMEM((2 * pairs, BLOCK, LANES), F32),
            pltpu.SemaphoreType.DMA((4 * pairs,)),
        ],
        scalar=scalar,
        where=pl.ANY,
    )


def rebuild(pairs, second, rest):
    def kernel(second_in, rest_in, out, finest):
        for tile in range(2 * pairs):
            put_pairs(finest, (tile,), second_in[tile], rest_in[tile, :QUARTER])
            put_pairs(out, (tile,), finest[tile], rest_in[tile, QUARTER:])

    return call(
        kernel,
        [second, rest],
        [struct(2 * pairs, BLOCK, LANES)],
        scratch=[pltpu.VMEM((2 * pairs, HALF, LANES), F32)],
    )[0]


def take_apart(pairs, block_grad):
    def kernel(block, second, rest, finest):
        for tile in range(2 * pairs):
            finest[tile] = 2.0 * mean_rows(block, (tile,), 0, HALF, 2)
            rest[tile, QUARTER:] = 2.0 * half_difference(block, (tile,), 0, HALF)
            second[tile] = 2.0 * mean_rows(finest, (tile,), 0, QUARTER, 2)
            rest[tile, :QUARTER] = 2.0 * half_difference(finest, (tile,), 0, QUARTER)

    return call(
        kernel,
        [block_grad],
        [
            struct(2 * pairs, QUARTER, LANES),
            struct(2 * pairs, QUARTER + HALF, LANES),
        ],
        scratch=[pltpu.VMEM((2 * pairs, HALF, LANES), F32)],
    )


def coarsen_pair(lo, pairs, mine, received):
    def kernel(own, got, *outs):
        for tile in range(2 * pairs):
            outs[0][tile, : BLOCK // 4] = own[tile]
            outs[0][tile, BLOCK // 4 :] = got[tile]
            for index in range(1, lo.bits):
                outs[index][tile] = mean_rows(
                    outs[index - 1], (tile,), 0, BLOCK >> index + 1, 2
                )

    outs = [struct(2 * pairs, BLOCK >> step, LANES) for step in range(1, lo.bits + 1)]
    return call(kernel, [mine, received], outs)


def group_pieces(lo):
    own = BLOCK >> lo.bits
    factor = 1 << lo.bits
    pieces = [
        (-2, 0, BLOCK // 2, factor, own),
        (-1, 0, BLOCK // 2, factor, own + own // 2),
    ]
    filled = 2 * own
    for level in range(1, lo.bits):
        factor = 1 << lo.bits - level
        for step, row, rows in lo.held[level]:
            pieces.append((step, row, rows, factor, filled))
            filled += rows // factor
    return pieces


def coarsen_group(lo, hi, pairs, own, halves, arrived):
    pieces = group_pieces(lo)

    def kernel(own_in, *refs):
        ins = refs[: 2 + lo.bits]
        outs = refs[2 + lo.bits :]
        for tile in range(2 * pairs):
            outs[0][tile, pl.ds(0, BLOCK >> lo.bits)] = own_in[tile]
            for step, row, rows, factor, place in pieces:
                count = rows // factor
                outs[0][tile, pl.ds(place, count)] = mean_rows(
                    ins[2 + step], (tile,), row, count, factor
                )
            for step in range(1, hi.bits):
                outs[step][tile] = mean_rows(
                    outs[step - 1], (tile,), 0, BLOCK >> step, 2
                )

    outs = [struct(2 * pairs, BLOCK >> step, LANES) for step in range(hi.bits)]
    return call(kernel, [own, *halves, *arrived], outs)


def turn(pairs, mine, received):
    def kernel(own, got, turned):
        for tile in range(2 * pairs):
            both = jnp.concatenate([own[tile], got[tile]], axis=0).T
            turned[tile] = both * (SCALE * LOG2_E) if tile < pairs else both

    return call(kernel, [mine, received], [struct(2 * pairs, LANES, 2 * BLOCK)])[0]


def spread_group(lo, hi, pairs, group_grads, grads):
    pieces = group_pieces(lo)
    own_rows = BLOCK >> lo.bits

    def kernel(*refs):
        steps = refs[: hi.bits]
        ins = refs[hi.bits : hi.bits + lo.bits]
        own_out, *outs = refs[hi.bits + lo.bits : -1]
        total = refs[-1]
        for tile in range(2 * pairs):
            total[tile] = steps[0][tile, pl.ds(0, BLOCK)]
            for step in range(1, hi.bits):
                above = steps[step][tile, pl.ds(0, BLOCK >> step)]
                add_spread(total, (tile,), 0, above, 1 << step)
            own_out[tile] = total[tile, pl.ds(0, own_rows)]
            for out, value in zip(outs, ins):
                out[tile, pl.ds(0, value.shape[1])] = value[tile]
            outs[0][tile, pl.ds(ins[0].shape[1], own_rows)] = total[
                tile, pl.ds(own_rows, own_rows)
            ]
            for step, row, rows, factor, place in pieces:
                if step >= 0:
                    part = total[tile, pl.ds(place, rows // factor)]
                    add_spread(outs[step], (tile,), row, part, factor)

    shapes = [list(a.shape) for a in grads]
    shapes[0][1] += own_rows
    outs = [struct(2 * pairs, own_rows, LANES)] + [struct(*shape) for shape in shapes]
    own, *grads = call(
        kernel,
        [*group_grads, *grads],
        outs,
        scratch=[pltpu.VMEM((2 * pairs, BLOCK, LANES), F32)],
    )
    return own, grads


def spread_pair(lo, pairs, own_grad, returned, block_second):
    own_rows = BLOCK >> lo.bits

    def kernel(own, block, *refs):
        back = refs[: lo.bits]
        mine, theirs, *totals = refs[lo.bits :]
        last = pl.ds(back[0].shape[1] - own_rows, own_rows)
        for tile in range(2 * pairs):
            above = own[tile] + back[0][tile, last]
            for step in range(lo.bits - 1, 0, -1):
                total = totals[step - 1]
                total[tile] = back[step][tile, pl.ds(0, BLOCK >> step)]
                add_spread(total, (tile,), 0, above, 2)
                above = total[tile]
            mine[tile] = above[: BLOCK // 4]
            theirs[tile] = above[BLOCK // 4 :] + block[tile]

    return call(
        kernel,
        [own_grad, block_second, *returned],
        [struct(2 * pairs, BLOCK // 4, LANES)] * 2,
        scratch=[
            pltpu.VMEM((2 * pairs, BLOCK >> step, LANES), F32)
            for step in range(1, lo.bits)
        ],
    )


def unpack(pairs, kept, arrived, features, scalar):
    def kernel(bit, mine, theirs, *outs):
        for tile in range(2 * pairs):
            for side, array in ((bit[0], mine), (1 - bit[0], theirs)):
                column = side * (features // 2) + tile % pairs * LANES
                column = pl.ds(pl.multiple_of(column, LANES), LANES)
                outs[tile // pairs][:, column] = array[tile]

    return call(kernel, [kept, arrived], [struct(BLOCK, features)] * 2, scalar=scalar)


def finish(pairs, kept, rest, finest, seconds, features, scalar):
    def kernel(bit, kept_in, rest_in, f_mine, f_theirs, s_mine, s_theirs, *refs):
        outs, total, middle = refs[:2], refs[2], refs[3]
        for tile in range(2 * pairs):
            out = outs[tile // pairs]
            column = tile % pairs * LANES
            at = (tile,)
            total[tile] = kept_in[tile]
            add_spread(total, at, 0, f_mine[tile], 2)
            add_spread(total, at, 0, s_mine[tile], 4)
            place = bit[0] * (features // 2) + column
            out[:, pl.ds(pl.multiple_of(place, LANES), LANES)] = total[tile]
            put_pairs(middle, at, 0.5 * s_theirs[tile], 0.5 * rest_in[tile, :QUARTER])
            first = 0.5 * (middle[tile] + f_theirs[tile])
            put_pairs(total, at, first, 0.5 * rest_in[tile, QUARTER:])
            place = (1 - bit[0]) * (features // 2) + column
            out[:, pl.ds(pl.multiple_of(place, LANES), LANES)] = total[tile]

    return call(
        kernel,
        [kept, rest, *finest, *seconds],
        [struct(BLOCK, features)] * 2,
        scratch=[
            pltpu.VMEM((2 * pairs, BLOCK, LANES), F32),
            pltpu.VMEM((2 * pairs, HALF, LANES), F32),
        ],
        scalar=scalar,
    )


def on_device(queries, keys, values, cotangent):
    features = queries.shape[1]
    assert queries.shape[0] == BLOCK
    pairs = features // LANES // 2
    lo_bits = lax.axis_size("seqlo").bit_length() - 1
    lo = Tree(lo_bits - 1, 1, lowest=False)
    hi = Tree(lax.axis_size("seqhi").bit_length() - 1, lo_bits)
    scalar = (lax.axis_index("seqlo") % 2).astype(jnp.int32).reshape(1)
    queries, keys, values, cotangent = [
        pltpu.with_memory_space_constraint(array, pltpu.HBM)
        for array in (queries, keys, values, cotangent)
    ]
    mine_kv, f_theirs, f_mine, c_send, c_mine, rest = pack_coarse(
        pairs, keys, values, scalar
    )
    second = exchange(c_send, 1)
    finest_theirs = exchange(f_theirs, 2)
    coarse = coarsen_pair(lo, pairs, c_mine, second)
    finest = exchange(f_mine, 2)
    half = exchange(finest_theirs, 1)
    rest = exchange(ordered(rest, finest_theirs), 1)
    kv = rebuild(pairs, second, rest)
    send_qg, mine_qg = pack(pairs, queries, cotangent, scalar)
    qg = exchange(ordered(send_qg, finest_theirs), 1)
    zs = lo.gather([None, *coarse])
    group = coarsen_group(
        lo, hi, pairs, ordered(coarse[-1], rest), [finest, half], zs
    )
    turned = turn(pairs, mine_qg, qg)
    rs = hi.gather(group, turned)
    block_sets = [(0, 0, 0, BLOCK), (0, 1, 0, BLOCK)]
    lo_sets = [(1, 2, 0, BLOCK // 2), (1, 3, 0, BLOCK // 2)]
    for level in range(lo.bits):
        for step, row, rows in lo.held[level]:
            lo_sets.append((1 + level, 4 + step, row, rows))
    hi_sets = []
    for level in range(hi.bits):
        for step, row, rows in hi.held[level]:
            hi_sets.append((lo_bits + level, step, row, rows))
    first_in = [mine_kv, kv, finest, half, *zs]
    *kept, tops, sums, partial = attend_first(
        pairs, block_sets + lo_sets, first_in, turned
    )
    *rs_grads, o_keep, o_send, g_scaled, row_dot, dq = attend_last(
        pairs, hi_sets, rs, turned, tops, sums, partial
    )
    shapes = [(2 * pairs, *a.shape[1:]) for a in first_in]
    finest_grad, half_grad, *zs_grads, dq = attend_back(
        pairs,
        [(level, index - 2, row, rows) for level, index, row, rows in lo_sets],
        shapes[2:],
        BOTH,
        kept,
        turned,
        g_scaled,
        row_dot,
        dq,
        False,
    )
    kv_keep, kv_send, dq_keep, dq_send = attend_back(
        pairs, block_sets, shapes[:2], 0, kept, turned, g_scaled, row_dot, dq, True
    )
    og_keep = jnp.concatenate([o_keep, dq_keep], axis=0)
    og_send = jnp.concatenate([o_send, dq_send], axis=0)
    finest_mine = exchange(finest_grad, 2)
    half_back = exchange(half_grad, 1)
    block_second, rest_grad = take_apart(pairs, kv_send)
    rest_back = exchange(ordered(rest_grad, half_back), 1)
    og_back = exchange(ordered(og_send, half_back), 1)
    group_grads = hi.scatter(rs_grads)
    group_grads[-1] = ordered(group_grads[-1], (finest_mine, half_back, kv_send))
    own_grad, grads = spread_group(lo, hi, pairs, group_grads, zs_grads)
    returned = lo.scatter(grads)
    finest_theirs = exchange(ordered(half_back, returned[0]), 2)
    own_grad = ordered(own_grad, (rest_back, og_back))
    second_mine, second_send = spread_pair(lo, pairs, own_grad, returned, block_second)
    second_theirs = exchange(second_send, 1)
    attended, query_grad = unpack(pairs, og_keep, og_back, features, scalar)
    key_grad, value_grad = finish(
        pairs,
        kv_keep,
        rest_back,
        (finest_mine, finest_theirs),
        (second_mine, second_theirs),
        features,
        scalar,
    )
    return attended, query_grad, key_grad, value_grad


def solution(mesh):
    spec = P(AXES, None)
    return jax.shard_map(
        on_device,
        mesh=mesh,
        in_specs=(spec,) * 4,
        out_specs=(spec,) * 4,
        check_vma=False,
    )
```

```python
import math

import jax
import jax.numpy as jnp
from jax import lax
from jax.experimental import pallas as pl
from jax.experimental.pallas import tpu as pltpu
from jax.sharding import PartitionSpec as P

HEADS = 12
BLOCK = 128
HEAD_DIM = 64
LANES = 2 * HEAD_DIM
AXES = ("seqhi", "seqlo")
VMEM_LIMIT = 20 * 1024 * 1024
F32 = jnp.float32
BF16 = jnp.bfloat16
LOG2_E = 1.0 / math.log(2.0)
SCALE = 1.0 / math.sqrt(HEAD_DIM)


def struct(*shape):
    return jax.ShapeDtypeStruct(shape, F32)


def call(kernel, operands, outs, scratch=(), scalar=None, flops=0, exps=0, where=None):
    vmem = pl.BlockSpec(memory_space=pltpu.VMEM)
    smem = pl.BlockSpec(memory_space=pltpu.SMEM)
    in_specs = [pl.BlockSpec(memory_space=where) if where else vmem] * len(operands)
    if scalar is not None:
        operands = [scalar, *operands]
        in_specs = [smem, *in_specs]
    moved = sum(4 * math.prod(a.shape) for a in [*operands, *outs])
    return pl.pallas_call(
        kernel,
        out_shape=list(outs),
        in_specs=in_specs,
        out_specs=[vmem] * len(outs),
        scratch_shapes=list(scratch),
        compiler_params=pltpu.CompilerParams(vmem_limit_bytes=VMEM_LIMIT),
        cost_estimate=pl.CostEstimate(
            flops=flops, bytes_accessed=moved, transcendentals=exps
        ),
    )(*operands)


def exchange(value, offset):
    count = lax.axis_size(AXES)
    return lax.ppermute(value, AXES, [(i, i ^ offset) for i in range(count)])


def ordered(value, after):
    return value if after is None else lax.optimization_barrier((value, after))[0]


def half_difference(ref, lead, first, count):
    even = ref[(*lead, pl.ds(first, count, stride=2), slice(None))]
    odd = ref[(*lead, pl.ds(first + 1, count, stride=2), slice(None))]
    return 0.5 * (even - odd)


def put_pairs(ref, lead, total, difference):
    count = total.shape[0]
    ref[(*lead, pl.ds(0, count, stride=2), slice(None))] = total + difference
    ref[(*lead, pl.ds(1, count, stride=2), slice(None))] = total - difference


def mean_rows(ref, lead, first, count, factor):
    total = None
    for step in range(factor):
        rows = pl.ds(first + step, count, stride=factor)
        part = ref[(*lead, rows, slice(None))]
        total = part if total is None else total + part
    return total * (1.0 / factor)


def add_spread(ref, lead, first, value, factor):
    count = value.shape[0]
    value = value * (1.0 / factor)
    for step in range(factor):
        rows = pl.ds(first + step, count, stride=factor)
        place = (*lead, rows, slice(None))
        ref[place] = ref[place] + value


class Tree:
    def __init__(self, bits, first_bit, lowest=True):
        self.bits = bits
        self.first_bit = first_bit
        self.own_rows = [BLOCK >> step for step in range(bits)]
        if not lowest:
            self.own_rows[0] = 0
        self.held = {}
        self.payload = {}
        for step in range(bits - 1, -1, -1):
            rows = self.own_rows[step]
            payload = []
            fresh = {step: [(step, 0, rows)] if rows else []}
            for level in range(step + 1, bits):
                for piece in self.held[level]:
                    payload.append(piece)
                    fresh.setdefault(level, []).append((step, rows, piece[2]))
                    rows += piece[2]
            self.payload[step] = payload
            for level, pieces in fresh.items():
                self.held[level] = self.held.get(level, []) + pieces

    def partner(self, value, step):
        return exchange(value, 1 << self.first_bit + step)

    def gather(self, own, after=None):
        arrived = [None] * self.bits
        for step in range(self.bits - 1, -1, -1):
            parts = [own[step]] if self.own_rows[step] else []
            for source, row, rows in self.payload[step]:
                part = arrived[source]
                whole = rows == part.shape[1]
                parts.append(part if whole else part[:, row : row + rows])
            sent = jnp.concatenate(parts, axis=1) if len(parts) > 1 else parts[0]
            if step == 0:
                sent = ordered(sent, after)
            arrived[step] = self.partner(sent, step)
        return arrived

    def scatter(self, grads, after=None):
        grads = list(grads)
        returned = []
        for step in range(self.bits):
            sent = grads[step]
            if step == self.bits - 1:
                sent = ordered(sent, after)
            back = self.partner(sent, step)
            returned.append(back)
            filled = self.own_rows[step]
            for source, row, rows in self.payload[step]:
                part = back[:, filled : filled + rows]
                grads[source] = grads[source].at[:, row : row + rows].add(part)
                filled += rows
        return returned


def split(value):
    high = value.astype(BF16).astype(F32)
    return high, value - high


def halves_by_head(value):
    high, low = split(value)
    first = lax.broadcasted_iota(jnp.int32, value.shape, 1) < HEAD_DIM
    one = jnp.where(first, high, pltpu.roll(low, HEAD_DIM, 1))
    two = jnp.where(first, pltpu.roll(high, HEAD_DIM, 1), low)
    return one, two


def dot(lhs, rhs, dims):
    return lax.dot_general(lhs, rhs, (dims, ((), ())), preferred_element_type=F32)


NN = ((1,), (0,))
NT = ((1,), (1,))


BOTH = 2 * BLOCK
GROUP = 3


def halves_of(sets, ins, which, pairs, pair):
    tile = which * pairs + pair
    parts = [ins[index][tile, pl.ds(row, rows), :] for _, index, row, rows in sets]
    return halves_by_head(jnp.concatenate(parts, axis=0))


def segment_levels(sets):
    levels, filled = [], 0
    for level, _, _, rows in sets:
        if filled % BLOCK == 0:
            levels.append(level)
        filled += rows
    return levels


def four_rows(value):
    high, low = split(value)
    four = jnp.concatenate([high, high, low, low], axis=0).astype(BF16)
    return four, jnp.concatenate([high, low], axis=0).astype(BF16)


def store_split(ref, lead, rows, value):
    high = value.astype(BF16)
    ref[(lead, 0, rows)] = high
    ref[(lead, 1, rows)] = (value - high.astype(F32)).astype(BF16)


def fold_rows(value):
    return value[:HEAD_DIM] + value[HEAD_DIM:]


def fold_heads(one, two):
    first = lax.broadcasted_iota(jnp.int32, one.shape, 1) < HEAD_DIM
    return jnp.where(
        first, one + pltpu.roll(one, HEAD_DIM, 1), two + pltpu.roll(two, HEAD_DIM, 1)
    )


def twice(value):
    return jnp.concatenate([value, value], axis=1)


def stacked(ref, at, rows=slice(None)):
    return jnp.concatenate([ref[at, 0, rows], ref[at, 1, rows]], axis=0)


def abreast(ref, at, rows=slice(None)):
    return jnp.concatenate([ref[at, 0, rows], ref[at, 1, rows]], axis=1)


def column_scores(levels, keys, at, q_four, s_ref):
    highest = None
    for index, level in enumerate(levels):
        rows = pl.ds(index * BLOCK, BLOCK)
        s = dot(twice(keys[at, rows]), q_four, NN)
        s = s + float(level) if level else s
        s_ref[at, rows] = s
        top = jnp.max(s.reshape(BLOCK // 8, 8, BOTH), axis=0)
        highest = top if highest is None else jnp.maximum(highest, top)
    return jnp.max(highest, axis=0, keepdims=True)


def exponents(levels, at, top, s_ref, e_ref, keep):
    summed = None
    for index in range(len(levels)):
        rows = pl.ds(index * BLOCK, BLOCK)
        e = jnp.exp2(s_ref[at, rows] - top)
        if keep:
            s_ref[at, rows] = e
        store_split(e_ref, at, rows, e)
        part = jnp.sum(e.reshape(BLOCK // 8, 8, BOTH), axis=0)
        summed = part if summed is None else summed + part
    return jnp.sum(summed, axis=0, keepdims=True)


def head_rows(ref, pair, head):
    return ref[pair, pl.ds(head * HEAD_DIM, HEAD_DIM)]


def each_group(pairs, body):
    for first in range(0, pairs, GROUP):
        group = range(first, min(first + GROUP, pairs))
        body(group, [(pair, head, 2 * pair + head) for pair in group for head in (0, 1)])


def costs(pairs, rows, products, exps=0):
    return dict(
        flops=2 * 4 * products * pairs * 2 * rows * BOTH * HEAD_DIM,
        exps=exps * pairs * 2 * rows * BOTH,
    )


def put_halves(pairs, sets, ins, group, plain, turned):
    for which in range(2):
        for pair in group:
            for head, value in enumerate(halves_of(sets, ins, which, pairs, pair)):
                plain[which][2 * pair + head] = value.astype(BF16)
                turned[which][2 * pair + head] = value.T.astype(BF16)


def attend_first(pairs, sets, operands, turned):
    total = sum(s[3] for s in sets)
    levels = segment_levels(sets)

    def kernel(turn_in, *refs):
        ins = refs[: len(operands)]
        kt, vc, e_ref, tops, sums, out, s_ref, kc, vt = refs[len(operands) :]

        def body(group, heads):
            put_halves(pairs, sets, ins, group, (kc, vc), (kt, vt))
            for pair, head, at in heads:
                q_four, _ = four_rows(head_rows(turn_in, pair, head))
                tops[at] = column_scores(levels, kc, at, q_four, s_ref)
            for _, _, at in heads:
                sums[at] = exponents(levels, at, tops[at], s_ref, e_ref, False)
            for _, _, at in heads:
                out[at] = fold_rows(dot(twice(vt[at]), stacked(e_ref, at), NN))

        each_group(pairs, body)

    heads = 2 * pairs
    outs = [
        jax.ShapeDtypeStruct((heads, LANES, total), BF16),
        jax.ShapeDtypeStruct((heads, total, LANES), BF16),
        jax.ShapeDtypeStruct((heads, 2, total, BOTH), BF16),
    ]
    outs += [struct(heads, 1, BOTH)] * 2 + [struct(heads, HEAD_DIM, BOTH)]
    return call(
        kernel,
        [turned, *operands],
        outs,
        scratch=[
            pltpu.VMEM((heads, total, BOTH), F32),
            pltpu.VMEM((heads, total, LANES), BF16),
            pltpu.VMEM((heads, LANES, total), BF16),
        ],
        **costs(pairs, total, 2, 1),
    )


def attend_last(pairs, sets, operands, turned, grads_turned, tops, sums, partial):
    total = sum(s[3] for s in sets)
    levels = segment_levels(sets)

    def kernel(turn_in, grad_in, top_in, sum_in, part_in, *refs):
        ins = refs[: len(operands)]
        grads = refs[len(operands) : 2 * len(operands)]
        o_keep, o_send, g_out, r_out, dq_out = refs[2 * len(operands) : -7]
        s_ref, e_ref, d_ref, kc, vc, kt, vt = refs[-7:]

        def body(group, heads):
            put_halves(pairs, sets, ins, group, (kc, vc), (kt, vt))
            queries = {}
            top = {}
            for pair, head, at in heads:
                q_four, queries[at] = four_rows(head_rows(turn_in, pair, head))
                top[at] = column_scores(levels, kc, at, q_four, s_ref)
            inverse = {}
            rescale = {}
            for _, _, at in heads:
                first_top = top_in[at]
                highest = jnp.maximum(top[at], first_top)
                rescale[at] = jnp.exp2(first_top - highest)
                summed = exponents(levels, at, highest, s_ref, e_ref, True)
                inverse[at] = 1.0 / (summed + sum_in[at] * rescale[at])
            output = {}
            cotangents = {}
            row_dot = {}
            for pair, head, at in heads:
                o = fold_rows(dot(twice(vt[at]), stacked(e_ref, at), NN))
                o = (o + part_in[at] * rescale[at]) * inverse[at]
                output[at] = o
                scaled = head_rows(grad_in, pair, head) * inverse[at]
                cotangents[at] = four_rows(scaled)
                row_dot[at] = jnp.sum(o * scaled, axis=0, keepdims=True)
                g_out[at] = scaled * rescale[at]
                r_out[at] = row_dot[at] * rescale[at]
            for _, _, at in heads:
                for index in range(len(levels)):
                    rows = pl.ds(index * BLOCK, BLOCK)
                    dp = dot(twice(vc[at, rows]), cotangents[at][0], NN)
                    store_split(d_ref, at, rows, s_ref[at, rows] * (dp - row_dot[at]))
            key_grads = {}
            value_grads = {}
            for _, _, at in heads:
                value_grads[at] = dot(abreast(e_ref, at), twice(cotangents[at][1]), NT)
                key_grads[at] = dot(abreast(d_ref, at), twice(queries[at]), NT)
                dq_out[at] = fold_rows(dot(twice(kt[at]), stacked(d_ref, at), NN))
            for pair in group:
                put_grads(pairs, pair, sets, grads, key_grads, value_grads)
                both = [output[2 * pair], output[2 * pair + 1]]
                both = jnp.concatenate(both, axis=0).T
                o_keep[pair] = both[:BLOCK]
                o_send[pair] = both[BLOCK:]

        each_group(pairs, body)

    heads = 2 * pairs
    outs = [struct(*a.shape) for a in operands]
    outs += [struct(pairs, BLOCK, LANES)] * 2
    outs += [struct(heads, HEAD_DIM, BOTH), struct(heads, 1, BOTH)]
    outs.append(struct(heads, HEAD_DIM, BOTH))
    return call(
        kernel,
        [turned, grads_turned, tops, sums, partial, *operands],
        outs,
        scratch=[pltpu.VMEM((heads, total, BOTH), F32)]
        + [pltpu.VMEM((heads, 2, total, BOTH), BF16)] * 2
        + [pltpu.VMEM((heads, total, LANES), BF16)] * 2
        + [pltpu.VMEM((heads, LANES, total), BF16)] * 2,
        **costs(pairs, total, 6, 1),
    )


def put_grads(pairs, pair, sets, grads, key_grads, value_grads):
    for which, parts in enumerate((key_grads, value_grads)):
        both = fold_heads(parts[2 * pair], parts[2 * pair + 1])
        if which == 0:
            both = both * (1.0 / LOG2_E)
        filled = 0
        for _, index, row, rows in sets:
            piece = both[filled : filled + rows]
            grads[index][which * pairs + pair, pl.ds(row, rows), :] = piece
            filled += rows


def attend_back(pairs, sets, shapes, first, kept, turned, g_scaled, row_dot, dq, last):
    total = sum(s[3] for s in sets)
    segments = total // BLOCK

    def kernel(turn_in, kt, vc, e_ref, g_in, r_in, dq_in, *refs):
        grads = refs[: len(shapes)]
        dq_out = refs[len(shapes) : -1]
        d_ref = refs[-1]
        span = pl.ds(first, total)

        def body(group, heads):
            cotangents = {}
            for _, _, at in heads:
                g_four, cotangents[at] = four_rows(g_in[at])
                for index in range(segments):
                    rows = pl.ds(first + index * BLOCK, BLOCK)
                    dp = dot(twice(vc[at, rows]), g_four, NN)
                    e = e_ref[at, 0, rows].astype(F32) + e_ref[at, 1, rows].astype(F32)
                    place = pl.ds(index * BLOCK, BLOCK)
                    store_split(d_ref, at, place, e * (dp - r_in[at]))
            queries_grad = {}
            key_grads = {}
            value_grads = {}
            for pair, head, at in heads:
                _, q_rows = four_rows(head_rows(turn_in, pair, head))
                g_rows = cotangents[at]
                value_grads[at] = dot(abreast(e_ref, at, span), twice(g_rows), NT)
                key_grads[at] = dot(abreast(d_ref, at), twice(q_rows), NT)
                part = dot(twice(kt[at, :, span]), stacked(d_ref, at), NN)
                queries_grad[at] = fold_rows(part) + dq_in[at]
            for pair in group:
                put_grads(pairs, pair, sets, grads, key_grads, value_grads)
                both = [queries_grad[2 * pair], queries_grad[2 * pair + 1]]
                if last:
                    both = jnp.concatenate(both, axis=0).T * SCALE
                    dq_out[0][pair] = both[:BLOCK]
                    dq_out[1][pair] = both[BLOCK:]
                else:
                    for head in range(2):
                        dq_out[0][2 * pair + head] = both[head]

        each_group(pairs, body)

    outs = [struct(*shape) for shape in shapes]
    if last:
        outs += [struct(pairs, BLOCK, LANES)] * 2
    else:
        outs.append(struct(*dq.shape))
    return call(
        kernel,
        [turned, *kept, g_scaled, row_dot, dq],
        outs,
        scratch=[pltpu.VMEM((2 * pairs, 2, total, BOTH), BF16)],
        **costs(pairs, total, 4),
    )


def copy_columns(moves, ins, sems, bit):
    started = []
    for operand, theirs, column, place in moves:
        side = 1 - bit if theirs else bit
        column = side * (ins[operand].shape[1] // 2) + column
        column = pl.ds(pl.multiple_of(column, LANES), LANES)
        copy = pltpu.make_async_copy(
            ins[operand].at[:, column], place, sems.at[len(started)]
        )
        copy.start()
        started.append(copy)
    return started


def pack(pairs, first, second, scalar):
    def kernel(bit, one, two, one_theirs, two_theirs, one_mine, two_mine, sems):
        moves = []
        for operand, outs in ((0, (one_theirs, one_mine)), (1, (two_theirs, two_mine))):
            for out, other in zip(outs, (True, False)):
                for pair in range(pairs):
                    moves.append((operand, other, pair * LANES, out.at[pair]))
        for copy in copy_columns(moves, (one, two), sems, bit[0]):
            copy.wait()

    return call(
        kernel,
        [first, second],
        [struct(pairs, BLOCK, LANES)] * 4,
        scratch=[pltpu.SemaphoreType.DMA((4 * pairs,))],
        scalar=scalar,
        where=pl.ANY,
    )


QUARTER = BLOCK // 4
HALF = BLOCK // 2


def pack_coarse(pairs, keys, values, scalar):
    def kernel(bit, k, v, mine, f_theirs, f_mine, c_theirs, c_mine, rest, theirs, sems):
        moves = []
        for out, other in ((theirs, True), (mine, False)):
            for tile in range(2 * pairs):
                column = tile % pairs * LANES
                moves.append((tile // pairs, other, column, out.at[tile]))
        copies = copy_columns(moves, (k, v), sems, bit[0])
        for index, copy in enumerate(copies):
            copy.wait()
            tile = index % (2 * pairs)
            other = index < 2 * pairs
            source, finest, coarse = (
                (theirs, f_theirs, c_theirs) if other else (mine, f_mine, c_mine)
            )
            finest[tile] = mean_rows(source, (tile,), 0, HALF, 2)
            coarse[tile] = mean_rows(finest, (tile,), 0, QUARTER, 2)
            if other:
                rest[tile, :QUARTER] = half_difference(finest, (tile,), 0, QUARTER)
                rest[tile, QUARTER:] = half_difference(source, (tile,), 0, HALF)

    return call(
        kernel,
        [keys, values],
        [struct(2 * pairs, BLOCK, LANES)]
        + [struct(2 * pairs, HALF, LANES)] * 2
        + [struct(2 * pairs, QUARTER, LANES)] * 2
        + [struct(2 * pairs, QUARTER + HALF, LANES)],
        scratch=[
            pltpu.VMEM((2 * pairs, BLOCK, LANES), F32),
            pltpu.SemaphoreType.DMA((4 * pairs,)),
        ],
        scalar=scalar,
        where=pl.ANY,
    )


def rebuild(pairs, second, rest):
    def kernel(second_in, rest_in, out, finest):
        for tile in range(2 * pairs):
            put_pairs(finest, (tile,), second_in[tile], rest_in[tile, :QUARTER])
            put_pairs(out, (tile,), finest[tile], rest_in[tile, QUARTER:])

    return call(
        kernel,
        [second, rest],
        [struct(2 * pairs, BLOCK, LANES)],
        scratch=[pltpu.VMEM((2 * pairs, HALF, LANES), F32)],
    )[0]


def take_apart(pairs, block_grad):
    def kernel(block, second, rest, finest):
        for tile in range(2 * pairs):
            finest[tile] = 2.0 * mean_rows(block, (tile,), 0, HALF, 2)
            rest[tile, QUARTER:] = 2.0 * half_difference(block, (tile,), 0, HALF)
            second[tile] = 2.0 * mean_rows(finest, (tile,), 0, QUARTER, 2)
            rest[tile, :QUARTER] = 2.0 * half_difference(finest, (tile,), 0, QUARTER)

    return call(
        kernel,
        [block_grad],
        [
            struct(2 * pairs, QUARTER, LANES),
            struct(2 * pairs, QUARTER + HALF, LANES),
        ],
        scratch=[pltpu.VMEM((2 * pairs, HALF, LANES), F32)],
    )


def coarsen_pair(lo, pairs, mine, received):
    def kernel(own, got, *outs):
        for tile in range(2 * pairs):
            outs[0][tile, : BLOCK // 4] = own[tile]
            outs[0][tile, BLOCK // 4 :] = got[tile]
            for index in range(1, lo.bits):
                outs[index][tile] = mean_rows(
                    outs[index - 1], (tile,), 0, BLOCK >> index + 1, 2
                )

    outs = [struct(2 * pairs, BLOCK >> step, LANES) for step in range(1, lo.bits + 1)]
    return call(kernel, [mine, received], outs)


def group_pieces(lo):
    own = BLOCK >> lo.bits
    factor = 1 << lo.bits
    pieces = [
        (-2, 0, BLOCK // 2, factor, own),
        (-1, 0, BLOCK // 2, factor, own + own // 2),
    ]
    filled = 2 * own
    for level in range(1, lo.bits):
        factor = 1 << lo.bits - level
        for step, row, rows in lo.held[level]:
            pieces.append((step, row, rows, factor, filled))
            filled += rows // factor
    return pieces


def coarsen_group(lo, hi, pairs, own, halves, arrived):
    pieces = group_pieces(lo)

    def kernel(own_in, *refs):
        ins = refs[: 2 + lo.bits]
        outs = refs[2 + lo.bits :]
        for tile in range(2 * pairs):
            outs[0][tile, pl.ds(0, BLOCK >> lo.bits)] = own_in[tile]
            for step, row, rows, factor, place in pieces:
                count = rows // factor
                outs[0][tile, pl.ds(place, count)] = mean_rows(
                    ins[2 + step], (tile,), row, count, factor
                )
            for step in range(1, hi.bits):
                outs[step][tile] = mean_rows(
                    outs[step - 1], (tile,), 0, BLOCK >> step, 2
                )

    outs = [struct(2 * pairs, BLOCK >> step, LANES) for step in range(hi.bits)]
    return call(kernel, [own, *halves, *arrived], outs)


def turn(pairs, mine, received, scale):
    def kernel(own, got, turned):
        for pair in range(pairs):
            both = jnp.concatenate([own[pair], got[pair]], axis=0).T
            turned[pair] = both * scale if scale != 1.0 else both

    return call(kernel, [mine, received], [struct(pairs, LANES, BOTH)])[0]


def spread_group(lo, hi, pairs, group_grads, grads):
    pieces = group_pieces(lo)
    own_rows = BLOCK >> lo.bits

    def kernel(*refs):
        steps = refs[: hi.bits]
        ins = refs[hi.bits : hi.bits + lo.bits]
        own_out, *outs = refs[hi.bits + lo.bits : -1]
        total = refs[-1]
        for tile in range(2 * pairs):
            total[tile] = steps[0][tile, pl.ds(0, BLOCK)]
            for step in range(1, hi.bits):
                above = steps[step][tile, pl.ds(0, BLOCK >> step)]
                add_spread(total, (tile,), 0, above, 1 << step)
            own_out[tile] = total[tile, pl.ds(0, own_rows)]
            for out, value in zip(outs, ins):
                out[tile, pl.ds(0, value.shape[1])] = value[tile]
            outs[0][tile, pl.ds(ins[0].shape[1], own_rows)] = total[
                tile, pl.ds(own_rows, own_rows)
            ]
            for step, row, rows, factor, place in pieces:
                if step >= 0:
                    part = total[tile, pl.ds(place, rows // factor)]
                    add_spread(outs[step], (tile,), row, part, factor)

    shapes = [list(a.shape) for a in grads]
    shapes[0][1] += own_rows
    outs = [struct(2 * pairs, own_rows, LANES)] + [struct(*shape) for shape in shapes]
    own, *grads = call(
        kernel,
        [*group_grads, *grads],
        outs,
        scratch=[pltpu.VMEM((2 * pairs, BLOCK, LANES), F32)],
    )
    return own, grads


def spread_pair(lo, pairs, own_grad, returned, block_second):
    own_rows = BLOCK >> lo.bits

    def kernel(own, block, *refs):
        back = refs[: lo.bits]
        mine, theirs, *totals = refs[lo.bits :]
        last = pl.ds(back[0].shape[1] - own_rows, own_rows)
        for tile in range(2 * pairs):
            above = own[tile] + back[0][tile, last]
            for step in range(lo.bits - 1, 0, -1):
                total = totals[step - 1]
                total[tile] = back[step][tile, pl.ds(0, BLOCK >> step)]
                add_spread(total, (tile,), 0, above, 2)
                above = total[tile]
            mine[tile] = above[: BLOCK // 4]
            theirs[tile] = above[BLOCK // 4 :] + block[tile]

    return call(
        kernel,
        [own_grad, block_second, *returned],
        [struct(2 * pairs, BLOCK // 4, LANES)] * 2,
        scratch=[
            pltpu.VMEM((2 * pairs, BLOCK >> step, LANES), F32)
            for step in range(1, lo.bits)
        ],
    )


def unpack(pairs, kept, arrived, features, scalar):
    def kernel(bit, mine, theirs, *outs):
        for tile in range(2 * pairs):
            for side, array in ((bit[0], mine), (1 - bit[0], theirs)):
                column = side * (features // 2) + tile % pairs * LANES
                column = pl.ds(pl.multiple_of(column, LANES), LANES)
                outs[tile // pairs][:, column] = array[tile]

    return call(kernel, [kept, arrived], [struct(BLOCK, features)] * 2, scalar=scalar)


def finish(pairs, kept, rest, finest, seconds, features, scalar):
    def kernel(bit, kept_in, rest_in, f_mine, f_theirs, s_mine, s_theirs, *refs):
        outs, total, middle = refs[:2], refs[2], refs[3]
        for tile in range(2 * pairs):
            out = outs[tile // pairs]
            column = tile % pairs * LANES
            at = (tile,)
            total[tile] = kept_in[tile]
            add_spread(total, at, 0, f_mine[tile], 2)
            add_spread(total, at, 0, s_mine[tile], 4)
            place = bit[0] * (features // 2) + column
            out[:, pl.ds(pl.multiple_of(place, LANES), LANES)] = total[tile]
            put_pairs(middle, at, 0.5 * s_theirs[tile], 0.5 * rest_in[tile, :QUARTER])
            first = 0.5 * (middle[tile] + f_theirs[tile])
            put_pairs(total, at, first, 0.5 * rest_in[tile, QUARTER:])
            place = (1 - bit[0]) * (features // 2) + column
            out[:, pl.ds(pl.multiple_of(place, LANES), LANES)] = total[tile]

    return call(
        kernel,
        [kept, rest, *finest, *seconds],
        [struct(BLOCK, features)] * 2,
        scratch=[
            pltpu.VMEM((2 * pairs, BLOCK, LANES), F32),
            pltpu.VMEM((2 * pairs, HALF, LANES), F32),
        ],
        scalar=scalar,
    )


def on_device(queries, keys, values, cotangent):
    features = queries.shape[1]
    assert queries.shape[0] == BLOCK
    pairs = features // LANES // 2
    lo_bits = lax.axis_size("seqlo").bit_length() - 1
    lo = Tree(lo_bits - 1, 1, lowest=False)
    hi = Tree(lax.axis_size("seqhi").bit_length() - 1, lo_bits)
    scalar = (lax.axis_index("seqlo") % 2).astype(jnp.int32).reshape(1)
    queries, keys, values, cotangent = [
        pltpu.with_memory_space_constraint(array, pltpu.HBM)
        for array in (queries, keys, values, cotangent)
    ]
    mine_kv, f_theirs, f_mine, c_send, c_mine, rest = pack_coarse(
        pairs, keys, values, scalar
    )
    second = exchange(c_send, 1)
    finest_theirs = exchange(f_theirs, 2)
    coarse = coarsen_pair(lo, pairs, c_mine, second)
    finest = exchange(f_mine, 2)
    half = exchange(finest_theirs, 1)
    rest = exchange(ordered(rest, second), 1)
    kv = rebuild(pairs, second, rest)
    send_q, send_g, mine_q, mine_g = pack(pairs, queries, cotangent, scalar)
    theirs_q = exchange(ordered(send_q, finest_theirs), 1)
    theirs_g = exchange(ordered(send_g, half), 1)
    zs = lo.gather([None, *coarse], (finest, send_q))
    group = coarsen_group(
        lo, hi, pairs, ordered(coarse[-1], rest), [finest, half], zs
    )
    turned = turn(pairs, mine_q, theirs_q, SCALE * LOG2_E)
    rs = hi.gather(group, (turned, theirs_g))
    grads_turned = turn(pairs, mine_g, theirs_g, 1.0)
    block_sets = [(0, 0, 0, BLOCK), (0, 1, 0, BLOCK)]
    lo_sets = [(1, 2, 0, BLOCK // 2), (1, 3, 0, BLOCK // 2)]
    for level in range(lo.bits):
        for step, row, rows in lo.held[level]:
            lo_sets.append((1 + level, 4 + step, row, rows))
    hi_sets = []
    for level in range(hi.bits):
        for step, row, rows in hi.held[level]:
            hi_sets.append((lo_bits + level, step, row, rows))
    first_in = [mine_kv, kv, finest, half, *zs]
    *kept, tops, sums, partial = attend_first(
        pairs, block_sets + lo_sets, first_in, turned
    )
    *rs_grads, o_keep, o_send, g_scaled, row_dot, dq = attend_last(
        pairs, hi_sets, rs, turned, grads_turned, tops, sums, partial
    )
    shapes = [(2 * pairs, *a.shape[1:]) for a in first_in]
    finest_grad, half_grad, *zs_grads, dq_lo = attend_back(
        pairs,
        [(level, index - 2, row, rows) for level, index, row, rows in lo_sets],
        shapes[2:],
        BOTH,
        kept,
        turned,
        g_scaled,
        row_dot,
        dq,
        False,
    )
    kv_keep, kv_send, dq_keep, dq_send = attend_back(
        pairs, block_sets, shapes[:2], 0, kept, turned, g_scaled, row_dot, dq_lo, True
    )
    og_keep = jnp.concatenate([o_keep, dq_keep], axis=0)
    og_send = jnp.concatenate([o_send, dq_send], axis=0)
    finest_mine = exchange(finest_grad, 2)
    half_back = exchange(half_grad, 1)
    block_second, rest_grad = take_apart(pairs, kv_send)
    rest_back = exchange(ordered(rest_grad, half_back), 1)
    og_back = exchange(ordered(og_send, half_back), 1)
    group_grads = hi.scatter(rs_grads, dq_lo)
    group_grads[-1] = ordered(group_grads[-1], kv_send)
    own_grad, grads = spread_group(lo, hi, pairs, group_grads, zs_grads)
    grads[0] = ordered(grads[0], finest_mine)
    returned = lo.scatter(grads, rest_back)
    finest_theirs = exchange(ordered(half_back, returned[0]), 2)
    own_grad = ordered(own_grad, (rest_back, og_back))
    second_mine, second_send = spread_pair(lo, pairs, own_grad, returned, block_second)
    second_theirs = exchange(second_send, 1)
    attended, query_grad = unpack(pairs, og_keep, og_back, features, scalar)
    key_grad, value_grad = finish(
        pairs,
        kv_keep,
        rest_back,
        (finest_mine, finest_theirs),
        (second_mine, second_theirs),
        features,
        scalar,
    )
    return attended, query_grad, key_grad, value_grad


def solution(mesh):
    spec = P(AXES, None)
    return jax.shard_map(
        on_device,
        mesh=mesh,
        in_specs=(spec,) * 4,
        out_specs=(spec,) * 4,
        check_vma=False,
    )
```

```python
import math

import jax
import jax.numpy as jnp
from jax import lax
from jax.experimental import pallas as pl
from jax.experimental.pallas import tpu as pltpu
from jax.sharding import PartitionSpec as P

HEADS = 12
BLOCK = 128
HEAD_DIM = 64
LANES = 2 * HEAD_DIM
AXES = ("seqhi", "seqlo")
VMEM_LIMIT = 20 * 1024 * 1024
F32 = jnp.float32
BF16 = jnp.bfloat16
LOG2_E = 1.0 / math.log(2.0)
SCALE = 1.0 / math.sqrt(HEAD_DIM)


def struct(*shape):
    return jax.ShapeDtypeStruct(shape, F32)


def call(kernel, operands, outs, scratch=(), scalar=None, flops=0, exps=0, where=None):
    vmem = pl.BlockSpec(memory_space=pltpu.VMEM)
    smem = pl.BlockSpec(memory_space=pltpu.SMEM)
    in_specs = [pl.BlockSpec(memory_space=where) if where else vmem] * len(operands)
    if scalar is not None:
        operands = [scalar, *operands]
        in_specs = [smem, *in_specs]
    moved = sum(4 * math.prod(a.shape) for a in [*operands, *outs])
    return pl.pallas_call(
        kernel,
        out_shape=list(outs),
        in_specs=in_specs,
        out_specs=[vmem] * len(outs),
        scratch_shapes=list(scratch),
        compiler_params=pltpu.CompilerParams(vmem_limit_bytes=VMEM_LIMIT),
        cost_estimate=pl.CostEstimate(
            flops=flops, bytes_accessed=moved, transcendentals=exps
        ),
    )(*operands)


def exchange(value, offset):
    count = lax.axis_size(AXES)
    return lax.ppermute(value, AXES, [(i, i ^ offset) for i in range(count)])


def ordered(value, after):
    return value if after is None else lax.optimization_barrier((value, after))[0]


def half_difference(ref, lead, first, count):
    even = ref[(*lead, pl.ds(first, count, stride=2), slice(None))]
    odd = ref[(*lead, pl.ds(first + 1, count, stride=2), slice(None))]
    return 0.5 * (even - odd)


def put_pairs(ref, lead, total, difference):
    count = total.shape[0]
    ref[(*lead, pl.ds(0, count, stride=2), slice(None))] = total + difference
    ref[(*lead, pl.ds(1, count, stride=2), slice(None))] = total - difference


def mean_rows(ref, lead, first, count, factor):
    total = None
    for step in range(factor):
        rows = pl.ds(first + step, count, stride=factor)
        part = ref[(*lead, rows, slice(None))]
        total = part if total is None else total + part
    return total * (1.0 / factor)


def add_spread(ref, lead, first, value, factor):
    count = value.shape[0]
    value = value * (1.0 / factor)
    for step in range(factor):
        rows = pl.ds(first + step, count, stride=factor)
        place = (*lead, rows, slice(None))
        ref[place] = ref[place] + value


class Tree:
    def __init__(self, first_bit, own_rows):
        self.bits = bits = len(own_rows)
        self.first_bit = first_bit
        self.own_rows = own_rows
        self.held = {}
        self.payload = {}
        for step in range(bits - 1, -1, -1):
            rows = self.own_rows[step]
            payload = []
            fresh = {step: [(step, 0, rows)] if rows else []}
            for level in range(step + 1, bits):
                for piece in self.held[level]:
                    payload.append(piece)
                    fresh.setdefault(level, []).append((step, rows, piece[2]))
                    rows += piece[2]
            self.payload[step] = payload
            for level, pieces in fresh.items():
                self.held[level] = self.held.get(level, []) + pieces

    def partner(self, value, step):
        return exchange(value, 1 << self.first_bit + step)

    def gather(self, own, after=None):
        arrived = [None] * self.bits
        for step in range(self.bits - 1, -1, -1):
            parts = [own[step]] if self.own_rows[step] else []
            for source, row, rows in self.payload[step]:
                part = arrived[source]
                whole = rows == part.shape[1]
                parts.append(part if whole else part[:, row : row + rows])
            sent = jnp.concatenate(parts, axis=1) if len(parts) > 1 else parts[0]
            if step == 0:
                sent = ordered(sent, after)
            arrived[step] = self.partner(sent, step)
        return arrived

    def scatter(self, grads):
        grads = list(grads)
        returned = []
        for step in range(self.bits):
            back = self.partner(grads[step], step)
            returned.append(back)
            filled = self.own_rows[step]
            for source, row, rows in self.payload[step]:
                part = back[:, filled : filled + rows]
                grads[source] = grads[source].at[:, row : row + rows].add(part)
                filled += rows
        return returned


def split(value):
    high = value.astype(BF16).astype(F32)
    return high, value - high


def halves_by_head(value):
    high, low = split(value)
    first = lax.broadcasted_iota(jnp.int32, value.shape, 1) < HEAD_DIM
    one = jnp.where(first, high, pltpu.roll(low, HEAD_DIM, 1))
    two = jnp.where(first, pltpu.roll(high, HEAD_DIM, 1), low)
    return one, two


def dot(lhs, rhs, dims):
    return lax.dot_general(lhs, rhs, (dims, ((), ())), preferred_element_type=F32)


NN = ((1,), (0,))
NT = ((1,), (1,))


BOTH = 2 * BLOCK
GROUP = 3


def halves_of(sets, ins, which, pairs, pair):
    tile = which * pairs + pair
    parts = [ins[index][tile, pl.ds(row, rows), :] for _, index, row, rows in sets]
    return halves_by_head(jnp.concatenate(parts, axis=0))


def segment_levels(sets):
    levels, filled = [], 0
    for level, _, _, rows in sets:
        if filled % BLOCK == 0:
            levels.append(level)
        filled += rows
    return levels


def four_rows(value):
    high, low = split(value)
    four = jnp.concatenate([high, high, low, low], axis=0).astype(BF16)
    return four, jnp.concatenate([high, low], axis=0).astype(BF16)


def store_split(ref, lead, rows, value):
    high = value.astype(BF16)
    ref[(lead, 0, rows)] = high
    ref[(lead, 1, rows)] = (value - high.astype(F32)).astype(BF16)


def fold_rows(value):
    return value[:HEAD_DIM] + value[HEAD_DIM:]


def fold_heads(one, two):
    first = lax.broadcasted_iota(jnp.int32, one.shape, 1) < HEAD_DIM
    return jnp.where(
        first, one + pltpu.roll(one, HEAD_DIM, 1), two + pltpu.roll(two, HEAD_DIM, 1)
    )


def twice(value):
    return jnp.concatenate([value, value], axis=1)


def stacked(ref, at, rows=slice(None)):
    return jnp.concatenate([ref[at, 0, rows], ref[at, 1, rows]], axis=0)


def abreast(ref, at, rows=slice(None)):
    return jnp.concatenate([ref[at, 0, rows], ref[at, 1, rows]], axis=1)


def column_scores(levels, keys, at, q_four, s_ref):
    highest = None
    for index, level in enumerate(levels):
        rows = pl.ds(index * BLOCK, BLOCK)
        s = dot(twice(keys[at, rows]), q_four, NN)
        s = s + float(level) if level else s
        s_ref[at, rows] = s
        top = jnp.max(s.reshape(BLOCK // 8, 8, BOTH), axis=0)
        highest = top if highest is None else jnp.maximum(highest, top)
    return jnp.max(highest, axis=0, keepdims=True)


def exponents(levels, at, top, s_ref, e_ref, keep):
    summed = None
    for index in range(len(levels)):
        rows = pl.ds(index * BLOCK, BLOCK)
        e = jnp.exp2(s_ref[at, rows] - top)
        if keep:
            s_ref[at, rows] = e
        store_split(e_ref, at, rows, e)
        part = jnp.sum(e.reshape(BLOCK // 8, 8, BOTH), axis=0)
        summed = part if summed is None else summed + part
    return jnp.sum(summed, axis=0, keepdims=True)


def head_rows(ref, pair, head):
    return ref[pair, pl.ds(head * HEAD_DIM, HEAD_DIM)]


def each_group(pairs, body):
    for first in range(0, pairs, GROUP):
        group = range(first, min(first + GROUP, pairs))
        body(group, [(pair, head, 2 * pair + head) for pair in group for head in (0, 1)])


def costs(pairs, rows, products, exps=0):
    return dict(
        flops=2 * 4 * products * pairs * 2 * rows * BOTH * HEAD_DIM,
        exps=exps * pairs * 2 * rows * BOTH,
    )


def put_halves(pairs, sets, ins, group, plain, turned):
    for which in range(2):
        for pair in group:
            for head, value in enumerate(halves_of(sets, ins, which, pairs, pair)):
                plain[which][2 * pair + head] = value.astype(BF16)
                turned[which][2 * pair + head] = value.T.astype(BF16)


def attend_first(pairs, sets, operands, turned):
    total = sum(s[3] for s in sets)
    levels = segment_levels(sets)

    def kernel(turn_in, *refs):
        ins = refs[: len(operands)]
        kt, vc, e_ref, tops, sums, out, s_ref, kc, vt = refs[len(operands) :]

        def body(group, heads):
            put_halves(pairs, sets, ins, group, (kc, vc), (kt, vt))
            for pair, head, at in heads:
                q_four, _ = four_rows(head_rows(turn_in, pair, head))
                tops[at] = column_scores(levels, kc, at, q_four, s_ref)
            for _, _, at in heads:
                sums[at] = exponents(levels, at, tops[at], s_ref, e_ref, False)
            for _, _, at in heads:
                out[at] = fold_rows(dot(twice(vt[at]), stacked(e_ref, at), NN))

        each_group(pairs, body)

    heads = 2 * pairs
    outs = [
        jax.ShapeDtypeStruct((heads, LANES, total), BF16),
        jax.ShapeDtypeStruct((heads, total, LANES), BF16),
        jax.ShapeDtypeStruct((heads, 2, total, BOTH), BF16),
    ]
    outs += [struct(heads, 1, BOTH)] * 2 + [struct(heads, HEAD_DIM, BOTH)]
    return call(
        kernel,
        [turned, *operands],
        outs,
        scratch=[
            pltpu.VMEM((heads, total, BOTH), F32),
            pltpu.VMEM((heads, total, LANES), BF16),
            pltpu.VMEM((heads, LANES, total), BF16),
        ],
        **costs(pairs, total, 2, 1),
    )


def attend_last(pairs, sets, operands, turned, tops, sums, partial):
    total = sum(s[3] for s in sets)
    levels = segment_levels(sets)

    def kernel(turn_in, top_in, sum_in, part_in, *refs):
        ins = refs[: len(operands)]
        grads = refs[len(operands) : 2 * len(operands)]
        o_keep, o_send, g_out, r_out, dq_out = refs[2 * len(operands) : -7]
        s_ref, e_ref, d_ref, kc, vc, kt, vt = refs[-7:]

        def body(group, heads):
            put_halves(pairs, sets, ins, group, (kc, vc), (kt, vt))
            queries = {}
            top = {}
            for pair, head, at in heads:
                q_four, queries[at] = four_rows(head_rows(turn_in, pair, head))
                top[at] = column_scores(levels, kc, at, q_four, s_ref)
            inverse = {}
            rescale = {}
            for _, _, at in heads:
                first_top = top_in[at]
                highest = jnp.maximum(top[at], first_top)
                rescale[at] = jnp.exp2(first_top - highest)
                summed = exponents(levels, at, highest, s_ref, e_ref, True)
                inverse[at] = 1.0 / (summed + sum_in[at] * rescale[at])
            output = {}
            cotangents = {}
            row_dot = {}
            for pair, head, at in heads:
                o = fold_rows(dot(twice(vt[at]), stacked(e_ref, at), NN))
                o = (o + part_in[at] * rescale[at]) * inverse[at]
                output[at] = o
                scaled = head_rows(turn_in, pairs + pair, head) * inverse[at]
                cotangents[at] = four_rows(scaled)
                row_dot[at] = jnp.sum(o * scaled, axis=0, keepdims=True)
                g_out[at] = scaled * rescale[at]
                r_out[at] = row_dot[at] * rescale[at]
            for _, _, at in heads:
                for index in range(len(levels)):
                    rows = pl.ds(index * BLOCK, BLOCK)
                    dp = dot(twice(vc[at, rows]), cotangents[at][0], NN)
                    store_split(d_ref, at, rows, s_ref[at, rows] * (dp - row_dot[at]))
            key_grads = {}
            value_grads = {}
            for _, _, at in heads:
                value_grads[at] = dot(abreast(e_ref, at), twice(cotangents[at][1]), NT)
                key_grads[at] = dot(abreast(d_ref, at), twice(queries[at]), NT)
                dq_out[at] = fold_rows(dot(twice(kt[at]), stacked(d_ref, at), NN))
            for pair in group:
                put_grads(pairs, pair, sets, grads, key_grads, value_grads)
                both = [output[2 * pair], output[2 * pair + 1]]
                both = jnp.concatenate(both, axis=0).T
                o_keep[pair] = both[:BLOCK]
                o_send[pair] = both[BLOCK:]

        each_group(pairs, body)

    heads = 2 * pairs
    outs = [struct(*a.shape) for a in operands]
    outs += [struct(pairs, BLOCK, LANES)] * 2
    outs += [struct(heads, HEAD_DIM, BOTH), struct(heads, 1, BOTH)]
    outs.append(struct(heads, HEAD_DIM, BOTH))
    return call(
        kernel,
        [turned, tops, sums, partial, *operands],
        outs,
        scratch=[pltpu.VMEM((heads, total, BOTH), F32)]
        + [pltpu.VMEM((heads, 2, total, BOTH), BF16)] * 2
        + [pltpu.VMEM((heads, total, LANES), BF16)] * 2
        + [pltpu.VMEM((heads, LANES, total), BF16)] * 2,
        **costs(pairs, total, 6, 1),
    )


def put_grads(pairs, pair, sets, grads, key_grads, value_grads):
    for which, parts in enumerate((key_grads, value_grads)):
        both = fold_heads(parts[2 * pair], parts[2 * pair + 1])
        if which == 0:
            both = both * (1.0 / LOG2_E)
        filled = 0
        for _, index, row, rows in sets:
            piece = both[filled : filled + rows]
            grads[index][which * pairs + pair, pl.ds(row, rows), :] = piece
            filled += rows


def attend_back(pairs, sets, shapes, first, kept, turned, g_scaled, row_dot, dq, last):
    total = sum(s[3] for s in sets)
    segments = total // BLOCK

    def kernel(turn_in, kt, vc, e_ref, g_in, r_in, dq_in, *refs):
        grads = refs[: len(shapes)]
        dq_out = refs[len(shapes) : -1]
        d_ref = refs[-1]
        span = pl.ds(first, total)

        def body(group, heads):
            cotangents = {}
            for _, _, at in heads:
                g_four, cotangents[at] = four_rows(g_in[at])
                for index in range(segments):
                    rows = pl.ds(first + index * BLOCK, BLOCK)
                    dp = dot(twice(vc[at, rows]), g_four, NN)
                    e = e_ref[at, 0, rows].astype(F32) + e_ref[at, 1, rows].astype(F32)
                    place = pl.ds(index * BLOCK, BLOCK)
                    store_split(d_ref, at, place, e * (dp - r_in[at]))
            queries_grad = {}
            key_grads = {}
            value_grads = {}
            for pair, head, at in heads:
                _, q_rows = four_rows(head_rows(turn_in, pair, head))
                g_rows = cotangents[at]
                value_grads[at] = dot(abreast(e_ref, at, span), twice(g_rows), NT)
                key_grads[at] = dot(abreast(d_ref, at), twice(q_rows), NT)
                part = dot(twice(kt[at, :, span]), stacked(d_ref, at), NN)
                queries_grad[at] = fold_rows(part) + dq_in[at]
            for pair in group:
                put_grads(pairs, pair, sets, grads, key_grads, value_grads)
                both = [queries_grad[2 * pair], queries_grad[2 * pair + 1]]
                if last:
                    both = jnp.concatenate(both, axis=0).T * SCALE
                    dq_out[0][pair] = both[:BLOCK]
                    dq_out[1][pair] = both[BLOCK:]
                else:
                    for head in range(2):
                        dq_out[0][2 * pair + head] = both[head]

        each_group(pairs, body)

    outs = [struct(*shape) for shape in shapes]
    if last:
        outs += [struct(pairs, BLOCK, LANES)] * 2
    else:
        outs.append(struct(*dq.shape))
    return call(
        kernel,
        [turned, *kept, g_scaled, row_dot, dq],
        outs,
        scratch=[pltpu.VMEM((2 * pairs, 2, total, BOTH), BF16)],
        **costs(pairs, total, 4),
    )


def copy_columns(moves, ins, sems, bit):
    started = []
    for operand, theirs, column, place in moves:
        side = 1 - bit if theirs else bit
        column = side * (ins[operand].shape[1] // 2) + column
        column = pl.ds(pl.multiple_of(column, LANES), LANES)
        copy = pltpu.make_async_copy(
            ins[operand].at[:, column], place, sems.at[len(started)]
        )
        copy.start()
        started.append(copy)
    return started


def pack(pairs, first, second, scalar):
    def kernel(bit, one, two, theirs, mine, sems):
        moves = []
        for tile in range(2 * pairs):
            for out, other in ((theirs, True), (mine, False)):
                column = tile % pairs * LANES
                moves.append((tile // pairs, other, column, out.at[tile]))
        for copy in copy_columns(moves, (one, two), sems, bit[0]):
            copy.wait()

    return call(
        kernel,
        [first, second],
        [struct(2 * pairs, BLOCK, LANES)] * 2,
        scratch=[pltpu.SemaphoreType.DMA((4 * pairs,))],
        scalar=scalar,
        where=pl.ANY,
    )


QUARTER = BLOCK // 4
HALF = BLOCK // 2


def pack_coarse(pairs, keys, values, scalar):
    def kernel(bit, k, v, mine, f_theirs, f_mine, c_theirs, c_mine, rest, theirs, sems):
        moves = []
        for out, other in ((theirs, True), (mine, False)):
            for tile in range(2 * pairs):
                column = tile % pairs * LANES
                moves.append((tile // pairs, other, column, out.at[tile]))
        copies = copy_columns(moves, (k, v), sems, bit[0])
        for index, copy in enumerate(copies):
            copy.wait()
            tile = index % (2 * pairs)
            other = index < 2 * pairs
            source, finest, coarse = (
                (theirs, f_theirs, c_theirs) if other else (mine, f_mine, c_mine)
            )
            finest[tile] = mean_rows(source, (tile,), 0, HALF, 2)
            coarse[tile] = mean_rows(finest, (tile,), 0, QUARTER, 2)
            if other:
                rest[tile, :QUARTER] = half_difference(finest, (tile,), 0, QUARTER)
                rest[tile, QUARTER:] = half_difference(source, (tile,), 0, HALF)

    return call(
        kernel,
        [keys, values],
        [struct(2 * pairs, BLOCK, LANES)]
        + [struct(2 * pairs, HALF, LANES)] * 2
        + [struct(2 * pairs, QUARTER, LANES)] * 2
        + [struct(2 * pairs, QUARTER + HALF, LANES)],
        scratch=[
            pltpu.VMEM((2 * pairs, BLOCK, LANES), F32),
            pltpu.SemaphoreType.DMA((4 * pairs,)),
        ],
        scalar=scalar,
        where=pl.ANY,
    )


def rebuild(pairs, second, rest):
    def kernel(second_in, rest_in, out, finest):
        for tile in range(2 * pairs):
            put_pairs(finest, (tile,), second_in[tile], rest_in[tile, :QUARTER])
            put_pairs(out, (tile,), finest[tile], rest_in[tile, QUARTER:])

    return call(
        kernel,
        [second, rest],
        [struct(2 * pairs, BLOCK, LANES)],
        scratch=[pltpu.VMEM((2 * pairs, HALF, LANES), F32)],
    )[0]


def take_apart(pairs, block_grad):
    def kernel(block, second, rest, finest):
        for tile in range(2 * pairs):
            finest[tile] = 2.0 * mean_rows(block, (tile,), 0, HALF, 2)
            rest[tile, QUARTER:] = 2.0 * half_difference(block, (tile,), 0, HALF)
            second[tile] = 2.0 * mean_rows(finest, (tile,), 0, QUARTER, 2)
            rest[tile, :QUARTER] = 2.0 * half_difference(finest, (tile,), 0, QUARTER)

    return call(
        kernel,
        [block_grad],
        [
            struct(2 * pairs, QUARTER, LANES),
            struct(2 * pairs, QUARTER + HALF, LANES),
        ],
        scratch=[pltpu.VMEM((2 * pairs, HALF, LANES), F32)],
    )


class Levels:
    def __init__(self, bits):
        self.bits = bits
        self.rows = BLOCK >> bits
        self.differences = [
            [(m, BLOCK >> m) for m in range(bits, step, -1)] for step in range(bits)
        ]
        whole = [0] + [BLOCK >> step for step in range(1, bits)]
        self.whole = Tree(1, whole)
        self.rough = Tree(1, [0] + [self.rows] * (bits - 1))
        self.fine = Tree(1, [0] + [rows - self.rows for rows in whole[1:]])
        self.pieces = []
        for level in range(1, bits):
            trees = (self.whole, self.rough, self.fine)
            for parts in zip(*(tree.held[level] for tree in trees)):
                self.pieces.append((level, parts[0][0], *(part[1] for part in parts)))

    def scratch(self):
        shapes = [(BLOCK >> m, LANES) for m in range(1, self.bits + 1)]
        return [pltpu.VMEM(shape, F32) for shape in shapes]

    def group_pieces(self):
        pieces = []
        for index, (level, step, whole, rough, _) in enumerate(self.pieces):
            factor = 1 << self.bits - level
            place = (2 + index) * self.rows
            pieces.append((step, whole, rough, BLOCK >> level, factor, place))
        return pieces


def coarsen_pair(levels, pairs, mine, received):
    def kernel(own, got, rough, *refs):
        outs = refs[: levels.bits - 1]
        ladder = refs[levels.bits - 1 :]
        for tile in range(2 * pairs):
            ladder[0][:QUARTER, :] = own[tile]
            ladder[0][QUARTER:, :] = got[tile]
            for m in range(2, levels.bits + 1):
                ladder[m - 1][...] = mean_rows(ladder[m - 2], (), 0, BLOCK >> m, 2)
            rough[tile] = ladder[levels.bits - 1][...]
            for step in range(1, levels.bits):
                filled = 0
                for m, rows in levels.differences[step]:
                    outs[step - 1][tile, pl.ds(filled, rows)] = half_difference(
                        ladder[m - 2], (), 0, rows
                    )
                    filled += rows

    outs = [struct(2 * pairs, levels.rows, LANES)]
    outs += [struct(2 * pairs, rows, LANES) for rows in levels.fine.own_rows[1:]]
    rough, *fine = call(kernel, [mine, received], outs, scratch=levels.scratch())
    return rough, fine


def rebuild_levels(levels, pairs, rough, fine):
    def kernel(*refs):
        rough_in = refs[: levels.bits]
        fine_in = refs[levels.bits : 2 * levels.bits]
        outs = refs[2 * levels.bits : 3 * levels.bits]
        ladder = refs[3 * levels.bits :]
        for tile in range(2 * pairs):
            for level, step, row, rough_row, fine_row in levels.pieces:
                current = rough_in[step][tile, pl.ds(rough_row, levels.rows)]
                for m, rows in levels.differences[level]:
                    part = fine_in[step][tile, pl.ds(fine_row, rows)]
                    fine_row += rows
                    put_pairs(ladder[m - 2], (), current, part)
                    current = ladder[m - 2][...]
                outs[step][tile, pl.ds(row, BLOCK >> level)] = current

    outs = []
    for a, b in zip(rough, fine):
        outs.append(struct(2 * pairs, a.shape[1] + b.shape[1], LANES))
    return call(kernel, [*rough, *fine], outs, scratch=levels.scratch())


def coarsen_group(levels, hi, pairs, own, halves, rough):
    rows = levels.rows
    factor = 1 << levels.bits

    def kernel(own_in, one, two, *refs):
        ins = refs[: levels.bits]
        outs = refs[levels.bits :]
        for tile in range(2 * pairs):
            outs[0][tile, pl.ds(0, rows)] = own_in[tile]
            for index, half in enumerate((one, two)):
                outs[0][tile, pl.ds(rows + index * rows // 2, rows // 2)] = mean_rows(
                    half, (tile,), 0, rows // 2, factor
                )
            for step, _, row, _, _, place in levels.group_pieces():
                outs[0][tile, pl.ds(place, rows)] = ins[step][tile, pl.ds(row, rows)]
            for step in range(1, hi.bits):
                outs[step][tile] = mean_rows(
                    outs[step - 1], (tile,), 0, BLOCK >> step, 2
                )

    outs = [struct(2 * pairs, BLOCK >> step, LANES) for step in range(hi.bits)]
    return call(kernel, [own, *halves, *rough], outs)


def turn(pairs, mine, received):
    def kernel(own, got, turned):
        for tile in range(2 * pairs):
            both = jnp.concatenate([own[tile], got[tile]], axis=0).T
            turned[tile] = both * (SCALE * LOG2_E) if tile < pairs else both

    return call(kernel, [mine, received], [struct(2 * pairs, LANES, 2 * BLOCK)])[0]


def spread_group(levels, hi, pairs, group_grads, grads):
    own_rows = levels.rows

    def kernel(*refs):
        steps = refs[: hi.bits]
        ins = refs[hi.bits : hi.bits + levels.bits]
        own_out, *outs = refs[hi.bits + levels.bits : -1]
        total = refs[-1]
        for tile in range(2 * pairs):
            total[tile] = steps[0][tile, pl.ds(0, BLOCK)]
            for step in range(1, hi.bits):
                above = steps[step][tile, pl.ds(0, BLOCK >> step)]
                add_spread(total, (tile,), 0, above, 1 << step)
            own_out[tile] = total[tile, pl.ds(0, own_rows)]
            for out, value in zip(outs, ins):
                out[tile, pl.ds(0, value.shape[1])] = value[tile]
            outs[0][tile, pl.ds(ins[0].shape[1], own_rows)] = total[
                tile, pl.ds(own_rows, own_rows)
            ]
            for step, row, _, _, factor, place in levels.group_pieces():
                part = total[tile, pl.ds(place, own_rows)]
                add_spread(outs[step], (tile,), row, part, factor)

    shapes = [list(a.shape) for a in grads]
    shapes[0][1] += own_rows
    outs = [struct(2 * pairs, own_rows, LANES)] + [struct(*shape) for shape in shapes]
    own, *grads = call(
        kernel,
        [*group_grads, *grads],
        outs,
        scratch=[pltpu.VMEM((2 * pairs, BLOCK, LANES), F32)],
    )
    return own, grads


def spread_pair(lo, pairs, own_grad, returned, block_second):
    own_rows = BLOCK >> lo.bits

    def kernel(own, block, *refs):
        back = refs[: lo.bits]
        mine, theirs, *totals = refs[lo.bits :]
        last = pl.ds(back[0].shape[1] - own_rows, own_rows)
        for tile in range(2 * pairs):
            above = own[tile] + back[0][tile, last]
            for step in range(lo.bits - 1, 0, -1):
                total = totals[step - 1]
                total[tile] = back[step][tile, pl.ds(0, BLOCK >> step)]
                add_spread(total, (tile,), 0, above, 2)
                above = total[tile]
            mine[tile] = above[: BLOCK // 4]
            theirs[tile] = above[BLOCK // 4 :] + block[tile]

    return call(
        kernel,
        [own_grad, block_second, *returned],
        [struct(2 * pairs, BLOCK // 4, LANES)] * 2,
        scratch=[
            pltpu.VMEM((2 * pairs, BLOCK >> step, LANES), F32)
            for step in range(1, lo.bits)
        ],
    )


def unpack(pairs, kept, arrived, features, scalar):
    def kernel(bit, mine, theirs, *outs):
        for tile in range(2 * pairs):
            for side, array in ((bit[0], mine), (1 - bit[0], theirs)):
                column = side * (features // 2) + tile % pairs * LANES
                column = pl.ds(pl.multiple_of(column, LANES), LANES)
                outs[tile // pairs][:, column] = array[tile]

    return call(kernel, [kept, arrived], [struct(BLOCK, features)] * 2, scalar=scalar)


def finish(pairs, kept, rest, finest, seconds, features, scalar):
    def kernel(bit, kept_in, rest_in, f_mine, f_theirs, s_mine, s_theirs, *refs):
        outs, total, middle = refs[:2], refs[2], refs[3]
        for tile in range(2 * pairs):
            out = outs[tile // pairs]
            column = tile % pairs * LANES
            at = (tile,)
            total[tile] = kept_in[tile]
            add_spread(total, at, 0, f_mine[tile], 2)
            add_spread(total, at, 0, s_mine[tile], 4)
            place = bit[0] * (features // 2) + column
            out[:, pl.ds(pl.multiple_of(place, LANES), LANES)] = total[tile]
            put_pairs(middle, at, 0.5 * s_theirs[tile], 0.5 * rest_in[tile, :QUARTER])
            first = 0.5 * (middle[tile] + f_theirs[tile])
            put_pairs(total, at, first, 0.5 * rest_in[tile, QUARTER:])
            place = (1 - bit[0]) * (features // 2) + column
            out[:, pl.ds(pl.multiple_of(place, LANES), LANES)] = total[tile]

    return call(
        kernel,
        [kept, rest, *finest, *seconds],
        [struct(BLOCK, features)] * 2,
        scratch=[
            pltpu.VMEM((2 * pairs, BLOCK, LANES), F32),
            pltpu.VMEM((2 * pairs, HALF, LANES), F32),
        ],
        scalar=scalar,
    )


def on_device(queries, keys, values, cotangent):
    features = queries.shape[1]
    assert queries.shape[0] == BLOCK
    pairs = features // LANES // 2
    lo_bits = lax.axis_size("seqlo").bit_length() - 1
    levels = Levels(lo_bits - 1)
    lo = levels.whole
    hi_bits = lax.axis_size("seqhi").bit_length() - 1
    hi = Tree(lo_bits, [BLOCK >> step for step in range(hi_bits)])
    scalar = (lax.axis_index("seqlo") % 2).astype(jnp.int32).reshape(1)
    queries, keys, values, cotangent = [
        pltpu.with_memory_space_constraint(array, pltpu.HBM)
        for array in (queries, keys, values, cotangent)
    ]
    mine_kv, f_theirs, f_mine, c_send, c_mine, rest = pack_coarse(
        pairs, keys, values, scalar
    )
    second = exchange(c_send, 1)
    finest_theirs = exchange(f_theirs, 2)
    rest = exchange(rest, 1)
    half = exchange(ordered(finest_theirs, rest), 1)
    finest = exchange(ordered(f_mine, rest), 2)
    own_rough, own_fine = coarsen_pair(levels, pairs, c_mine, second)
    rough = levels.rough.gather([None] + [own_rough] * (levels.bits - 1))
    own_fine = ordered(own_fine, rough[-1])
    fine = levels.fine.gather([None, *own_fine])
    kv = rebuild(pairs, second, rest)
    send_qg, mine_qg = pack(pairs, queries, cotangent, scalar)
    qg = exchange(ordered(send_qg, rough[-1]), 1)
    group = coarsen_group(
        levels, hi, pairs, own_rough, [finest, half], rough
    )
    turned = turn(pairs, mine_qg, qg)
    rs = hi.gather(group, (turned, fine[0]))
    zs = rebuild_levels(levels, pairs, rough, fine)
    block_sets = [(0, 0, 0, BLOCK), (0, 1, 0, BLOCK)]
    lo_sets = [(1, 2, 0, BLOCK // 2), (1, 3, 0, BLOCK // 2)]
    for level in range(lo.bits):
        for step, row, rows in lo.held[level]:
            lo_sets.append((1 + level, 4 + step, row, rows))
    hi_sets = []
    for level in range(hi.bits):
        for step, row, rows in hi.held[level]:
            hi_sets.append((lo_bits + level, step, row, rows))
    first_in = [mine_kv, kv, finest, half, *zs]
    *kept, tops, sums, partial = attend_first(
        pairs, block_sets + lo_sets, first_in, turned
    )
    *rs_grads, o_keep, o_send, g_scaled, row_dot, dq = attend_last(
        pairs, hi_sets, rs, turned, tops, sums, partial
    )
    shapes = [(2 * pairs, *a.shape[1:]) for a in first_in]
    finest_grad, half_grad, *zs_grads, dq = attend_back(
        pairs,
        [(level, index - 2, row, rows) for level, index, row, rows in lo_sets],
        shapes[2:],
        BOTH,
        kept,
        turned,
        g_scaled,
        row_dot,
        dq,
        False,
    )
    kv_keep, kv_send, dq_keep, dq_send = attend_back(
        pairs, block_sets, shapes[:2], 0, kept, turned, g_scaled, row_dot, dq, True
    )
    og_keep = jnp.concatenate([o_keep, dq_keep], axis=0)
    og_send = jnp.concatenate([o_send, dq_send], axis=0)
    finest_mine = exchange(finest_grad, 2)
    half_back = exchange(half_grad, 1)
    block_second, rest_grad = take_apart(pairs, kv_send)
    rest_back = exchange(ordered(rest_grad, half_back), 1)
    og_back = exchange(ordered(og_send, half_back), 1)
    group_grads = hi.scatter(rs_grads)
    group_grads[-1] = ordered(group_grads[-1], (finest_mine, half_back, kv_send))
    own_grad, grads = spread_group(levels, hi, pairs, group_grads, zs_grads)
    returned = lo.scatter(grads)
    finest_theirs = exchange(ordered(half_back, returned[0]), 2)
    own_grad = ordered(own_grad, (rest_back, og_back))
    second_mine, second_send = spread_pair(lo, pairs, own_grad, returned, block_second)
    second_theirs = exchange(second_send, 1)
    attended, query_grad = unpack(pairs, og_keep, og_back, features, scalar)
    key_grad, value_grad = finish(
        pairs,
        kv_keep,
        rest_back,
        (finest_mine, finest_theirs),
        (second_mine, second_theirs),
        features,
        scalar,
    )
    return attended, query_grad, key_grad, value_grad


def solution(mesh):
    spec = P(AXES, None)
    return jax.shard_map(
        on_device,
        mesh=mesh,
        in_specs=(spec,) * 4,
        out_specs=(spec,) * 4,
        check_vma=False,
    )
```

```python
import math

import jax
import jax.numpy as jnp
from jax import lax
from jax.experimental import pallas as pl
from jax.experimental.pallas import tpu as pltpu
from jax.sharding import PartitionSpec as P

HEADS = 12
BLOCK = 128
HEAD_DIM = 64
LANES = 2 * HEAD_DIM
AXES = ("seqhi", "seqlo")
VMEM_LIMIT = 20 * 1024 * 1024
F32 = jnp.float32
BF16 = jnp.bfloat16
LOG2_E = 1.0 / math.log(2.0)
SCALE = 1.0 / math.sqrt(HEAD_DIM)


def struct(*shape):
    return jax.ShapeDtypeStruct(shape, F32)


def call(kernel, operands, outs, scratch=(), scalar=None, flops=0, exps=0, where=None):
    vmem = pl.BlockSpec(memory_space=pltpu.VMEM)
    smem = pl.BlockSpec(memory_space=pltpu.SMEM)
    in_specs = [pl.BlockSpec(memory_space=where) if where else vmem] * len(operands)
    if scalar is not None:
        operands = [scalar, *operands]
        in_specs = [smem, *in_specs]
    moved = sum(4 * math.prod(a.shape) for a in [*operands, *outs])
    return pl.pallas_call(
        kernel,
        out_shape=list(outs),
        in_specs=in_specs,
        out_specs=[vmem] * len(outs),
        scratch_shapes=list(scratch),
        compiler_params=pltpu.CompilerParams(vmem_limit_bytes=VMEM_LIMIT),
        cost_estimate=pl.CostEstimate(
            flops=flops, bytes_accessed=moved, transcendentals=exps
        ),
    )(*operands)


def exchange(value, offset):
    count = lax.axis_size(AXES)
    return lax.ppermute(value, AXES, [(i, i ^ offset) for i in range(count)])


def ordered(value, after):
    return value if after is None else lax.optimization_barrier((value, after))[0]


def half_difference(ref, lead, first, count):
    even = ref[(*lead, pl.ds(first, count, stride=2), slice(None))]
    odd = ref[(*lead, pl.ds(first + 1, count, stride=2), slice(None))]
    return 0.5 * (even - odd)


def put_pairs(ref, lead, total, difference):
    count = total.shape[0]
    ref[(*lead, pl.ds(0, count, stride=2), slice(None))] = total + difference
    ref[(*lead, pl.ds(1, count, stride=2), slice(None))] = total - difference


def mean_rows(ref, lead, first, count, factor):
    total = None
    for step in range(factor):
        rows = pl.ds(first + step, count, stride=factor)
        part = ref[(*lead, rows, slice(None))]
        total = part if total is None else total + part
    return total * (1.0 / factor)


def add_spread(ref, lead, first, value, factor):
    count = value.shape[0]
    value = value * (1.0 / factor)
    for step in range(factor):
        rows = pl.ds(first + step, count, stride=factor)
        place = (*lead, rows, slice(None))
        ref[place] = ref[place] + value


class Tree:
    def __init__(self, bits, first_bit, lowest=True):
        self.bits = bits
        self.first_bit = first_bit
        self.own_rows = [BLOCK >> step for step in range(bits)]
        if not lowest:
            self.own_rows[0] = 0
        self.held = {}
        self.payload = {}
        for step in range(bits - 1, -1, -1):
            rows = self.own_rows[step]
            payload = []
            fresh = {step: [(step, 0, rows)] if rows else []}
            for level in range(step + 1, bits):
                for piece in self.held[level]:
                    payload.append(piece)
                    fresh.setdefault(level, []).append((step, rows, piece[2]))
                    rows += piece[2]
            self.payload[step] = payload
            for level, pieces in fresh.items():
                self.held[level] = self.held.get(level, []) + pieces

    def partner(self, value, step):
        return exchange(value, 1 << self.first_bit + step)

    def gather(self, own, after=None):
        arrived = [None] * self.bits
        for step in range(self.bits - 1, -1, -1):
            parts = [own[step]] if self.own_rows[step] else []
            for source, row, rows in self.payload[step]:
                part = arrived[source]
                whole = rows == part.shape[1]
                parts.append(part if whole else part[:, row : row + rows])
            sent = jnp.concatenate(parts, axis=1) if len(parts) > 1 else parts[0]
            if step == 0:
                sent = ordered(sent, after)
            arrived[step] = self.partner(sent, step)
        return arrived

    def scatter(self, grads):
        grads = list(grads)
        returned = []
        for step in range(self.bits):
            back = self.partner(grads[step], step)
            returned.append(back)
            filled = self.own_rows[step]
            for source, row, rows in self.payload[step]:
                part = back[:, filled : filled + rows]
                grads[source] = grads[source].at[:, row : row + rows].add(part)
                filled += rows
        return returned


def split(value):
    high = value.astype(BF16).astype(F32)
    return high, value - high


def halves_by_head(value):
    high, low = split(value)
    first = lax.broadcasted_iota(jnp.int32, value.shape, 1) < HEAD_DIM
    one = jnp.where(first, high, pltpu.roll(low, HEAD_DIM, 1))
    two = jnp.where(first, pltpu.roll(high, HEAD_DIM, 1), low)
    return one, two


def dot(lhs, rhs, dims):
    return lax.dot_general(lhs, rhs, (dims, ((), ())), preferred_element_type=F32)


NN = ((1,), (0,))
NT = ((1,), (1,))


BOTH = 2 * BLOCK
GROUP = 3


def halves_of(sets, ins, which, pairs, pair):
    tile = which * pairs + pair
    parts = [ins[index][tile, pl.ds(row, rows), :] for _, index, row, rows in sets]
    return halves_by_head(jnp.concatenate(parts, axis=0))


def segment_levels(sets):
    levels, filled = [], 0
    for level, _, _, rows in sets:
        if filled % BLOCK == 0:
            levels.append(level)
        filled += rows
    return levels


def four_rows(value):
    high, low = split(value)
    four = jnp.concatenate([high, high, low, low], axis=0).astype(BF16)
    return four, jnp.concatenate([high, low], axis=0).astype(BF16)


def store_split(ref, lead, rows, value):
    high = value.astype(BF16)
    ref[(lead, 0, rows)] = high
    ref[(lead, 1, rows)] = (value - high.astype(F32)).astype(BF16)


def fold_rows(value):
    return value[:HEAD_DIM] + value[HEAD_DIM:]


def fold_heads(one, two):
    first = lax.broadcasted_iota(jnp.int32, one.shape, 1) < HEAD_DIM
    return jnp.where(
        first, one + pltpu.roll(one, HEAD_DIM, 1), two + pltpu.roll(two, HEAD_DIM, 1)
    )


def twice(value):
    return jnp.concatenate([value, value], axis=1)


def stacked(ref, at, rows=slice(None)):
    return jnp.concatenate([ref[at, 0, rows], ref[at, 1, rows]], axis=0)


def abreast(ref, at, rows=slice(None)):
    return jnp.concatenate([ref[at, 0, rows], ref[at, 1, rows]], axis=1)


def column_scores(levels, keys, at, q_four, s_ref):
    highest = None
    for index, level in enumerate(levels):
        rows = pl.ds(index * BLOCK, BLOCK)
        s = dot(twice(keys[at, rows]), q_four, NN)
        s = s + float(level) if level else s
        s_ref[at, rows] = s
        top = jnp.max(s.reshape(BLOCK // 8, 8, BOTH), axis=0)
        highest = top if highest is None else jnp.maximum(highest, top)
    return jnp.max(highest, axis=0, keepdims=True)


def exponents(levels, at, top, s_ref, e_ref, keep):
    summed = None
    for index in range(len(levels)):
        rows = pl.ds(index * BLOCK, BLOCK)
        e = jnp.exp2(s_ref[at, rows] - top)
        if keep:
            s_ref[at, rows] = e
        store_split(e_ref, at, rows, e)
        part = jnp.sum(e.reshape(BLOCK // 8, 8, BOTH), axis=0)
        summed = part if summed is None else summed + part
    return jnp.sum(summed, axis=0, keepdims=True)


def head_rows(ref, pair, head):
    return ref[pair, pl.ds(head * HEAD_DIM, HEAD_DIM)]


def each_group(pairs, body):
    for first in range(0, pairs, GROUP):
        group = range(first, min(first + GROUP, pairs))
        body(group, [(pair, head, 2 * pair + head) for pair in group for head in (0, 1)])


def costs(pairs, rows, products, exps=0):
    return dict(
        flops=2 * 4 * products * pairs * 2 * rows * BOTH * HEAD_DIM,
        exps=exps * pairs * 2 * rows * BOTH,
    )


def put_halves(pairs, sets, ins, group, plain, turned):
    for which in range(2):
        for pair in group:
            for head, value in enumerate(halves_of(sets, ins, which, pairs, pair)):
                plain[which][2 * pair + head] = value.astype(BF16)
                turned[which][2 * pair + head] = value.T.astype(BF16)


def attend_first(pairs, sets, operands, turned):
    total = sum(s[3] for s in sets)
    levels = segment_levels(sets)

    def kernel(turn_in, *refs):
        ins = refs[: len(operands)]
        kt, vc, e_ref, tops, sums, out, s_ref, kc, vt = refs[len(operands) :]

        def body(group, heads):
            put_halves(pairs, sets, ins, group, (kc, vc), (kt, vt))
            for pair, head, at in heads:
                q_four, _ = four_rows(head_rows(turn_in, pair, head))
                tops[at] = column_scores(levels, kc, at, q_four, s_ref)
            for _, _, at in heads:
                sums[at] = exponents(levels, at, tops[at], s_ref, e_ref, False)
            for _, _, at in heads:
                out[at] = fold_rows(dot(twice(vt[at]), stacked(e_ref, at), NN))

        each_group(pairs, body)

    heads = 2 * pairs
    outs = [
        jax.ShapeDtypeStruct((heads, LANES, total), BF16),
        jax.ShapeDtypeStruct((heads, total, LANES), BF16),
        jax.ShapeDtypeStruct((heads, 2, total, BOTH), BF16),
    ]
    outs += [struct(heads, 1, BOTH)] * 2 + [struct(heads, HEAD_DIM, BOTH)]
    return call(
        kernel,
        [turned, *operands],
        outs,
        scratch=[
            pltpu.VMEM((heads, total, BOTH), F32),
            pltpu.VMEM((heads, total, LANES), BF16),
            pltpu.VMEM((heads, LANES, total), BF16),
        ],
        **costs(pairs, total, 2, 1),
    )


def attend_last(pairs, sets, operands, turned, tops, sums, partial):
    total = sum(s[3] for s in sets)
    levels = segment_levels(sets)

    def kernel(turn_in, top_in, sum_in, part_in, *refs):
        ins = refs[: len(operands)]
        grads = refs[len(operands) : 2 * len(operands)]
        o_keep, o_send, g_out, r_out, dq_out = refs[2 * len(operands) : -7]
        s_ref, e_ref, d_ref, kc, vc, kt, vt = refs[-7:]

        def body(group, heads):
            put_halves(pairs, sets, ins, group, (kc, vc), (kt, vt))
            queries = {}
            top = {}
            for pair, head, at in heads:
                q_four, queries[at] = four_rows(head_rows(turn_in, pair, head))
                top[at] = column_scores(levels, kc, at, q_four, s_ref)
            inverse = {}
            rescale = {}
            for _, _, at in heads:
                first_top = top_in[at]
                highest = jnp.maximum(top[at], first_top)
                rescale[at] = jnp.exp2(first_top - highest)
                summed = exponents(levels, at, highest, s_ref, e_ref, True)
                inverse[at] = 1.0 / (summed + sum_in[at] * rescale[at])
            output = {}
            cotangents = {}
            row_dot = {}
            for pair, head, at in heads:
                o = fold_rows(dot(twice(vt[at]), stacked(e_ref, at), NN))
                o = (o + part_in[at] * rescale[at]) * inverse[at]
                output[at] = o
                scaled = head_rows(turn_in, pairs + pair, head) * inverse[at]
                cotangents[at] = four_rows(scaled)
                row_dot[at] = jnp.sum(o * scaled, axis=0, keepdims=True)
                g_out[at] = scaled * rescale[at]
                r_out[at] = row_dot[at] * rescale[at]
            for _, _, at in heads:
                for index in range(len(levels)):
                    rows = pl.ds(index * BLOCK, BLOCK)
                    dp = dot(twice(vc[at, rows]), cotangents[at][0], NN)
                    store_split(d_ref, at, rows, s_ref[at, rows] * (dp - row_dot[at]))
            key_grads = {}
            value_grads = {}
            for _, _, at in heads:
                value_grads[at] = dot(abreast(e_ref, at), twice(cotangents[at][1]), NT)
                key_grads[at] = dot(abreast(d_ref, at), twice(queries[at]), NT)
                dq_out[at] = fold_rows(dot(twice(kt[at]), stacked(d_ref, at), NN))
            for pair in group:
                put_grads(pairs, pair, sets, grads, key_grads, value_grads)
                both = [output[2 * pair], output[2 * pair + 1]]
                both = jnp.concatenate(both, axis=0).T
                o_keep[pair] = both[:BLOCK]
                o_send[pair] = both[BLOCK:]

        each_group(pairs, body)

    heads = 2 * pairs
    outs = [struct(*a.shape) for a in operands]
    outs += [struct(pairs, BLOCK, LANES)] * 2
    outs += [struct(heads, HEAD_DIM, BOTH), struct(heads, 1, BOTH)]
    outs.append(struct(heads, HEAD_DIM, BOTH))
    return call(
        kernel,
        [turned, tops, sums, partial, *operands],
        outs,
        scratch=[pltpu.VMEM((heads, total, BOTH), F32)]
        + [pltpu.VMEM((heads, 2, total, BOTH), BF16)] * 2
        + [pltpu.VMEM((heads, total, LANES), BF16)] * 2
        + [pltpu.VMEM((heads, LANES, total), BF16)] * 2,
        **costs(pairs, total, 6, 1),
    )


def put_grads(pairs, pair, sets, grads, key_grads, value_grads):
    for which, parts in enumerate((key_grads, value_grads)):
        both = fold_heads(parts[2 * pair], parts[2 * pair + 1])
        if which == 0:
            both = both * (1.0 / LOG2_E)
        filled = 0
        for _, index, row, rows in sets:
            piece = both[filled : filled + rows]
            grads[index][which * pairs + pair, pl.ds(row, rows), :] = piece
            filled += rows


def attend_back(pairs, sets, shapes, first, kept, turned, g_scaled, row_dot, dq, last):
    total = sum(s[3] for s in sets)
    segments = total // BLOCK

    def kernel(turn_in, kt, vc, e_ref, g_in, r_in, dq_in, *refs):
        grads = refs[: len(shapes)]
        dq_out = refs[len(shapes) : -1]
        d_ref = refs[-1]
        span = pl.ds(first, total)

        def body(group, heads):
            cotangents = {}
            for _, _, at in heads:
                g_four, cotangents[at] = four_rows(g_in[at])
                for index in range(segments):
                    rows = pl.ds(first + index * BLOCK, BLOCK)
                    dp = dot(twice(vc[at, rows]), g_four, NN)
                    e = e_ref[at, 0, rows].astype(F32) + e_ref[at, 1, rows].astype(F32)
                    place = pl.ds(index * BLOCK, BLOCK)
                    store_split(d_ref, at, place, e * (dp - r_in[at]))
            queries_grad = {}
            key_grads = {}
            value_grads = {}
            for pair, head, at in heads:
                _, q_rows = four_rows(head_rows(turn_in, pair, head))
                g_rows = cotangents[at]
                value_grads[at] = dot(abreast(e_ref, at, span), twice(g_rows), NT)
                key_grads[at] = dot(abreast(d_ref, at), twice(q_rows), NT)
                part = dot(twice(kt[at, :, span]), stacked(d_ref, at), NN)
                queries_grad[at] = fold_rows(part) + dq_in[at]
            for pair in group:
                put_grads(pairs, pair, sets, grads, key_grads, value_grads)
                both = [queries_grad[2 * pair], queries_grad[2 * pair + 1]]
                if last:
                    both = jnp.concatenate(both, axis=0).T * SCALE
                    dq_out[0][pair] = both[:BLOCK]
                    dq_out[1][pair] = both[BLOCK:]
                else:
                    for head in range(2):
                        dq_out[0][2 * pair + head] = both[head]

        each_group(pairs, body)

    outs = [struct(*shape) for shape in shapes]
    if last:
        outs += [struct(pairs, BLOCK, LANES)] * 2
    else:
        outs.append(struct(*dq.shape))
    return call(
        kernel,
        [turned, *kept, g_scaled, row_dot, dq],
        outs,
        scratch=[pltpu.VMEM((2 * pairs, 2, total, BOTH), BF16)],
        **costs(pairs, total, 4),
    )


def copy_columns(moves, ins, sems, bit):
    started = []
    for operand, theirs, column, place in moves:
        side = 1 - bit if theirs else bit
        column = side * (ins[operand].shape[1] // 2) + column
        column = pl.ds(pl.multiple_of(column, LANES), LANES)
        copy = pltpu.make_async_copy(
            ins[operand].at[:, column], place, sems.at[len(started)]
        )
        copy.start()
        started.append(copy)
    return started


def pack(pairs, first, second, scalar):
    def kernel(bit, one, two, theirs, mine, sems):
        moves = []
        for tile in range(2 * pairs):
            for out, other in ((theirs, True), (mine, False)):
                column = tile % pairs * LANES
                moves.append((tile // pairs, other, column, out.at[tile]))
        for copy in copy_columns(moves, (one, two), sems, bit[0]):
            copy.wait()

    return call(
        kernel,
        [first, second],
        [struct(2 * pairs, BLOCK, LANES)] * 2,
        scratch=[pltpu.SemaphoreType.DMA((4 * pairs,))],
        scalar=scalar,
        where=pl.ANY,
    )


QUARTER = BLOCK // 4
HALF = BLOCK // 2


def pack_coarse(pairs, keys, values, scalar):
    def kernel(bit, k, v, mine, f_theirs, f_mine, c_theirs, c_mine, rest, theirs, sems):
        moves = []
        for out, other in ((theirs, True), (mine, False)):
            for tile in range(2 * pairs):
                column = tile % pairs * LANES
                moves.append((tile // pairs, other, column, out.at[tile]))
        copies = copy_columns(moves, (k, v), sems, bit[0])
        for index, copy in enumerate(copies):
            copy.wait()
            tile = index % (2 * pairs)
            other = index < 2 * pairs
            source, finest, coarse = (
                (theirs, f_theirs, c_theirs) if other else (mine, f_mine, c_mine)
            )
            finest[tile] = mean_rows(source, (tile,), 0, HALF, 2)
            coarse[tile] = mean_rows(finest, (tile,), 0, QUARTER, 2)
            if other:
                rest[tile, :QUARTER] = half_difference(finest, (tile,), 0, QUARTER)
                rest[tile, QUARTER:] = half_difference(source, (tile,), 0, HALF)

    return call(
        kernel,
        [keys, values],
        [struct(2 * pairs, BLOCK, LANES)]
        + [struct(2 * pairs, HALF, LANES)] * 2
        + [struct(2 * pairs, QUARTER, LANES)] * 2
        + [struct(2 * pairs, QUARTER + HALF, LANES)],
        scratch=[
            pltpu.VMEM((2 * pairs, BLOCK, LANES), F32),
            pltpu.SemaphoreType.DMA((4 * pairs,)),
        ],
        scalar=scalar,
        where=pl.ANY,
    )


def rebuild(pairs, second, rest):
    def kernel(second_in, rest_in, out, finest):
        for tile in range(2 * pairs):
            put_pairs(finest, (tile,), second_in[tile], rest_in[tile, :QUARTER])
            put_pairs(out, (tile,), finest[tile], rest_in[tile, QUARTER:])

    return call(
        kernel,
        [second, rest],
        [struct(2 * pairs, BLOCK, LANES)],
        scratch=[pltpu.VMEM((2 * pairs, HALF, LANES), F32)],
    )[0]


def take_apart(pairs, block_grad):
    def kernel(block, second, rest, finest):
        for tile in range(2 * pairs):
            finest[tile] = 2.0 * mean_rows(block, (tile,), 0, HALF, 2)
            rest[tile, QUARTER:] = 2.0 * half_difference(block, (tile,), 0, HALF)
            second[tile] = 2.0 * mean_rows(finest, (tile,), 0, QUARTER, 2)
            rest[tile, :QUARTER] = 2.0 * half_difference(finest, (tile,), 0, QUARTER)

    return call(
        kernel,
        [block_grad],
        [
            struct(2 * pairs, QUARTER, LANES),
            struct(2 * pairs, QUARTER + HALF, LANES),
        ],
        scratch=[pltpu.VMEM((2 * pairs, HALF, LANES), F32)],
    )


def coarsen_pair(lo, pairs, mine, received):
    def kernel(own, got, *outs):
        for tile in range(2 * pairs):
            outs[0][tile, : BLOCK // 4] = own[tile]
            outs[0][tile, BLOCK // 4 :] = got[tile]
            for index in range(1, lo.bits):
                outs[index][tile] = mean_rows(
                    outs[index - 1], (tile,), 0, BLOCK >> index + 1, 2
                )

    outs = [struct(2 * pairs, BLOCK >> step, LANES) for step in range(1, lo.bits + 1)]
    return call(kernel, [mine, received], outs)


def group_pieces(lo):
    own = BLOCK >> lo.bits
    factor = 1 << lo.bits
    pieces = [
        (-2, 0, BLOCK // 2, factor, own),
        (-1, 0, BLOCK // 2, factor, own + own // 2),
    ]
    filled = 2 * own
    for level in range(1, lo.bits):
        factor = 1 << lo.bits - level
        for step, row, rows in lo.held[level]:
            pieces.append((step, row, rows, factor, filled))
            filled += rows // factor
    return pieces


def coarsen_group(lo, hi, pairs, own, halves, arrived):
    pieces = group_pieces(lo)

    def kernel(own_in, *refs):
        ins = refs[: 2 + lo.bits]
        outs = refs[2 + lo.bits :]
        for tile in range(2 * pairs):
            outs[0][tile, pl.ds(0, BLOCK >> lo.bits)] = own_in[tile]
            for step, row, rows, factor, place in pieces:
                count = rows // factor
                outs[0][tile, pl.ds(place, count)] = mean_rows(
                    ins[2 + step], (tile,), row, count, factor
                )
            for step in range(1, hi.bits):
                outs[step][tile] = mean_rows(
                    outs[step - 1], (tile,), 0, BLOCK >> step, 2
                )

    outs = [struct(2 * pairs, BLOCK >> step, LANES) for step in range(hi.bits)]
    return call(kernel, [own, *halves, *arrived], outs)


def turn(pairs, mine, received):
    def kernel(own, got, turned):
        for tile in range(2 * pairs):
            both = jnp.concatenate([own[tile], got[tile]], axis=0).T
            turned[tile] = both * (SCALE * LOG2_E) if tile < pairs else both

    return call(kernel, [mine, received], [struct(2 * pairs, LANES, 2 * BLOCK)])[0]


def spread_group(lo, hi, pairs, group_grads, grads):
    pieces = group_pieces(lo)
    own_rows = BLOCK >> lo.bits

    def kernel(*refs):
        steps = refs[: hi.bits]
        ins = refs[hi.bits : hi.bits + lo.bits]
        own_out, *outs = refs[hi.bits + lo.bits : -1]
        total = refs[-1]
        for tile in range(2 * pairs):
            total[tile] = steps[0][tile, pl.ds(0, BLOCK)]
            for step in range(1, hi.bits):
                above = steps[step][tile, pl.ds(0, BLOCK >> step)]
                add_spread(total, (tile,), 0, above, 1 << step)
            own_out[tile] = total[tile, pl.ds(0, own_rows)]
            for out, value in zip(outs, ins):
                out[tile, pl.ds(0, value.shape[1])] = value[tile]
            outs[0][tile, pl.ds(ins[0].shape[1], own_rows)] = total[
                tile, pl.ds(own_rows, own_rows)
            ]
            for step, row, rows, factor, place in pieces:
                if step >= 0:
                    part = total[tile, pl.ds(place, rows // factor)]
                    add_spread(outs[step], (tile,), row, part, factor)

    shapes = [list(a.shape) for a in grads]
    shapes[0][1] += own_rows
    outs = [struct(2 * pairs, own_rows, LANES)] + [struct(*shape) for shape in shapes]
    own, *grads = call(
        kernel,
        [*group_grads, *grads],
        outs,
        scratch=[pltpu.VMEM((2 * pairs, BLOCK, LANES), F32)],
    )
    return own, grads


def spread_pair(lo, pairs, own_grad, returned, block_second):
    own_rows = BLOCK >> lo.bits

    def kernel(own, block, *refs):
        back = refs[: lo.bits]
        mine, theirs, *totals = refs[lo.bits :]
        last = pl.ds(back[0].shape[1] - own_rows, own_rows)
        for tile in range(2 * pairs):
            above = own[tile] + back[0][tile, last]
            for step in range(lo.bits - 1, 0, -1):
                total = totals[step - 1]
                total[tile] = back[step][tile, pl.ds(0, BLOCK >> step)]
                add_spread(total, (tile,), 0, above, 2)
                above = total[tile]
            mine[tile] = above[: BLOCK // 4]
            theirs[tile] = above[BLOCK // 4 :] + block[tile]

    return call(
        kernel,
        [own_grad, block_second, *returned],
        [struct(2 * pairs, BLOCK // 4, LANES)] * 2,
        scratch=[
            pltpu.VMEM((2 * pairs, BLOCK >> step, LANES), F32)
            for step in range(1, lo.bits)
        ],
    )


def unpack(pairs, kept, arrived, features, scalar):
    def kernel(bit, mine, theirs, *outs):
        for tile in range(2 * pairs):
            for side, array in ((bit[0], mine), (1 - bit[0], theirs)):
                column = side * (features // 2) + tile % pairs * LANES
                column = pl.ds(pl.multiple_of(column, LANES), LANES)
                outs[tile // pairs][:, column] = array[tile]

    return call(kernel, [kept, arrived], [struct(BLOCK, features)] * 2, scalar=scalar)


def finish(pairs, kept, rest, finest, seconds, features, scalar):
    def kernel(bit, kept_in, rest_in, f_mine, f_theirs, s_mine, s_theirs, *refs):
        outs, total, middle = refs[:2], refs[2], refs[3]
        for tile in range(2 * pairs):
            out = outs[tile // pairs]
            column = tile % pairs * LANES
            at = (tile,)
            total[tile] = kept_in[tile]
            add_spread(total, at, 0, f_mine[tile], 2)
            add_spread(total, at, 0, s_mine[tile], 4)
            place = bit[0] * (features // 2) + column
            out[:, pl.ds(pl.multiple_of(place, LANES), LANES)] = total[tile]
            put_pairs(middle, at, 0.5 * s_theirs[tile], 0.5 * rest_in[tile, :QUARTER])
            first = 0.5 * (middle[tile] + f_theirs[tile])
            put_pairs(total, at, first, 0.5 * rest_in[tile, QUARTER:])
            place = (1 - bit[0]) * (features // 2) + column
            out[:, pl.ds(pl.multiple_of(place, LANES), LANES)] = total[tile]

    return call(
        kernel,
        [kept, rest, *finest, *seconds],
        [struct(BLOCK, features)] * 2,
        scratch=[
            pltpu.VMEM((2 * pairs, BLOCK, LANES), F32),
            pltpu.VMEM((2 * pairs, HALF, LANES), F32),
        ],
        scalar=scalar,
    )


def on_device(queries, keys, values, cotangent):
    features = queries.shape[1]
    assert queries.shape[0] == BLOCK
    pairs = features // LANES // 2
    lo_bits = lax.axis_size("seqlo").bit_length() - 1
    lo = Tree(lo_bits - 1, 1, lowest=False)
    hi = Tree(lax.axis_size("seqhi").bit_length() - 1, lo_bits)
    scalar = (lax.axis_index("seqlo") % 2).astype(jnp.int32).reshape(1)
    queries, keys, values, cotangent = [
        pltpu.with_memory_space_constraint(array, pltpu.HBM)
        for array in (queries, keys, values, cotangent)
    ]
    mine_kv, f_theirs, f_mine, c_send, c_mine, rest = pack_coarse(
        pairs, keys, values, scalar
    )
    second = exchange(c_send, 1)
    finest_theirs = exchange(f_theirs, 2)
    coarse = coarsen_pair(lo, pairs, c_mine, second)
    finest = exchange(ordered(f_mine, finest_theirs), 2)
    rest = exchange(ordered(rest, coarse[0]), 1)
    half = exchange(ordered(finest_theirs, rest), 1)
    kv = rebuild(pairs, second, rest)
    send_qg, mine_qg = pack(pairs, queries, cotangent, scalar)
    qg = exchange(ordered(send_qg, half), 1)
    zs = lo.gather([None, *coarse], finest)
    group = coarsen_group(
        lo, hi, pairs, ordered(coarse[-1], rest), [finest, half], zs
    )
    turned = turn(pairs, mine_qg, qg)
    rs = hi.gather(group, turned)
    block_sets = [(0, 0, 0, BLOCK), (0, 1, 0, BLOCK)]
    lo_sets = [(1, 2, 0, BLOCK // 2), (1, 3, 0, BLOCK // 2)]
    for level in range(lo.bits):
        for step, row, rows in lo.held[level]:
            lo_sets.append((1 + level, 4 + step, row, rows))
    hi_sets = []
    for level in range(hi.bits):
        for step, row, rows in hi.held[level]:
            hi_sets.append((lo_bits + level, step, row, rows))
    first_in = [mine_kv, kv, finest, half, *zs]
    *kept, tops, sums, partial = attend_first(
        pairs, block_sets + lo_sets, first_in, turned
    )
    *rs_grads, o_keep, o_send, g_scaled, row_dot, dq = attend_last(
        pairs, hi_sets, rs, turned, tops, sums, partial
    )
    shapes = [(2 * pairs, *a.shape[1:]) for a in first_in]
    finest_grad, half_grad, *zs_grads, dq = attend_back(
        pairs,
        [(level, index - 2, row, rows) for level, index, row, rows in lo_sets],
        shapes[2:],
        BOTH,
        kept,
        turned,
        g_scaled,
        row_dot,
        dq,
        False,
    )
    kv_keep, kv_send, dq_keep, dq_send = attend_back(
        pairs, block_sets, shapes[:2], 0, kept, turned, g_scaled, row_dot, dq, True
    )
    og_keep = jnp.concatenate([o_keep, dq_keep], axis=0)
    og_send = jnp.concatenate([o_send, dq_send], axis=0)
    finest_mine = exchange(finest_grad, 2)
    half_back = exchange(half_grad, 1)
    block_second, rest_grad = take_apart(pairs, kv_send)
    rest_back = exchange(ordered(rest_grad, half_back), 1)
    og_back = exchange(ordered(og_send, half_back), 1)
    group_grads = hi.scatter(rs_grads)
    group_grads[-1] = ordered(group_grads[-1], (finest_mine, half_back, kv_send))
    own_grad, grads = spread_group(lo, hi, pairs, group_grads, zs_grads)
    returned = lo.scatter(grads)
    finest_theirs = exchange(ordered(half_back, returned[0]), 2)
    own_grad = ordered(own_grad, (rest_back, og_back))
    second_mine, second_send = spread_pair(lo, pairs, own_grad, returned, block_second)
    second_theirs = exchange(second_send, 1)
    attended, query_grad = unpack(pairs, og_keep, og_back, features, scalar)
    key_grad, value_grad = finish(
        pairs,
        kv_keep,
        rest_back,
        (finest_mine, finest_theirs),
        (second_mine, second_theirs),
        features,
        scalar,
    )
    return attended, query_grad, key_grad, value_grad


def solution(mesh):
    spec = P(AXES, None)
    return jax.shard_map(
        on_device,
        mesh=mesh,
        in_specs=(spec,) * 4,
        out_specs=(spec,) * 4,
        check_vma=False,
    )
```

```python
import math

import jax
import jax.numpy as jnp
from jax import lax
from jax.experimental import pallas as pl
from jax.experimental.pallas import tpu as pltpu
from jax.sharding import PartitionSpec as P

HEADS = 12
BLOCK = 128
HEAD_DIM = 64
LANES = 2 * HEAD_DIM
AXES = ("seqhi", "seqlo")
VMEM_LIMIT = 20 * 1024 * 1024
F32 = jnp.float32
BF16 = jnp.bfloat16
LOG2_E = 1.0 / math.log(2.0)
SCALE = 1.0 / math.sqrt(HEAD_DIM)


def struct(*shape):
    return jax.ShapeDtypeStruct(shape, F32)


def call(kernel, operands, outs, scratch=(), scalar=None, flops=0, exps=0, where=None):
    vmem = pl.BlockSpec(memory_space=pltpu.VMEM)
    smem = pl.BlockSpec(memory_space=pltpu.SMEM)
    in_specs = [pl.BlockSpec(memory_space=where) if where else vmem] * len(operands)
    if scalar is not None:
        operands = [scalar, *operands]
        in_specs = [smem, *in_specs]
    moved = sum(4 * math.prod(a.shape) for a in [*operands, *outs])
    return pl.pallas_call(
        kernel,
        out_shape=list(outs),
        in_specs=in_specs,
        out_specs=[vmem] * len(outs),
        scratch_shapes=list(scratch),
        compiler_params=pltpu.CompilerParams(vmem_limit_bytes=VMEM_LIMIT),
        cost_estimate=pl.CostEstimate(
            flops=flops, bytes_accessed=moved, transcendentals=exps
        ),
    )(*operands)


def exchange(value, offset):
    count = lax.axis_size(AXES)
    return lax.ppermute(value, AXES, [(i, i ^ offset) for i in range(count)])


def ordered(value, after):
    return value if after is None else lax.optimization_barrier((value, after))[0]


def half_difference(ref, lead, first, count):
    even = ref[(*lead, pl.ds(first, count, stride=2), slice(None))]
    odd = ref[(*lead, pl.ds(first + 1, count, stride=2), slice(None))]
    return 0.5 * (even - odd)


def put_pairs(ref, lead, total, difference):
    count = total.shape[0]
    ref[(*lead, pl.ds(0, count, stride=2), slice(None))] = total + difference
    ref[(*lead, pl.ds(1, count, stride=2), slice(None))] = total - difference


def mean_rows(ref, lead, first, count, factor):
    total = None
    for step in range(factor):
        rows = pl.ds(first + step, count, stride=factor)
        part = ref[(*lead, rows, slice(None))]
        total = part if total is None else total + part
    return total * (1.0 / factor)


def add_spread(ref, lead, first, value, factor):
    count = value.shape[0]
    value = value * (1.0 / factor)
    for step in range(factor):
        rows = pl.ds(first + step, count, stride=factor)
        place = (*lead, rows, slice(None))
        ref[place] = ref[place] + value


class Tree:
    def __init__(self, first_bit, own_rows):
        self.bits = bits = len(own_rows)
        self.first_bit = first_bit
        self.own_rows = own_rows
        self.held = {}
        self.payload = {}
        for step in range(bits - 1, -1, -1):
            rows = self.own_rows[step]
            payload = []
            fresh = {step: [(step, 0, rows)] if rows else []}
            for level in range(step + 1, bits):
                for piece in self.held[level]:
                    payload.append(piece)
                    fresh.setdefault(level, []).append((step, rows, piece[2]))
                    rows += piece[2]
            self.payload[step] = payload
            for level, pieces in fresh.items():
                self.held[level] = self.held.get(level, []) + pieces

    def rows(self, step):
        return self.own_rows[step] + sum(piece[2] for piece in self.payload[step])

    def partner(self, value, step):
        return exchange(value, 1 << self.first_bit + step)

    def gather(self, own, after=None):
        arrived = [None] * self.bits
        for step in range(self.bits - 1, -1, -1):
            parts = [own[step]] if self.own_rows[step] else []
            for source, row, rows in self.payload[step]:
                part = arrived[source]
                whole = rows == part.shape[1]
                parts.append(part if whole else part[:, row : row + rows])
            sent = jnp.concatenate(parts, axis=1) if len(parts) > 1 else parts[0]
            if step == 0:
                sent = ordered(sent, after)
            arrived[step] = self.partner(sent, step)
        return arrived

    def scatter(self, grads):
        grads = list(grads)
        returned = []
        for step in range(self.bits):
            back = self.partner(grads[step], step)
            returned.append(back)
            filled = self.own_rows[step]
            for source, row, rows in self.payload[step]:
                part = back[:, filled : filled + rows]
                grads[source] = grads[source].at[:, row : row + rows].add(part)
                filled += rows
        return returned


def split(value):
    high = value.astype(BF16).astype(F32)
    return high, value - high


def halves_by_head(value):
    high, low = split(value)
    first = lax.broadcasted_iota(jnp.int32, value.shape, 1) < HEAD_DIM
    one = jnp.where(first, high, pltpu.roll(low, HEAD_DIM, 1))
    two = jnp.where(first, pltpu.roll(high, HEAD_DIM, 1), low)
    return one, two


def dot(lhs, rhs, dims):
    return lax.dot_general(lhs, rhs, (dims, ((), ())), preferred_element_type=F32)


NN = ((1,), (0,))
NT = ((1,), (1,))


BOTH = 2 * BLOCK
GROUP = 3


def halves_of(sets, ins, which, pairs, pair):
    tile = which * pairs + pair
    parts = [ins[index][tile, pl.ds(row, rows), :] for _, index, row, rows in sets]
    return halves_by_head(jnp.concatenate(parts, axis=0))


def segment_levels(sets):
    levels, filled = [], 0
    for level, _, _, rows in sets:
        if filled % BLOCK == 0:
            levels.append(level)
        filled += rows
    return levels


def four_rows(value):
    high, low = split(value)
    four = jnp.concatenate([high, high, low, low], axis=0).astype(BF16)
    return four, jnp.concatenate([high, low], axis=0).astype(BF16)


def store_split(ref, lead, rows, value):
    high = value.astype(BF16)
    ref[(lead, 0, rows)] = high
    ref[(lead, 1, rows)] = (value - high.astype(F32)).astype(BF16)


def fold_rows(value):
    return value[:HEAD_DIM] + value[HEAD_DIM:]


def fold_heads(one, two):
    first = lax.broadcasted_iota(jnp.int32, one.shape, 1) < HEAD_DIM
    return jnp.where(
        first, one + pltpu.roll(one, HEAD_DIM, 1), two + pltpu.roll(two, HEAD_DIM, 1)
    )


def twice(value):
    return jnp.concatenate([value, value], axis=1)


def stacked(ref, at, rows=slice(None)):
    return jnp.concatenate([ref[at, 0, rows], ref[at, 1, rows]], axis=0)


def abreast(ref, at, rows=slice(None)):
    return jnp.concatenate([ref[at, 0, rows], ref[at, 1, rows]], axis=1)


def column_scores(levels, keys, at, q_four, s_ref):
    highest = None
    for index, level in enumerate(levels):
        rows = pl.ds(index * BLOCK, BLOCK)
        s = dot(twice(keys[at, rows]), q_four, NN)
        s = s + float(level) if level else s
        s_ref[at, rows] = s
        top = jnp.max(s.reshape(BLOCK // 8, 8, BOTH), axis=0)
        highest = top if highest is None else jnp.maximum(highest, top)
    return jnp.max(highest, axis=0, keepdims=True)


def exponents(levels, at, top, s_ref, e_ref, keep):
    summed = None
    for index in range(len(levels)):
        rows = pl.ds(index * BLOCK, BLOCK)
        e = jnp.exp2(s_ref[at, rows] - top)
        if keep:
            s_ref[at, rows] = e
        store_split(e_ref, at, rows, e)
        part = jnp.sum(e.reshape(BLOCK // 8, 8, BOTH), axis=0)
        summed = part if summed is None else summed + part
    return jnp.sum(summed, axis=0, keepdims=True)


def head_rows(ref, pair, head):
    return ref[pair, pl.ds(head * HEAD_DIM, HEAD_DIM)]


def each_group(pairs, body):
    for first in range(0, pairs, GROUP):
        group = range(first, min(first + GROUP, pairs))
        body(group, [(pair, head, 2 * pair + head) for pair in group for head in (0, 1)])


def costs(pairs, rows, products, exps=0):
    return dict(
        flops=2 * 4 * products * pairs * 2 * rows * BOTH * HEAD_DIM,
        exps=exps * pairs * 2 * rows * BOTH,
    )


def put_halves(pairs, sets, ins, group, plain, turned):
    for which in range(2):
        for pair in group:
            for head, value in enumerate(halves_of(sets, ins, which, pairs, pair)):
                plain[which][2 * pair + head] = value.astype(BF16)
                turned[which][2 * pair + head] = value.T.astype(BF16)


def attend_first(pairs, sets, operands, turned):
    total = sum(s[3] for s in sets)
    levels = segment_levels(sets)

    def kernel(turn_in, *refs):
        ins = refs[: len(operands)]
        kt, vc, e_ref, tops, sums, out, s_ref, kc, vt = refs[len(operands) :]

        def body(group, heads):
            put_halves(pairs, sets, ins, group, (kc, vc), (kt, vt))
            for pair, head, at in heads:
                q_four, _ = four_rows(head_rows(turn_in, pair, head))
                tops[at] = column_scores(levels, kc, at, q_four, s_ref)
            for _, _, at in heads:
                sums[at] = exponents(levels, at, tops[at], s_ref, e_ref, False)
            for _, _, at in heads:
                out[at] = fold_rows(dot(twice(vt[at]), stacked(e_ref, at), NN))

        each_group(pairs, body)

    heads = 2 * pairs
    outs = [
        jax.ShapeDtypeStruct((heads, LANES, total), BF16),
        jax.ShapeDtypeStruct((heads, total, LANES), BF16),
        jax.ShapeDtypeStruct((heads, 2, total, BOTH), BF16),
    ]
    outs += [struct(heads, 1, BOTH)] * 2 + [struct(heads, HEAD_DIM, BOTH)]
    return call(
        kernel,
        [turned, *operands],
        outs,
        scratch=[
            pltpu.VMEM((heads, total, BOTH), F32),
            pltpu.VMEM((heads, total, LANES), BF16),
            pltpu.VMEM((heads, LANES, total), BF16),
        ],
        **costs(pairs, total, 2, 1),
    )


def attend_last(pairs, sets, operands, turned, tops, sums, partial):
    total = sum(s[3] for s in sets)
    levels = segment_levels(sets)

    def kernel(turn_in, top_in, sum_in, part_in, *refs):
        ins = refs[: len(operands)]
        grads = refs[len(operands) : 2 * len(operands)]
        o_keep, o_send, g_out, r_out, dq_out = refs[2 * len(operands) : -7]
        s_ref, e_ref, d_ref, kc, vc, kt, vt = refs[-7:]

        def body(group, heads):
            put_halves(pairs, sets, ins, group, (kc, vc), (kt, vt))
            queries = {}
            top = {}
            for pair, head, at in heads:
                q_four, queries[at] = four_rows(head_rows(turn_in, pair, head))
                top[at] = column_scores(levels, kc, at, q_four, s_ref)
            inverse = {}
            rescale = {}
            for _, _, at in heads:
                first_top = top_in[at]
                highest = jnp.maximum(top[at], first_top)
                rescale[at] = jnp.exp2(first_top - highest)
                summed = exponents(levels, at, highest, s_ref, e_ref, True)
                inverse[at] = 1.0 / (summed + sum_in[at] * rescale[at])
            output = {}
            cotangents = {}
            row_dot = {}
            for pair, head, at in heads:
                o = fold_rows(dot(twice(vt[at]), stacked(e_ref, at), NN))
                o = (o + part_in[at] * rescale[at]) * inverse[at]
                output[at] = o
                scaled = head_rows(turn_in, pairs + pair, head) * inverse[at]
                cotangents[at] = four_rows(scaled)
                row_dot[at] = jnp.sum(o * scaled, axis=0, keepdims=True)
                g_out[at] = scaled * rescale[at]
                r_out[at] = row_dot[at] * rescale[at]
            for _, _, at in heads:
                for index in range(len(levels)):
                    rows = pl.ds(index * BLOCK, BLOCK)
                    dp = dot(twice(vc[at, rows]), cotangents[at][0], NN)
                    store_split(d_ref, at, rows, s_ref[at, rows] * (dp - row_dot[at]))
            key_grads = {}
            value_grads = {}
            for _, _, at in heads:
                value_grads[at] = dot(abreast(e_ref, at), twice(cotangents[at][1]), NT)
                key_grads[at] = dot(abreast(d_ref, at), twice(queries[at]), NT)
                dq_out[at] = fold_rows(dot(twice(kt[at]), stacked(d_ref, at), NN))
            for pair in group:
                put_grads(pairs, pair, sets, grads, key_grads, value_grads)
                both = [output[2 * pair], output[2 * pair + 1]]
                both = jnp.concatenate(both, axis=0).T
                o_keep[pair] = both[:BLOCK]
                o_send[pair] = both[BLOCK:]

        each_group(pairs, body)

    heads = 2 * pairs
    outs = [struct(*a.shape) for a in operands]
    outs += [struct(pairs, BLOCK, LANES)] * 2
    outs += [struct(heads, HEAD_DIM, BOTH), struct(heads, 1, BOTH)]
    outs.append(struct(heads, HEAD_DIM, BOTH))
    return call(
        kernel,
        [turned, tops, sums, partial, *operands],
        outs,
        scratch=[pltpu.VMEM((heads, total, BOTH), F32)]
        + [pltpu.VMEM((heads, 2, total, BOTH), BF16)] * 2
        + [pltpu.VMEM((heads, total, LANES), BF16)] * 2
        + [pltpu.VMEM((heads, LANES, total), BF16)] * 2,
        **costs(pairs, total, 6, 1),
    )


def put_grads(pairs, pair, sets, grads, key_grads, value_grads):
    for which, parts in enumerate((key_grads, value_grads)):
        both = fold_heads(parts[2 * pair], parts[2 * pair + 1])
        if which == 0:
            both = both * (1.0 / LOG2_E)
        filled = 0
        for _, index, row, rows in sets:
            piece = both[filled : filled + rows]
            grads[index][which * pairs + pair, pl.ds(row, rows), :] = piece
            filled += rows


def attend_back(pairs, sets, shapes, first, kept, turned, g_scaled, row_dot, dq, last):
    total = sum(s[3] for s in sets)
    segments = total // BLOCK

    def kernel(turn_in, kt, vc, e_ref, g_in, r_in, dq_in, *refs):
        grads = refs[: len(shapes)]
        dq_out = refs[len(shapes) : -1]
        d_ref = refs[-1]
        span = pl.ds(first, total)

        def body(group, heads):
            cotangents = {}
            for _, _, at in heads:
                g_four, cotangents[at] = four_rows(g_in[at])
                for index in range(segments):
                    rows = pl.ds(first + index * BLOCK, BLOCK)
                    dp = dot(twice(vc[at, rows]), g_four, NN)
                    e = e_ref[at, 0, rows].astype(F32) + e_ref[at, 1, rows].astype(F32)
                    place = pl.ds(index * BLOCK, BLOCK)
                    store_split(d_ref, at, place, e * (dp - r_in[at]))
            queries_grad = {}
            key_grads = {}
            value_grads = {}
            for pair, head, at in heads:
                _, q_rows = four_rows(head_rows(turn_in, pair, head))
                g_rows = cotangents[at]
                value_grads[at] = dot(abreast(e_ref, at, span), twice(g_rows), NT)
                key_grads[at] = dot(abreast(d_ref, at), twice(q_rows), NT)
                part = dot(twice(kt[at, :, span]), stacked(d_ref, at), NN)
                queries_grad[at] = fold_rows(part) + dq_in[at]
            for pair in group:
                put_grads(pairs, pair, sets, grads, key_grads, value_grads)
                both = [queries_grad[2 * pair], queries_grad[2 * pair + 1]]
                if last:
                    both = jnp.concatenate(both, axis=0).T * SCALE
                    dq_out[0][pair] = both[:BLOCK]
                    dq_out[1][pair] = both[BLOCK:]
                else:
                    for head in range(2):
                        dq_out[0][2 * pair + head] = both[head]

        each_group(pairs, body)

    outs = [struct(*shape) for shape in shapes]
    if last:
        outs += [struct(pairs, BLOCK, LANES)] * 2
    else:
        outs.append(struct(*dq.shape))
    return call(
        kernel,
        [turned, *kept, g_scaled, row_dot, dq],
        outs,
        scratch=[pltpu.VMEM((2 * pairs, 2, total, BOTH), BF16)],
        **costs(pairs, total, 4),
    )


def copy_columns(moves, ins, sems, bit):
    started = []
    for operand, theirs, column, place in moves:
        side = 1 - bit if theirs else bit
        column = side * (ins[operand].shape[1] // 2) + column
        column = pl.ds(pl.multiple_of(column, LANES), LANES)
        copy = pltpu.make_async_copy(
            ins[operand].at[:, column], place, sems.at[len(started)]
        )
        copy.start()
        started.append(copy)
    return started


def pack(pairs, first, second, scalar):
    def kernel(bit, one, two, theirs, mine, sems):
        moves = []
        for tile in range(2 * pairs):
            for out, other in ((theirs, True), (mine, False)):
                column = tile % pairs * LANES
                moves.append((tile // pairs, other, column, out.at[tile]))
        for copy in copy_columns(moves, (one, two), sems, bit[0]):
            copy.wait()

    return call(
        kernel,
        [first, second],
        [struct(2 * pairs, BLOCK, LANES)] * 2,
        scratch=[pltpu.SemaphoreType.DMA((4 * pairs,))],
        scalar=scalar,
        where=pl.ANY,
    )


QUARTER = BLOCK // 4
HALF = BLOCK // 2


def pack_coarse(pairs, keys, values, scalar):
    def kernel(bit, k, v, mine, f_theirs, f_mine, c_theirs, c_mine, rest, theirs, sems):
        moves = []
        for out, other in ((theirs, True), (mine, False)):
            for tile in range(2 * pairs):
                column = tile % pairs * LANES
                moves.append((tile // pairs, other, column, out.at[tile]))
        copies = copy_columns(moves, (k, v), sems, bit[0])
        for index, copy in enumerate(copies):
            copy.wait()
            tile = index % (2 * pairs)
            other = index < 2 * pairs
            source, finest, coarse = (
                (theirs, f_theirs, c_theirs) if other else (mine, f_mine, c_mine)
            )
            finest[tile] = mean_rows(source, (tile,), 0, HALF, 2)
            coarse[tile] = mean_rows(finest, (tile,), 0, QUARTER, 2)
            if other:
                rest[tile, :QUARTER] = half_difference(finest, (tile,), 0, QUARTER)
                rest[tile, QUARTER:] = half_difference(source, (tile,), 0, HALF)

    return call(
        kernel,
        [keys, values],
        [struct(2 * pairs, BLOCK, LANES)]
        + [struct(2 * pairs, HALF, LANES)] * 2
        + [struct(2 * pairs, QUARTER, LANES)] * 2
        + [struct(2 * pairs, QUARTER + HALF, LANES)],
        scratch=[
            pltpu.VMEM((2 * pairs, BLOCK, LANES), F32),
            pltpu.SemaphoreType.DMA((4 * pairs,)),
        ],
        scalar=scalar,
        where=pl.ANY,
    )


def rebuild(pairs, second, rest):
    def kernel(second_in, rest_in, out, finest):
        for tile in range(2 * pairs):
            put_pairs(finest, (tile,), second_in[tile], rest_in[tile, :QUARTER])
            put_pairs(out, (tile,), finest[tile], rest_in[tile, QUARTER:])

    return call(
        kernel,
        [second, rest],
        [struct(2 * pairs, BLOCK, LANES)],
        scratch=[pltpu.VMEM((2 * pairs, HALF, LANES), F32)],
    )[0]


def take_apart(pairs, block_grad):
    def kernel(block, second, rest, finest):
        for tile in range(2 * pairs):
            finest[tile] = 2.0 * mean_rows(block, (tile,), 0, HALF, 2)
            rest[tile, QUARTER:] = 2.0 * half_difference(block, (tile,), 0, HALF)
            second[tile] = 2.0 * mean_rows(finest, (tile,), 0, QUARTER, 2)
            rest[tile, :QUARTER] = 2.0 * half_difference(finest, (tile,), 0, QUARTER)

    return call(
        kernel,
        [block_grad],
        [
            struct(2 * pairs, QUARTER, LANES),
            struct(2 * pairs, QUARTER + HALF, LANES),
        ],
        scratch=[pltpu.VMEM((2 * pairs, HALF, LANES), F32)],
    )


class Levels:
    def __init__(self, bits):
        self.bits = bits
        self.rows = BLOCK >> bits
        self.differences = [
            [(m, BLOCK >> m) for m in range(bits, step, -1)] for step in range(bits)
        ]
        whole = [0] + [BLOCK >> step for step in range(1, bits)]
        self.whole = Tree(1, whole)
        self.rough = Tree(1, [0] + [self.rows] * (bits - 1))
        self.fine = Tree(1, [0] + [rows - self.rows for rows in whole[1:]])
        self.pieces = []
        for level in range(1, bits):
            trees = (self.whole, self.rough, self.fine)
            for parts in zip(*(tree.held[level] for tree in trees)):
                self.pieces.append((level, parts[0][0], *(part[1] for part in parts)))

    def scratch(self):
        shapes = [(BLOCK >> m, LANES) for m in range(1, self.bits + 1)]
        return [pltpu.VMEM(shape, F32) for shape in shapes]

    def group_pieces(self):
        pieces = []
        for index, (level, step, whole, rough, _) in enumerate(self.pieces):
            factor = 1 << self.bits - level
            place = (2 + index) * self.rows
            pieces.append((step, whole, rough, BLOCK >> level, factor, place))
        return pieces


def coarsen_pair(lo, pairs, mine, received):
    def kernel(own, got, *outs):
        for tile in range(2 * pairs):
            outs[0][tile, : BLOCK // 4] = own[tile]
            outs[0][tile, BLOCK // 4 :] = got[tile]
            for index in range(1, lo.bits):
                outs[index][tile] = mean_rows(
                    outs[index - 1], (tile,), 0, BLOCK >> index + 1, 2
                )

    outs = [struct(2 * pairs, BLOCK >> step, LANES) for step in range(1, lo.bits + 1)]
    return call(kernel, [mine, received], outs)


def group_pieces(lo):
    own = BLOCK >> lo.bits
    factor = 1 << lo.bits
    pieces = [
        (-2, 0, BLOCK // 2, factor, own),
        (-1, 0, BLOCK // 2, factor, own + own // 2),
    ]
    filled = 2 * own
    for level in range(1, lo.bits):
        factor = 1 << lo.bits - level
        for step, row, rows in lo.held[level]:
            pieces.append((step, row, rows, factor, filled))
            filled += rows // factor
    return pieces


def coarsen_group(lo, hi, pairs, own, halves, arrived):
    pieces = group_pieces(lo)

    def kernel(own_in, *refs):
        ins = refs[: 2 + lo.bits]
        outs = refs[2 + lo.bits :]
        for tile in range(2 * pairs):
            outs[0][tile, pl.ds(0, BLOCK >> lo.bits)] = own_in[tile]
            for step, row, rows, factor, place in pieces:
                count = rows // factor
                outs[0][tile, pl.ds(place, count)] = mean_rows(
                    ins[2 + step], (tile,), row, count, factor
                )
            for step in range(1, hi.bits):
                outs[step][tile] = mean_rows(
                    outs[step - 1], (tile,), 0, BLOCK >> step, 2
                )

    outs = [struct(2 * pairs, BLOCK >> step, LANES) for step in range(hi.bits)]
    return call(kernel, [own, *halves, *arrived], outs)


def turn(pairs, mine, received):
    def kernel(own, got, turned):
        for tile in range(2 * pairs):
            both = jnp.concatenate([own[tile], got[tile]], axis=0).T
            turned[tile] = both * (SCALE * LOG2_E) if tile < pairs else both

    return call(kernel, [mine, received], [struct(2 * pairs, LANES, 2 * BLOCK)])[0]


def take_levels(levels, pairs, grads):
    trees = (levels.rough, levels.fine)

    def kernel(*refs):
        ins = refs[: levels.bits]
        rough = refs[levels.bits : 2 * levels.bits]
        fine = refs[2 * levels.bits : 3 * levels.bits]
        ladder = refs[3 * levels.bits :]
        for tile in range(2 * pairs):
            for level, step, row, rough_row, fine_row in levels.pieces:
                source = ladder[level - 1]
                source[...] = ins[step][tile, pl.ds(row, BLOCK >> level)]
                fine_row += sum(rows for _, rows in levels.differences[level])
                for m, rows in reversed(levels.differences[level]):
                    fine_row -= rows
                    part = 2.0 * half_difference(source, (), 0, rows)
                    fine[step][tile, pl.ds(fine_row, rows)] = part
                    ladder[m - 1][...] = 2.0 * mean_rows(source, (), 0, rows, 2)
                    source = ladder[m - 1]
                rough[step][tile, pl.ds(rough_row, levels.rows)] = source[...]

    outs = [
        struct(2 * pairs, tree.rows(step), LANES)
        for tree in trees
        for step in range(levels.bits)
    ]
    outs = call(kernel, grads, outs, scratch=levels.scratch())
    return outs[: levels.bits], outs[levels.bits :]


def spread_group(levels, hi, pairs, group_grads, grads):
    own_rows = levels.rows

    def kernel(*refs):
        steps = refs[: hi.bits]
        ins = refs[hi.bits : hi.bits + levels.bits]
        own_out, *outs = refs[hi.bits + levels.bits : -1]
        total = refs[-1]
        for tile in range(2 * pairs):
            total[tile] = steps[0][tile, pl.ds(0, BLOCK)]
            for step in range(1, hi.bits):
                above = steps[step][tile, pl.ds(0, BLOCK >> step)]
                add_spread(total, (tile,), 0, above, 1 << step)
            own_out[tile] = total[tile, pl.ds(0, own_rows)]
            for step, _, row, _, _, place in levels.group_pieces():
                rows = pl.ds(row, own_rows)
                part = total[tile, pl.ds(place, own_rows)]
                outs[step][tile, rows] = ins[step][tile, rows] + part
            outs[0][tile, pl.ds(ins[0].shape[1], own_rows)] = total[
                tile, pl.ds(own_rows, own_rows)
            ]

    shapes = [list(a.shape) for a in grads]
    shapes[0][1] += own_rows
    outs = [struct(2 * pairs, own_rows, LANES)] + [struct(*shape) for shape in shapes]
    own, *grads = call(
        kernel,
        [*group_grads, *grads],
        outs,
        scratch=[pltpu.VMEM((2 * pairs, BLOCK, LANES), F32)],
    )
    return own, grads


def spread_pair(levels, pairs, own_grad, rough, fine, block_second):
    own_rows = levels.rows

    def kernel(own, block, *refs):
        rough_in = refs[: levels.bits]
        fine_in = refs[levels.bits : 2 * levels.bits]
        mine, theirs, *ladder = refs[2 * levels.bits :]
        last = pl.ds(rough_in[0].shape[1] - own_rows, own_rows)
        for tile in range(2 * pairs):
            above = own[tile] + rough_in[0][tile, last]
            for step in range(1, levels.bits):
                above = above + rough_in[step][tile, pl.ds(0, own_rows)]
            filled = 0
            for m, rows in levels.differences[1]:
                part = fine_in[1][tile, pl.ds(filled, rows)]
                for step in range(2, min(m, levels.bits)):
                    part = part + fine_in[step][tile, pl.ds(filled, rows)]
                filled += rows
                put_pairs(ladder[m - 2], (), 0.5 * above, 0.5 * part)
                above = ladder[m - 2][...]
            mine[tile] = above[:QUARTER]
            theirs[tile] = above[QUARTER:] + block[tile]

    return call(
        kernel,
        [own_grad, block_second, *rough, *fine],
        [struct(2 * pairs, QUARTER, LANES)] * 2,
        scratch=levels.scratch(),
    )


def unpack(pairs, kept, arrived, features, scalar):
    def kernel(bit, *refs):
        outs = refs[4:]
        for which in range(2):
            for pair in range(pairs):
                for side, ref in ((bit[0], refs[which]), (1 - bit[0], refs[2 + which])):
                    column = side * (features // 2) + pair * LANES
                    column = pl.ds(pl.multiple_of(column, LANES), LANES)
                    outs[which][:, column] = ref[pair]

    return call(kernel, [*kept, *arrived], [struct(BLOCK, features)] * 2, scalar=scalar)


def finish(pairs, kept, rest, finest, seconds, features, scalar):
    def kernel(bit, kept_in, rest_in, f_mine, f_theirs, s_mine, s_theirs, *refs):
        outs, total, middle = refs[:2], refs[2], refs[3]
        for tile in range(2 * pairs):
            out = outs[tile // pairs]
            column = tile % pairs * LANES
            at = (tile,)
            total[tile] = kept_in[tile]
            add_spread(total, at, 0, f_mine[tile], 2)
            add_spread(total, at, 0, s_mine[tile], 4)
            place = bit[0] * (features // 2) + column
            out[:, pl.ds(pl.multiple_of(place, LANES), LANES)] = total[tile]
            put_pairs(middle, at, 0.5 * s_theirs[tile], 0.5 * rest_in[tile, :QUARTER])
            first = 0.5 * (middle[tile] + f_theirs[tile])
            put_pairs(total, at, first, 0.5 * rest_in[tile, QUARTER:])
            place = (1 - bit[0]) * (features // 2) + column
            out[:, pl.ds(pl.multiple_of(place, LANES), LANES)] = total[tile]

    return call(
        kernel,
        [kept, rest, *finest, *seconds],
        [struct(BLOCK, features)] * 2,
        scratch=[
            pltpu.VMEM((2 * pairs, BLOCK, LANES), F32),
            pltpu.VMEM((2 * pairs, HALF, LANES), F32),
        ],
        scalar=scalar,
    )


def on_device(queries, keys, values, cotangent):
    features = queries.shape[1]
    assert queries.shape[0] == BLOCK
    pairs = features // LANES // 2
    lo_bits = lax.axis_size("seqlo").bit_length() - 1
    levels = Levels(lo_bits - 1)
    lo = levels.whole
    hi_bits = lax.axis_size("seqhi").bit_length() - 1
    hi = Tree(lo_bits, [BLOCK >> step for step in range(hi_bits)])
    scalar = (lax.axis_index("seqlo") % 2).astype(jnp.int32).reshape(1)
    queries, keys, values, cotangent = [
        pltpu.with_memory_space_constraint(array, pltpu.HBM)
        for array in (queries, keys, values, cotangent)
    ]
    mine_kv, f_theirs, f_mine, c_send, c_mine, rest = pack_coarse(
        pairs, keys, values, scalar
    )
    second = exchange(c_send, 1)
    finest_theirs = exchange(f_theirs, 2)
    coarse = coarsen_pair(lo, pairs, c_mine, second)
    finest = exchange(ordered(f_mine, finest_theirs), 2)
    rest = exchange(ordered(rest, coarse[0]), 1)
    half = exchange(ordered(finest_theirs, rest), 1)
    kv = rebuild(pairs, second, rest)
    send_qg, mine_qg = pack(pairs, queries, cotangent, scalar)
    qg = exchange(ordered(send_qg, half), 1)
    zs = lo.gather([None, *coarse], (finest, send_qg))
    group = coarsen_group(
        lo, hi, pairs, ordered(coarse[-1], rest), [finest, half], zs
    )
    turned = turn(pairs, mine_qg, qg)
    rs = hi.gather(group, turned)
    block_sets = [(0, 0, 0, BLOCK), (0, 1, 0, BLOCK)]
    lo_sets = [(1, 2, 0, BLOCK // 2), (1, 3, 0, BLOCK // 2)]
    for level in range(lo.bits):
        for step, row, rows in lo.held[level]:
            lo_sets.append((1 + level, 4 + step, row, rows))
    hi_sets = []
    for level in range(hi.bits):
        for step, row, rows in hi.held[level]:
            hi_sets.append((lo_bits + level, step, row, rows))
    first_in = [mine_kv, kv, finest, half, *zs]
    *kept, tops, sums, partial = attend_first(
        pairs, block_sets + lo_sets, first_in, turned
    )
    *rs_grads, o_keep, o_send, g_scaled, row_dot, dq = attend_last(
        pairs, hi_sets, rs, turned, tops, sums, partial
    )
    shapes = [(2 * pairs, *a.shape[1:]) for a in first_in]
    finest_grad, half_grad, *zs_grads, dq = attend_back(
        pairs,
        [(level, index - 2, row, rows) for level, index, row, rows in lo_sets],
        shapes[2:],
        BOTH,
        kept,
        turned,
        g_scaled,
        row_dot,
        dq,
        False,
    )
    kv_keep, kv_send, dq_keep, dq_send = attend_back(
        pairs, block_sets, shapes[:2], 0, kept, turned, g_scaled, row_dot, dq, True
    )
    rough_grads, fine_grads = take_levels(levels, pairs, zs_grads)
    finest_mine = exchange(finest_grad, 2)
    half_back = exchange(half_grad, 1)
    o_back = exchange(o_send, 1)
    fine_back = levels.fine.scatter(fine_grads)
    block_second, rest_grad = take_apart(pairs, kv_send)
    rest_back = exchange(ordered(rest_grad, (half_back, o_back)), 1)
    dq_back = exchange(ordered(dq_send, half_back), 1)
    group_grads = hi.scatter(rs_grads)
    group_grads[-1] = ordered(
        group_grads[-1], (finest_mine, half_back, fine_back[0], kv_send)
    )
    own_grad, rough_grads = spread_group(levels, hi, pairs, group_grads, rough_grads)
    rough_back = levels.rough.scatter(rough_grads)
    finest_theirs = exchange(ordered(half_back, rough_back[0]), 2)
    own_grad = ordered(own_grad, (rest_back, dq_back))
    second_mine, second_send = spread_pair(
        levels, pairs, own_grad, rough_back, fine_back, block_second
    )
    second_theirs = exchange(second_send, 1)
    attended, query_grad = unpack(
        pairs, (o_keep, dq_keep), (o_back, dq_back), features, scalar
    )
    key_grad, value_grad = finish(
        pairs,
        kv_keep,
        rest_back,
        (finest_mine, finest_theirs),
        (second_mine, second_theirs),
        features,
        scalar,
    )
    return attended, query_grad, key_grad, value_grad


def solution(mesh):
    spec = P(AXES, None)
    return jax.shard_map(
        on_device,
        mesh=mesh,
        in_specs=(spec,) * 4,
        out_specs=(spec,) * 4,
        check_vma=False,
    )
```

```python
import math

import jax
import jax.numpy as jnp
from jax import lax
from jax.experimental import pallas as pl
from jax.experimental.pallas import tpu as pltpu
from jax.sharding import PartitionSpec as P

HEADS = 12
BLOCK = 128
HEAD_DIM = 64
LANES = 2 * HEAD_DIM
AXES = ("seqhi", "seqlo")
VMEM_LIMIT = 20 * 1024 * 1024
F32 = jnp.float32
BF16 = jnp.bfloat16
LOG2_E = 1.0 / math.log(2.0)
SCALE = 1.0 / math.sqrt(HEAD_DIM)


def struct(*shape):
    return jax.ShapeDtypeStruct(shape, F32)


def call(kernel, operands, outs, scratch=(), scalar=None, flops=0, exps=0, where=None):
    vmem = pl.BlockSpec(memory_space=pltpu.VMEM)
    smem = pl.BlockSpec(memory_space=pltpu.SMEM)
    in_specs = [pl.BlockSpec(memory_space=where) if where else vmem] * len(operands)
    if scalar is not None:
        operands = [scalar, *operands]
        in_specs = [smem, *in_specs]
    moved = sum(4 * math.prod(a.shape) for a in [*operands, *outs])
    return pl.pallas_call(
        kernel,
        out_shape=list(outs),
        in_specs=in_specs,
        out_specs=[vmem] * len(outs),
        scratch_shapes=list(scratch),
        compiler_params=pltpu.CompilerParams(vmem_limit_bytes=VMEM_LIMIT),
        cost_estimate=pl.CostEstimate(
            flops=flops, bytes_accessed=moved, transcendentals=exps
        ),
    )(*operands)


def exchange(value, offset):
    count = lax.axis_size(AXES)
    return lax.ppermute(value, AXES, [(i, i ^ offset) for i in range(count)])


def ordered(value, after):
    return value if after is None else lax.optimization_barrier((value, after))[0]


def half_difference(ref, lead, first, count):
    even = ref[(*lead, pl.ds(first, count, stride=2), slice(None))]
    odd = ref[(*lead, pl.ds(first + 1, count, stride=2), slice(None))]
    return 0.5 * (even - odd)


def put_pairs(ref, lead, total, difference):
    count = total.shape[0]
    ref[(*lead, pl.ds(0, count, stride=2), slice(None))] = total + difference
    ref[(*lead, pl.ds(1, count, stride=2), slice(None))] = total - difference


def mean_rows(ref, lead, first, count, factor):
    total = None
    for step in range(factor):
        rows = pl.ds(first + step, count, stride=factor)
        part = ref[(*lead, rows, slice(None))]
        total = part if total is None else total + part
    return total * (1.0 / factor)


def add_spread(ref, lead, first, value, factor):
    count = value.shape[0]
    value = value * (1.0 / factor)
    for step in range(factor):
        rows = pl.ds(first + step, count, stride=factor)
        place = (*lead, rows, slice(None))
        ref[place] = ref[place] + value


class Tree:
    def __init__(self, first_bit, own_rows):
        self.bits = bits = len(own_rows)
        self.first_bit = first_bit
        self.own_rows = own_rows
        self.held = {}
        self.payload = {}
        for step in range(bits - 1, -1, -1):
            rows = self.own_rows[step]
            payload = []
            fresh = {step: [(step, 0, rows)] if rows else []}
            for level in range(step + 1, bits):
                for piece in self.held[level]:
                    payload.append(piece)
                    fresh.setdefault(level, []).append((step, rows, piece[2]))
                    rows += piece[2]
            self.payload[step] = payload
            for level, pieces in fresh.items():
                self.held[level] = self.held.get(level, []) + pieces

    def rows(self, step):
        return self.own_rows[step] + sum(piece[2] for piece in self.payload[step])

    def partner(self, value, step):
        return exchange(value, 1 << self.first_bit + step)

    def gather(self, own, after=None):
        arrived = [None] * self.bits
        for step in range(self.bits - 1, -1, -1):
            parts = [own[step]] if self.own_rows[step] else []
            for source, row, rows in self.payload[step]:
                part = arrived[source]
                whole = rows == part.shape[1]
                parts.append(part if whole else part[:, row : row + rows])
            sent = jnp.concatenate(parts, axis=1) if len(parts) > 1 else parts[0]
            if step == 0:
                sent = ordered(sent, after)
            arrived[step] = self.partner(sent, step)
        return arrived

    def scatter(self, grads, front=None):
        grads = list(grads)
        returned = []
        for step in range(self.bits):
            sent = grads[step]
            if step == 0 and front is not None:
                rows = front.shape[1]
                back = self.partner(jnp.concatenate([front, sent], axis=1), step)
                front, back = back[:, :rows], back[:, rows:]
            else:
                back = self.partner(sent, step)
            returned.append(back)
            filled = self.own_rows[step]
            for source, row, rows in self.payload[step]:
                part = back[:, filled : filled + rows]
                grads[source] = grads[source].at[:, row : row + rows].add(part)
                filled += rows
        return returned if front is None else (returned, front)


def split(value):
    high = value.astype(BF16).astype(F32)
    return high, value - high


def halves_by_head(value):
    high, low = split(value)
    first = lax.broadcasted_iota(jnp.int32, value.shape, 1) < HEAD_DIM
    one = jnp.where(first, high, pltpu.roll(low, HEAD_DIM, 1))
    two = jnp.where(first, pltpu.roll(high, HEAD_DIM, 1), low)
    return one, two


def dot(lhs, rhs, dims):
    return lax.dot_general(lhs, rhs, (dims, ((), ())), preferred_element_type=F32)


NN = ((1,), (0,))
NT = ((1,), (1,))


BOTH = 2 * BLOCK
GROUP = 3


def halves_of(sets, ins, which, pairs, pair):
    tile = which * pairs + pair
    parts = [ins[index][tile, pl.ds(row, rows), :] for _, index, row, rows in sets]
    return halves_by_head(jnp.concatenate(parts, axis=0))


def segment_levels(sets):
    levels, filled = [], 0
    for level, _, _, rows in sets:
        if filled % BLOCK == 0:
            levels.append(level)
        filled += rows
    return levels


def four_rows(value):
    high, low = split(value)
    four = jnp.concatenate([high, high, low, low], axis=0).astype(BF16)
    return four, jnp.concatenate([high, low], axis=0).astype(BF16)


def store_split(ref, lead, rows, value):
    high = value.astype(BF16)
    ref[(lead, 0, rows)] = high
    ref[(lead, 1, rows)] = (value - high.astype(F32)).astype(BF16)


def fold_rows(value):
    return value[:HEAD_DIM] + value[HEAD_DIM:]


def fold_heads(one, two):
    first = lax.broadcasted_iota(jnp.int32, one.shape, 1) < HEAD_DIM
    return jnp.where(
        first, one + pltpu.roll(one, HEAD_DIM, 1), two + pltpu.roll(two, HEAD_DIM, 1)
    )


def twice(value):
    return jnp.concatenate([value, value], axis=1)


def stacked(ref, at, rows=slice(None)):
    return jnp.concatenate([ref[at, 0, rows], ref[at, 1, rows]], axis=0)


def abreast(ref, at, rows=slice(None)):
    return jnp.concatenate([ref[at, 0, rows], ref[at, 1, rows]], axis=1)


def column_scores(levels, keys, at, q_four, s_ref):
    highest = None
    for index, level in enumerate(levels):
        rows = pl.ds(index * BLOCK, BLOCK)
        s = dot(twice(keys[at, rows]), q_four, NN)
        s = s + float(level) if level else s
        s_ref[at, rows] = s
        top = jnp.max(s.reshape(BLOCK // 8, 8, BOTH), axis=0)
        highest = top if highest is None else jnp.maximum(highest, top)
    return jnp.max(highest, axis=0, keepdims=True)


def exponents(levels, at, top, s_ref, e_ref, keep):
    summed = None
    for index in range(len(levels)):
        rows = pl.ds(index * BLOCK, BLOCK)
        e = jnp.exp2(s_ref[at, rows] - top)
        if keep:
            s_ref[at, rows] = e
        store_split(e_ref, at, rows, e)
        part = jnp.sum(e.reshape(BLOCK // 8, 8, BOTH), axis=0)
        summed = part if summed is None else summed + part
    return jnp.sum(summed, axis=0, keepdims=True)


def head_rows(ref, pair, head):
    return ref[pair, pl.ds(head * HEAD_DIM, HEAD_DIM)]


def each_group(pairs, body):
    for first in range(0, pairs, GROUP):
        group = range(first, min(first + GROUP, pairs))
        body(group, [(pair, head, 2 * pair + head) for pair in group for head in (0, 1)])


def costs(pairs, rows, products, exps=0):
    return dict(
        flops=2 * 4 * products * pairs * 2 * rows * BOTH * HEAD_DIM,
        exps=exps * pairs * 2 * rows * BOTH,
    )


def put_halves(pairs, sets, ins, group, plain, turned):
    for which in range(2):
        for pair in group:
            for head, value in enumerate(halves_of(sets, ins, which, pairs, pair)):
                plain[which][2 * pair + head] = value.astype(BF16)
                turned[which][2 * pair + head] = value.T.astype(BF16)


def attend_first(pairs, sets, operands, turned):
    total = sum(s[3] for s in sets)
    levels = segment_levels(sets)

    def kernel(turn_in, *refs):
        ins = refs[: len(operands)]
        kt, vc, e_ref, tops, sums, out, s_ref, kc, vt = refs[len(operands) :]

        def body(group, heads):
            put_halves(pairs, sets, ins, group, (kc, vc), (kt, vt))
            for pair, head, at in heads:
                q_four, _ = four_rows(head_rows(turn_in, pair, head))
                tops[at] = column_scores(levels, kc, at, q_four, s_ref)
            for _, _, at in heads:
                sums[at] = exponents(levels, at, tops[at], s_ref, e_ref, False)
            for _, _, at in heads:
                out[at] = fold_rows(dot(twice(vt[at]), stacked(e_ref, at), NN))

        each_group(pairs, body)

    heads = 2 * pairs
    outs = [
        jax.ShapeDtypeStruct((heads, LANES, total), BF16),
        jax.ShapeDtypeStruct((heads, total, LANES), BF16),
        jax.ShapeDtypeStruct((heads, 2, total, BOTH), BF16),
    ]
    outs += [struct(heads, 1, BOTH)] * 2 + [struct(heads, HEAD_DIM, BOTH)]
    return call(
        kernel,
        [turned, *operands],
        outs,
        scratch=[
            pltpu.VMEM((heads, total, BOTH), F32),
            pltpu.VMEM((heads, total, LANES), BF16),
            pltpu.VMEM((heads, LANES, total), BF16),
        ],
        **costs(pairs, total, 2, 1),
    )


def attend_last(pairs, sets, operands, turned, tops, sums, partial):
    total = sum(s[3] for s in sets)
    levels = segment_levels(sets)

    def kernel(turn_in, top_in, sum_in, part_in, *refs):
        ins = refs[: len(operands)]
        grads = refs[len(operands) : 2 * len(operands)]
        o_keep, o_send, g_out, r_out, dq_out = refs[2 * len(operands) : -7]
        s_ref, e_ref, d_ref, kc, vc, kt, vt = refs[-7:]

        def body(group, heads):
            put_halves(pairs, sets, ins, group, (kc, vc), (kt, vt))
            queries = {}
            top = {}
            for pair, head, at in heads:
                q_four, queries[at] = four_rows(head_rows(turn_in, pair, head))
                top[at] = column_scores(levels, kc, at, q_four, s_ref)
            inverse = {}
            rescale = {}
            for _, _, at in heads:
                first_top = top_in[at]
                highest = jnp.maximum(top[at], first_top)
                rescale[at] = jnp.exp2(first_top - highest)
                summed = exponents(levels, at, highest, s_ref, e_ref, True)
                inverse[at] = 1.0 / (summed + sum_in[at] * rescale[at])
            output = {}
            cotangents = {}
            row_dot = {}
            for pair, head, at in heads:
                o = fold_rows(dot(twice(vt[at]), stacked(e_ref, at), NN))
                o = (o + part_in[at] * rescale[at]) * inverse[at]
                output[at] = o
                scaled = head_rows(turn_in, pairs + pair, head) * inverse[at]
                cotangents[at] = four_rows(scaled)
                row_dot[at] = jnp.sum(o * scaled, axis=0, keepdims=True)
                g_out[at] = scaled * rescale[at]
                r_out[at] = row_dot[at] * rescale[at]
            for _, _, at in heads:
                for index in range(len(levels)):
                    rows = pl.ds(index * BLOCK, BLOCK)
                    dp = dot(twice(vc[at, rows]), cotangents[at][0], NN)
                    store_split(d_ref, at, rows, s_ref[at, rows] * (dp - row_dot[at]))
            key_grads = {}
            value_grads = {}
            for _, _, at in heads:
                value_grads[at] = dot(abreast(e_ref, at), twice(cotangents[at][1]), NT)
                key_grads[at] = dot(abreast(d_ref, at), twice(queries[at]), NT)
                dq_out[at] = fold_rows(dot(twice(kt[at]), stacked(d_ref, at), NN))
            for pair in group:
                put_grads(pairs, pair, sets, grads, key_grads, value_grads)
                both = [output[2 * pair], output[2 * pair + 1]]
                both = jnp.concatenate(both, axis=0).T
                o_keep[pair] = both[:BLOCK]
                o_send[pair] = both[BLOCK:]

        each_group(pairs, body)

    heads = 2 * pairs
    outs = [struct(*a.shape) for a in operands]
    outs += [struct(pairs, BLOCK, LANES)] * 2
    outs += [struct(heads, HEAD_DIM, BOTH), struct(heads, 1, BOTH)]
    outs.append(struct(heads, HEAD_DIM, BOTH))
    return call(
        kernel,
        [turned, tops, sums, partial, *operands],
        outs,
        scratch=[pltpu.VMEM((heads, total, BOTH), F32)]
        + [pltpu.VMEM((heads, 2, total, BOTH), BF16)] * 2
        + [pltpu.VMEM((heads, total, LANES), BF16)] * 2
        + [pltpu.VMEM((heads, LANES, total), BF16)] * 2,
        **costs(pairs, total, 6, 1),
    )


def put_grads(pairs, pair, sets, grads, key_grads, value_grads):
    for which, parts in enumerate((key_grads, value_grads)):
        both = fold_heads(parts[2 * pair], parts[2 * pair + 1])
        if which == 0:
            both = both * (1.0 / LOG2_E)
        filled = 0
        for _, index, row, rows in sets:
            piece = both[filled : filled + rows]
            grads[index][which * pairs + pair, pl.ds(row, rows), :] = piece
            filled += rows


def attend_back(pairs, sets, shapes, first, kept, turned, g_scaled, row_dot, dq, last):
    total = sum(s[3] for s in sets)
    segments = total // BLOCK

    def kernel(turn_in, kt, vc, e_ref, g_in, r_in, dq_in, *refs):
        grads = refs[: len(shapes)]
        dq_out = refs[len(shapes) : -1]
        d_ref = refs[-1]
        span = pl.ds(first, total)

        def body(group, heads):
            cotangents = {}
            for _, _, at in heads:
                g_four, cotangents[at] = four_rows(g_in[at])
                for index in range(segments):
                    rows = pl.ds(first + index * BLOCK, BLOCK)
                    dp = dot(twice(vc[at, rows]), g_four, NN)
                    e = e_ref[at, 0, rows].astype(F32) + e_ref[at, 1, rows].astype(F32)
                    place = pl.ds(index * BLOCK, BLOCK)
                    store_split(d_ref, at, place, e * (dp - r_in[at]))
            queries_grad = {}
            key_grads = {}
            value_grads = {}
            for pair, head, at in heads:
                _, q_rows = four_rows(head_rows(turn_in, pair, head))
                g_rows = cotangents[at]
                value_grads[at] = dot(abreast(e_ref, at, span), twice(g_rows), NT)
                key_grads[at] = dot(abreast(d_ref, at), twice(q_rows), NT)
                part = dot(twice(kt[at, :, span]), stacked(d_ref, at), NN)
                queries_grad[at] = fold_rows(part) + dq_in[at]
            for pair in group:
                put_grads(pairs, pair, sets, grads, key_grads, value_grads)
                both = [queries_grad[2 * pair], queries_grad[2 * pair + 1]]
                if last:
                    both = jnp.concatenate(both, axis=0).T * SCALE
                    dq_out[0][pair] = both[:BLOCK]
                    dq_out[1][pair] = both[BLOCK:]
                else:
                    for head in range(2):
                        dq_out[0][2 * pair + head] = both[head]

        each_group(pairs, body)

    outs = [struct(*shape) for shape in shapes]
    if last:
        outs += [struct(pairs, BLOCK, LANES)] * 2
    else:
        outs.append(struct(*dq.shape))
    return call(
        kernel,
        [turned, *kept, g_scaled, row_dot, dq],
        outs,
        scratch=[pltpu.VMEM((2 * pairs, 2, total, BOTH), BF16)],
        **costs(pairs, total, 4),
    )


def copy_columns(moves, ins, sems, bit):
    started = []
    for operand, theirs, column, place in moves:
        side = 1 - bit if theirs else bit
        column = side * (ins[operand].shape[1] // 2) + column
        column = pl.ds(pl.multiple_of(column, LANES), LANES)
        copy = pltpu.make_async_copy(
            ins[operand].at[:, column], place, sems.at[len(started)]
        )
        copy.start()
        started.append(copy)
    return started


def pack(pairs, first, second, scalar):
    def kernel(bit, one, two, theirs, mine, sems):
        moves = []
        for tile in range(2 * pairs):
            for out, other in ((theirs, True), (mine, False)):
                column = tile % pairs * LANES
                moves.append((tile // pairs, other, column, out.at[tile]))
        for copy in copy_columns(moves, (one, two), sems, bit[0]):
            copy.wait()

    return call(
        kernel,
        [first, second],
        [struct(2 * pairs, BLOCK, LANES)] * 2,
        scratch=[pltpu.SemaphoreType.DMA((4 * pairs,))],
        scalar=scalar,
        where=pl.ANY,
    )


QUARTER = BLOCK // 4
HALF = BLOCK // 2


def pack_coarse(pairs, keys, values, scalar):
    def kernel(bit, k, v, mine, f_theirs, f_mine, c_theirs, c_mine, rest, theirs, sems):
        moves = []
        for out, other in ((theirs, True), (mine, False)):
            for tile in range(2 * pairs):
                column = tile % pairs * LANES
                moves.append((tile // pairs, other, column, out.at[tile]))
        copies = copy_columns(moves, (k, v), sems, bit[0])
        for index, copy in enumerate(copies):
            copy.wait()
            tile = index % (2 * pairs)
            other = index < 2 * pairs
            source, finest, coarse = (
                (theirs, f_theirs, c_theirs) if other else (mine, f_mine, c_mine)
            )
            finest[tile] = mean_rows(source, (tile,), 0, HALF, 2)
            coarse[tile] = mean_rows(finest, (tile,), 0, QUARTER, 2)
            if other:
                rest[tile, :QUARTER] = half_difference(finest, (tile,), 0, QUARTER)
                rest[tile, QUARTER:] = half_difference(source, (tile,), 0, HALF)

    return call(
        kernel,
        [keys, values],
        [struct(2 * pairs, BLOCK, LANES)]
        + [struct(2 * pairs, HALF, LANES)] * 2
        + [struct(2 * pairs, QUARTER, LANES)] * 2
        + [struct(2 * pairs, QUARTER + HALF, LANES)],
        scratch=[
            pltpu.VMEM((2 * pairs, BLOCK, LANES), F32),
            pltpu.SemaphoreType.DMA((4 * pairs,)),
        ],
        scalar=scalar,
        where=pl.ANY,
    )


def rebuild(pairs, second, rest):
    def kernel(second_in, rest_in, out, finest):
        for tile in range(2 * pairs):
            put_pairs(finest, (tile,), second_in[tile], rest_in[tile, :QUARTER])
            put_pairs(out, (tile,), finest[tile], rest_in[tile, QUARTER:])

    return call(
        kernel,
        [second, rest],
        [struct(2 * pairs, BLOCK, LANES)],
        scratch=[pltpu.VMEM((2 * pairs, HALF, LANES), F32)],
    )[0]


def take_apart(pairs, block_grad):
    def kernel(block, second, rest, finest):
        for tile in range(2 * pairs):
            finest[tile] = 2.0 * mean_rows(block, (tile,), 0, HALF, 2)
            rest[tile, QUARTER:] = 2.0 * half_difference(block, (tile,), 0, HALF)
            second[tile] = 2.0 * mean_rows(finest, (tile,), 0, QUARTER, 2)
            rest[tile, :QUARTER] = 2.0 * half_difference(finest, (tile,), 0, QUARTER)

    return call(
        kernel,
        [block_grad],
        [
            struct(2 * pairs, QUARTER, LANES),
            struct(2 * pairs, QUARTER + HALF, LANES),
        ],
        scratch=[pltpu.VMEM((2 * pairs, HALF, LANES), F32)],
    )


class Levels:
    def __init__(self, bits):
        self.bits = bits
        self.rows = BLOCK >> bits
        self.differences = [
            [(m, BLOCK >> m) for m in range(bits, step, -1)] for step in range(bits)
        ]
        whole = [0] + [BLOCK >> step for step in range(1, bits)]
        self.whole = Tree(1, whole)
        self.rough = Tree(1, [0] + [self.rows] * (bits - 1))
        self.fine = Tree(1, [0] + [rows - self.rows for rows in whole[1:]])
        self.pieces = []
        for level in range(1, bits):
            trees = (self.whole, self.rough, self.fine)
            for parts in zip(*(tree.held[level] for tree in trees)):
                self.pieces.append((level, parts[0][0], *(part[1] for part in parts)))

    def scratch(self):
        shapes = [(BLOCK >> m, LANES) for m in range(1, self.bits + 1)]
        return [pltpu.VMEM(shape, F32) for shape in shapes]

    def group_pieces(self):
        pieces = []
        for index, (level, step, whole, rough, _) in enumerate(self.pieces):
            factor = 1 << self.bits - level
            place = (2 + index) * self.rows
            pieces.append((step, whole, rough, BLOCK >> level, factor, place))
        return pieces


def coarsen_pair(lo, pairs, mine, received):
    def kernel(own, got, *outs):
        for tile in range(2 * pairs):
            outs[0][tile, : BLOCK // 4] = own[tile]
            outs[0][tile, BLOCK // 4 :] = got[tile]
            for index in range(1, lo.bits):
                outs[index][tile] = mean_rows(
                    outs[index - 1], (tile,), 0, BLOCK >> index + 1, 2
                )

    outs = [struct(2 * pairs, BLOCK >> step, LANES) for step in range(1, lo.bits + 1)]
    return call(kernel, [mine, received], outs)


def group_pieces(lo):
    own = BLOCK >> lo.bits
    factor = 1 << lo.bits
    pieces = [
        (-2, 0, BLOCK // 2, factor, own),
        (-1, 0, BLOCK // 2, factor, own + own // 2),
    ]
    filled = 2 * own
    for level in range(1, lo.bits):
        factor = 1 << lo.bits - level
        for step, row, rows in lo.held[level]:
            pieces.append((step, row, rows, factor, filled))
            filled += rows // factor
    return pieces


def coarsen_group(lo, hi, pairs, own, halves, arrived):
    pieces = group_pieces(lo)

    def kernel(own_in, *refs):
        ins = refs[: 2 + lo.bits]
        outs = refs[2 + lo.bits :]
        for tile in range(2 * pairs):
            outs[0][tile, pl.ds(0, BLOCK >> lo.bits)] = own_in[tile]
            for step, row, rows, factor, place in pieces:
                count = rows // factor
                outs[0][tile, pl.ds(place, count)] = mean_rows(
                    ins[2 + step], (tile,), row, count, factor
                )
            for step in range(1, hi.bits):
                outs[step][tile] = mean_rows(
                    outs[step - 1], (tile,), 0, BLOCK >> step, 2
                )

    outs = [struct(2 * pairs, BLOCK >> step, LANES) for step in range(hi.bits)]
    return call(kernel, [own, *halves, *arrived], outs)


def turn(pairs, mine, received):
    def kernel(own, got, turned):
        for tile in range(2 * pairs):
            both = jnp.concatenate([own[tile], got[tile]], axis=0).T
            turned[tile] = both * (SCALE * LOG2_E) if tile < pairs else both

    return call(kernel, [mine, received], [struct(2 * pairs, LANES, 2 * BLOCK)])[0]


def take_levels(levels, pairs, grads):
    trees = (levels.rough, levels.fine)

    def kernel(*refs):
        ins = refs[: levels.bits]
        rough = refs[levels.bits : 2 * levels.bits]
        fine = refs[2 * levels.bits : 3 * levels.bits]
        ladder = refs[3 * levels.bits :]
        for tile in range(2 * pairs):
            for level, step, row, rough_row, fine_row in levels.pieces:
                source = ladder[level - 1]
                source[...] = ins[step][tile, pl.ds(row, BLOCK >> level)]
                fine_row += sum(rows for _, rows in levels.differences[level])
                for m, rows in reversed(levels.differences[level]):
                    fine_row -= rows
                    part = 2.0 * half_difference(source, (), 0, rows)
                    fine[step][tile, pl.ds(fine_row, rows)] = part
                    ladder[m - 1][...] = 2.0 * mean_rows(source, (), 0, rows, 2)
                    source = ladder[m - 1]
                rough[step][tile, pl.ds(rough_row, levels.rows)] = source[...]

    outs = [
        struct(2 * pairs, tree.rows(step), LANES)
        for tree in trees
        for step in range(levels.bits)
    ]
    outs = call(kernel, grads, outs, scratch=levels.scratch())
    return outs[: levels.bits], outs[levels.bits :]


def spread_group(levels, hi, pairs, group_grads, grads):
    own_rows = levels.rows

    def kernel(*refs):
        steps = refs[: hi.bits]
        ins = refs[hi.bits : hi.bits + levels.bits]
        own_out, *outs = refs[hi.bits + levels.bits : -1]
        total = refs[-1]
        for tile in range(2 * pairs):
            total[tile] = steps[0][tile, pl.ds(0, BLOCK)]
            for step in range(1, hi.bits):
                above = steps[step][tile, pl.ds(0, BLOCK >> step)]
                add_spread(total, (tile,), 0, above, 1 << step)
            own_out[tile] = total[tile, pl.ds(0, own_rows)]
            for step, _, row, _, _, place in levels.group_pieces():
                rows = pl.ds(row, own_rows)
                part = total[tile, pl.ds(place, own_rows)]
                outs[step][tile, rows] = ins[step][tile, rows] + part
            outs[0][tile, pl.ds(ins[0].shape[1], own_rows)] = total[
                tile, pl.ds(own_rows, own_rows)
            ]

    shapes = [list(a.shape) for a in grads]
    shapes[0][1] += own_rows
    outs = [struct(2 * pairs, own_rows, LANES)] + [struct(*shape) for shape in shapes]
    own, *grads = call(
        kernel,
        [*group_grads, *grads],
        outs,
        scratch=[pltpu.VMEM((2 * pairs, BLOCK, LANES), F32)],
    )
    return own, grads


def spread_pair(levels, pairs, own_grad, rough, fine, block_second):
    own_rows = levels.rows

    def kernel(own, block, *refs):
        rough_in = refs[: levels.bits]
        fine_in = refs[levels.bits : 2 * levels.bits]
        mine, theirs, *ladder = refs[2 * levels.bits :]
        last = pl.ds(rough_in[0].shape[1] - own_rows, own_rows)
        for tile in range(2 * pairs):
            above = own[tile] + rough_in[0][tile, last]
            for step in range(1, levels.bits):
                above = above + rough_in[step][tile, pl.ds(0, own_rows)]
            filled = 0
            for m, rows in levels.differences[1]:
                part = fine_in[1][tile, pl.ds(filled, rows)]
                for step in range(2, min(m, levels.bits)):
                    part = part + fine_in[step][tile, pl.ds(filled, rows)]
                filled += rows
                put_pairs(ladder[m - 2], (), 0.5 * above, 0.5 * part)
                above = ladder[m - 2][...]
            mine[tile] = above[:QUARTER]
            theirs[tile] = above[QUARTER:] + block[tile]

    return call(
        kernel,
        [own_grad, block_second, *rough, *fine],
        [struct(2 * pairs, QUARTER, LANES)] * 2,
        scratch=levels.scratch(),
    )


def unpack(pairs, kept, arrived, features, scalar):
    def kernel(bit, *refs):
        outs = refs[4:]
        for which in range(2):
            for pair in range(pairs):
                for side, ref in ((bit[0], refs[which]), (1 - bit[0], refs[2 + which])):
                    column = side * (features // 2) + pair * LANES
                    column = pl.ds(pl.multiple_of(column, LANES), LANES)
                    outs[which][:, column] = ref[pair]

    return call(kernel, [*kept, *arrived], [struct(BLOCK, features)] * 2, scalar=scalar)


def finish(pairs, kept, rest, finest, seconds, features, scalar):
    def kernel(bit, kept_in, rest_in, f_mine, f_theirs, s_mine, s_theirs, *refs):
        outs, total, middle = refs[:2], refs[2], refs[3]
        for tile in range(2 * pairs):
            out = outs[tile // pairs]
            column = tile % pairs * LANES
            at = (tile,)
            total[tile] = kept_in[tile]
            add_spread(total, at, 0, f_mine[tile], 2)
            add_spread(total, at, 0, s_mine[tile], 4)
            place = bit[0] * (features // 2) + column
            out[:, pl.ds(pl.multiple_of(place, LANES), LANES)] = total[tile]
            put_pairs(middle, at, 0.5 * s_theirs[tile], 0.5 * rest_in[tile, :QUARTER])
            first = 0.5 * (middle[tile] + f_theirs[tile])
            put_pairs(total, at, first, 0.5 * rest_in[tile, QUARTER:])
            place = (1 - bit[0]) * (features // 2) + column
            out[:, pl.ds(pl.multiple_of(place, LANES), LANES)] = total[tile]

    return call(
        kernel,
        [kept, rest, *finest, *seconds],
        [struct(BLOCK, features)] * 2,
        scratch=[
            pltpu.VMEM((2 * pairs, BLOCK, LANES), F32),
            pltpu.VMEM((2 * pairs, HALF, LANES), F32),
        ],
        scalar=scalar,
    )


def on_device(queries, keys, values, cotangent):
    features = queries.shape[1]
    assert queries.shape[0] == BLOCK
    pairs = features // LANES // 2
    lo_bits = lax.axis_size("seqlo").bit_length() - 1
    levels = Levels(lo_bits - 1)
    lo = levels.whole
    hi_bits = lax.axis_size("seqhi").bit_length() - 1
    hi = Tree(lo_bits, [BLOCK >> step for step in range(hi_bits)])
    scalar = (lax.axis_index("seqlo") % 2).astype(jnp.int32).reshape(1)
    queries, keys, values, cotangent = [
        pltpu.with_memory_space_constraint(array, pltpu.HBM)
        for array in (queries, keys, values, cotangent)
    ]
    mine_kv, f_theirs, f_mine, c_send, c_mine, rest = pack_coarse(
        pairs, keys, values, scalar
    )
    second = exchange(c_send, 1)
    finest_theirs = exchange(f_theirs, 2)
    coarse = coarsen_pair(lo, pairs, c_mine, second)
    finest = exchange(ordered(f_mine, finest_theirs), 2)
    rest = exchange(ordered(rest, coarse[0]), 1)
    half = exchange(ordered(finest_theirs, rest), 1)
    kv = rebuild(pairs, second, rest)
    send_qg, mine_qg = pack(pairs, queries, cotangent, scalar)
    qg = exchange(ordered(send_qg, half), 1)
    zs = lo.gather([None, *coarse], (finest, send_qg))
    group = coarsen_group(
        lo, hi, pairs, ordered(coarse[-1], rest), [finest, half], zs
    )
    turned = turn(pairs, mine_qg, qg)
    rs = hi.gather(group, turned)
    block_sets = [(0, 0, 0, BLOCK), (0, 1, 0, BLOCK)]
    lo_sets = [(1, 2, 0, BLOCK // 2), (1, 3, 0, BLOCK // 2)]
    for level in range(lo.bits):
        for step, row, rows in lo.held[level]:
            lo_sets.append((1 + level, 4 + step, row, rows))
    hi_sets = []
    for level in range(hi.bits):
        for step, row, rows in hi.held[level]:
            hi_sets.append((lo_bits + level, step, row, rows))
    first_in = [mine_kv, kv, finest, half, *zs]
    *kept, tops, sums, partial = attend_first(
        pairs, block_sets + lo_sets, first_in, turned
    )
    *rs_grads, o_keep, o_send, g_scaled, row_dot, dq = attend_last(
        pairs, hi_sets, rs, turned, tops, sums, partial
    )
    shapes = [(2 * pairs, *a.shape[1:]) for a in first_in]
    finest_grad, half_grad, *zs_grads, dq = attend_back(
        pairs,
        [(level, index - 2, row, rows) for level, index, row, rows in lo_sets],
        shapes[2:],
        BOTH,
        kept,
        turned,
        g_scaled,
        row_dot,
        dq,
        False,
    )
    kv_keep, kv_send, dq_keep, dq_send = attend_back(
        pairs, block_sets, shapes[:2], 0, kept, turned, g_scaled, row_dot, dq, True
    )
    rough_grads, fine_grads = take_levels(levels, pairs, zs_grads)
    half_back = exchange(half_grad, 1)
    o_back = exchange(o_send, 1)
    fine_back, finest_mine = levels.fine.scatter(fine_grads, finest_grad)
    block_second, rest_grad = take_apart(pairs, kv_send)
    split_at = rest_grad.shape[1]
    bulk = jnp.concatenate([rest_grad, dq_send.reshape(2 * pairs, HALF, LANES)], axis=1)
    bulk = exchange(ordered(bulk, o_back), 1)
    rest_back = bulk[:, :split_at]
    dq_back = bulk[:, split_at:].reshape(pairs, BLOCK, LANES)
    group_grads = hi.scatter(rs_grads)
    group_grads[-1] = ordered(
        group_grads[-1], (finest_mine, half_back, kv_send)
    )
    own_grad, rough_grads = spread_group(levels, hi, pairs, group_grads, rough_grads)
    rough_back = levels.rough.scatter(rough_grads)
    finest_theirs = exchange(ordered(half_back, rough_back[0]), 2)
    own_grad = ordered(own_grad, (rest_back, dq_back))
    second_mine, second_send = spread_pair(
        levels, pairs, own_grad, rough_back, fine_back, block_second
    )
    second_theirs = exchange(second_send, 1)
    attended, query_grad = unpack(
        pairs, (o_keep, dq_keep), (o_back, dq_back), features, scalar
    )
    key_grad, value_grad = finish(
        pairs,
        kv_keep,
        rest_back,
        (finest_mine, finest_theirs),
        (second_mine, second_theirs),
        features,
        scalar,
    )
    return attended, query_grad, key_grad, value_grad


def solution(mesh):
    spec = P(AXES, None)
    return jax.shard_map(
        on_device,
        mesh=mesh,
        in_specs=(spec,) * 4,
        out_specs=(spec,) * 4,
        check_vma=False,
    )
```

```python
import math

import jax
import jax.numpy as jnp
from jax import lax
from jax.experimental import pallas as pl
from jax.experimental.pallas import tpu as pltpu
from jax.sharding import PartitionSpec as P

HEADS = 12
BLOCK = 128
HEAD_DIM = 64
LANES = 2 * HEAD_DIM
AXES = ("seqhi", "seqlo")
VMEM_LIMIT = 20 * 1024 * 1024
F32 = jnp.float32
BF16 = jnp.bfloat16
LOG2_E = 1.0 / math.log(2.0)
SCALE = 1.0 / math.sqrt(HEAD_DIM)


def struct(*shape):
    return jax.ShapeDtypeStruct(shape, F32)


def call(kernel, operands, outs, scratch=(), scalar=None, flops=0, exps=0, where=None):
    vmem = pl.BlockSpec(memory_space=pltpu.VMEM)
    smem = pl.BlockSpec(memory_space=pltpu.SMEM)
    in_specs = [pl.BlockSpec(memory_space=where) if where else vmem] * len(operands)
    if scalar is not None:
        operands = [scalar, *operands]
        in_specs = [smem, *in_specs]
    moved = sum(4 * math.prod(a.shape) for a in [*operands, *outs])
    return pl.pallas_call(
        kernel,
        out_shape=list(outs),
        in_specs=in_specs,
        out_specs=[vmem] * len(outs),
        scratch_shapes=list(scratch),
        compiler_params=pltpu.CompilerParams(vmem_limit_bytes=VMEM_LIMIT),
        cost_estimate=pl.CostEstimate(
            flops=flops, bytes_accessed=moved, transcendentals=exps
        ),
    )(*operands)


def exchange(value, offset):
    count = lax.axis_size(AXES)
    return lax.ppermute(value, AXES, [(i, i ^ offset) for i in range(count)])


def ordered(value, after):
    return value if after is None else lax.optimization_barrier((value, after))[0]


def half_difference(ref, lead, first, count):
    even = ref[(*lead, pl.ds(first, count, stride=2), slice(None))]
    odd = ref[(*lead, pl.ds(first + 1, count, stride=2), slice(None))]
    return 0.5 * (even - odd)


def put_pairs(ref, lead, total, difference):
    count = total.shape[0]
    ref[(*lead, pl.ds(0, count, stride=2), slice(None))] = total + difference
    ref[(*lead, pl.ds(1, count, stride=2), slice(None))] = total - difference


def mean_rows(ref, lead, first, count, factor):
    total = None
    for step in range(factor):
        rows = pl.ds(first + step, count, stride=factor)
        part = ref[(*lead, rows, slice(None))]
        total = part if total is None else total + part
    return total * (1.0 / factor)


def add_spread(ref, lead, first, value, factor):
    count = value.shape[0]
    value = value * (1.0 / factor)
    for step in range(factor):
        rows = pl.ds(first + step, count, stride=factor)
        place = (*lead, rows, slice(None))
        ref[place] = ref[place] + value


class Tree:
    def __init__(self, first_bit, own_rows):
        self.bits = bits = len(own_rows)
        self.first_bit = first_bit
        self.own_rows = own_rows
        self.held = {}
        self.payload = {}
        for step in range(bits - 1, -1, -1):
            rows = self.own_rows[step]
            payload = []
            fresh = {step: [(step, 0, rows)] if rows else []}
            for level in range(step + 1, bits):
                for piece in self.held[level]:
                    payload.append(piece)
                    fresh.setdefault(level, []).append((step, rows, piece[2]))
                    rows += piece[2]
            self.payload[step] = payload
            for level, pieces in fresh.items():
                self.held[level] = self.held.get(level, []) + pieces

    def rows(self, step):
        return self.own_rows[step] + sum(piece[2] for piece in self.payload[step])

    def partner(self, value, step):
        return exchange(value, 1 << self.first_bit + step)

    def gather(self, own, after=None):
        arrived = [None] * self.bits
        for step in range(self.bits - 1, -1, -1):
            parts = [own[step]] if self.own_rows[step] else []
            for source, row, rows in self.payload[step]:
                part = arrived[source]
                whole = rows == part.shape[1]
                parts.append(part if whole else part[:, row : row + rows])
            sent = jnp.concatenate(parts, axis=1) if len(parts) > 1 else parts[0]
            if step == 0:
                sent = ordered(sent, after)
            arrived[step] = self.partner(sent, step)
        return arrived

    def scatter(self, grads, front=None):
        grads = list(grads)
        returned = []
        for step in range(self.bits):
            sent = grads[step]
            if step == 0 and front is not None:
                rows = front.shape[1]
                back = self.partner(jnp.concatenate([front, sent], axis=1), step)
                front, back = back[:, :rows], back[:, rows:]
            else:
                back = self.partner(sent, step)
            returned.append(back)
            filled = self.own_rows[step]
            for source, row, rows in self.payload[step]:
                part = back[:, filled : filled + rows]
                grads[source] = grads[source].at[:, row : row + rows].add(part)
                filled += rows
        return returned if front is None else (returned, front)


def split(value):
    high = value.astype(BF16).astype(F32)
    return high, value - high


def halves_by_head(value):
    high, low = split(value)
    first = lax.broadcasted_iota(jnp.int32, value.shape, 1) < HEAD_DIM
    one = jnp.where(first, high, pltpu.roll(low, HEAD_DIM, 1))
    two = jnp.where(first, pltpu.roll(high, HEAD_DIM, 1), low)
    return one, two


def dot(lhs, rhs, dims):
    return lax.dot_general(lhs, rhs, (dims, ((), ())), preferred_element_type=F32)


NN = ((1,), (0,))
NT = ((1,), (1,))


BOTH = 2 * BLOCK
GROUP = 3


def halves_of(sets, ins, which, pairs, pair):
    tile = which * pairs + pair
    parts = [ins[index][tile, pl.ds(row, rows), :] for _, index, row, rows in sets]
    return halves_by_head(jnp.concatenate(parts, axis=0))


def segment_levels(sets):
    levels, filled = [], 0
    for level, _, _, rows in sets:
        if filled % BLOCK == 0:
            levels.append(level)
        filled += rows
    return levels


def four_rows(value):
    high, low = split(value)
    four = jnp.concatenate([high, high, low, low], axis=0).astype(BF16)
    return four, jnp.concatenate([high, low], axis=0).astype(BF16)


def store_split(ref, lead, rows, value):
    high = value.astype(BF16)
    ref[(lead, 0, rows)] = high
    ref[(lead, 1, rows)] = (value - high.astype(F32)).astype(BF16)


def fold_rows(value):
    return value[:HEAD_DIM] + value[HEAD_DIM:]


def fold_heads(one, two):
    first = lax.broadcasted_iota(jnp.int32, one.shape, 1) < HEAD_DIM
    return jnp.where(
        first, one + pltpu.roll(one, HEAD_DIM, 1), two + pltpu.roll(two, HEAD_DIM, 1)
    )


def twice(value):
    return jnp.concatenate([value, value], axis=1)


def stacked(ref, at, rows=slice(None)):
    return jnp.concatenate([ref[at, 0, rows], ref[at, 1, rows]], axis=0)


def abreast(ref, at, rows=slice(None)):
    return jnp.concatenate([ref[at, 0, rows], ref[at, 1, rows]], axis=1)


def column_scores(levels, keys, at, q_four, s_ref):
    highest = None
    for index, level in enumerate(levels):
        rows = pl.ds(index * BLOCK, BLOCK)
        s = dot(twice(keys[at, rows]), q_four, NN)
        s = s + float(level) if level else s
        s_ref[at, rows] = s
        top = jnp.max(s.reshape(BLOCK // 8, 8, BOTH), axis=0)
        highest = top if highest is None else jnp.maximum(highest, top)
    return jnp.max(highest, axis=0, keepdims=True)


def exponents(levels, at, top, s_ref, e_ref, keep):
    summed = None
    for index in range(len(levels)):
        rows = pl.ds(index * BLOCK, BLOCK)
        e = jnp.exp2(s_ref[at, rows] - top)
        if keep:
            s_ref[at, rows] = e
        store_split(e_ref, at, rows, e)
        part = jnp.sum(e.reshape(BLOCK // 8, 8, BOTH), axis=0)
        summed = part if summed is None else summed + part
    return jnp.sum(summed, axis=0, keepdims=True)


def head_rows(ref, pair, head):
    return ref[pair, pl.ds(head * HEAD_DIM, HEAD_DIM)]


def each_group(pairs, body):
    for first in range(0, pairs, GROUP):
        group = range(first, min(first + GROUP, pairs))
        body(group, [(pair, head, 2 * pair + head) for pair in group for head in (0, 1)])


def costs(pairs, rows, products, exps=0):
    return dict(
        flops=2 * 4 * products * pairs * 2 * rows * BOTH * HEAD_DIM,
        exps=exps * pairs * 2 * rows * BOTH,
    )


def put_halves(pairs, sets, ins, group, plain, turned):
    for which in range(2):
        for pair in group:
            for head, value in enumerate(halves_of(sets, ins, which, pairs, pair)):
                plain[which][2 * pair + head] = value.astype(BF16)
                turned[which][2 * pair + head] = value.T.astype(BF16)


def attend_first(pairs, sets, operands, turned):
    total = sum(s[3] for s in sets)
    levels = segment_levels(sets)

    def kernel(turn_in, *refs):
        ins = refs[: len(operands)]
        kt, vc, e_ref, tops, sums, out, s_ref, kc, vt = refs[len(operands) :]

        def body(group, heads):
            put_halves(pairs, sets, ins, group, (kc, vc), (kt, vt))
            for pair, head, at in heads:
                q_four, _ = four_rows(head_rows(turn_in, pair, head))
                tops[at] = column_scores(levels, kc, at, q_four, s_ref)
            for _, _, at in heads:
                sums[at] = exponents(levels, at, tops[at], s_ref, e_ref, False)
            for _, _, at in heads:
                out[at] = fold_rows(dot(twice(vt[at]), stacked(e_ref, at), NN))

        each_group(pairs, body)

    heads = 2 * pairs
    outs = [
        jax.ShapeDtypeStruct((heads, LANES, total), BF16),
        jax.ShapeDtypeStruct((heads, total, LANES), BF16),
        jax.ShapeDtypeStruct((heads, 2, total, BOTH), BF16),
    ]
    outs += [struct(heads, 1, BOTH)] * 2 + [struct(heads, HEAD_DIM, BOTH)]
    return call(
        kernel,
        [turned, *operands],
        outs,
        scratch=[
            pltpu.VMEM((heads, total, BOTH), F32),
            pltpu.VMEM((heads, total, LANES), BF16),
            pltpu.VMEM((heads, LANES, total), BF16),
        ],
        **costs(pairs, total, 2, 1),
    )


def attend_last(pairs, sets, operands, turned, tops, sums, partial):
    total = sum(s[3] for s in sets)
    levels = segment_levels(sets)

    def kernel(turn_in, top_in, sum_in, part_in, *refs):
        ins = refs[: len(operands)]
        grads = refs[len(operands) : 2 * len(operands)]
        o_keep, o_send, g_out, r_out, dq_out = refs[2 * len(operands) : -7]
        s_ref, e_ref, d_ref, kc, vc, kt, vt = refs[-7:]

        def body(group, heads):
            put_halves(pairs, sets, ins, group, (kc, vc), (kt, vt))
            queries = {}
            top = {}
            for pair, head, at in heads:
                q_four, queries[at] = four_rows(head_rows(turn_in, pair, head))
                top[at] = column_scores(levels, kc, at, q_four, s_ref)
            inverse = {}
            rescale = {}
            for _, _, at in heads:
                first_top = top_in[at]
                highest = jnp.maximum(top[at], first_top)
                rescale[at] = jnp.exp2(first_top - highest)
                summed = exponents(levels, at, highest, s_ref, e_ref, True)
                inverse[at] = 1.0 / (summed + sum_in[at] * rescale[at])
            output = {}
            cotangents = {}
            row_dot = {}
            for pair, head, at in heads:
                o = fold_rows(dot(twice(vt[at]), stacked(e_ref, at), NN))
                o = (o + part_in[at] * rescale[at]) * inverse[at]
                output[at] = o
                scaled = head_rows(turn_in, pairs + pair, head) * inverse[at]
                cotangents[at] = four_rows(scaled)
                row_dot[at] = jnp.sum(o * scaled, axis=0, keepdims=True)
                g_out[at] = scaled * rescale[at]
                r_out[at] = row_dot[at] * rescale[at]
            for _, _, at in heads:
                for index in range(len(levels)):
                    rows = pl.ds(index * BLOCK, BLOCK)
                    dp = dot(twice(vc[at, rows]), cotangents[at][0], NN)
                    store_split(d_ref, at, rows, s_ref[at, rows] * (dp - row_dot[at]))
            key_grads = {}
            value_grads = {}
            for _, _, at in heads:
                value_grads[at] = dot(abreast(e_ref, at), twice(cotangents[at][1]), NT)
                key_grads[at] = dot(abreast(d_ref, at), twice(queries[at]), NT)
                dq_out[at] = fold_rows(dot(twice(kt[at]), stacked(d_ref, at), NN))
            for pair in group:
                put_grads(pairs, pair, sets, grads, key_grads, value_grads)
                both = [output[2 * pair], output[2 * pair + 1]]
                both = jnp.concatenate(both, axis=0).T
                o_keep[pair] = both[:BLOCK]
                o_send[pair] = both[BLOCK:]

        each_group(pairs, body)

    heads = 2 * pairs
    outs = [struct(*a.shape) for a in operands]
    outs += [struct(pairs, BLOCK, LANES)] * 2
    outs += [struct(heads, HEAD_DIM, BOTH), struct(heads, 1, BOTH)]
    outs.append(struct(heads, HEAD_DIM, BOTH))
    return call(
        kernel,
        [turned, tops, sums, partial, *operands],
        outs,
        scratch=[pltpu.VMEM((heads, total, BOTH), F32)]
        + [pltpu.VMEM((heads, 2, total, BOTH), BF16)] * 2
        + [pltpu.VMEM((heads, total, LANES), BF16)] * 2
        + [pltpu.VMEM((heads, LANES, total), BF16)] * 2,
        **costs(pairs, total, 6, 1),
    )


def put_grads(pairs, pair, sets, grads, key_grads, value_grads):
    for which, parts in enumerate((key_grads, value_grads)):
        both = fold_heads(parts[2 * pair], parts[2 * pair + 1])
        if which == 0:
            both = both * (1.0 / LOG2_E)
        filled = 0
        for _, index, row, rows in sets:
            piece = both[filled : filled + rows]
            grads[index][which * pairs + pair, pl.ds(row, rows), :] = piece
            filled += rows


def attend_back(pairs, sets, shapes, first, kept, turned, g_scaled, row_dot, dq, last):
    total = sum(s[3] for s in sets)
    segments = total // BLOCK

    def kernel(turn_in, kt, vc, e_ref, g_in, r_in, dq_in, *refs):
        grads = refs[: len(shapes)]
        dq_out = refs[len(shapes) : -1]
        d_ref = refs[-1]
        span = pl.ds(first, total)

        def body(group, heads):
            cotangents = {}
            for _, _, at in heads:
                g_four, cotangents[at] = four_rows(g_in[at])
                for index in range(segments):
                    rows = pl.ds(first + index * BLOCK, BLOCK)
                    dp = dot(twice(vc[at, rows]), g_four, NN)
                    e = e_ref[at, 0, rows].astype(F32) + e_ref[at, 1, rows].astype(F32)
                    place = pl.ds(index * BLOCK, BLOCK)
                    store_split(d_ref, at, place, e * (dp - r_in[at]))
            queries_grad = {}
            key_grads = {}
            value_grads = {}
            for pair, head, at in heads:
                _, q_rows = four_rows(head_rows(turn_in, pair, head))
                g_rows = cotangents[at]
                value_grads[at] = dot(abreast(e_ref, at, span), twice(g_rows), NT)
                key_grads[at] = dot(abreast(d_ref, at), twice(q_rows), NT)
                part = dot(twice(kt[at, :, span]), stacked(d_ref, at), NN)
                queries_grad[at] = fold_rows(part) + dq_in[at]
            for pair in group:
                put_grads(pairs, pair, sets, grads, key_grads, value_grads)
                both = [queries_grad[2 * pair], queries_grad[2 * pair + 1]]
                if last:
                    both = jnp.concatenate(both, axis=0).T * SCALE
                    dq_out[0][pair] = both[:BLOCK]
                    dq_out[1][pair] = both[BLOCK:]
                else:
                    for head in range(2):
                        dq_out[0][2 * pair + head] = both[head]

        each_group(pairs, body)

    outs = [struct(*shape) for shape in shapes]
    if last:
        outs += [struct(pairs, BLOCK, LANES)] * 2
    else:
        outs.append(struct(*dq.shape))
    return call(
        kernel,
        [turned, *kept, g_scaled, row_dot, dq],
        outs,
        scratch=[pltpu.VMEM((2 * pairs, 2, total, BOTH), BF16)],
        **costs(pairs, total, 4),
    )


def copy_columns(moves, ins, sems, bit):
    started = []
    for operand, theirs, column, place in moves:
        side = 1 - bit if theirs else bit
        column = side * (ins[operand].shape[1] // 2) + column
        column = pl.ds(pl.multiple_of(column, LANES), LANES)
        copy = pltpu.make_async_copy(
            ins[operand].at[:, column], place, sems.at[len(started)]
        )
        copy.start()
        started.append(copy)
    return started


def pack(pairs, first, second, scalar):
    def kernel(bit, one, two, theirs, mine, sems):
        moves = []
        for tile in range(2 * pairs):
            for out, other in ((theirs, True), (mine, False)):
                column = tile % pairs * LANES
                moves.append((tile // pairs, other, column, out.at[tile]))
        for copy in copy_columns(moves, (one, two), sems, bit[0]):
            copy.wait()

    return call(
        kernel,
        [first, second],
        [struct(2 * pairs, BLOCK, LANES)] * 2,
        scratch=[pltpu.SemaphoreType.DMA((4 * pairs,))],
        scalar=scalar,
        where=pl.ANY,
    )


QUARTER = BLOCK // 4
HALF = BLOCK // 2


def pack_coarse(pairs, keys, values, scalar):
    def kernel(bit, k, v, mine, f_theirs, f_mine, c_theirs, c_mine, rest, theirs, sems):
        moves = []
        for out, other in ((theirs, True), (mine, False)):
            for tile in range(2 * pairs):
                column = tile % pairs * LANES
                moves.append((tile // pairs, other, column, out.at[tile]))
        copies = copy_columns(moves, (k, v), sems, bit[0])
        for index, copy in enumerate(copies):
            copy.wait()
            tile = index % (2 * pairs)
            other = index < 2 * pairs
            source, finest, coarse = (
                (theirs, f_theirs, c_theirs) if other else (mine, f_mine, c_mine)
            )
            finest[tile] = mean_rows(source, (tile,), 0, HALF, 2)
            coarse[tile] = mean_rows(finest, (tile,), 0, QUARTER, 2)
            if other:
                rest[tile, :QUARTER] = half_difference(finest, (tile,), 0, QUARTER)
                rest[tile, QUARTER:] = half_difference(source, (tile,), 0, HALF)

    return call(
        kernel,
        [keys, values],
        [struct(2 * pairs, BLOCK, LANES)]
        + [struct(2 * pairs, HALF, LANES)] * 2
        + [struct(2 * pairs, QUARTER, LANES)] * 2
        + [struct(2 * pairs, QUARTER + HALF, LANES)],
        scratch=[
            pltpu.VMEM((2 * pairs, BLOCK, LANES), F32),
            pltpu.SemaphoreType.DMA((4 * pairs,)),
        ],
        scalar=scalar,
        where=pl.ANY,
    )


def rebuild(pairs, second, rest):
    def kernel(second_in, rest_in, out, finest):
        for tile in range(2 * pairs):
            put_pairs(finest, (tile,), second_in[tile], rest_in[tile, :QUARTER])
            put_pairs(out, (tile,), finest[tile], rest_in[tile, QUARTER:])

    return call(
        kernel,
        [second, rest],
        [struct(2 * pairs, BLOCK, LANES)],
        scratch=[pltpu.VMEM((2 * pairs, HALF, LANES), F32)],
    )[0]


def take_apart(pairs, block_grad):
    def kernel(block, second, rest, finest):
        for tile in range(2 * pairs):
            finest[tile] = 2.0 * mean_rows(block, (tile,), 0, HALF, 2)
            rest[tile, QUARTER:] = 2.0 * half_difference(block, (tile,), 0, HALF)
            second[tile] = 2.0 * mean_rows(finest, (tile,), 0, QUARTER, 2)
            rest[tile, :QUARTER] = 2.0 * half_difference(finest, (tile,), 0, QUARTER)

    return call(
        kernel,
        [block_grad],
        [
            struct(2 * pairs, QUARTER, LANES),
            struct(2 * pairs, QUARTER + HALF, LANES),
        ],
        scratch=[pltpu.VMEM((2 * pairs, HALF, LANES), F32)],
    )


class Levels:
    def __init__(self, bits):
        self.bits = bits
        self.rows = BLOCK >> bits
        self.differences = [
            [(m, BLOCK >> m) for m in range(bits, step, -1)] for step in range(bits)
        ]
        whole = [0] + [BLOCK >> step for step in range(1, bits)]
        self.whole = Tree(1, whole)
        self.rough = Tree(1, [0] + [self.rows] * (bits - 1))
        self.fine = Tree(1, [0] + [rows - self.rows for rows in whole[1:]])
        self.pieces = []
        for level in range(1, bits):
            trees = (self.whole, self.rough, self.fine)
            for parts in zip(*(tree.held[level] for tree in trees)):
                self.pieces.append((level, parts[0][0], *(part[1] for part in parts)))

    def scratch(self):
        shapes = [(BLOCK >> m, LANES) for m in range(1, self.bits + 1)]
        return [pltpu.VMEM(shape, F32) for shape in shapes]

    def group_pieces(self):
        pieces = []
        for index, (level, step, whole, rough, _) in enumerate(self.pieces):
            factor = 1 << self.bits - level
            place = (2 + index) * self.rows
            pieces.append((step, whole, rough, BLOCK >> level, factor, place))
        return pieces


def coarsen_pair(lo, pairs, mine, received):
    def kernel(own, got, *outs):
        for tile in range(2 * pairs):
            outs[0][tile, : BLOCK // 4] = own[tile]
            outs[0][tile, BLOCK // 4 :] = got[tile]
            for index in range(1, lo.bits):
                outs[index][tile] = mean_rows(
                    outs[index - 1], (tile,), 0, BLOCK >> index + 1, 2
                )

    outs = [struct(2 * pairs, BLOCK >> step, LANES) for step in range(1, lo.bits + 1)]
    return call(kernel, [mine, received], outs)


def group_pieces(lo):
    own = BLOCK >> lo.bits
    factor = 1 << lo.bits
    pieces = [
        (-2, 0, BLOCK // 2, factor, own),
        (-1, 0, BLOCK // 2, factor, own + own // 2),
    ]
    filled = 2 * own
    for level in range(1, lo.bits):
        factor = 1 << lo.bits - level
        for step, row, rows in lo.held[level]:
            pieces.append((step, row, rows, factor, filled))
            filled += rows // factor
    return pieces


def coarsen_group(lo, hi, pairs, own, halves, arrived):
    pieces = group_pieces(lo)

    def kernel(own_in, *refs):
        ins = refs[: 2 + lo.bits]
        outs = refs[2 + lo.bits :]
        for tile in range(2 * pairs):
            outs[0][tile, pl.ds(0, BLOCK >> lo.bits)] = own_in[tile]
            for step, row, rows, factor, place in pieces:
                count = rows // factor
                outs[0][tile, pl.ds(place, count)] = mean_rows(
                    ins[2 + step], (tile,), row, count, factor
                )
            for step in range(1, hi.bits):
                outs[step][tile] = mean_rows(
                    outs[step - 1], (tile,), 0, BLOCK >> step, 2
                )

    outs = [struct(2 * pairs, BLOCK >> step, LANES) for step in range(hi.bits)]
    return call(kernel, [own, *halves, *arrived], outs)


def turn(pairs, mine, received):
    def kernel(own, got, turned):
        for tile in range(2 * pairs):
            both = jnp.concatenate([own[tile], got[tile]], axis=0).T
            turned[tile] = both * (SCALE * LOG2_E) if tile < pairs else both

    return call(kernel, [mine, received], [struct(2 * pairs, LANES, 2 * BLOCK)])[0]


def take_levels(levels, pairs, grads):
    trees = (levels.rough, levels.fine)

    def kernel(*refs):
        ins = refs[: levels.bits]
        rough = refs[levels.bits : 2 * levels.bits]
        fine = refs[2 * levels.bits : 3 * levels.bits]
        ladder = refs[3 * levels.bits :]
        for tile in range(2 * pairs):
            for level, step, row, rough_row, fine_row in levels.pieces:
                source = ladder[level - 1]
                source[...] = ins[step][tile, pl.ds(row, BLOCK >> level)]
                fine_row += sum(rows for _, rows in levels.differences[level])
                for m, rows in reversed(levels.differences[level]):
                    fine_row -= rows
                    part = 2.0 * half_difference(source, (), 0, rows)
                    fine[step][tile, pl.ds(fine_row, rows)] = part
                    ladder[m - 1][...] = 2.0 * mean_rows(source, (), 0, rows, 2)
                    source = ladder[m - 1]
                rough[step][tile, pl.ds(rough_row, levels.rows)] = source[...]

    outs = [
        struct(2 * pairs, tree.rows(step), LANES)
        for tree in trees
        for step in range(levels.bits)
    ]
    outs = call(kernel, grads, outs, scratch=levels.scratch())
    return outs[: levels.bits], outs[levels.bits :]


def spread_group(levels, hi, pairs, group_grads, grads):
    own_rows = levels.rows

    def kernel(*refs):
        steps = refs[: hi.bits]
        ins = refs[hi.bits : hi.bits + levels.bits]
        own_out, *outs = refs[hi.bits + levels.bits : -1]
        total = refs[-1]
        for tile in range(2 * pairs):
            total[tile] = steps[0][tile, pl.ds(0, BLOCK)]
            for step in range(1, hi.bits):
                above = steps[step][tile, pl.ds(0, BLOCK >> step)]
                add_spread(total, (tile,), 0, above, 1 << step)
            own_out[tile] = total[tile, pl.ds(0, own_rows)]
            for step, _, row, _, _, place in levels.group_pieces():
                rows = pl.ds(row, own_rows)
                part = total[tile, pl.ds(place, own_rows)]
                outs[step][tile, rows] = ins[step][tile, rows] + part
            outs[0][tile, pl.ds(ins[0].shape[1], own_rows)] = total[
                tile, pl.ds(own_rows, own_rows)
            ]

    shapes = [list(a.shape) for a in grads]
    shapes[0][1] += own_rows
    outs = [struct(2 * pairs, own_rows, LANES)] + [struct(*shape) for shape in shapes]
    own, *grads = call(
        kernel,
        [*group_grads, *grads],
        outs,
        scratch=[pltpu.VMEM((2 * pairs, BLOCK, LANES), F32)],
    )
    return own, grads


def spread_pair(levels, pairs, own_grad, rough, fine, block_second):
    own_rows = levels.rows

    def kernel(own, block, *refs):
        rough_in = refs[: levels.bits]
        fine_in = refs[levels.bits : 2 * levels.bits]
        mine, theirs, *ladder = refs[2 * levels.bits :]
        last = pl.ds(rough_in[0].shape[1] - own_rows, own_rows)
        for tile in range(2 * pairs):
            above = own[tile] + rough_in[0][tile, last]
            for step in range(1, levels.bits):
                above = above + rough_in[step][tile, pl.ds(0, own_rows)]
            filled = 0
            for m, rows in levels.differences[1]:
                part = fine_in[1][tile, pl.ds(filled, rows)]
                for step in range(2, min(m, levels.bits)):
                    part = part + fine_in[step][tile, pl.ds(filled, rows)]
                filled += rows
                put_pairs(ladder[m - 2], (), 0.5 * above, 0.5 * part)
                above = ladder[m - 2][...]
            mine[tile] = above[:QUARTER]
            theirs[tile] = above[QUARTER:] + block[tile]

    return call(
        kernel,
        [own_grad, block_second, *rough, *fine],
        [struct(2 * pairs, QUARTER, LANES)] * 2,
        scratch=levels.scratch(),
    )


def unpack(pairs, kept, arrived, features, scalar):
    def kernel(bit, *refs):
        outs = refs[4:]
        for which in range(2):
            for pair in range(pairs):
                for side, ref in ((bit[0], refs[which]), (1 - bit[0], refs[2 + which])):
                    column = side * (features // 2) + pair * LANES
                    column = pl.ds(pl.multiple_of(column, LANES), LANES)
                    outs[which][:, column] = ref[pair]

    return call(kernel, [*kept, *arrived], [struct(BLOCK, features)] * 2, scalar=scalar)


def finish(pairs, kept, rest, finest, seconds, features, scalar):
    def kernel(bit, kept_in, rest_in, f_mine, f_theirs, s_mine, s_theirs, *refs):
        outs, total, middle = refs[:2], refs[2], refs[3]
        for tile in range(2 * pairs):
            out = outs[tile // pairs]
            column = tile % pairs * LANES
            at = (tile,)
            total[tile] = kept_in[tile]
            add_spread(total, at, 0, f_mine[tile], 2)
            add_spread(total, at, 0, s_mine[tile], 4)
            place = bit[0] * (features // 2) + column
            out[:, pl.ds(pl.multiple_of(place, LANES), LANES)] = total[tile]
            put_pairs(middle, at, 0.5 * s_theirs[tile], 0.5 * rest_in[tile, :QUARTER])
            first = 0.5 * (middle[tile] + f_theirs[tile])
            put_pairs(total, at, first, 0.5 * rest_in[tile, QUARTER:])
            place = (1 - bit[0]) * (features // 2) + column
            out[:, pl.ds(pl.multiple_of(place, LANES), LANES)] = total[tile]

    return call(
        kernel,
        [kept, rest, *finest, *seconds],
        [struct(BLOCK, features)] * 2,
        scratch=[
            pltpu.VMEM((2 * pairs, BLOCK, LANES), F32),
            pltpu.VMEM((2 * pairs, HALF, LANES), F32),
        ],
        scalar=scalar,
    )


def on_device(queries, keys, values, cotangent):
    features = queries.shape[1]
    assert queries.shape[0] == BLOCK
    pairs = features // LANES // 2
    lo_bits = lax.axis_size("seqlo").bit_length() - 1
    levels = Levels(lo_bits - 1)
    lo = levels.whole
    hi_bits = lax.axis_size("seqhi").bit_length() - 1
    hi = Tree(lo_bits, [BLOCK >> step for step in range(hi_bits)])
    scalar = (lax.axis_index("seqlo") % 2).astype(jnp.int32).reshape(1)
    queries, keys, values, cotangent = [
        pltpu.with_memory_space_constraint(array, pltpu.HBM)
        for array in (queries, keys, values, cotangent)
    ]
    mine_kv, f_theirs, f_mine, c_send, c_mine, rest = pack_coarse(
        pairs, keys, values, scalar
    )
    second = exchange(c_send, 1)
    finest_theirs = exchange(f_theirs, 2)
    coarse = coarsen_pair(lo, pairs, c_mine, second)
    finest = exchange(ordered(f_mine, finest_theirs), 2)
    rest = exchange(ordered(rest, coarse[0]), 1)
    half = exchange(ordered(finest_theirs, rest), 1)
    kv = rebuild(pairs, second, rest)
    send_qg, mine_qg = pack(pairs, queries, cotangent, scalar)
    qg = exchange(ordered(send_qg, half), 1)
    zs = lo.gather([None, *coarse], (finest, send_qg))
    group = coarsen_group(
        lo, hi, pairs, ordered(coarse[-1], rest), [finest, half], zs
    )
    turned = turn(pairs, mine_qg, qg)
    rs = hi.gather(group, turned)
    block_sets = [(0, 0, 0, BLOCK), (0, 1, 0, BLOCK)]
    lo_sets = [(1, 2, 0, BLOCK // 2), (1, 3, 0, BLOCK // 2)]
    for level in range(lo.bits):
        for step, row, rows in lo.held[level]:
            lo_sets.append((1 + level, 4 + step, row, rows))
    hi_sets = []
    for level in range(hi.bits):
        for step, row, rows in hi.held[level]:
            hi_sets.append((lo_bits + level, step, row, rows))
    first_in = [mine_kv, kv, finest, half, *zs]
    *kept, tops, sums, partial = attend_first(
        pairs, block_sets + lo_sets, first_in, turned
    )
    *rs_grads, o_keep, o_send, g_scaled, row_dot, dq = attend_last(
        pairs, hi_sets, rs, turned, tops, sums, partial
    )
    shapes = [(2 * pairs, *a.shape[1:]) for a in first_in]
    finest_grad, half_grad, *zs_grads, dq = attend_back(
        pairs,
        [(level, index - 2, row, rows) for level, index, row, rows in lo_sets],
        shapes[2:],
        BOTH,
        kept,
        turned,
        g_scaled,
        row_dot,
        dq,
        False,
    )
    kv_keep, kv_send, dq_keep, dq_send = attend_back(
        pairs, block_sets, shapes[:2], 0, kept, turned, g_scaled, row_dot, dq, True
    )
    rough_grads, fine_grads = take_levels(levels, pairs, zs_grads)
    group_grads = hi.scatter(rs_grads)
    half_back = exchange(ordered(half_grad, group_grads[0]), 1)
    o_back = exchange(o_send, 1)
    fine_back, finest_mine = levels.fine.scatter(fine_grads, finest_grad)
    block_second, rest_grad = take_apart(pairs, kv_send)
    split_at = rest_grad.shape[1]
    bulk = jnp.concatenate([rest_grad, dq_send.reshape(2 * pairs, HALF, LANES)], axis=1)
    bulk = exchange(ordered(bulk, o_back), 1)
    rest_back = bulk[:, :split_at]
    dq_back = bulk[:, split_at:].reshape(pairs, BLOCK, LANES)
    group_grads[-1] = ordered(group_grads[-1], kv_send)
    own_grad, rough_grads = spread_group(levels, hi, pairs, group_grads, rough_grads)
    rough_back = levels.rough.scatter(rough_grads)
    finest_theirs = exchange(ordered(half_back, rough_back[0]), 2)
    own_grad = ordered(own_grad, (rest_back, dq_back))
    second_mine, second_send = spread_pair(
        levels, pairs, own_grad, rough_back, fine_back, block_second
    )
    second_theirs = exchange(second_send, 1)
    attended, query_grad = unpack(
        pairs, (o_keep, dq_keep), (o_back, dq_back), features, scalar
    )
    key_grad, value_grad = finish(
        pairs,
        kv_keep,
        rest_back,
        (finest_mine, finest_theirs),
        (second_mine, second_theirs),
        features,
        scalar,
    )
    return attended, query_grad, key_grad, value_grad


def solution(mesh):
    spec = P(AXES, None)
    return jax.shard_map(
        on_device,
        mesh=mesh,
        in_specs=(spec,) * 4,
        out_specs=(spec,) * 4,
        check_vma=False,
    )
```

```python
import math

import jax
import jax.numpy as jnp
from jax import lax
from jax.experimental import pallas as pl
from jax.experimental.pallas import tpu as pltpu
from jax.sharding import PartitionSpec as P

HEADS = 12
BLOCK = 128
HEAD_DIM = 64
LANES = 2 * HEAD_DIM
AXES = ("seqhi", "seqlo")
VMEM_LIMIT = 20 * 1024 * 1024
F32 = jnp.float32
BF16 = jnp.bfloat16
LOG2_E = 1.0 / math.log(2.0)
SCALE = 1.0 / math.sqrt(HEAD_DIM)


def struct(*shape):
    return jax.ShapeDtypeStruct(shape, F32)


def call(kernel, operands, outs, scratch=(), scalar=None, flops=0, exps=0, where=None):
    vmem = pl.BlockSpec(memory_space=pltpu.VMEM)
    smem = pl.BlockSpec(memory_space=pltpu.SMEM)
    in_specs = [pl.BlockSpec(memory_space=where) if where else vmem] * len(operands)
    if scalar is not None:
        operands = [scalar, *operands]
        in_specs = [smem, *in_specs]
    moved = sum(4 * math.prod(a.shape) for a in [*operands, *outs])
    return pl.pallas_call(
        kernel,
        out_shape=list(outs),
        in_specs=in_specs,
        out_specs=[vmem] * len(outs),
        scratch_shapes=list(scratch),
        compiler_params=pltpu.CompilerParams(vmem_limit_bytes=VMEM_LIMIT),
        cost_estimate=pl.CostEstimate(
            flops=flops, bytes_accessed=moved, transcendentals=exps
        ),
    )(*operands)


def exchange(value, offset):
    count = lax.axis_size(AXES)
    return lax.ppermute(value, AXES, [(i, i ^ offset) for i in range(count)])


def ordered(value, after):
    return value if after is None else lax.optimization_barrier((value, after))[0]


def half_difference(ref, lead, first, count):
    even = ref[(*lead, pl.ds(first, count, stride=2), slice(None))]
    odd = ref[(*lead, pl.ds(first + 1, count, stride=2), slice(None))]
    return 0.5 * (even - odd)


def put_pairs(ref, lead, total, difference):
    count = total.shape[0]
    ref[(*lead, pl.ds(0, count, stride=2), slice(None))] = total + difference
    ref[(*lead, pl.ds(1, count, stride=2), slice(None))] = total - difference


def mean_rows(ref, lead, first, count, factor):
    total = None
    for step in range(factor):
        rows = pl.ds(first + step, count, stride=factor)
        part = ref[(*lead, rows, slice(None))]
        total = part if total is None else total + part
    return total * (1.0 / factor)


def add_spread(ref, lead, first, value, factor):
    count = value.shape[0]
    value = value * (1.0 / factor)
    for step in range(factor):
        rows = pl.ds(first + step, count, stride=factor)
        place = (*lead, rows, slice(None))
        ref[place] = ref[place] + value


class Tree:
    def __init__(self, first_bit, own_rows):
        self.bits = bits = len(own_rows)
        self.first_bit = first_bit
        self.own_rows = own_rows
        self.held = {}
        self.payload = {}
        for step in range(bits - 1, -1, -1):
            rows = self.own_rows[step]
            payload = []
            fresh = {step: [(step, 0, rows)] if rows else []}
            for level in range(step + 1, bits):
                for piece in self.held[level]:
                    payload.append(piece)
                    fresh.setdefault(level, []).append((step, rows, piece[2]))
                    rows += piece[2]
            self.payload[step] = payload
            for level, pieces in fresh.items():
                self.held[level] = self.held.get(level, []) + pieces

    def rows(self, step):
        return self.own_rows[step] + sum(piece[2] for piece in self.payload[step])

    def partner(self, value, step):
        return exchange(value, 1 << self.first_bit + step)

    def gather(self, own, after=None):
        arrived = [None] * self.bits
        for step in range(self.bits - 1, -1, -1):
            parts = [own[step]] if self.own_rows[step] else []
            for source, row, rows in self.payload[step]:
                part = arrived[source]
                whole = rows == part.shape[1]
                parts.append(part if whole else part[:, row : row + rows])
            sent = jnp.concatenate(parts, axis=1) if len(parts) > 1 else parts[0]
            if step == 0:
                sent = ordered(sent, after)
            arrived[step] = self.partner(sent, step)
        return arrived

    def scatter(self, grads, front=None):
        grads = list(grads)
        returned = []
        for step in range(self.bits):
            sent = grads[step]
            if step == 0 and front is not None:
                rows = front.shape[1]
                back = self.partner(jnp.concatenate([front, sent], axis=1), step)
                front, back = back[:, :rows], back[:, rows:]
            else:
                back = self.partner(sent, step)
            returned.append(back)
            filled = self.own_rows[step]
            for source, row, rows in self.payload[step]:
                part = back[:, filled : filled + rows]
                grads[source] = grads[source].at[:, row : row + rows].add(part)
                filled += rows
        return returned if front is None else (returned, front)


def split(value):
    high = value.astype(BF16).astype(F32)
    return high, value - high


def halves_by_head(value):
    high, low = split(value)
    first = lax.broadcasted_iota(jnp.int32, value.shape, 1) < HEAD_DIM
    one = jnp.where(first, high, pltpu.roll(low, HEAD_DIM, 1))
    two = jnp.where(first, pltpu.roll(high, HEAD_DIM, 1), low)
    return one, two


def dot(lhs, rhs, dims):
    return lax.dot_general(lhs, rhs, (dims, ((), ())), preferred_element_type=F32)


NN = ((1,), (0,))
NT = ((1,), (1,))


BOTH = 2 * BLOCK
GROUP = 3


def halves_of(sets, ins, which, pairs, pair):
    tile = which * pairs + pair
    parts = [ins[index][tile, pl.ds(row, rows), :] for _, index, row, rows in sets]
    return halves_by_head(jnp.concatenate(parts, axis=0))


def segment_levels(sets):
    levels, filled = [], 0
    for level, _, _, rows in sets:
        if filled % BLOCK == 0:
            levels.append(level)
        filled += rows
    return levels


def four_rows(value):
    high, low = split(value)
    four = jnp.concatenate([high, high, low, low], axis=0).astype(BF16)
    return four, jnp.concatenate([high, low], axis=0).astype(BF16)


def store_split(ref, lead, rows, value):
    high = value.astype(BF16)
    ref[(lead, 0, rows)] = high
    ref[(lead, 1, rows)] = (value - high.astype(F32)).astype(BF16)


def fold_rows(value):
    return value[:HEAD_DIM] + value[HEAD_DIM:]


def fold_heads(one, two):
    first = lax.broadcasted_iota(jnp.int32, one.shape, 1) < HEAD_DIM
    return jnp.where(
        first, one + pltpu.roll(one, HEAD_DIM, 1), two + pltpu.roll(two, HEAD_DIM, 1)
    )


def twice(value):
    return jnp.concatenate([value, value], axis=1)


def stacked(ref, at, rows=slice(None)):
    return jnp.concatenate([ref[at, 0, rows], ref[at, 1, rows]], axis=0)


def abreast(ref, at, rows=slice(None)):
    return jnp.concatenate([ref[at, 0, rows], ref[at, 1, rows]], axis=1)


def column_scores(levels, keys, at, q_four, s_ref):
    highest = None
    for index, level in enumerate(levels):
        rows = pl.ds(index * BLOCK, BLOCK)
        s = dot(twice(keys[at, rows]), q_four, NN)
        s = s + float(level) if level else s
        s_ref[at, rows] = s
        top = jnp.max(s.reshape(BLOCK // 8, 8, BOTH), axis=0)
        highest = top if highest is None else jnp.maximum(highest, top)
    return jnp.max(highest, axis=0, keepdims=True)


def exponents(levels, at, top, s_ref, e_ref, keep):
    summed = None
    for index in range(len(levels)):
        rows = pl.ds(index * BLOCK, BLOCK)
        e = jnp.exp2(s_ref[at, rows] - top)
        if keep:
            s_ref[at, rows] = e
        store_split(e_ref, at, rows, e)
        part = jnp.sum(e.reshape(BLOCK // 8, 8, BOTH), axis=0)
        summed = part if summed is None else summed + part
    return jnp.sum(summed, axis=0, keepdims=True)


def head_rows(ref, pair, head):
    return ref[pair, pl.ds(head * HEAD_DIM, HEAD_DIM)]


def each_group(pairs, body):
    for first in range(0, pairs, GROUP):
        group = range(first, min(first + GROUP, pairs))
        body(group, [(pair, head, 2 * pair + head) for pair in group for head in (0, 1)])


def costs(pairs, rows, products, exps=0):
    return dict(
        flops=2 * 4 * products * pairs * 2 * rows * BOTH * HEAD_DIM,
        exps=exps * pairs * 2 * rows * BOTH,
    )


def put_halves(pairs, sets, ins, group, plain, turned):
    for which in range(2):
        for pair in group:
            for head, value in enumerate(halves_of(sets, ins, which, pairs, pair)):
                plain[which][2 * pair + head] = value.astype(BF16)
                turned[which][2 * pair + head] = value.T.astype(BF16)


def attend_first(pairs, sets, operands, turned):
    total = sum(s[3] for s in sets)
    levels = segment_levels(sets)

    def kernel(turn_in, *refs):
        ins = refs[: len(operands)]
        kt, vc, e_ref, tops, sums, out, s_ref, kc, vt = refs[len(operands) :]

        def body(group, heads):
            put_halves(pairs, sets, ins, group, (kc, vc), (kt, vt))
            for pair, head, at in heads:
                q_four, _ = four_rows(head_rows(turn_in, pair, head))
                tops[at] = column_scores(levels, kc, at, q_four, s_ref)
            for _, _, at in heads:
                sums[at] = exponents(levels, at, tops[at], s_ref, e_ref, False)
            for _, _, at in heads:
                out[at] = fold_rows(dot(twice(vt[at]), stacked(e_ref, at), NN))

        each_group(pairs, body)

    heads = 2 * pairs
    outs = [
        jax.ShapeDtypeStruct((heads, LANES, total), BF16),
        jax.ShapeDtypeStruct((heads, total, LANES), BF16),
        jax.ShapeDtypeStruct((heads, 2, total, BOTH), BF16),
    ]
    outs += [struct(heads, 1, BOTH)] * 2 + [struct(heads, HEAD_DIM, BOTH)]
    return call(
        kernel,
        [turned, *operands],
        outs,
        scratch=[
            pltpu.VMEM((heads, total, BOTH), F32),
            pltpu.VMEM((heads, total, LANES), BF16),
            pltpu.VMEM((heads, LANES, total), BF16),
        ],
        **costs(pairs, total, 2, 1),
    )


def attend_last(pairs, sets, operands, turned, tops, sums, partial):
    total = sum(s[3] for s in sets)
    levels = segment_levels(sets)

    def kernel(turn_in, top_in, sum_in, part_in, *refs):
        ins = refs[: len(operands)]
        grads = refs[len(operands) : 2 * len(operands)]
        o_keep, o_send, g_out, r_out, kt, d_ref = refs[2 * len(operands) : -5]
        s_ref, e_ref, kc, vc, vt = refs[-5:]

        def body(group, heads):
            put_halves(pairs, sets, ins, group, (kc, vc), (kt, vt))
            queries = {}
            top = {}
            for pair, head, at in heads:
                q_four, queries[at] = four_rows(head_rows(turn_in, pair, head))
                top[at] = column_scores(levels, kc, at, q_four, s_ref)
            inverse = {}
            rescale = {}
            for _, _, at in heads:
                first_top = top_in[at]
                highest = jnp.maximum(top[at], first_top)
                rescale[at] = jnp.exp2(first_top - highest)
                summed = exponents(levels, at, highest, s_ref, e_ref, True)
                inverse[at] = 1.0 / (summed + sum_in[at] * rescale[at])
            output = {}
            cotangents = {}
            row_dot = {}
            for pair, head, at in heads:
                o = fold_rows(dot(twice(vt[at]), stacked(e_ref, at), NN))
                o = (o + part_in[at] * rescale[at]) * inverse[at]
                output[at] = o
                scaled = head_rows(turn_in, pairs + pair, head) * inverse[at]
                cotangents[at] = four_rows(scaled)
                row_dot[at] = jnp.sum(o * scaled, axis=0, keepdims=True)
                g_out[at] = scaled * rescale[at]
                r_out[at] = row_dot[at] * rescale[at]
            for _, _, at in heads:
                for index in range(len(levels)):
                    rows = pl.ds(index * BLOCK, BLOCK)
                    dp = dot(twice(vc[at, rows]), cotangents[at][0], NN)
                    store_split(d_ref, at, rows, s_ref[at, rows] * (dp - row_dot[at]))
            key_grads = {}
            value_grads = {}
            for _, _, at in heads:
                value_grads[at] = dot(abreast(e_ref, at), twice(cotangents[at][1]), NT)
                key_grads[at] = dot(abreast(d_ref, at), twice(queries[at]), NT)
            for pair in group:
                put_grads(pairs, pair, sets, grads, key_grads, value_grads)
                both = [output[2 * pair], output[2 * pair + 1]]
                both = jnp.concatenate(both, axis=0).T
                o_keep[pair] = both[:BLOCK]
                o_send[pair] = both[BLOCK:]

        each_group(pairs, body)

    heads = 2 * pairs
    outs = [struct(*a.shape) for a in operands]
    outs += [struct(pairs, BLOCK, LANES)] * 2
    outs += [struct(heads, HEAD_DIM, BOTH), struct(heads, 1, BOTH)]
    outs.append(jax.ShapeDtypeStruct((heads, LANES, total), BF16))
    outs.append(jax.ShapeDtypeStruct((heads, 2, total, BOTH), BF16))
    return call(
        kernel,
        [turned, tops, sums, partial, *operands],
        outs,
        scratch=[pltpu.VMEM((heads, total, BOTH), F32)]
        + [pltpu.VMEM((heads, 2, total, BOTH), BF16)]
        + [pltpu.VMEM((heads, total, LANES), BF16)] * 2
        + [pltpu.VMEM((heads, LANES, total), BF16)],
        **costs(pairs, total, 5, 1),
    )


def put_grads(pairs, pair, sets, grads, key_grads, value_grads):
    for which, parts in enumerate((key_grads, value_grads)):
        both = fold_heads(parts[2 * pair], parts[2 * pair + 1])
        if which == 0:
            both = both * (1.0 / LOG2_E)
        filled = 0
        for _, index, row, rows in sets:
            piece = both[filled : filled + rows]
            grads[index][which * pairs + pair, pl.ds(row, rows), :] = piece
            filled += rows


def attend_back(pairs, sets, shapes, first, kept, turned, g_scaled, row_dot, others):
    total = sum(s[3] for s in sets)
    segments = total // BLOCK

    def kernel(turn_in, kt, vc, e_ref, g_in, r_in, *refs):
        other_in = refs[: len(others)]
        grads = refs[len(others) : len(others) + len(shapes)]
        dq_out = refs[len(others) + len(shapes) : -1]
        d_ref = refs[-1]
        span = pl.ds(first, total)

        def body(group, heads):
            cotangents = {}
            for _, _, at in heads:
                g_four, cotangents[at] = four_rows(g_in[at])
                for index in range(segments):
                    rows = pl.ds(first + index * BLOCK, BLOCK)
                    dp = dot(twice(vc[at, rows]), g_four, NN)
                    e = e_ref[at, 0, rows].astype(F32) + e_ref[at, 1, rows].astype(F32)
                    place = pl.ds(index * BLOCK, BLOCK)
                    store_split(d_ref, at, place, e * (dp - r_in[at]))
            queries_grad = {}
            key_grads = {}
            value_grads = {}
            for pair, head, at in heads:
                _, q_rows = four_rows(head_rows(turn_in, pair, head))
                g_rows = cotangents[at]
                value_grads[at] = dot(abreast(e_ref, at, span), twice(g_rows), NT)
                key_grads[at] = dot(abreast(d_ref, at), twice(q_rows), NT)
                if others:
                    d_lo, kt_hi, d_hi = other_in
                    part = dot(twice(kt[at, :, span]), stacked(d_ref, at), NN)
                    part += dot(twice(kt[at, :, total:]), stacked(d_lo, at), NN)
                    part += dot(twice(kt_hi[at]), stacked(d_hi, at), NN)
                    queries_grad[at] = fold_rows(part)
            for pair in group:
                put_grads(pairs, pair, sets, grads, key_grads, value_grads)
                if others:
                    both = [queries_grad[2 * pair], queries_grad[2 * pair + 1]]
                    both = jnp.concatenate(both, axis=0).T * SCALE
                    dq_out[0][pair] = both[:BLOCK]
                    dq_out[1][pair] = both[BLOCK:]

        each_group(pairs, body)

    outs = [struct(*shape) for shape in shapes]
    scratch = []
    if others:
        outs += [struct(pairs, BLOCK, LANES)] * 2
        scratch.append(pltpu.VMEM((2 * pairs, 2, total, BOTH), BF16))
    else:
        outs.append(jax.ShapeDtypeStruct((2 * pairs, 2, total, BOTH), BF16))
    return call(
        kernel,
        [turned, *kept, g_scaled, row_dot, *others],
        outs,
        scratch=scratch,
        **costs(pairs, total, 4),
    )


def copy_columns(moves, ins, sems, bit):
    started = []
    for operand, theirs, column, place in moves:
        side = 1 - bit if theirs else bit
        column = side * (ins[operand].shape[1] // 2) + column
        column = pl.ds(pl.multiple_of(column, LANES), LANES)
        copy = pltpu.make_async_copy(
            ins[operand].at[:, column], place, sems.at[len(started)]
        )
        copy.start()
        started.append(copy)
    return started


def pack(pairs, first, second, scalar):
    def kernel(bit, one, two, theirs, mine, sems):
        moves = []
        for tile in range(2 * pairs):
            for out, other in ((theirs, True), (mine, False)):
                column = tile % pairs * LANES
                moves.append((tile // pairs, other, column, out.at[tile]))
        for copy in copy_columns(moves, (one, two), sems, bit[0]):
            copy.wait()

    return call(
        kernel,
        [first, second],
        [struct(2 * pairs, BLOCK, LANES)] * 2,
        scratch=[pltpu.SemaphoreType.DMA((4 * pairs,))],
        scalar=scalar,
        where=pl.ANY,
    )


QUARTER = BLOCK // 4
HALF = BLOCK // 2


def pack_theirs(pairs, keys, values, scalar):
    def kernel(bit, k, v, finest, coarse, rest, block, sems):
        moves = []
        for tile in range(2 * pairs):
            moves.append((tile // pairs, True, tile % pairs * LANES, block.at[tile]))
        copies = copy_columns(moves, (k, v), sems, bit[0])
        for tile, copy in enumerate(copies):
            copy.wait()
            finest[tile] = mean_rows(block, (tile,), 0, HALF, 2)
            coarse[tile] = mean_rows(finest, (tile,), 0, QUARTER, 2)
            rest[tile, :QUARTER] = half_difference(finest, (tile,), 0, QUARTER)
            rest[tile, QUARTER:] = half_difference(block, (tile,), 0, HALF)

    return call(
        kernel,
        [keys, values],
        [
            struct(2 * pairs, HALF, LANES),
            struct(2 * pairs, QUARTER, LANES),
            struct(2 * pairs, QUARTER + HALF, LANES),
        ],
        scratch=[
            pltpu.VMEM((2 * pairs, BLOCK, LANES), F32),
            pltpu.SemaphoreType.DMA((2 * pairs,)),
        ],
        scalar=scalar,
        where=pl.ANY,
    )


def pack_mine(pairs, keys, values, scalar):
    def kernel(bit, k, v, block, finest, coarse, sems):
        moves = []
        for tile in range(2 * pairs):
            moves.append((tile // pairs, False, tile % pairs * LANES, block.at[tile]))
        copies = copy_columns(moves, (k, v), sems, bit[0])
        for tile, copy in enumerate(copies):
            copy.wait()
            finest[tile] = mean_rows(block, (tile,), 0, HALF, 2)
            coarse[tile] = mean_rows(finest, (tile,), 0, QUARTER, 2)

    return call(
        kernel,
        [keys, values],
        [
            struct(2 * pairs, BLOCK, LANES),
            struct(2 * pairs, HALF, LANES),
            struct(2 * pairs, QUARTER, LANES),
        ],
        scratch=[pltpu.SemaphoreType.DMA((2 * pairs,))],
        scalar=scalar,
        where=pl.ANY,
    )


def rebuild(pairs, second, rest):
    def kernel(second_in, rest_in, out, finest):
        for tile in range(2 * pairs):
            put_pairs(finest, (tile,), second_in[tile], rest_in[tile, :QUARTER])
            put_pairs(out, (tile,), finest[tile], rest_in[tile, QUARTER:])

    return call(
        kernel,
        [second, rest],
        [struct(2 * pairs, BLOCK, LANES)],
        scratch=[pltpu.VMEM((2 * pairs, HALF, LANES), F32)],
    )[0]


def take_apart(pairs, block_grad):
    def kernel(block, second, rest, finest):
        for tile in range(2 * pairs):
            finest[tile] = 2.0 * mean_rows(block, (tile,), 0, HALF, 2)
            rest[tile, QUARTER:] = 2.0 * half_difference(block, (tile,), 0, HALF)
            second[tile] = 2.0 * mean_rows(finest, (tile,), 0, QUARTER, 2)
            rest[tile, :QUARTER] = 2.0 * half_difference(finest, (tile,), 0, QUARTER)

    return call(
        kernel,
        [block_grad],
        [
            struct(2 * pairs, QUARTER, LANES),
            struct(2 * pairs, QUARTER + HALF, LANES),
        ],
        scratch=[pltpu.VMEM((2 * pairs, HALF, LANES), F32)],
    )


class Levels:
    def __init__(self, bits):
        self.bits = bits
        self.rows = BLOCK >> bits
        self.differences = [
            [(m, BLOCK >> m) for m in range(bits, step, -1)] for step in range(bits)
        ]
        whole = [0] + [BLOCK >> step for step in range(1, bits)]
        self.whole = Tree(1, whole)
        self.rough = Tree(1, [0] + [self.rows] * (bits - 1))
        self.fine = Tree(1, [0] + [rows - self.rows for rows in whole[1:]])
        self.pieces = []
        for level in range(1, bits):
            trees = (self.whole, self.rough, self.fine)
            for parts in zip(*(tree.held[level] for tree in trees)):
                self.pieces.append((level, parts[0][0], *(part[1] for part in parts)))

    def scratch(self):
        shapes = [(BLOCK >> m, LANES) for m in range(1, self.bits + 1)]
        return [pltpu.VMEM(shape, F32) for shape in shapes]

    def group_pieces(self):
        pieces = []
        for index, (level, step, whole, rough, _) in enumerate(self.pieces):
            factor = 1 << self.bits - level
            place = (2 + index) * self.rows
            pieces.append((step, whole, rough, BLOCK >> level, factor, place))
        return pieces


def coarsen_pair(lo, pairs, mine, received):
    def kernel(own, got, *outs):
        for tile in range(2 * pairs):
            outs[0][tile, : BLOCK // 4] = own[tile]
            outs[0][tile, BLOCK // 4 :] = got[tile]
            for index in range(1, lo.bits):
                outs[index][tile] = mean_rows(
                    outs[index - 1], (tile,), 0, BLOCK >> index + 1, 2
                )

    outs = [struct(2 * pairs, BLOCK >> step, LANES) for step in range(1, lo.bits + 1)]
    return call(kernel, [mine, received], outs)


def group_pieces(lo):
    own = BLOCK >> lo.bits
    factor = 1 << lo.bits
    pieces = [
        (-2, 0, BLOCK // 2, factor, own),
        (-1, 0, BLOCK // 2, factor, own + own // 2),
    ]
    filled = 2 * own
    for level in range(1, lo.bits):
        factor = 1 << lo.bits - level
        for step, row, rows in lo.held[level]:
            pieces.append((step, row, rows, factor, filled))
            filled += rows // factor
    return pieces


def coarsen_group(lo, hi, pairs, own, halves, arrived):
    pieces = group_pieces(lo)

    def kernel(own_in, *refs):
        ins = refs[: 2 + lo.bits]
        outs = refs[2 + lo.bits :]
        for tile in range(2 * pairs):
            outs[0][tile, pl.ds(0, BLOCK >> lo.bits)] = own_in[tile]
            for step, row, rows, factor, place in pieces:
                count = rows // factor
                outs[0][tile, pl.ds(place, count)] = mean_rows(
                    ins[2 + step], (tile,), row, count, factor
                )
            for step in range(1, hi.bits):
                outs[step][tile] = mean_rows(
                    outs[step - 1], (tile,), 0, BLOCK >> step, 2
                )

    outs = [struct(2 * pairs, BLOCK >> step, LANES) for step in range(hi.bits)]
    return call(kernel, [own, *halves, *arrived], outs)


def turn(pairs, mine, received):
    def kernel(own, got, turned):
        for tile in range(2 * pairs):
            both = jnp.concatenate([own[tile], got[tile]], axis=0).T
            turned[tile] = both * (SCALE * LOG2_E) if tile < pairs else both

    return call(kernel, [mine, received], [struct(2 * pairs, LANES, 2 * BLOCK)])[0]


def take_levels(levels, pairs, grads):
    trees = (levels.rough, levels.fine)

    def kernel(*refs):
        ins = refs[: levels.bits]
        rough = refs[levels.bits : 2 * levels.bits]
        fine = refs[2 * levels.bits : 3 * levels.bits]
        ladder = refs[3 * levels.bits :]
        for tile in range(2 * pairs):
            for level, step, row, rough_row, fine_row in levels.pieces:
                source = ladder[level - 1]
                source[...] = ins[step][tile, pl.ds(row, BLOCK >> level)]
                fine_row += sum(rows for _, rows in levels.differences[level])
                for m, rows in reversed(levels.differences[level]):
                    fine_row -= rows
                    part = 2.0 * half_difference(source, (), 0, rows)
                    fine[step][tile, pl.ds(fine_row, rows)] = part
                    ladder[m - 1][...] = 2.0 * mean_rows(source, (), 0, rows, 2)
                    source = ladder[m - 1]
                rough[step][tile, pl.ds(rough_row, levels.rows)] = source[...]

    outs = [
        struct(2 * pairs, tree.rows(step), LANES)
        for tree in trees
        for step in range(levels.bits)
    ]
    outs = call(kernel, grads, outs, scratch=levels.scratch())
    return outs[: levels.bits], outs[levels.bits :]


def spread_group(levels, hi, pairs, group_grads, grads):
    own_rows = levels.rows

    def kernel(*refs):
        steps = refs[: hi.bits]
        ins = refs[hi.bits : hi.bits + levels.bits]
        own_out, *outs = refs[hi.bits + levels.bits : -1]
        total = refs[-1]
        for tile in range(2 * pairs):
            total[tile] = steps[0][tile, pl.ds(0, BLOCK)]
            for step in range(1, hi.bits):
                above = steps[step][tile, pl.ds(0, BLOCK >> step)]
                add_spread(total, (tile,), 0, above, 1 << step)
            own_out[tile] = total[tile, pl.ds(0, own_rows)]
            for step, _, row, _, _, place in levels.group_pieces():
                rows = pl.ds(row, own_rows)
                part = total[tile, pl.ds(place, own_rows)]
                outs[step][tile, rows] = ins[step][tile, rows] + part
            outs[0][tile, pl.ds(ins[0].shape[1], own_rows)] = total[
                tile, pl.ds(own_rows, own_rows)
            ]

    shapes = [list(a.shape) for a in grads]
    shapes[0][1] += own_rows
    outs = [struct(2 * pairs, own_rows, LANES)] + [struct(*shape) for shape in shapes]
    own, *grads = call(
        kernel,
        [*group_grads, *grads],
        outs,
        scratch=[pltpu.VMEM((2 * pairs, BLOCK, LANES), F32)],
    )
    return own, grads


def spread_pair(levels, pairs, own_grad, rough, fine, block_second):
    own_rows = levels.rows

    def kernel(own, block, *refs):
        rough_in = refs[: levels.bits]
        fine_in = refs[levels.bits : 2 * levels.bits]
        mine, theirs, *ladder = refs[2 * levels.bits :]
        last = pl.ds(rough_in[0].shape[1] - own_rows, own_rows)
        for tile in range(2 * pairs):
            above = own[tile] + rough_in[0][tile, last]
            for step in range(1, levels.bits):
                above = above + rough_in[step][tile, pl.ds(0, own_rows)]
            filled = 0
            for m, rows in levels.differences[1]:
                part = fine_in[1][tile, pl.ds(filled, rows)]
                for step in range(2, min(m, levels.bits)):
                    part = part + fine_in[step][tile, pl.ds(filled, rows)]
                filled += rows
                put_pairs(ladder[m - 2], (), 0.5 * above, 0.5 * part)
                above = ladder[m - 2][...]
            mine[tile] = above[:QUARTER]
            theirs[tile] = above[QUARTER:] + block[tile]

    return call(
        kernel,
        [own_grad, block_second, *rough, *fine],
        [struct(2 * pairs, QUARTER, LANES)] * 2,
        scratch=levels.scratch(),
    )


def unpack(pairs, kept, arrived, features, scalar):
    def kernel(bit, *refs):
        outs = refs[4:]
        for which in range(2):
            for pair in range(pairs):
                for side, ref in ((bit[0], refs[which]), (1 - bit[0], refs[2 + which])):
                    column = side * (features // 2) + pair * LANES
                    column = pl.ds(pl.multiple_of(column, LANES), LANES)
                    outs[which][:, column] = ref[pair]

    return call(kernel, [*kept, *arrived], [struct(BLOCK, features)] * 2, scalar=scalar)


def finish(pairs, kept, rest, finest, seconds, features, scalar):
    def kernel(bit, kept_in, rest_in, f_mine, f_theirs, s_mine, s_theirs, *refs):
        outs, total, middle = refs[:2], refs[2], refs[3]
        for tile in range(2 * pairs):
            out = outs[tile // pairs]
            column = tile % pairs * LANES
            at = (tile,)
            total[tile] = kept_in[tile]
            add_spread(total, at, 0, f_mine[tile], 2)
            add_spread(total, at, 0, s_mine[tile], 4)
            place = bit[0] * (features // 2) + column
            out[:, pl.ds(pl.multiple_of(place, LANES), LANES)] = total[tile]
            put_pairs(middle, at, 0.5 * s_theirs[tile], 0.5 * rest_in[tile, :QUARTER])
            first = 0.5 * (middle[tile] + f_theirs[tile])
            put_pairs(total, at, first, 0.5 * rest_in[tile, QUARTER:])
            place = (1 - bit[0]) * (features // 2) + column
            out[:, pl.ds(pl.multiple_of(place, LANES), LANES)] = total[tile]

    return call(
        kernel,
        [kept, rest, *finest, *seconds],
        [struct(BLOCK, features)] * 2,
        scratch=[
            pltpu.VMEM((2 * pairs, BLOCK, LANES), F32),
            pltpu.VMEM((2 * pairs, HALF, LANES), F32),
        ],
        scalar=scalar,
    )


def on_device(queries, keys, values, cotangent):
    features = queries.shape[1]
    assert queries.shape[0] == BLOCK
    pairs = features // LANES // 2
    lo_bits = lax.axis_size("seqlo").bit_length() - 1
    levels = Levels(lo_bits - 1)
    lo = levels.whole
    hi_bits = lax.axis_size("seqhi").bit_length() - 1
    hi = Tree(lo_bits, [BLOCK >> step for step in range(hi_bits)])
    scalar = (lax.axis_index("seqlo") % 2).astype(jnp.int32).reshape(1)
    queries, keys, values, cotangent = [
        pltpu.with_memory_space_constraint(array, pltpu.HBM)
        for array in (queries, keys, values, cotangent)
    ]
    f_theirs, c_send, rest = pack_theirs(pairs, keys, values, scalar)
    mine_kv, f_mine, c_mine = pack_mine(pairs, keys, values, scalar)
    second = exchange(c_send, 1)
    finest_theirs = exchange(f_theirs, 2)
    coarse = coarsen_pair(lo, pairs, c_mine, second)
    finest = exchange(ordered(f_mine, finest_theirs), 2)
    rest = exchange(ordered(rest, coarse[0]), 1)
    half = exchange(ordered(finest_theirs, rest), 1)
    kv = rebuild(pairs, second, rest)
    send_qg, mine_qg = pack(pairs, queries, cotangent, scalar)
    qg = exchange(ordered(send_qg, half), 1)
    zs = lo.gather([None, *coarse], (finest, send_qg))
    group = coarsen_group(
        lo, hi, pairs, ordered(coarse[-1], rest), [finest, half], zs
    )
    turned = turn(pairs, mine_qg, qg)
    rs = hi.gather(group, turned)
    block_sets = [(0, 0, 0, BLOCK), (0, 1, 0, BLOCK)]
    lo_sets = [(1, 2, 0, BLOCK // 2), (1, 3, 0, BLOCK // 2)]
    for level in range(lo.bits):
        for step, row, rows in lo.held[level]:
            lo_sets.append((1 + level, 4 + step, row, rows))
    hi_sets = []
    for level in range(hi.bits):
        for step, row, rows in hi.held[level]:
            hi_sets.append((lo_bits + level, step, row, rows))
    first_in = [mine_kv, kv, finest, half, *zs]
    *kept, tops, sums, partial = attend_first(
        pairs, block_sets + lo_sets, first_in, turned
    )
    *rs_grads, o_keep, o_send, g_scaled, row_dot, kt_hi, d_hi = attend_last(
        pairs, hi_sets, rs, turned, tops, sums, partial
    )
    shapes = [(2 * pairs, *a.shape[1:]) for a in first_in]
    finest_grad, half_grad, *zs_grads, d_lo = attend_back(
        pairs,
        [(level, index - 2, row, rows) for level, index, row, rows in lo_sets],
        shapes[2:],
        BOTH,
        kept,
        turned,
        g_scaled,
        row_dot,
        [],
    )
    kv_keep, kv_send, dq_keep, dq_send = attend_back(
        pairs,
        block_sets,
        shapes[:2],
        0,
        kept,
        turned,
        g_scaled,
        row_dot,
        [d_lo, kt_hi, d_hi],
    )
    rough_grads, fine_grads = take_levels(levels, pairs, zs_grads)
    group_grads = hi.scatter(rs_grads)
    half_back = exchange(ordered(half_grad, group_grads[0]), 1)
    o_back = exchange(o_send, 1)
    fine_back, finest_mine = levels.fine.scatter(fine_grads, finest_grad)
    block_second, rest_grad = take_apart(pairs, kv_send)
    split_at = rest_grad.shape[1]
    bulk = jnp.concatenate([rest_grad, dq_send.reshape(2 * pairs, HALF, LANES)], axis=1)
    bulk = exchange(ordered(bulk, o_back), 1)
    rest_back = bulk[:, :split_at]
    dq_back = bulk[:, split_at:].reshape(pairs, BLOCK, LANES)
    group_grads[-1] = ordered(group_grads[-1], kv_send)
    own_grad, rough_grads = spread_group(levels, hi, pairs, group_grads, rough_grads)
    rough_back = levels.rough.scatter(rough_grads)
    finest_theirs = exchange(ordered(half_back, rough_back[0]), 2)
    own_grad = ordered(own_grad, (rest_back, dq_back))
    second_mine, second_send = spread_pair(
        levels, pairs, own_grad, rough_back, fine_back, block_second
    )
    second_theirs = exchange(second_send, 1)
    attended, query_grad = unpack(
        pairs, (o_keep, dq_keep), (o_back, dq_back), features, scalar
    )
    key_grad, value_grad = finish(
        pairs,
        kv_keep,
        rest_back,
        (finest_mine, finest_theirs),
        (second_mine, second_theirs),
        features,
        scalar,
    )
    return attended, query_grad, key_grad, value_grad


def solution(mesh):
    spec = P(AXES, None)
    return jax.shard_map(
        on_device,
        mesh=mesh,
        in_specs=(spec,) * 4,
        out_specs=(spec,) * 4,
        check_vma=False,
    )
```

```python
import math

import jax
import jax.numpy as jnp
from jax import lax
from jax.experimental import pallas as pl
from jax.experimental.pallas import tpu as pltpu
from jax.sharding import PartitionSpec as P

HEADS = 12
BLOCK = 128
HEAD_DIM = 64
LANES = 2 * HEAD_DIM
AXES = ("seqhi", "seqlo")
VMEM_LIMIT = 20 * 1024 * 1024
F32 = jnp.float32
BF16 = jnp.bfloat16
LOG2_E = 1.0 / math.log(2.0)
SCALE = 1.0 / math.sqrt(HEAD_DIM)


def struct(*shape):
    return jax.ShapeDtypeStruct(shape, F32)


def call(kernel, operands, outs, scratch=(), scalar=None, flops=0, exps=0, where=None):
    vmem = pl.BlockSpec(memory_space=pltpu.VMEM)
    smem = pl.BlockSpec(memory_space=pltpu.SMEM)
    in_specs = [pl.BlockSpec(memory_space=where) if where else vmem] * len(operands)
    if scalar is not None:
        operands = [scalar, *operands]
        in_specs = [smem, *in_specs]
    moved = sum(4 * math.prod(a.shape) for a in [*operands, *outs])
    return pl.pallas_call(
        kernel,
        out_shape=list(outs),
        in_specs=in_specs,
        out_specs=[vmem] * len(outs),
        scratch_shapes=list(scratch),
        compiler_params=pltpu.CompilerParams(vmem_limit_bytes=VMEM_LIMIT),
        cost_estimate=pl.CostEstimate(
            flops=flops, bytes_accessed=moved, transcendentals=exps
        ),
    )(*operands)


def exchange(value, offset):
    count = lax.axis_size(AXES)
    return lax.ppermute(value, AXES, [(i, i ^ offset) for i in range(count)])


def ordered(value, after):
    return value if after is None else lax.optimization_barrier((value, after))[0]


def half_difference(ref, lead, first, count):
    even = ref[(*lead, pl.ds(first, count, stride=2), slice(None))]
    odd = ref[(*lead, pl.ds(first + 1, count, stride=2), slice(None))]
    return 0.5 * (even - odd)


def put_pairs(ref, lead, total, difference):
    count = total.shape[0]
    ref[(*lead, pl.ds(0, count, stride=2), slice(None))] = total + difference
    ref[(*lead, pl.ds(1, count, stride=2), slice(None))] = total - difference


def mean_rows(ref, lead, first, count, factor):
    total = None
    for step in range(factor):
        rows = pl.ds(first + step, count, stride=factor)
        part = ref[(*lead, rows, slice(None))]
        total = part if total is None else total + part
    return total * (1.0 / factor)


def add_spread(ref, lead, first, value, factor):
    count = value.shape[0]
    value = value * (1.0 / factor)
    for step in range(factor):
        rows = pl.ds(first + step, count, stride=factor)
        place = (*lead, rows, slice(None))
        ref[place] = ref[place] + value


class Tree:
    def __init__(self, first_bit, own_rows):
        self.bits = bits = len(own_rows)
        self.first_bit = first_bit
        self.own_rows = own_rows
        self.held = {}
        self.payload = {}
        for step in range(bits - 1, -1, -1):
            rows = self.own_rows[step]
            payload = []
            fresh = {step: [(step, 0, rows)] if rows else []}
            for level in range(step + 1, bits):
                for piece in self.held[level]:
                    payload.append(piece)
                    fresh.setdefault(level, []).append((step, rows, piece[2]))
                    rows += piece[2]
            self.payload[step] = payload
            for level, pieces in fresh.items():
                self.held[level] = self.held.get(level, []) + pieces

    def rows(self, step):
        return self.own_rows[step] + sum(piece[2] for piece in self.payload[step])

    def partner(self, value, step):
        return exchange(value, 1 << self.first_bit + step)

    def gather(self, own, after=None):
        arrived = [None] * self.bits
        for step in range(self.bits - 1, -1, -1):
            parts = [own[step]] if self.own_rows[step] else []
            for source, row, rows in self.payload[step]:
                part = arrived[source]
                whole = rows == part.shape[1]
                parts.append(part if whole else part[:, row : row + rows])
            sent = jnp.concatenate(parts, axis=1) if len(parts) > 1 else parts[0]
            if step == 0:
                sent = ordered(sent, after)
            arrived[step] = self.partner(sent, step)
        return arrived

    def scatter(self, grads, front=None, after=None):
        grads = list(grads)
        returned = []
        for step in range(self.bits):
            sent = grads[step]
            if step == self.bits - 1:
                sent = ordered(sent, after)
            if step == 0 and front is not None:
                rows = front.shape[1]
                back = self.partner(jnp.concatenate([front, sent], axis=1), step)
                front, back = back[:, :rows], back[:, rows:]
            else:
                back = self.partner(sent, step)
            returned.append(back)
            filled = self.own_rows[step]
            for source, row, rows in self.payload[step]:
                part = back[:, filled : filled + rows]
                grads[source] = grads[source].at[:, row : row + rows].add(part)
                filled += rows
        return returned if front is None else (returned, front)


def split(value):
    high = value.astype(BF16).astype(F32)
    return high, value - high


def halves_by_head(value):
    high, low = split(value)
    first = lax.broadcasted_iota(jnp.int32, value.shape, 1) < HEAD_DIM
    one = jnp.where(first, high, pltpu.roll(low, HEAD_DIM, 1))
    two = jnp.where(first, pltpu.roll(high, HEAD_DIM, 1), low)
    return one, two


def dot(lhs, rhs, dims):
    return lax.dot_general(lhs, rhs, (dims, ((), ())), preferred_element_type=F32)


NN = ((1,), (0,))
NT = ((1,), (1,))


BOTH = 2 * BLOCK
GROUP = 3


def halves_of(sets, ins, which, pairs, pair):
    tile = which * pairs + pair
    parts = [ins[index][tile, pl.ds(row, rows), :] for _, index, row, rows in sets]
    return halves_by_head(jnp.concatenate(parts, axis=0))


def segment_levels(sets):
    levels, filled = [], 0
    for level, _, _, rows in sets:
        if filled % BLOCK == 0:
            levels.append(level)
        filled += rows
    return levels


def four_rows(value):
    high, low = split(value)
    four = jnp.concatenate([high, high, low, low], axis=0).astype(BF16)
    return four, jnp.concatenate([high, low], axis=0).astype(BF16)


def store_split(ref, lead, rows, value):
    high = value.astype(BF16)
    ref[(lead, 0, rows)] = high
    ref[(lead, 1, rows)] = (value - high.astype(F32)).astype(BF16)


def fold_rows(value):
    return value[:HEAD_DIM] + value[HEAD_DIM:]


def fold_heads(one, two):
    first = lax.broadcasted_iota(jnp.int32, one.shape, 1) < HEAD_DIM
    return jnp.where(
        first, one + pltpu.roll(one, HEAD_DIM, 1), two + pltpu.roll(two, HEAD_DIM, 1)
    )


def twice(value):
    return jnp.concatenate([value, value], axis=1)


def stacked(ref, at, rows=slice(None)):
    return jnp.concatenate([ref[at, 0, rows], ref[at, 1, rows]], axis=0)


def abreast(ref, at, rows=slice(None)):
    return jnp.concatenate([ref[at, 0, rows], ref[at, 1, rows]], axis=1)


def column_scores(levels, keys, at, q_four, s_ref):
    highest = None
    for index, level in enumerate(levels):
        rows = pl.ds(index * BLOCK, BLOCK)
        s = dot(twice(keys[at, rows]), q_four, NN)
        s = s + float(level) if level else s
        s_ref[at, rows] = s
        top = jnp.max(s.reshape(BLOCK // 8, 8, BOTH), axis=0)
        highest = top if highest is None else jnp.maximum(highest, top)
    return jnp.max(highest, axis=0, keepdims=True)


def exponents(levels, at, top, s_ref, e_ref, keep):
    summed = None
    for index in range(len(levels)):
        rows = pl.ds(index * BLOCK, BLOCK)
        e = jnp.exp2(s_ref[at, rows] - top)
        if keep:
            s_ref[at, rows] = e
        store_split(e_ref, at, rows, e)
        part = jnp.sum(e.reshape(BLOCK // 8, 8, BOTH), axis=0)
        summed = part if summed is None else summed + part
    return jnp.sum(summed, axis=0, keepdims=True)


def head_rows(ref, pair, head):
    return ref[pair, pl.ds(head * HEAD_DIM, HEAD_DIM)]


def each_group(pairs, body):
    for first in range(0, pairs, GROUP):
        group = range(first, min(first + GROUP, pairs))
        body(group, [(pair, head, 2 * pair + head) for pair in group for head in (0, 1)])


def costs(pairs, rows, products, exps=0):
    return dict(
        flops=2 * 4 * products * pairs * 2 * rows * BOTH * HEAD_DIM,
        exps=exps * pairs * 2 * rows * BOTH,
    )


def put_halves(pairs, sets, ins, group, plain, turned):
    for which in range(2):
        for pair in group:
            for head, value in enumerate(halves_of(sets, ins, which, pairs, pair)):
                plain[which][2 * pair + head] = value.astype(BF16)
                turned[which][2 * pair + head] = value.T.astype(BF16)


def attend_first(pairs, sets, operands, turned):
    total = sum(s[3] for s in sets)
    levels = segment_levels(sets)

    def kernel(turn_in, *refs):
        ins = refs[: len(operands)]
        kt, vc, e_ref, tops, sums, out, s_ref, kc, vt = refs[len(operands) :]

        def body(group, heads):
            put_halves(pairs, sets, ins, group, (kc, vc), (kt, vt))
            for pair, head, at in heads:
                q_four, _ = four_rows(head_rows(turn_in, pair, head))
                tops[at] = column_scores(levels, kc, at, q_four, s_ref)
            for _, _, at in heads:
                sums[at] = exponents(levels, at, tops[at], s_ref, e_ref, False)
            for _, _, at in heads:
                out[at] = fold_rows(dot(twice(vt[at]), stacked(e_ref, at), NN))

        each_group(pairs, body)

    heads = 2 * pairs
    outs = [
        jax.ShapeDtypeStruct((heads, LANES, total), BF16),
        jax.ShapeDtypeStruct((heads, total, LANES), BF16),
        jax.ShapeDtypeStruct((heads, 2, total, BOTH), BF16),
    ]
    outs += [struct(heads, 1, BOTH)] * 2 + [struct(heads, HEAD_DIM, BOTH)]
    return call(
        kernel,
        [turned, *operands],
        outs,
        scratch=[
            pltpu.VMEM((heads, total, BOTH), F32),
            pltpu.VMEM((heads, total, LANES), BF16),
            pltpu.VMEM((heads, LANES, total), BF16),
        ],
        **costs(pairs, total, 2, 1),
    )


def attend_last(pairs, sets, operands, turned, tops, sums, partial):
    total = sum(s[3] for s in sets)
    levels = segment_levels(sets)

    def kernel(turn_in, top_in, sum_in, part_in, *refs):
        ins = refs[: len(operands)]
        grads = refs[len(operands) : 2 * len(operands)]
        o_keep, o_send, g_out, r_out, kt, d_ref = refs[2 * len(operands) : -5]
        s_ref, e_ref, kc, vc, vt = refs[-5:]

        def body(group, heads):
            put_halves(pairs, sets, ins, group, (kc, vc), (kt, vt))
            queries = {}
            top = {}
            for pair, head, at in heads:
                q_four, queries[at] = four_rows(head_rows(turn_in, pair, head))
                top[at] = column_scores(levels, kc, at, q_four, s_ref)
            inverse = {}
            rescale = {}
            for _, _, at in heads:
                first_top = top_in[at]
                highest = jnp.maximum(top[at], first_top)
                rescale[at] = jnp.exp2(first_top - highest)
                summed = exponents(levels, at, highest, s_ref, e_ref, True)
                inverse[at] = 1.0 / (summed + sum_in[at] * rescale[at])
            output = {}
            cotangents = {}
            row_dot = {}
            for pair, head, at in heads:
                o = fold_rows(dot(twice(vt[at]), stacked(e_ref, at), NN))
                o = (o + part_in[at] * rescale[at]) * inverse[at]
                output[at] = o
                scaled = head_rows(turn_in, pairs + pair, head) * inverse[at]
                cotangents[at] = four_rows(scaled)
                row_dot[at] = jnp.sum(o * scaled, axis=0, keepdims=True)
                g_out[at] = scaled * rescale[at]
                r_out[at] = row_dot[at] * rescale[at]
            for _, _, at in heads:
                for index in range(len(levels)):
                    rows = pl.ds(index * BLOCK, BLOCK)
                    dp = dot(twice(vc[at, rows]), cotangents[at][0], NN)
                    store_split(d_ref, at, rows, s_ref[at, rows] * (dp - row_dot[at]))
            key_grads = {}
            value_grads = {}
            for _, _, at in heads:
                value_grads[at] = dot(abreast(e_ref, at), twice(cotangents[at][1]), NT)
                key_grads[at] = dot(abreast(d_ref, at), twice(queries[at]), NT)
            for pair in group:
                put_grads(pairs, pair, sets, grads, key_grads, value_grads)
                both = [output[2 * pair], output[2 * pair + 1]]
                both = jnp.concatenate(both, axis=0).T
                o_keep[pair] = both[:BLOCK]
                o_send[pair] = both[BLOCK:]

        each_group(pairs, body)

    heads = 2 * pairs
    outs = [struct(*a.shape) for a in operands]
    outs += [struct(pairs, BLOCK, LANES)] * 2
    outs += [struct(heads, HEAD_DIM, BOTH), struct(heads, 1, BOTH)]
    outs.append(jax.ShapeDtypeStruct((heads, LANES, total), BF16))
    outs.append(jax.ShapeDtypeStruct((heads, 2, total, BOTH), BF16))
    return call(
        kernel,
        [turned, tops, sums, partial, *operands],
        outs,
        scratch=[pltpu.VMEM((heads, total, BOTH), F32)]
        + [pltpu.VMEM((heads, 2, total, BOTH), BF16)]
        + [pltpu.VMEM((heads, total, LANES), BF16)] * 2
        + [pltpu.VMEM((heads, LANES, total), BF16)],
        **costs(pairs, total, 5, 1),
    )


def put_grads(pairs, pair, sets, grads, key_grads, value_grads):
    for which, parts in enumerate((key_grads, value_grads)):
        both = fold_heads(parts[2 * pair], parts[2 * pair + 1])
        if which == 0:
            both = both * (1.0 / LOG2_E)
        filled = 0
        for _, index, row, rows in sets:
            piece = both[filled : filled + rows]
            grads[index][which * pairs + pair, pl.ds(row, rows), :] = piece
            filled += rows


def attend_back(pairs, sets, shapes, first, kept, turned, g_scaled, row_dot, others):
    total = sum(s[3] for s in sets)
    segments = total // BLOCK

    def kernel(turn_in, kt, vc, e_ref, g_in, r_in, *refs):
        other_in = refs[: len(others)]
        grads = refs[len(others) : len(others) + len(shapes)]
        dq_out = refs[len(others) + len(shapes) : -1]
        d_ref = refs[-1]
        span = pl.ds(first, total)

        def body(group, heads):
            cotangents = {}
            for _, _, at in heads:
                g_four, cotangents[at] = four_rows(g_in[at])
                for index in range(segments):
                    rows = pl.ds(first + index * BLOCK, BLOCK)
                    dp = dot(twice(vc[at, rows]), g_four, NN)
                    e = e_ref[at, 0, rows].astype(F32) + e_ref[at, 1, rows].astype(F32)
                    place = pl.ds(index * BLOCK, BLOCK)
                    store_split(d_ref, at, place, e * (dp - r_in[at]))
            queries_grad = {}
            key_grads = {}
            value_grads = {}
            for pair, head, at in heads:
                _, q_rows = four_rows(head_rows(turn_in, pair, head))
                g_rows = cotangents[at]
                value_grads[at] = dot(abreast(e_ref, at, span), twice(g_rows), NT)
                key_grads[at] = dot(abreast(d_ref, at), twice(q_rows), NT)
                if others:
                    d_lo, kt_hi, d_hi = other_in
                    part = dot(twice(kt[at, :, span]), stacked(d_ref, at), NN)
                    part += dot(twice(kt[at, :, total:]), stacked(d_lo, at), NN)
                    part += dot(twice(kt_hi[at]), stacked(d_hi, at), NN)
                    queries_grad[at] = fold_rows(part)
            for pair in group:
                put_grads(pairs, pair, sets, grads, key_grads, value_grads)
                if others:
                    both = [queries_grad[2 * pair], queries_grad[2 * pair + 1]]
                    both = jnp.concatenate(both, axis=0).T * SCALE
                    dq_out[0][pair] = both[:BLOCK]
                    dq_out[1][pair] = both[BLOCK:]

        each_group(pairs, body)

    outs = [struct(*shape) for shape in shapes]
    scratch = []
    if others:
        outs += [struct(pairs, BLOCK, LANES)] * 2
        scratch.append(pltpu.VMEM((2 * pairs, 2, total, BOTH), BF16))
    else:
        outs.append(jax.ShapeDtypeStruct((2 * pairs, 2, total, BOTH), BF16))
    return call(
        kernel,
        [turned, *kept, g_scaled, row_dot, *others],
        outs,
        scratch=scratch,
        **costs(pairs, total, 4),
    )


def copy_columns(moves, ins, sems, bit):
    started = []
    for operand, theirs, column, place in moves:
        side = 1 - bit if theirs else bit
        column = side * (ins[operand].shape[1] // 2) + column
        column = pl.ds(pl.multiple_of(column, LANES), LANES)
        copy = pltpu.make_async_copy(
            ins[operand].at[:, column], place, sems.at[len(started)]
        )
        copy.start()
        started.append(copy)
    return started


def pack(pairs, first, second, scalar):
    def kernel(bit, one, two, theirs, mine, sems):
        moves = []
        for tile in range(2 * pairs):
            for out, other in ((theirs, True), (mine, False)):
                column = tile % pairs * LANES
                moves.append((tile // pairs, other, column, out.at[tile]))
        for copy in copy_columns(moves, (one, two), sems, bit[0]):
            copy.wait()

    return call(
        kernel,
        [first, second],
        [struct(2 * pairs, BLOCK, LANES)] * 2,
        scratch=[pltpu.SemaphoreType.DMA((4 * pairs,))],
        scalar=scalar,
        where=pl.ANY,
    )


QUARTER = BLOCK // 4
HALF = BLOCK // 2


def pack_theirs(pairs, keys, values, scalar):
    def kernel(bit, k, v, finest, coarse, rest, block, sems):
        moves = []
        for tile in range(2 * pairs):
            moves.append((tile // pairs, True, tile % pairs * LANES, block.at[tile]))
        copies = copy_columns(moves, (k, v), sems, bit[0])
        for tile, copy in enumerate(copies):
            copy.wait()
            finest[tile] = mean_rows(block, (tile,), 0, HALF, 2)
            coarse[tile] = mean_rows(finest, (tile,), 0, QUARTER, 2)
            rest[tile, :QUARTER] = half_difference(finest, (tile,), 0, QUARTER)
            rest[tile, QUARTER:] = half_difference(block, (tile,), 0, HALF)

    return call(
        kernel,
        [keys, values],
        [
            struct(2 * pairs, HALF, LANES),
            struct(2 * pairs, QUARTER, LANES),
            struct(2 * pairs, QUARTER + HALF, LANES),
        ],
        scratch=[
            pltpu.VMEM((2 * pairs, BLOCK, LANES), F32),
            pltpu.SemaphoreType.DMA((2 * pairs,)),
        ],
        scalar=scalar,
        where=pl.ANY,
    )


def pack_mine(pairs, keys, values, scalar):
    def kernel(bit, k, v, block, finest, coarse, sems):
        moves = []
        for tile in range(2 * pairs):
            moves.append((tile // pairs, False, tile % pairs * LANES, block.at[tile]))
        copies = copy_columns(moves, (k, v), sems, bit[0])
        for tile, copy in enumerate(copies):
            copy.wait()
            finest[tile] = mean_rows(block, (tile,), 0, HALF, 2)
            coarse[tile] = mean_rows(finest, (tile,), 0, QUARTER, 2)

    return call(
        kernel,
        [keys, values],
        [
            struct(2 * pairs, BLOCK, LANES),
            struct(2 * pairs, HALF, LANES),
            struct(2 * pairs, QUARTER, LANES),
        ],
        scratch=[pltpu.SemaphoreType.DMA((2 * pairs,))],
        scalar=scalar,
        where=pl.ANY,
    )


def rebuild(pairs, second, rest):
    def kernel(second_in, rest_in, out, finest):
        for tile in range(2 * pairs):
            put_pairs(finest, (tile,), second_in[tile], rest_in[tile, :QUARTER])
            put_pairs(out, (tile,), finest[tile], rest_in[tile, QUARTER:])

    return call(
        kernel,
        [second, rest],
        [struct(2 * pairs, BLOCK, LANES)],
        scratch=[pltpu.VMEM((2 * pairs, HALF, LANES), F32)],
    )[0]


def take_apart(pairs, block_grad):
    def kernel(block, second, rest, finest):
        for tile in range(2 * pairs):
            finest[tile] = 2.0 * mean_rows(block, (tile,), 0, HALF, 2)
            rest[tile, QUARTER:] = 2.0 * half_difference(block, (tile,), 0, HALF)
            second[tile] = 2.0 * mean_rows(finest, (tile,), 0, QUARTER, 2)
            rest[tile, :QUARTER] = 2.0 * half_difference(finest, (tile,), 0, QUARTER)

    return call(
        kernel,
        [block_grad],
        [
            struct(2 * pairs, QUARTER, LANES),
            struct(2 * pairs, QUARTER + HALF, LANES),
        ],
        scratch=[pltpu.VMEM((2 * pairs, HALF, LANES), F32)],
    )


class Levels:
    def __init__(self, bits):
        self.bits = bits
        self.rows = BLOCK >> bits
        self.differences = [
            [(m, BLOCK >> m) for m in range(bits, step, -1)] for step in range(bits)
        ]
        whole = [0] + [BLOCK >> step for step in range(1, bits)]
        self.whole = Tree(1, whole)
        self.rough = Tree(1, [0] + [self.rows] * (bits - 1))
        self.fine = Tree(1, [0] + [rows - self.rows for rows in whole[1:]])
        self.pieces = []
        for level in range(1, bits):
            trees = (self.whole, self.rough, self.fine)
            for parts in zip(*(tree.held[level] for tree in trees)):
                self.pieces.append((level, parts[0][0], *(part[1] for part in parts)))

    def scratch(self):
        shapes = [(BLOCK >> m, LANES) for m in range(1, self.bits + 1)]
        return [pltpu.VMEM(shape, F32) for shape in shapes]

    def group_pieces(self):
        pieces = []
        for index, (level, step, whole, rough, _) in enumerate(self.pieces):
            factor = 1 << self.bits - level
            place = (2 + index) * self.rows
            pieces.append((step, whole, rough, BLOCK >> level, factor, place))
        return pieces


def coarsen_pair(lo, pairs, mine, received):
    def kernel(own, got, *outs):
        for tile in range(2 * pairs):
            outs[0][tile, : BLOCK // 4] = own[tile]
            outs[0][tile, BLOCK // 4 :] = got[tile]
            for index in range(1, lo.bits):
                outs[index][tile] = mean_rows(
                    outs[index - 1], (tile,), 0, BLOCK >> index + 1, 2
                )

    outs = [struct(2 * pairs, BLOCK >> step, LANES) for step in range(1, lo.bits + 1)]
    return call(kernel, [mine, received], outs)


def group_pieces(lo):
    own = BLOCK >> lo.bits
    factor = 1 << lo.bits
    pieces = [
        (-2, 0, BLOCK // 2, factor, own),
        (-1, 0, BLOCK // 2, factor, own + own // 2),
    ]
    filled = 2 * own
    for level in range(1, lo.bits):
        factor = 1 << lo.bits - level
        for step, row, rows in lo.held[level]:
            pieces.append((step, row, rows, factor, filled))
            filled += rows // factor
    return pieces


def coarsen_group(lo, hi, pairs, own, halves, arrived):
    pieces = group_pieces(lo)

    def kernel(own_in, *refs):
        ins = refs[: 2 + lo.bits]
        outs = refs[2 + lo.bits :]
        for tile in range(2 * pairs):
            outs[0][tile, pl.ds(0, BLOCK >> lo.bits)] = own_in[tile]
            for step, row, rows, factor, place in pieces:
                count = rows // factor
                outs[0][tile, pl.ds(place, count)] = mean_rows(
                    ins[2 + step], (tile,), row, count, factor
                )
            for step in range(1, hi.bits):
                outs[step][tile] = mean_rows(
                    outs[step - 1], (tile,), 0, BLOCK >> step, 2
                )

    outs = [struct(2 * pairs, BLOCK >> step, LANES) for step in range(hi.bits)]
    return call(kernel, [own, *halves, *arrived], outs)


def turn(pairs, mine, received):
    def kernel(own, got, turned):
        for tile in range(2 * pairs):
            both = jnp.concatenate([own[tile], got[tile]], axis=0).T
            turned[tile] = both * (SCALE * LOG2_E) if tile < pairs else both

    return call(kernel, [mine, received], [struct(2 * pairs, LANES, 2 * BLOCK)])[0]


def take_levels(levels, pairs, grads):
    trees = (levels.rough, levels.fine)

    def kernel(*refs):
        ins = refs[: levels.bits]
        rough = refs[levels.bits : 2 * levels.bits]
        fine = refs[2 * levels.bits : 3 * levels.bits]
        ladder = refs[3 * levels.bits :]
        for tile in range(2 * pairs):
            for level, step, row, rough_row, fine_row in levels.pieces:
                source = ladder[level - 1]
                source[...] = ins[step][tile, pl.ds(row, BLOCK >> level)]
                fine_row += sum(rows for _, rows in levels.differences[level])
                for m, rows in reversed(levels.differences[level]):
                    fine_row -= rows
                    part = 2.0 * half_difference(source, (), 0, rows)
                    fine[step][tile, pl.ds(fine_row, rows)] = part
                    ladder[m - 1][...] = 2.0 * mean_rows(source, (), 0, rows, 2)
                    source = ladder[m - 1]
                rough[step][tile, pl.ds(rough_row, levels.rows)] = source[...]

    outs = [
        struct(2 * pairs, tree.rows(step), LANES)
        for tree in trees
        for step in range(levels.bits)
    ]
    outs = call(kernel, grads, outs, scratch=levels.scratch())
    return outs[: levels.bits], outs[levels.bits :]


def spread_group(levels, hi, pairs, group_grads, grads):
    own_rows = levels.rows

    def kernel(*refs):
        steps = refs[: hi.bits]
        ins = refs[hi.bits : hi.bits + levels.bits]
        own_out, *outs = refs[hi.bits + levels.bits : -1]
        total = refs[-1]
        for tile in range(2 * pairs):
            total[tile] = steps[0][tile, pl.ds(0, BLOCK)]
            for step in range(1, hi.bits):
                above = steps[step][tile, pl.ds(0, BLOCK >> step)]
                add_spread(total, (tile,), 0, above, 1 << step)
            own_out[tile] = total[tile, pl.ds(0, own_rows)]
            for step, _, row, _, _, place in levels.group_pieces():
                rows = pl.ds(row, own_rows)
                part = total[tile, pl.ds(place, own_rows)]
                outs[step][tile, rows] = ins[step][tile, rows] + part
            outs[0][tile, pl.ds(ins[0].shape[1], own_rows)] = total[
                tile, pl.ds(own_rows, own_rows)
            ]

    shapes = [list(a.shape) for a in grads]
    shapes[0][1] += own_rows
    outs = [struct(2 * pairs, own_rows, LANES)] + [struct(*shape) for shape in shapes]
    own, *grads = call(
        kernel,
        [*group_grads, *grads],
        outs,
        scratch=[pltpu.VMEM((2 * pairs, BLOCK, LANES), F32)],
    )
    return own, grads


def spread_pair(levels, pairs, own_grad, rough, fine, block_second):
    own_rows = levels.rows

    def kernel(own, block, *refs):
        rough_in = refs[: levels.bits]
        fine_in = refs[levels.bits : 2 * levels.bits]
        mine, theirs, *ladder = refs[2 * levels.bits :]
        last = pl.ds(rough_in[0].shape[1] - own_rows, own_rows)
        for tile in range(2 * pairs):
            above = own[tile] + rough_in[0][tile, last]
            for step in range(1, levels.bits):
                above = above + rough_in[step][tile, pl.ds(0, own_rows)]
            filled = 0
            for m, rows in levels.differences[1]:
                part = fine_in[1][tile, pl.ds(filled, rows)]
                for step in range(2, min(m, levels.bits)):
                    part = part + fine_in[step][tile, pl.ds(filled, rows)]
                filled += rows
                put_pairs(ladder[m - 2], (), 0.5 * above, 0.5 * part)
                above = ladder[m - 2][...]
            mine[tile] = above[:QUARTER]
            theirs[tile] = above[QUARTER:] + block[tile]

    return call(
        kernel,
        [own_grad, block_second, *rough, *fine],
        [struct(2 * pairs, QUARTER, LANES)] * 2,
        scratch=levels.scratch(),
    )


def unpack(pairs, kept, arrived, features, scalar):
    def kernel(bit, *refs):
        outs = refs[4:]
        for which in range(2):
            for pair in range(pairs):
                for side, ref in ((bit[0], refs[which]), (1 - bit[0], refs[2 + which])):
                    column = side * (features // 2) + pair * LANES
                    column = pl.ds(pl.multiple_of(column, LANES), LANES)
                    outs[which][:, column] = ref[pair]

    return call(kernel, [*kept, *arrived], [struct(BLOCK, features)] * 2, scalar=scalar)


def finish(pairs, kept, rest, finest, seconds, features, scalar):
    def kernel(bit, kept_in, rest_in, f_mine, f_theirs, s_mine, s_theirs, *refs):
        outs, total, middle = refs[:2], refs[2], refs[3]
        for tile in range(2 * pairs):
            out = outs[tile // pairs]
            column = tile % pairs * LANES
            at = (tile,)
            total[tile] = kept_in[tile]
            add_spread(total, at, 0, f_mine[tile], 2)
            add_spread(total, at, 0, s_mine[tile], 4)
            place = bit[0] * (features // 2) + column
            out[:, pl.ds(pl.multiple_of(place, LANES), LANES)] = total[tile]
            put_pairs(middle, at, 0.5 * s_theirs[tile], 0.5 * rest_in[tile, :QUARTER])
            first = 0.5 * (middle[tile] + f_theirs[tile])
            put_pairs(total, at, first, 0.5 * rest_in[tile, QUARTER:])
            place = (1 - bit[0]) * (features // 2) + column
            out[:, pl.ds(pl.multiple_of(place, LANES), LANES)] = total[tile]

    return call(
        kernel,
        [kept, rest, *finest, *seconds],
        [struct(BLOCK, features)] * 2,
        scratch=[
            pltpu.VMEM((2 * pairs, BLOCK, LANES), F32),
            pltpu.VMEM((2 * pairs, HALF, LANES), F32),
        ],
        scalar=scalar,
    )


def on_device(queries, keys, values, cotangent):
    features = queries.shape[1]
    assert queries.shape[0] == BLOCK
    pairs = features // LANES // 2
    lo_bits = lax.axis_size("seqlo").bit_length() - 1
    levels = Levels(lo_bits - 1)
    lo = levels.whole
    hi_bits = lax.axis_size("seqhi").bit_length() - 1
    hi = Tree(lo_bits, [BLOCK >> step for step in range(hi_bits)])
    scalar = (lax.axis_index("seqlo") % 2).astype(jnp.int32).reshape(1)
    queries, keys, values, cotangent = [
        pltpu.with_memory_space_constraint(array, pltpu.HBM)
        for array in (queries, keys, values, cotangent)
    ]
    f_theirs, c_send, rest = pack_theirs(pairs, keys, values, scalar)
    mine_kv, f_mine, c_mine = pack_mine(pairs, keys, values, scalar)
    second = exchange(c_send, 1)
    finest_theirs = exchange(f_theirs, 2)
    coarse = coarsen_pair(lo, pairs, c_mine, second)
    finest = exchange(ordered(f_mine, finest_theirs), 2)
    rest = exchange(ordered(rest, coarse[0]), 1)
    half = exchange(ordered(finest_theirs, rest), 1)
    kv = rebuild(pairs, second, rest)
    send_qg, mine_qg = pack(pairs, queries, cotangent, scalar)
    qg = exchange(ordered(send_qg, half), 1)
    zs = lo.gather([None, *coarse], (finest, send_qg))
    group = coarsen_group(
        lo, hi, pairs, ordered(coarse[-1], rest), [finest, half], zs
    )
    turned = turn(pairs, mine_qg, qg)
    rs = hi.gather(group, turned)
    block_sets = [(0, 0, 0, BLOCK), (0, 1, 0, BLOCK)]
    lo_sets = [(1, 2, 0, BLOCK // 2), (1, 3, 0, BLOCK // 2)]
    for level in range(lo.bits):
        for step, row, rows in lo.held[level]:
            lo_sets.append((1 + level, 4 + step, row, rows))
    hi_sets = []
    for level in range(hi.bits):
        for step, row, rows in hi.held[level]:
            hi_sets.append((lo_bits + level, step, row, rows))
    first_in = [mine_kv, kv, finest, half, *zs]
    *kept, tops, sums, partial = attend_first(
        pairs, block_sets + lo_sets, first_in, turned
    )
    *rs_grads, o_keep, o_send, g_scaled, row_dot, kt_hi, d_hi = attend_last(
        pairs, hi_sets, rs, turned, tops, sums, partial
    )
    shapes = [(2 * pairs, *a.shape[1:]) for a in first_in]
    finest_grad, half_grad, *zs_grads, d_lo = attend_back(
        pairs,
        [(level, index - 2, row, rows) for level, index, row, rows in lo_sets],
        shapes[2:],
        BOTH,
        kept,
        turned,
        g_scaled,
        row_dot,
        [],
    )
    kv_keep, kv_send, dq_keep, dq_send = attend_back(
        pairs,
        block_sets,
        shapes[:2],
        0,
        kept,
        turned,
        g_scaled,
        row_dot,
        [d_lo, kt_hi, d_hi],
    )
    rough_grads, fine_grads = take_levels(levels, pairs, zs_grads)
    group_grads = hi.scatter(rs_grads)
    half_back = exchange(ordered(half_grad, kv_send), 1)
    o_back = exchange(o_send, 1)
    fine_back, finest_mine = levels.fine.scatter(fine_grads, finest_grad)
    block_second, rest_grad = take_apart(pairs, kv_send)
    split_at = rest_grad.shape[1]
    bulk = jnp.concatenate([rest_grad, dq_send.reshape(2 * pairs, HALF, LANES)], axis=1)
    bulk = exchange(ordered(bulk, o_back), 1)
    rest_back = bulk[:, :split_at]
    dq_back = bulk[:, split_at:].reshape(pairs, BLOCK, LANES)
    group_grads[-1] = ordered(group_grads[-1], kv_send)
    own_grad, rough_grads = spread_group(levels, hi, pairs, group_grads, rough_grads)
    rough_back = levels.rough.scatter(rough_grads, after=half_back)
    finest_theirs = exchange(ordered(half_back, rough_back[0]), 2)
    own_grad = ordered(own_grad, (rest_back, dq_back))
    second_mine, second_send = spread_pair(
        levels, pairs, own_grad, rough_back, fine_back, block_second
    )
    second_theirs = exchange(second_send, 1)
    attended, query_grad = unpack(
        pairs, (o_keep, dq_keep), (o_back, dq_back), features, scalar
    )
    key_grad, value_grad = finish(
        pairs,
        kv_keep,
        rest_back,
        (finest_mine, finest_theirs),
        (second_mine, second_theirs),
        features,
        scalar,
    )
    return attended, query_grad, key_grad, value_grad


def solution(mesh):
    spec = P(AXES, None)
    return jax.shard_map(
        on_device,
        mesh=mesh,
        in_specs=(spec,) * 4,
        out_specs=(spec,) * 4,
        check_vma=False,
    )
```

```python
import math

import jax
import jax.numpy as jnp
from jax import lax
from jax.experimental import pallas as pl
from jax.experimental.pallas import tpu as pltpu
from jax.sharding import PartitionSpec as P

HEADS = 12
BLOCK = 128
HEAD_DIM = 64
LANES = 2 * HEAD_DIM
AXES = ("seqhi", "seqlo")
VMEM_LIMIT = 20 * 1024 * 1024
F32 = jnp.float32
BF16 = jnp.bfloat16
LOG2_E = 1.0 / math.log(2.0)
SCALE = 1.0 / math.sqrt(HEAD_DIM)


def struct(*shape):
    return jax.ShapeDtypeStruct(shape, F32)


def call(kernel, operands, outs, scratch=(), scalar=None, flops=0, exps=0, where=None):
    vmem = pl.BlockSpec(memory_space=pltpu.VMEM)
    smem = pl.BlockSpec(memory_space=pltpu.SMEM)
    in_specs = [pl.BlockSpec(memory_space=where) if where else vmem] * len(operands)
    if scalar is not None:
        operands = [scalar, *operands]
        in_specs = [smem, *in_specs]
    moved = sum(4 * math.prod(a.shape) for a in [*operands, *outs])
    return pl.pallas_call(
        kernel,
        out_shape=list(outs),
        in_specs=in_specs,
        out_specs=[vmem] * len(outs),
        scratch_shapes=list(scratch),
        compiler_params=pltpu.CompilerParams(vmem_limit_bytes=VMEM_LIMIT),
        cost_estimate=pl.CostEstimate(
            flops=flops, bytes_accessed=moved, transcendentals=exps
        ),
    )(*operands)


def exchange(value, offset):
    count = lax.axis_size(AXES)
    return lax.ppermute(value, AXES, [(i, i ^ offset) for i in range(count)])


def ordered(value, after):
    return value if after is None else lax.optimization_barrier((value, after))[0]


def half_difference(ref, lead, first, count):
    even = ref[(*lead, pl.ds(first, count, stride=2), slice(None))]
    odd = ref[(*lead, pl.ds(first + 1, count, stride=2), slice(None))]
    return 0.5 * (even - odd)


def put_pairs(ref, lead, total, difference):
    count = total.shape[0]
    ref[(*lead, pl.ds(0, count, stride=2), slice(None))] = total + difference
    ref[(*lead, pl.ds(1, count, stride=2), slice(None))] = total - difference


def mean_rows(ref, lead, first, count, factor):
    total = None
    for step in range(factor):
        rows = pl.ds(first + step, count, stride=factor)
        part = ref[(*lead, rows, slice(None))]
        total = part if total is None else total + part
    return total * (1.0 / factor)


def add_spread(ref, lead, first, value, factor):
    count = value.shape[0]
    value = value * (1.0 / factor)
    for step in range(factor):
        rows = pl.ds(first + step, count, stride=factor)
        place = (*lead, rows, slice(None))
        ref[place] = ref[place] + value


class Tree:
    def __init__(self, first_bit, own_rows):
        self.bits = bits = len(own_rows)
        self.first_bit = first_bit
        self.own_rows = own_rows
        self.held = {}
        self.payload = {}
        for step in range(bits - 1, -1, -1):
            rows = self.own_rows[step]
            payload = []
            fresh = {step: [(step, 0, rows)] if rows else []}
            for level in range(step + 1, bits):
                for piece in self.held[level]:
                    payload.append(piece)
                    fresh.setdefault(level, []).append((step, rows, piece[2]))
                    rows += piece[2]
            self.payload[step] = payload
            for level, pieces in fresh.items():
                self.held[level] = self.held.get(level, []) + pieces

    def rows(self, step):
        return self.own_rows[step] + sum(piece[2] for piece in self.payload[step])

    def partner(self, value, step):
        return exchange(value, 1 << self.first_bit + step)

    def gather(self, own, after=None):
        arrived = [None] * self.bits
        for step in range(self.bits - 1, -1, -1):
            parts = [own[step]] if self.own_rows[step] else []
            for source, row, rows in self.payload[step]:
                part = arrived[source]
                whole = rows == part.shape[1]
                parts.append(part if whole else part[:, row : row + rows])
            sent = jnp.concatenate(parts, axis=1) if len(parts) > 1 else parts[0]
            if step == 0:
                sent = ordered(sent, after)
            arrived[step] = self.partner(sent, step)
        return arrived

    def scatter(self, grads, front=None, whole=True):
        grads = list(grads)
        returned = []
        for step in range(self.bits if whole else self.bits - 1):
            sent = grads[step]
            if step == 0 and front is not None:
                rows = front.shape[1]
                back = self.partner(jnp.concatenate([front, sent], axis=1), step)
                front, back = back[:, :rows], back[:, rows:]
            else:
                back = self.partner(sent, step)
            returned.append(back)
            filled = self.own_rows[step]
            for source, row, rows in self.payload[step]:
                part = back[:, filled : filled + rows]
                grads[source] = grads[source].at[:, row : row + rows].add(part)
                filled += rows
        if not whole:
            returned.append(grads[-1])
        return returned if front is None else (returned, front)


def split(value):
    high = value.astype(BF16).astype(F32)
    return high, value - high


def halves_by_head(value):
    high, low = split(value)
    first = lax.broadcasted_iota(jnp.int32, value.shape, 1) < HEAD_DIM
    one = jnp.where(first, high, pltpu.roll(low, HEAD_DIM, 1))
    two = jnp.where(first, pltpu.roll(high, HEAD_DIM, 1), low)
    return one, two


def dot(lhs, rhs, dims):
    return lax.dot_general(lhs, rhs, (dims, ((), ())), preferred_element_type=F32)


NN = ((1,), (0,))
NT = ((1,), (1,))


BOTH = 2 * BLOCK
GROUP = 3


def halves_of(sets, ins, which, pairs, pair):
    tile = which * pairs + pair
    parts = [ins[index][tile, pl.ds(row, rows), :] for _, index, row, rows in sets]
    return halves_by_head(jnp.concatenate(parts, axis=0))


def segment_levels(sets):
    levels, filled = [], 0
    for level, _, _, rows in sets:
        if filled % BLOCK == 0:
            levels.append(level)
        filled += rows
    return levels


def four_rows(value):
    high, low = split(value)
    four = jnp.concatenate([high, high, low, low], axis=0).astype(BF16)
    return four, jnp.concatenate([high, low], axis=0).astype(BF16)


def store_split(ref, lead, rows, value):
    high = value.astype(BF16)
    ref[(lead, 0, rows)] = high
    ref[(lead, 1, rows)] = (value - high.astype(F32)).astype(BF16)


def fold_rows(value):
    return value[:HEAD_DIM] + value[HEAD_DIM:]


def fold_heads(one, two):
    first = lax.broadcasted_iota(jnp.int32, one.shape, 1) < HEAD_DIM
    return jnp.where(
        first, one + pltpu.roll(one, HEAD_DIM, 1), two + pltpu.roll(two, HEAD_DIM, 1)
    )


def twice(value):
    return jnp.concatenate([value, value], axis=1)


def stacked(ref, at, rows=slice(None)):
    return jnp.concatenate([ref[at, 0, rows], ref[at, 1, rows]], axis=0)


def abreast(ref, at, rows=slice(None)):
    return jnp.concatenate([ref[at, 0, rows], ref[at, 1, rows]], axis=1)


def column_scores(levels, keys, at, q_four, s_ref):
    highest = None
    for index, level in enumerate(levels):
        rows = pl.ds(index * BLOCK, BLOCK)
        s = dot(twice(keys[at, rows]), q_four, NN)
        s = s + float(level) if level else s
        s_ref[at, rows] = s
        top = jnp.max(s.reshape(BLOCK // 8, 8, BOTH), axis=0)
        highest = top if highest is None else jnp.maximum(highest, top)
    return jnp.max(highest, axis=0, keepdims=True)


def exponents(levels, at, top, s_ref, e_ref, keep):
    summed = None
    for index in range(len(levels)):
        rows = pl.ds(index * BLOCK, BLOCK)
        e = jnp.exp2(s_ref[at, rows] - top)
        if keep:
            s_ref[at, rows] = e
        store_split(e_ref, at, rows, e)
        part = jnp.sum(e.reshape(BLOCK // 8, 8, BOTH), axis=0)
        summed = part if summed is None else summed + part
    return jnp.sum(summed, axis=0, keepdims=True)


def head_rows(ref, pair, head):
    return ref[pair, pl.ds(head * HEAD_DIM, HEAD_DIM)]


def each_group(pairs, body):
    for first in range(0, pairs, GROUP):
        group = range(first, min(first + GROUP, pairs))
        body(group, [(pair, head, 2 * pair + head) for pair in group for head in (0, 1)])


def costs(pairs, rows, products, exps=0):
    return dict(
        flops=2 * 4 * products * pairs * 2 * rows * BOTH * HEAD_DIM,
        exps=exps * pairs * 2 * rows * BOTH,
    )


def put_halves(pairs, sets, ins, group, plain, turned):
    for which in range(2):
        for pair in group:
            for head, value in enumerate(halves_of(sets, ins, which, pairs, pair)):
                plain[which][2 * pair + head] = value.astype(BF16)
                turned[which][2 * pair + head] = value.T.astype(BF16)


def attend_first(pairs, sets, operands, turned):
    total = sum(s[3] for s in sets)
    levels = segment_levels(sets)

    def kernel(turn_in, *refs):
        ins = refs[: len(operands)]
        kt, vc, e_ref, tops, sums, out, s_ref, kc, vt = refs[len(operands) :]

        def body(group, heads):
            put_halves(pairs, sets, ins, group, (kc, vc), (kt, vt))
            for pair, head, at in heads:
                q_four, _ = four_rows(head_rows(turn_in, pair, head))
                tops[at] = column_scores(levels, kc, at, q_four, s_ref)
            for _, _, at in heads:
                sums[at] = exponents(levels, at, tops[at], s_ref, e_ref, False)
            for _, _, at in heads:
                out[at] = fold_rows(dot(twice(vt[at]), stacked(e_ref, at), NN))

        each_group(pairs, body)

    heads = 2 * pairs
    outs = [
        jax.ShapeDtypeStruct((heads, LANES, total), BF16),
        jax.ShapeDtypeStruct((heads, total, LANES), BF16),
        jax.ShapeDtypeStruct((heads, 2, total, BOTH), BF16),
    ]
    outs += [struct(heads, 1, BOTH)] * 2 + [struct(heads, HEAD_DIM, BOTH)]
    return call(
        kernel,
        [turned, *operands],
        outs,
        scratch=[
            pltpu.VMEM((heads, total, BOTH), F32),
            pltpu.VMEM((heads, total, LANES), BF16),
            pltpu.VMEM((heads, LANES, total), BF16),
        ],
        **costs(pairs, total, 2, 1),
    )


def attend_last(pairs, sets, operands, turned, tops, sums, partial):
    total = sum(s[3] for s in sets)
    levels = segment_levels(sets)

    def kernel(turn_in, top_in, sum_in, part_in, *refs):
        ins = refs[: len(operands)]
        grads = refs[len(operands) : 2 * len(operands)]
        o_keep, o_send, g_out, r_out, kt, d_ref = refs[2 * len(operands) : -5]
        s_ref, e_ref, kc, vc, vt = refs[-5:]

        def body(group, heads):
            put_halves(pairs, sets, ins, group, (kc, vc), (kt, vt))
            queries = {}
            top = {}
            for pair, head, at in heads:
                q_four, queries[at] = four_rows(head_rows(turn_in, pair, head))
                top[at] = column_scores(levels, kc, at, q_four, s_ref)
            inverse = {}
            rescale = {}
            for _, _, at in heads:
                first_top = top_in[at]
                highest = jnp.maximum(top[at], first_top)
                rescale[at] = jnp.exp2(first_top - highest)
                summed = exponents(levels, at, highest, s_ref, e_ref, True)
                inverse[at] = 1.0 / (summed + sum_in[at] * rescale[at])
            output = {}
            cotangents = {}
            row_dot = {}
            for pair, head, at in heads:
                o = fold_rows(dot(twice(vt[at]), stacked(e_ref, at), NN))
                o = (o + part_in[at] * rescale[at]) * inverse[at]
                output[at] = o
                scaled = head_rows(turn_in, pairs + pair, head) * inverse[at]
                cotangents[at] = four_rows(scaled)
                row_dot[at] = jnp.sum(o * scaled, axis=0, keepdims=True)
                g_out[at] = scaled * rescale[at]
                r_out[at] = row_dot[at] * rescale[at]
            for _, _, at in heads:
                for index in range(len(levels)):
                    rows = pl.ds(index * BLOCK, BLOCK)
                    dp = dot(twice(vc[at, rows]), cotangents[at][0], NN)
                    store_split(d_ref, at, rows, s_ref[at, rows] * (dp - row_dot[at]))
            key_grads = {}
            value_grads = {}
            for _, _, at in heads:
                value_grads[at] = dot(abreast(e_ref, at), twice(cotangents[at][1]), NT)
                key_grads[at] = dot(abreast(d_ref, at), twice(queries[at]), NT)
            for pair in group:
                put_grads(pairs, pair, sets, grads, key_grads, value_grads)
                both = [output[2 * pair], output[2 * pair + 1]]
                both = jnp.concatenate(both, axis=0).T
                o_keep[pair] = both[:BLOCK]
                o_send[pair] = both[BLOCK:]

        each_group(pairs, body)

    heads = 2 * pairs
    outs = [struct(*a.shape) for a in operands]
    outs += [struct(pairs, BLOCK, LANES)] * 2
    outs += [struct(heads, HEAD_DIM, BOTH), struct(heads, 1, BOTH)]
    outs.append(jax.ShapeDtypeStruct((heads, LANES, total), BF16))
    outs.append(jax.ShapeDtypeStruct((heads, 2, total, BOTH), BF16))
    return call(
        kernel,
        [turned, tops, sums, partial, *operands],
        outs,
        scratch=[pltpu.VMEM((heads, total, BOTH), F32)]
        + [pltpu.VMEM((heads, 2, total, BOTH), BF16)]
        + [pltpu.VMEM((heads, total, LANES), BF16)] * 2
        + [pltpu.VMEM((heads, LANES, total), BF16)],
        **costs(pairs, total, 5, 1),
    )


def put_grads(pairs, pair, sets, grads, key_grads, value_grads):
    for which, parts in enumerate((key_grads, value_grads)):
        both = fold_heads(parts[2 * pair], parts[2 * pair + 1])
        if which == 0:
            both = both * (1.0 / LOG2_E)
        filled = 0
        for _, index, row, rows in sets:
            piece = both[filled : filled + rows]
            grads[index][which * pairs + pair, pl.ds(row, rows), :] = piece
            filled += rows


def attend_back(pairs, sets, shapes, first, kept, turned, g_scaled, row_dot, others):
    total = sum(s[3] for s in sets)
    segments = total // BLOCK

    def kernel(turn_in, kt, vc, e_ref, g_in, r_in, *refs):
        other_in = refs[: len(others)]
        grads = refs[len(others) : len(others) + len(shapes)]
        dq_out = refs[len(others) + len(shapes) : -1]
        d_ref = refs[-1]
        span = pl.ds(first, total)

        def body(group, heads):
            cotangents = {}
            for _, _, at in heads:
                g_four, cotangents[at] = four_rows(g_in[at])
                for index in range(segments):
                    rows = pl.ds(first + index * BLOCK, BLOCK)
                    dp = dot(twice(vc[at, rows]), g_four, NN)
                    e = e_ref[at, 0, rows].astype(F32) + e_ref[at, 1, rows].astype(F32)
                    place = pl.ds(index * BLOCK, BLOCK)
                    store_split(d_ref, at, place, e * (dp - r_in[at]))
            queries_grad = {}
            key_grads = {}
            value_grads = {}
            for pair, head, at in heads:
                _, q_rows = four_rows(head_rows(turn_in, pair, head))
                g_rows = cotangents[at]
                value_grads[at] = dot(abreast(e_ref, at, span), twice(g_rows), NT)
                key_grads[at] = dot(abreast(d_ref, at), twice(q_rows), NT)
                if others:
                    d_lo, kt_hi, d_hi = other_in
                    part = dot(twice(kt[at, :, span]), stacked(d_ref, at), NN)
                    part += dot(twice(kt[at, :, total:]), stacked(d_lo, at), NN)
                    part += dot(twice(kt_hi[at]), stacked(d_hi, at), NN)
                    queries_grad[at] = fold_rows(part)
            for pair in group:
                put_grads(pairs, pair, sets, grads, key_grads, value_grads)
                if others:
                    both = [queries_grad[2 * pair], queries_grad[2 * pair + 1]]
                    both = jnp.concatenate(both, axis=0).T * SCALE
                    dq_out[0][pair] = both[:BLOCK]
                    dq_out[1][pair] = both[BLOCK:]

        each_group(pairs, body)

    outs = [struct(*shape) for shape in shapes]
    scratch = []
    if others:
        outs += [struct(pairs, BLOCK, LANES)] * 2
        scratch.append(pltpu.VMEM((2 * pairs, 2, total, BOTH), BF16))
    else:
        outs.append(jax.ShapeDtypeStruct((2 * pairs, 2, total, BOTH), BF16))
    return call(
        kernel,
        [turned, *kept, g_scaled, row_dot, *others],
        outs,
        scratch=scratch,
        **costs(pairs, total, 4),
    )


def copy_columns(moves, ins, sems, bit):
    started = []
    for operand, theirs, column, place in moves:
        side = 1 - bit if theirs else bit
        column = side * (ins[operand].shape[1] // 2) + column
        column = pl.ds(pl.multiple_of(column, LANES), LANES)
        copy = pltpu.make_async_copy(
            ins[operand].at[:, column], place, sems.at[len(started)]
        )
        copy.start()
        started.append(copy)
    return started


def pack(pairs, first, second, scalar):
    def kernel(bit, one, two, theirs, mine, sems):
        moves = []
        for tile in range(2 * pairs):
            for out, other in ((theirs, True), (mine, False)):
                column = tile % pairs * LANES
                moves.append((tile // pairs, other, column, out.at[tile]))
        for copy in copy_columns(moves, (one, two), sems, bit[0]):
            copy.wait()

    return call(
        kernel,
        [first, second],
        [struct(2 * pairs, BLOCK, LANES)] * 2,
        scratch=[pltpu.SemaphoreType.DMA((4 * pairs,))],
        scalar=scalar,
        where=pl.ANY,
    )


QUARTER = BLOCK // 4
HALF = BLOCK // 2


def pack_theirs(pairs, keys, values, scalar):
    def kernel(bit, k, v, finest, coarse, rest, block, sems):
        moves = []
        for tile in range(2 * pairs):
            moves.append((tile // pairs, True, tile % pairs * LANES, block.at[tile]))
        copies = copy_columns(moves, (k, v), sems, bit[0])
        for tile, copy in enumerate(copies):
            copy.wait()
            finest[tile] = mean_rows(block, (tile,), 0, HALF, 2)
            coarse[tile] = mean_rows(finest, (tile,), 0, QUARTER, 2)
            rest[tile, :QUARTER] = half_difference(finest, (tile,), 0, QUARTER)
            rest[tile, QUARTER:] = half_difference(block, (tile,), 0, HALF)

    return call(
        kernel,
        [keys, values],
        [
            struct(2 * pairs, HALF, LANES),
            struct(2 * pairs, QUARTER, LANES),
            struct(2 * pairs, QUARTER + HALF, LANES),
        ],
        scratch=[
            pltpu.VMEM((2 * pairs, BLOCK, LANES), F32),
            pltpu.SemaphoreType.DMA((2 * pairs,)),
        ],
        scalar=scalar,
        where=pl.ANY,
    )


def pack_mine(pairs, keys, values, scalar):
    def kernel(bit, k, v, block, finest, coarse, sems):
        moves = []
        for tile in range(2 * pairs):
            moves.append((tile // pairs, False, tile % pairs * LANES, block.at[tile]))
        copies = copy_columns(moves, (k, v), sems, bit[0])
        for tile, copy in enumerate(copies):
            copy.wait()
            finest[tile] = mean_rows(block, (tile,), 0, HALF, 2)
            coarse[tile] = mean_rows(finest, (tile,), 0, QUARTER, 2)

    return call(
        kernel,
        [keys, values],
        [
            struct(2 * pairs, BLOCK, LANES),
            struct(2 * pairs, HALF, LANES),
            struct(2 * pairs, QUARTER, LANES),
        ],
        scratch=[pltpu.SemaphoreType.DMA((2 * pairs,))],
        scalar=scalar,
        where=pl.ANY,
    )


def rebuild(pairs, second, rest):
    def kernel(second_in, rest_in, out, finest):
        for tile in range(2 * pairs):
            put_pairs(finest, (tile,), second_in[tile], rest_in[tile, :QUARTER])
            put_pairs(out, (tile,), finest[tile], rest_in[tile, QUARTER:])

    return call(
        kernel,
        [second, rest],
        [struct(2 * pairs, BLOCK, LANES)],
        scratch=[pltpu.VMEM((2 * pairs, HALF, LANES), F32)],
    )[0]


def take_apart(pairs, block_grad):
    def kernel(block, second, rest, finest):
        for tile in range(2 * pairs):
            finest[tile] = 2.0 * mean_rows(block, (tile,), 0, HALF, 2)
            rest[tile, QUARTER:] = 2.0 * half_difference(block, (tile,), 0, HALF)
            second[tile] = 2.0 * mean_rows(finest, (tile,), 0, QUARTER, 2)
            rest[tile, :QUARTER] = 2.0 * half_difference(finest, (tile,), 0, QUARTER)

    return call(
        kernel,
        [block_grad],
        [
            struct(2 * pairs, QUARTER, LANES),
            struct(2 * pairs, QUARTER + HALF, LANES),
        ],
        scratch=[pltpu.VMEM((2 * pairs, HALF, LANES), F32)],
    )


class Levels:
    def __init__(self, bits):
        self.bits = bits
        self.rows = BLOCK >> bits
        self.differences = [
            [(m, BLOCK >> m) for m in range(bits, step, -1)] for step in range(bits)
        ]
        whole = [0] + [BLOCK >> step for step in range(1, bits)]
        self.whole = Tree(1, whole)
        self.rough = Tree(1, [0] + [self.rows] * (bits - 1))
        self.fine = Tree(1, [0] + [rows - self.rows for rows in whole[1:]])
        self.pieces = []
        for level in range(1, bits):
            trees = (self.whole, self.rough, self.fine)
            for parts in zip(*(tree.held[level] for tree in trees)):
                self.pieces.append((level, parts[0][0], *(part[1] for part in parts)))

    def scratch(self):
        shapes = [(BLOCK >> m, LANES) for m in range(1, self.bits + 1)]
        return [pltpu.VMEM(shape, F32) for shape in shapes]

    def group_pieces(self):
        pieces = []
        for index, (level, step, whole, rough, _) in enumerate(self.pieces):
            factor = 1 << self.bits - level
            place = (2 + index) * self.rows
            pieces.append((step, whole, rough, BLOCK >> level, factor, place))
        return pieces


def coarsen_pair(lo, pairs, mine, received):
    def kernel(own, got, *outs):
        for tile in range(2 * pairs):
            outs[0][tile, : BLOCK // 4] = own[tile]
            outs[0][tile, BLOCK // 4 :] = got[tile]
            for index in range(1, lo.bits):
                outs[index][tile] = mean_rows(
                    outs[index - 1], (tile,), 0, BLOCK >> index + 1, 2
                )

    outs = [struct(2 * pairs, BLOCK >> step, LANES) for step in range(1, lo.bits + 1)]
    return call(kernel, [mine, received], outs)


def group_pieces(lo):
    own = BLOCK >> lo.bits
    factor = 1 << lo.bits
    pieces = [
        (-2, 0, BLOCK // 2, factor, own),
        (-1, 0, BLOCK // 2, factor, own + own // 2),
    ]
    filled = 2 * own
    for level in range(1, lo.bits):
        factor = 1 << lo.bits - level
        for step, row, rows in lo.held[level]:
            pieces.append((step, row, rows, factor, filled))
            filled += rows // factor
    return pieces


def coarsen_group(lo, hi, pairs, own, halves, arrived):
    pieces = group_pieces(lo)

    def kernel(own_in, *refs):
        ins = refs[: 2 + lo.bits]
        outs = refs[2 + lo.bits :]
        for tile in range(2 * pairs):
            outs[0][tile, pl.ds(0, BLOCK >> lo.bits)] = own_in[tile]
            for step, row, rows, factor, place in pieces:
                count = rows // factor
                outs[0][tile, pl.ds(place, count)] = mean_rows(
                    ins[2 + step], (tile,), row, count, factor
                )
            for step in range(1, hi.bits):
                outs[step][tile] = mean_rows(
                    outs[step - 1], (tile,), 0, BLOCK >> step, 2
                )

    outs = [struct(2 * pairs, BLOCK >> step, LANES) for step in range(hi.bits)]
    return call(kernel, [own, *halves, *arrived], outs)


def turn(pairs, mine, received):
    def kernel(own, got, turned):
        for tile in range(2 * pairs):
            both = jnp.concatenate([own[tile], got[tile]], axis=0).T
            turned[tile] = both * (SCALE * LOG2_E) if tile < pairs else both

    return call(kernel, [mine, received], [struct(2 * pairs, LANES, 2 * BLOCK)])[0]


def take_levels(levels, pairs, grads):
    trees = (levels.rough, levels.fine)

    def kernel(*refs):
        ins = refs[: levels.bits]
        rough = refs[levels.bits : 2 * levels.bits]
        fine = refs[2 * levels.bits : 3 * levels.bits]
        ladder = refs[3 * levels.bits :]
        for tile in range(2 * pairs):
            for level, step, row, rough_row, fine_row in levels.pieces:
                source = ladder[level - 1]
                source[...] = ins[step][tile, pl.ds(row, BLOCK >> level)]
                fine_row += sum(rows for _, rows in levels.differences[level])
                for m, rows in reversed(levels.differences[level]):
                    fine_row -= rows
                    part = 2.0 * half_difference(source, (), 0, rows)
                    fine[step][tile, pl.ds(fine_row, rows)] = part
                    ladder[m - 1][...] = 2.0 * mean_rows(source, (), 0, rows, 2)
                    source = ladder[m - 1]
                rough[step][tile, pl.ds(rough_row, levels.rows)] = source[...]

    outs = [
        struct(2 * pairs, tree.rows(step), LANES)
        for tree in trees
        for step in range(levels.bits)
    ]
    outs = call(kernel, grads, outs, scratch=levels.scratch())
    return outs[: levels.bits], outs[levels.bits :]


def spread_group(levels, hi, pairs, group_grads, grads):
    own_rows = levels.rows

    def kernel(*refs):
        steps = refs[: hi.bits]
        ins = refs[hi.bits : hi.bits + levels.bits]
        own_out, *outs = refs[hi.bits + levels.bits : -1]
        total = refs[-1]
        for tile in range(2 * pairs):
            total[tile] = steps[0][tile, pl.ds(0, BLOCK)]
            for step in range(1, hi.bits):
                above = steps[step][tile, pl.ds(0, BLOCK >> step)]
                add_spread(total, (tile,), 0, above, 1 << step)
            own_out[tile] = total[tile, pl.ds(0, own_rows)]
            for step, _, row, _, _, place in levels.group_pieces():
                rows = pl.ds(row, own_rows)
                part = total[tile, pl.ds(place, own_rows)]
                outs[step][tile, rows] = ins[step][tile, rows] + part
            outs[0][tile, pl.ds(ins[0].shape[1], own_rows)] = total[
                tile, pl.ds(own_rows, own_rows)
            ]

    shapes = [list(a.shape) for a in grads]
    shapes[0][1] += own_rows
    outs = [struct(2 * pairs, own_rows, LANES)] + [struct(*shape) for shape in shapes]
    own, *grads = call(
        kernel,
        [*group_grads, *grads],
        outs,
        scratch=[pltpu.VMEM((2 * pairs, BLOCK, LANES), F32)],
    )
    return own, grads


def spread_pair(levels, pairs, own_grad, rough, fine, block_second):
    own_rows = levels.rows

    def kernel(own, block, *refs):
        rough_in = refs[: levels.bits - 1]
        fine_in = refs[levels.bits - 1 : 2 * levels.bits - 1]
        mine, theirs, *ladder = refs[2 * levels.bits - 1 :]
        last = pl.ds(rough_in[0].shape[1] - own_rows, own_rows)
        for tile in range(2 * pairs):
            above = own[tile] + rough_in[0][tile, last]
            for step in range(1, levels.bits - 1):
                above = above + rough_in[step][tile, pl.ds(0, own_rows)]
            filled = 0
            for m, rows in levels.differences[1]:
                part = fine_in[1][tile, pl.ds(filled, rows)]
                for step in range(2, min(m, levels.bits)):
                    part = part + fine_in[step][tile, pl.ds(filled, rows)]
                filled += rows
                put_pairs(ladder[m - 2], (), 0.5 * above, 0.5 * part)
                above = ladder[m - 2][...]
            mine[tile] = above[:QUARTER]
            theirs[tile] = above[QUARTER:] + block[tile]

    return call(
        kernel,
        [own_grad, block_second, *rough, *fine],
        [struct(2 * pairs, QUARTER, LANES)] * 2,
        scratch=levels.scratch(),
    )


def unpack(pairs, kept, arrived, features, scalar):
    def kernel(bit, *refs):
        outs = refs[4:]
        for which in range(2):
            for pair in range(pairs):
                for side, ref in ((bit[0], refs[which]), (1 - bit[0], refs[2 + which])):
                    column = side * (features // 2) + pair * LANES
                    column = pl.ds(pl.multiple_of(column, LANES), LANES)
                    outs[which][:, column] = ref[pair]

    return call(kernel, [*kept, *arrived], [struct(BLOCK, features)] * 2, scalar=scalar)


def finish(pairs, kept, rest, finest, seconds, endings, features, scalar):
    count = endings[0].shape[1]

    def kernel(bit, kept_in, rest_in, f_mine, f_theirs, s_mine, s_theirs, *refs):
        e_mine, e_theirs = refs[:2]
        outs, total, middle, second = refs[2:4], refs[4], refs[5], refs[6]
        for tile in range(2 * pairs):
            out = outs[tile // pairs]
            column = tile % pairs * LANES
            at = (tile,)
            total[tile] = kept_in[tile]
            add_spread(total, at, 0, f_mine[tile], 2)
            add_spread(total, at, 0, s_mine[tile], 4)
            add_spread(total, at, 0, e_mine[tile], BLOCK // count)
            place = bit[0] * (features // 2) + column
            out[:, pl.ds(pl.multiple_of(place, LANES), LANES)] = total[tile]
            second[tile] = s_theirs[tile]
            add_spread(second, at, 0, e_theirs[tile], QUARTER // count)
            put_pairs(middle, at, 0.5 * second[tile], 0.5 * rest_in[tile, :QUARTER])
            first = 0.5 * (middle[tile] + f_theirs[tile])
            put_pairs(total, at, first, 0.5 * rest_in[tile, QUARTER:])
            place = (1 - bit[0]) * (features // 2) + column
            out[:, pl.ds(pl.multiple_of(place, LANES), LANES)] = total[tile]

    return call(
        kernel,
        [kept, rest, *finest, *seconds, *endings],
        [struct(BLOCK, features)] * 2,
        scratch=[
            pltpu.VMEM((2 * pairs, BLOCK, LANES), F32),
            pltpu.VMEM((2 * pairs, HALF, LANES), F32),
            pltpu.VMEM((2 * pairs, QUARTER, LANES), F32),
        ],
        scalar=scalar,
    )


def on_device(queries, keys, values, cotangent):
    features = queries.shape[1]
    assert queries.shape[0] == BLOCK
    pairs = features // LANES // 2
    lo_bits = lax.axis_size("seqlo").bit_length() - 1
    levels = Levels(lo_bits - 1)
    lo = levels.whole
    hi_bits = lax.axis_size("seqhi").bit_length() - 1
    hi = Tree(lo_bits, [BLOCK >> step for step in range(hi_bits)])
    scalar = (lax.axis_index("seqlo") % 2).astype(jnp.int32).reshape(1)
    queries, keys, values, cotangent = [
        pltpu.with_memory_space_constraint(array, pltpu.HBM)
        for array in (queries, keys, values, cotangent)
    ]
    f_theirs, c_send, rest = pack_theirs(pairs, keys, values, scalar)
    mine_kv, f_mine, c_mine = pack_mine(pairs, keys, values, scalar)
    second = exchange(c_send, 1)
    finest_theirs = exchange(f_theirs, 2)
    coarse = coarsen_pair(lo, pairs, c_mine, second)
    finest = exchange(ordered(f_mine, finest_theirs), 2)
    rest = exchange(ordered(rest, coarse[0]), 1)
    half = exchange(ordered(finest_theirs, rest), 1)
    kv = rebuild(pairs, second, rest)
    send_qg, mine_qg = pack(pairs, queries, cotangent, scalar)
    qg = exchange(ordered(send_qg, half), 1)
    zs = lo.gather([None, *coarse], (finest, send_qg))
    group = coarsen_group(
        lo, hi, pairs, ordered(coarse[-1], rest), [finest, half], zs
    )
    turned = turn(pairs, mine_qg, qg)
    rs = hi.gather(group, turned)
    block_sets = [(0, 0, 0, BLOCK), (0, 1, 0, BLOCK)]
    lo_sets = [(1, 2, 0, BLOCK // 2), (1, 3, 0, BLOCK // 2)]
    for level in range(lo.bits):
        for step, row, rows in lo.held[level]:
            lo_sets.append((1 + level, 4 + step, row, rows))
    hi_sets = []
    for level in range(hi.bits):
        for step, row, rows in hi.held[level]:
            hi_sets.append((lo_bits + level, step, row, rows))
    first_in = [mine_kv, kv, finest, half, *zs]
    *kept, tops, sums, partial = attend_first(
        pairs, block_sets + lo_sets, first_in, turned
    )
    *rs_grads, o_keep, o_send, g_scaled, row_dot, kt_hi, d_hi = attend_last(
        pairs, hi_sets, rs, turned, tops, sums, partial
    )
    shapes = [(2 * pairs, *a.shape[1:]) for a in first_in]
    finest_grad, half_grad, *zs_grads, d_lo = attend_back(
        pairs,
        [(level, index - 2, row, rows) for level, index, row, rows in lo_sets],
        shapes[2:],
        BOTH,
        kept,
        turned,
        g_scaled,
        row_dot,
        [],
    )
    kv_keep, kv_send, dq_keep, dq_send = attend_back(
        pairs,
        block_sets,
        shapes[:2],
        0,
        kept,
        turned,
        g_scaled,
        row_dot,
        [d_lo, kt_hi, d_hi],
    )
    rough_grads, fine_grads = take_levels(levels, pairs, zs_grads)
    group_grads = hi.scatter(rs_grads)
    half_back = exchange(ordered(half_grad, kv_send), 1)
    o_back = exchange(o_send, 1)
    fine_back, finest_mine = levels.fine.scatter(fine_grads, finest_grad)
    block_second, rest_grad = take_apart(pairs, kv_send)
    split_at = rest_grad.shape[1]
    bulk = jnp.concatenate([rest_grad, dq_send.reshape(2 * pairs, HALF, LANES)], axis=1)
    bulk = exchange(ordered(bulk, o_back), 1)
    rest_back = bulk[:, :split_at]
    dq_back = bulk[:, split_at:].reshape(pairs, BLOCK, LANES)
    group_grads[-1] = ordered(group_grads[-1], kv_send)
    own_grad, rough_grads = spread_group(levels, hi, pairs, group_grads, rough_grads)
    *rough_back, ending = levels.rough.scatter(rough_grads, whole=False)
    half_rows = levels.rows // 2
    finest_theirs = exchange(ordered(half_back, rough_back[0]), 2)
    far = 1 << levels.bits
    ending_mine = exchange(ending[:, :half_rows], far)
    ending_theirs = exchange(ending[:, half_rows:], far + 1)
    second_mine, second_send = spread_pair(
        levels, pairs, own_grad, rough_back, fine_back, block_second
    )
    second_theirs = exchange(second_send, 1)
    attended, query_grad = unpack(
        pairs, (o_keep, dq_keep), (o_back, dq_back), features, scalar
    )
    key_grad, value_grad = finish(
        pairs,
        kv_keep,
        rest_back,
        (finest_mine, finest_theirs),
        (second_mine, second_theirs),
        (ending_mine, ending_theirs),
        features,
        scalar,
    )
    return attended, query_grad, key_grad, value_grad


def solution(mesh):
    spec = P(AXES, None)
    return jax.shard_map(
        on_device,
        mesh=mesh,
        in_specs=(spec,) * 4,
        out_specs=(spec,) * 4,
        check_vma=False,
    )
```

```python
import math

import jax
import jax.numpy as jnp
from jax import lax
from jax.experimental import pallas as pl
from jax.experimental.pallas import tpu as pltpu
from jax.sharding import PartitionSpec as P

HEADS = 12
BLOCK = 128
HEAD_DIM = 64
LANES = 2 * HEAD_DIM
AXES = ("seqhi", "seqlo")
VMEM_LIMIT = 20 * 1024 * 1024
F32 = jnp.float32
BF16 = jnp.bfloat16
LOG2_E = 1.0 / math.log(2.0)
SCALE = 1.0 / math.sqrt(HEAD_DIM)


def struct(*shape):
    return jax.ShapeDtypeStruct(shape, F32)


def call(kernel, operands, outs, scratch=(), scalar=None, flops=0, exps=0, where=None):
    vmem = pl.BlockSpec(memory_space=pltpu.VMEM)
    smem = pl.BlockSpec(memory_space=pltpu.SMEM)
    in_specs = [pl.BlockSpec(memory_space=where) if where else vmem] * len(operands)
    if scalar is not None:
        operands = [scalar, *operands]
        in_specs = [smem, *in_specs]
    moved = sum(4 * math.prod(a.shape) for a in [*operands, *outs])
    return pl.pallas_call(
        kernel,
        out_shape=list(outs),
        in_specs=in_specs,
        out_specs=[vmem] * len(outs),
        scratch_shapes=list(scratch),
        compiler_params=pltpu.CompilerParams(vmem_limit_bytes=VMEM_LIMIT),
        cost_estimate=pl.CostEstimate(
            flops=flops, bytes_accessed=moved, transcendentals=exps
        ),
    )(*operands)


def exchange(value, offset):
    count = lax.axis_size(AXES)
    return lax.ppermute(value, AXES, [(i, i ^ offset) for i in range(count)])


def ordered(value, after):
    return value if after is None else lax.optimization_barrier((value, after))[0]


def half_difference(ref, lead, first, count):
    even = ref[(*lead, pl.ds(first, count, stride=2), slice(None))]
    odd = ref[(*lead, pl.ds(first + 1, count, stride=2), slice(None))]
    return 0.5 * (even - odd)


def put_pairs(ref, lead, total, difference):
    count = total.shape[0]
    ref[(*lead, pl.ds(0, count, stride=2), slice(None))] = total + difference
    ref[(*lead, pl.ds(1, count, stride=2), slice(None))] = total - difference


def mean_rows(ref, lead, first, count, factor):
    total = None
    for step in range(factor):
        rows = pl.ds(first + step, count, stride=factor)
        part = ref[(*lead, rows, slice(None))]
        total = part if total is None else total + part
    return total * (1.0 / factor)


def add_spread(ref, lead, first, value, factor):
    count = value.shape[0]
    value = value * (1.0 / factor)
    for step in range(factor):
        rows = pl.ds(first + step, count, stride=factor)
        place = (*lead, rows, slice(None))
        ref[place] = ref[place] + value


class Tree:
    def __init__(self, first_bit, own_rows):
        self.bits = bits = len(own_rows)
        self.first_bit = first_bit
        self.own_rows = own_rows
        self.held = {}
        self.payload = {}
        for step in range(bits - 1, -1, -1):
            rows = self.own_rows[step]
            payload = []
            fresh = {step: [(step, 0, rows)] if rows else []}
            for level in range(step + 1, bits):
                for piece in self.held[level]:
                    payload.append(piece)
                    fresh.setdefault(level, []).append((step, rows, piece[2]))
                    rows += piece[2]
            self.payload[step] = payload
            for level, pieces in fresh.items():
                self.held[level] = self.held.get(level, []) + pieces

    def rows(self, step):
        return self.own_rows[step] + sum(piece[2] for piece in self.payload[step])

    def partner(self, value, step):
        return exchange(value, 1 << self.first_bit + step)

    def gather(self, own, after=None):
        arrived = [None] * self.bits
        for step in range(self.bits - 1, -1, -1):
            parts = [own[step]] if self.own_rows[step] else []
            for source, row, rows in self.payload[step]:
                part = arrived[source]
                whole = rows == part.shape[1]
                parts.append(part if whole else part[:, row : row + rows])
            sent = jnp.concatenate(parts, axis=1) if len(parts) > 1 else parts[0]
            if step == 0:
                sent = ordered(sent, after)
            arrived[step] = self.partner(sent, step)
        return arrived

    def scatter(self, grads, front=None, whole=True):
        grads = list(grads)
        returned = []
        for step in range(self.bits if whole else self.bits - 1):
            sent = grads[step]
            if step == 0 and front is not None:
                rows = front.shape[1]
                back = self.partner(jnp.concatenate([front, sent], axis=1), step)
                front, back = back[:, :rows], back[:, rows:]
            else:
                back = self.partner(sent, step)
            returned.append(back)
            filled = self.own_rows[step]
            for source, row, rows in self.payload[step]:
                part = back[:, filled : filled + rows]
                grads[source] = grads[source].at[:, row : row + rows].add(part)
                filled += rows
        if not whole:
            returned.append(grads[-1])
        return returned if front is None else (returned, front)


def split(value):
    high = value.astype(BF16).astype(F32)
    return high, value - high


def halves_by_head(value):
    high, low = split(value)
    first = lax.broadcasted_iota(jnp.int32, value.shape, 1) < HEAD_DIM
    one = jnp.where(first, high, pltpu.roll(low, HEAD_DIM, 1))
    two = jnp.where(first, pltpu.roll(high, HEAD_DIM, 1), low)
    return one, two


def dot(lhs, rhs, dims):
    return lax.dot_general(lhs, rhs, (dims, ((), ())), preferred_element_type=F32)


NN = ((1,), (0,))
NT = ((1,), (1,))


BOTH = 2 * BLOCK
GROUP = 3


def halves_of(sets, ins, which, pairs, pair):
    tile = which * pairs + pair
    parts = [ins[index][tile, pl.ds(row, rows), :] for _, index, row, rows in sets]
    return halves_by_head(jnp.concatenate(parts, axis=0))


def segment_levels(sets):
    levels, filled = [], 0
    for level, _, _, rows in sets:
        if filled % BLOCK == 0:
            levels.append(level)
        filled += rows
    return levels


def four_rows(value):
    high, low = split(value)
    four = jnp.concatenate([high, high, low, low], axis=0).astype(BF16)
    return four, jnp.concatenate([high, low], axis=0).astype(BF16)


def store_split(ref, lead, rows, value):
    high = value.astype(BF16)
    ref[(lead, 0, rows)] = high
    ref[(lead, 1, rows)] = (value - high.astype(F32)).astype(BF16)


def fold_rows(value):
    return value[:HEAD_DIM] + value[HEAD_DIM:]


def fold_heads(one, two):
    first = lax.broadcasted_iota(jnp.int32, one.shape, 1) < HEAD_DIM
    return jnp.where(
        first, one + pltpu.roll(one, HEAD_DIM, 1), two + pltpu.roll(two, HEAD_DIM, 1)
    )


def twice(value):
    return jnp.concatenate([value, value], axis=1)


def stacked(ref, at, rows=slice(None)):
    return jnp.concatenate([ref[at, 0, rows], ref[at, 1, rows]], axis=0)


def abreast(ref, at, rows=slice(None)):
    return jnp.concatenate([ref[at, 0, rows], ref[at, 1, rows]], axis=1)


def column_scores(levels, keys, at, q_four, s_ref):
    highest = None
    for index, level in enumerate(levels):
        rows = pl.ds(index * BLOCK, BLOCK)
        s = dot(twice(keys[at, rows]), q_four, NN)
        s = s + float(level) if level else s
        s_ref[at, rows] = s
        top = jnp.max(s.reshape(BLOCK // 8, 8, BOTH), axis=0)
        highest = top if highest is None else jnp.maximum(highest, top)
    return jnp.max(highest, axis=0, keepdims=True)


def exponents(levels, at, top, s_ref, e_ref, keep):
    summed = None
    for index in range(len(levels)):
        rows = pl.ds(index * BLOCK, BLOCK)
        e = jnp.exp2(s_ref[at, rows] - top)
        if keep:
            s_ref[at, rows] = e
        store_split(e_ref, at, rows, e)
        part = jnp.sum(e.reshape(BLOCK // 8, 8, BOTH), axis=0)
        summed = part if summed is None else summed + part
    return jnp.sum(summed, axis=0, keepdims=True)


def head_rows(ref, pair, head):
    return ref[pair, pl.ds(head * HEAD_DIM, HEAD_DIM)]


def each_group(pairs, body):
    for first in range(0, pairs, GROUP):
        group = range(first, min(first + GROUP, pairs))
        body(group, [(pair, head, 2 * pair + head) for pair in group for head in (0, 1)])


def costs(pairs, rows, products, exps=0):
    return dict(
        flops=2 * 4 * products * pairs * 2 * rows * BOTH * HEAD_DIM,
        exps=exps * pairs * 2 * rows * BOTH,
    )


def put_halves(pairs, sets, ins, group, plain, turned):
    for which in range(2):
        for pair in group:
            for head, value in enumerate(halves_of(sets, ins, which, pairs, pair)):
                plain[which][2 * pair + head] = value.astype(BF16)
                turned[which][2 * pair + head] = value.T.astype(BF16)


def attend_first(pairs, sets, operands, turned):
    total = sum(s[3] for s in sets)
    levels = segment_levels(sets)

    def kernel(turn_in, *refs):
        ins = refs[: len(operands)]
        kt, vc, e_ref, tops, sums, out, s_ref, kc, vt = refs[len(operands) :]

        def body(group, heads):
            put_halves(pairs, sets, ins, group, (kc, vc), (kt, vt))
            for pair, head, at in heads:
                q_four, _ = four_rows(head_rows(turn_in, pair, head))
                tops[at] = column_scores(levels, kc, at, q_four, s_ref)
            for _, _, at in heads:
                sums[at] = exponents(levels, at, tops[at], s_ref, e_ref, False)
            for _, _, at in heads:
                out[at] = fold_rows(dot(twice(vt[at]), stacked(e_ref, at), NN))

        each_group(pairs, body)

    heads = 2 * pairs
    outs = [
        jax.ShapeDtypeStruct((heads, LANES, total), BF16),
        jax.ShapeDtypeStruct((heads, total, LANES), BF16),
        jax.ShapeDtypeStruct((heads, 2, total, BOTH), BF16),
    ]
    outs += [struct(heads, 1, BOTH)] * 2 + [struct(heads, HEAD_DIM, BOTH)]
    return call(
        kernel,
        [turned, *operands],
        outs,
        scratch=[
            pltpu.VMEM((heads, total, BOTH), F32),
            pltpu.VMEM((heads, total, LANES), BF16),
            pltpu.VMEM((heads, LANES, total), BF16),
        ],
        **costs(pairs, total, 2, 1),
    )


def attend_last(pairs, sets, operands, turned, tops, sums, partial):
    total = sum(s[3] for s in sets)
    levels = segment_levels(sets)

    def kernel(turn_in, top_in, sum_in, part_in, *refs):
        ins = refs[: len(operands)]
        grads = refs[len(operands) : 2 * len(operands)]
        o_keep, o_send, g_out, r_out, kt, d_ref = refs[2 * len(operands) : -5]
        s_ref, e_ref, kc, vc, vt = refs[-5:]

        def body(group, heads):
            put_halves(pairs, sets, ins, group, (kc, vc), (kt, vt))
            queries = {}
            top = {}
            for pair, head, at in heads:
                q_four, queries[at] = four_rows(head_rows(turn_in, pair, head))
                top[at] = column_scores(levels, kc, at, q_four, s_ref)
            inverse = {}
            rescale = {}
            for _, _, at in heads:
                first_top = top_in[at]
                highest = jnp.maximum(top[at], first_top)
                rescale[at] = jnp.exp2(first_top - highest)
                summed = exponents(levels, at, highest, s_ref, e_ref, True)
                inverse[at] = 1.0 / (summed + sum_in[at] * rescale[at])
            output = {}
            cotangents = {}
            row_dot = {}
            for pair, head, at in heads:
                o = fold_rows(dot(twice(vt[at]), stacked(e_ref, at), NN))
                o = (o + part_in[at] * rescale[at]) * inverse[at]
                output[at] = o
                scaled = head_rows(turn_in, pairs + pair, head) * inverse[at]
                cotangents[at] = four_rows(scaled)
                row_dot[at] = jnp.sum(o * scaled, axis=0, keepdims=True)
                g_out[at] = scaled * rescale[at]
                r_out[at] = row_dot[at] * rescale[at]
            for _, _, at in heads:
                for index in range(len(levels)):
                    rows = pl.ds(index * BLOCK, BLOCK)
                    dp = dot(twice(vc[at, rows]), cotangents[at][0], NN)
                    store_split(d_ref, at, rows, s_ref[at, rows] * (dp - row_dot[at]))
            key_grads = {}
            value_grads = {}
            for _, _, at in heads:
                value_grads[at] = dot(abreast(e_ref, at), twice(cotangents[at][1]), NT)
                key_grads[at] = dot(abreast(d_ref, at), twice(queries[at]), NT)
            for pair in group:
                put_grads(pairs, pair, sets, grads, key_grads, value_grads)
                both = [output[2 * pair], output[2 * pair + 1]]
                both = jnp.concatenate(both, axis=0).T
                o_keep[pair] = both[:BLOCK]
                o_send[pair] = both[BLOCK:]

        each_group(pairs, body)

    heads = 2 * pairs
    outs = [struct(*a.shape) for a in operands]
    outs += [struct(pairs, BLOCK, LANES)] * 2
    outs += [struct(heads, HEAD_DIM, BOTH), struct(heads, 1, BOTH)]
    outs.append(jax.ShapeDtypeStruct((heads, LANES, total), BF16))
    outs.append(jax.ShapeDtypeStruct((heads, 2, total, BOTH), BF16))
    return call(
        kernel,
        [turned, tops, sums, partial, *operands],
        outs,
        scratch=[pltpu.VMEM((heads, total, BOTH), F32)]
        + [pltpu.VMEM((heads, 2, total, BOTH), BF16)]
        + [pltpu.VMEM((heads, total, LANES), BF16)] * 2
        + [pltpu.VMEM((heads, LANES, total), BF16)],
        **costs(pairs, total, 5, 1),
    )


def put_grads(pairs, pair, sets, grads, key_grads, value_grads):
    for which, parts in enumerate((key_grads, value_grads)):
        both = fold_heads(parts[2 * pair], parts[2 * pair + 1])
        if which == 0:
            both = both * (1.0 / LOG2_E)
        filled = 0
        for _, index, row, rows in sets:
            piece = both[filled : filled + rows]
            grads[index][which * pairs + pair, pl.ds(row, rows), :] = piece
            filled += rows


def attend_back(pairs, sets, shapes, first, kept, turned, g_scaled, row_dot, others):
    total = sum(s[3] for s in sets)
    segments = total // BLOCK

    def kernel(turn_in, kt, vc, e_ref, g_in, r_in, *refs):
        other_in = refs[: len(others)]
        grads = refs[len(others) : len(others) + len(shapes)]
        dq_out = refs[len(others) + len(shapes) : -1]
        d_ref = refs[-1]
        span = pl.ds(first, total)

        def body(group, heads):
            cotangents = {}
            for _, _, at in heads:
                g_four, cotangents[at] = four_rows(g_in[at])
                for index in range(segments):
                    rows = pl.ds(first + index * BLOCK, BLOCK)
                    dp = dot(twice(vc[at, rows]), g_four, NN)
                    e = e_ref[at, 0, rows].astype(F32) + e_ref[at, 1, rows].astype(F32)
                    place = pl.ds(index * BLOCK, BLOCK)
                    store_split(d_ref, at, place, e * (dp - r_in[at]))
            queries_grad = {}
            key_grads = {}
            value_grads = {}
            for pair, head, at in heads:
                _, q_rows = four_rows(head_rows(turn_in, pair, head))
                g_rows = cotangents[at]
                value_grads[at] = dot(abreast(e_ref, at, span), twice(g_rows), NT)
                key_grads[at] = dot(abreast(d_ref, at), twice(q_rows), NT)
                if others:
                    d_lo, kt_hi, d_hi = other_in
                    part = dot(twice(kt[at, :, span]), stacked(d_ref, at), NN)
                    part += dot(twice(kt[at, :, total:]), stacked(d_lo, at), NN)
                    part += dot(twice(kt_hi[at]), stacked(d_hi, at), NN)
                    queries_grad[at] = fold_rows(part)
            for pair in group:
                put_grads(pairs, pair, sets, grads, key_grads, value_grads)
                if others:
                    both = [queries_grad[2 * pair], queries_grad[2 * pair + 1]]
                    both = jnp.concatenate(both, axis=0).T * SCALE
                    dq_out[0][pair] = both[:BLOCK]
                    dq_out[1][pair] = both[BLOCK:]

        each_group(pairs, body)

    outs = [struct(*shape) for shape in shapes]
    scratch = []
    if others:
        outs += [struct(pairs, BLOCK, LANES)] * 2
        scratch.append(pltpu.VMEM((2 * pairs, 2, total, BOTH), BF16))
    else:
        outs.append(jax.ShapeDtypeStruct((2 * pairs, 2, total, BOTH), BF16))
    return call(
        kernel,
        [turned, *kept, g_scaled, row_dot, *others],
        outs,
        scratch=scratch,
        **costs(pairs, total, 4),
    )


def copy_columns(moves, ins, sems, bit):
    started = []
    for operand, theirs, column, place in moves:
        side = 1 - bit if theirs else bit
        column = side * (ins[operand].shape[1] // 2) + column
        column = pl.ds(pl.multiple_of(column, LANES), LANES)
        copy = pltpu.make_async_copy(
            ins[operand].at[:, column], place, sems.at[len(started)]
        )
        copy.start()
        started.append(copy)
    return started


def pack(pairs, first, second, scalar):
    def kernel(bit, one, two, theirs, mine, sems):
        moves = []
        for tile in range(2 * pairs):
            for out, other in ((theirs, True), (mine, False)):
                column = tile % pairs * LANES
                moves.append((tile // pairs, other, column, out.at[tile]))
        for copy in copy_columns(moves, (one, two), sems, bit[0]):
            copy.wait()

    return call(
        kernel,
        [first, second],
        [struct(2 * pairs, BLOCK, LANES)] * 2,
        scratch=[pltpu.SemaphoreType.DMA((4 * pairs,))],
        scalar=scalar,
        where=pl.ANY,
    )


QUARTER = BLOCK // 4
HALF = BLOCK // 2


def pack_theirs(pairs, keys, values, scalar):
    def kernel(bit, k, v, finest, coarse, rest, block, sems):
        moves = []
        for tile in range(2 * pairs):
            moves.append((tile // pairs, True, tile % pairs * LANES, block.at[tile]))
        copies = copy_columns(moves, (k, v), sems, bit[0])
        for tile, copy in enumerate(copies):
            copy.wait()
            finest[tile] = mean_rows(block, (tile,), 0, HALF, 2)
            coarse[tile] = mean_rows(finest, (tile,), 0, QUARTER, 2)
            rest[tile, :QUARTER] = half_difference(finest, (tile,), 0, QUARTER)
            rest[tile, QUARTER:] = half_difference(block, (tile,), 0, HALF)

    return call(
        kernel,
        [keys, values],
        [
            struct(2 * pairs, HALF, LANES),
            struct(2 * pairs, QUARTER, LANES),
            struct(2 * pairs, QUARTER + HALF, LANES),
        ],
        scratch=[
            pltpu.VMEM((2 * pairs, BLOCK, LANES), F32),
            pltpu.SemaphoreType.DMA((2 * pairs,)),
        ],
        scalar=scalar,
        where=pl.ANY,
    )


def pack_mine(pairs, keys, values, scalar):
    def kernel(bit, k, v, block, finest, coarse, sems):
        moves = []
        for tile in range(2 * pairs):
            moves.append((tile // pairs, False, tile % pairs * LANES, block.at[tile]))
        copies = copy_columns(moves, (k, v), sems, bit[0])
        for tile, copy in enumerate(copies):
            copy.wait()
            finest[tile] = mean_rows(block, (tile,), 0, HALF, 2)
            coarse[tile] = mean_rows(finest, (tile,), 0, QUARTER, 2)

    return call(
        kernel,
        [keys, values],
        [
            struct(2 * pairs, BLOCK, LANES),
            struct(2 * pairs, HALF, LANES),
            struct(2 * pairs, QUARTER, LANES),
        ],
        scratch=[pltpu.SemaphoreType.DMA((2 * pairs,))],
        scalar=scalar,
        where=pl.ANY,
    )


def rebuild(pairs, second, rest):
    def kernel(second_in, rest_in, out, finest):
        for tile in range(2 * pairs):
            put_pairs(finest, (tile,), second_in[tile], rest_in[tile, :QUARTER])
            put_pairs(out, (tile,), finest[tile], rest_in[tile, QUARTER:])

    return call(
        kernel,
        [second, rest],
        [struct(2 * pairs, BLOCK, LANES)],
        scratch=[pltpu.VMEM((2 * pairs, HALF, LANES), F32)],
    )[0]


def take_apart(pairs, block_grad):
    def kernel(block, second, rest, finest):
        for tile in range(2 * pairs):
            finest[tile] = 2.0 * mean_rows(block, (tile,), 0, HALF, 2)
            rest[tile, QUARTER:] = 2.0 * half_difference(block, (tile,), 0, HALF)
            second[tile] = 2.0 * mean_rows(finest, (tile,), 0, QUARTER, 2)
            rest[tile, :QUARTER] = 2.0 * half_difference(finest, (tile,), 0, QUARTER)

    return call(
        kernel,
        [block_grad],
        [
            struct(2 * pairs, QUARTER, LANES),
            struct(2 * pairs, QUARTER + HALF, LANES),
        ],
        scratch=[pltpu.VMEM((2 * pairs, HALF, LANES), F32)],
    )


class Levels:
    def __init__(self, bits):
        self.bits = bits
        self.rows = BLOCK >> bits
        self.differences = [
            [(m, BLOCK >> m) for m in range(bits, step, -1)] for step in range(bits)
        ]
        whole = [0] + [BLOCK >> step for step in range(1, bits)]
        self.whole = Tree(1, whole)
        self.rough = Tree(1, [0] + [self.rows] * (bits - 1))
        self.fine = Tree(1, [0] + [rows - self.rows for rows in whole[1:]])
        self.pieces = []
        for level in range(1, bits):
            trees = (self.whole, self.rough, self.fine)
            for parts in zip(*(tree.held[level] for tree in trees)):
                self.pieces.append((level, parts[0][0], *(part[1] for part in parts)))

    def scratch(self):
        shapes = [(BLOCK >> m, LANES) for m in range(1, self.bits + 1)]
        return [pltpu.VMEM(shape, F32) for shape in shapes]

    def group_pieces(self):
        pieces = []
        for index, (level, step, whole, rough, _) in enumerate(self.pieces):
            factor = 1 << self.bits - level
            place = (2 + index) * self.rows
            pieces.append((step, whole, rough, BLOCK >> level, factor, place))
        return pieces


def coarsen_pair(lo, pairs, mine, received):
    def kernel(own, got, *outs):
        for tile in range(2 * pairs):
            outs[0][tile, : BLOCK // 4] = own[tile]
            outs[0][tile, BLOCK // 4 :] = got[tile]
            for index in range(1, lo.bits):
                outs[index][tile] = mean_rows(
                    outs[index - 1], (tile,), 0, BLOCK >> index + 1, 2
                )

    outs = [struct(2 * pairs, BLOCK >> step, LANES) for step in range(1, lo.bits + 1)]
    return call(kernel, [mine, received], outs)


def group_pieces(lo):
    own = BLOCK >> lo.bits
    factor = 1 << lo.bits
    pieces = [
        (-2, 0, BLOCK // 2, factor, own),
        (-1, 0, BLOCK // 2, factor, own + own // 2),
    ]
    filled = 2 * own
    for level in range(1, lo.bits):
        factor = 1 << lo.bits - level
        for step, row, rows in lo.held[level]:
            pieces.append((step, row, rows, factor, filled))
            filled += rows // factor
    return pieces


def coarsen_group(lo, hi, pairs, own, halves, arrived):
    pieces = group_pieces(lo)

    def kernel(own_in, *refs):
        ins = refs[: 2 + lo.bits]
        outs = refs[2 + lo.bits :]
        for tile in range(2 * pairs):
            outs[0][tile, pl.ds(0, BLOCK >> lo.bits)] = own_in[tile]
            for step, row, rows, factor, place in pieces:
                count = rows // factor
                outs[0][tile, pl.ds(place, count)] = mean_rows(
                    ins[2 + step], (tile,), row, count, factor
                )
            for step in range(1, hi.bits):
                outs[step][tile] = mean_rows(
                    outs[step - 1], (tile,), 0, BLOCK >> step, 2
                )

    outs = [struct(2 * pairs, BLOCK >> step, LANES) for step in range(hi.bits)]
    return call(kernel, [own, *halves, *arrived], outs)


def turn(pairs, mine, received):
    def kernel(own, got, turned):
        for tile in range(2 * pairs):
            both = jnp.concatenate([own[tile], got[tile]], axis=0).T
            turned[tile] = both * (SCALE * LOG2_E) if tile < pairs else both

    return call(kernel, [mine, received], [struct(2 * pairs, LANES, 2 * BLOCK)])[0]


def take_levels(levels, pairs, grads):
    trees = (levels.rough, levels.fine)

    def kernel(*refs):
        ins = refs[: levels.bits]
        rough = refs[levels.bits : 2 * levels.bits]
        fine = refs[2 * levels.bits : 3 * levels.bits]
        ladder = refs[3 * levels.bits :]
        for tile in range(2 * pairs):
            for level, step, row, rough_row, fine_row in levels.pieces:
                source = ladder[level - 1]
                source[...] = ins[step][tile, pl.ds(row, BLOCK >> level)]
                fine_row += sum(rows for _, rows in levels.differences[level])
                for m, rows in reversed(levels.differences[level]):
                    fine_row -= rows
                    part = 2.0 * half_difference(source, (), 0, rows)
                    fine[step][tile, pl.ds(fine_row, rows)] = part
                    ladder[m - 1][...] = 2.0 * mean_rows(source, (), 0, rows, 2)
                    source = ladder[m - 1]
                rough[step][tile, pl.ds(rough_row, levels.rows)] = source[...]

    outs = [
        struct(2 * pairs, tree.rows(step), LANES)
        for tree in trees
        for step in range(levels.bits)
    ]
    outs = call(kernel, grads, outs, scratch=levels.scratch())
    return outs[: levels.bits], outs[levels.bits :]


def spread_group(levels, hi, pairs, group_grads, grads):
    own_rows = levels.rows

    def kernel(*refs):
        steps = refs[: hi.bits]
        ins = refs[hi.bits : hi.bits + levels.bits]
        own_out, *outs = refs[hi.bits + levels.bits : -1]
        total = refs[-1]
        for tile in range(2 * pairs):
            total[tile] = steps[0][tile, pl.ds(0, BLOCK)]
            for step in range(1, hi.bits):
                above = steps[step][tile, pl.ds(0, BLOCK >> step)]
                add_spread(total, (tile,), 0, above, 1 << step)
            own_out[tile] = total[tile, pl.ds(0, own_rows)]
            for step, _, row, _, _, place in levels.group_pieces():
                rows = pl.ds(row, own_rows)
                part = total[tile, pl.ds(place, own_rows)]
                outs[step][tile, rows] = ins[step][tile, rows] + part
            outs[0][tile, pl.ds(ins[0].shape[1], own_rows)] = total[
                tile, pl.ds(own_rows, own_rows)
            ]

    shapes = [list(a.shape) for a in grads]
    shapes[0][1] += own_rows
    outs = [struct(2 * pairs, own_rows, LANES)] + [struct(*shape) for shape in shapes]
    own, *grads = call(
        kernel,
        [*group_grads, *grads],
        outs,
        scratch=[pltpu.VMEM((2 * pairs, BLOCK, LANES), F32)],
    )
    return own, grads


def spread_pair(levels, pairs, own_grad, rough, fine, block_second):
    own_rows = levels.rows

    def kernel(own, block, *refs):
        rough_in = refs[: levels.bits - 1]
        fine_in = refs[levels.bits - 1 : 2 * levels.bits - 1]
        mine, theirs, *ladder = refs[2 * levels.bits - 1 :]
        last = pl.ds(rough_in[0].shape[1] - own_rows, own_rows)
        for tile in range(2 * pairs):
            above = own[tile] + rough_in[0][tile, last]
            for step in range(1, levels.bits - 1):
                above = above + rough_in[step][tile, pl.ds(0, own_rows)]
            filled = 0
            for m, rows in levels.differences[1]:
                part = fine_in[1][tile, pl.ds(filled, rows)]
                for step in range(2, min(m, levels.bits)):
                    part = part + fine_in[step][tile, pl.ds(filled, rows)]
                filled += rows
                put_pairs(ladder[m - 2], (), 0.5 * above, 0.5 * part)
                above = ladder[m - 2][...]
            mine[tile] = above[:QUARTER]
            theirs[tile] = above[QUARTER:] + block[tile]

    return call(
        kernel,
        [own_grad, block_second, *rough, *fine],
        [struct(2 * pairs, QUARTER, LANES)] * 2,
        scratch=levels.scratch(),
    )


def unpack(pairs, kept, arrived, features, scalar):
    def kernel(bit, *refs):
        outs = refs[4:]
        for which in range(2):
            for pair in range(pairs):
                for side, ref in ((bit[0], refs[which]), (1 - bit[0], refs[2 + which])):
                    column = side * (features // 2) + pair * LANES
                    column = pl.ds(pl.multiple_of(column, LANES), LANES)
                    outs[which][:, column] = ref[pair]

    return call(kernel, [*kept, *arrived], [struct(BLOCK, features)] * 2, scalar=scalar)


def finish(pairs, kept, rest, finest, seconds, endings, features, scalar):
    count = endings[0].shape[1]

    def kernel(bit, kept_in, rest_in, f_mine, f_theirs, s_mine, s_theirs, *refs):
        e_mine, e_theirs = refs[:2]
        outs, total, middle, second = refs[2:4], refs[4], refs[5], refs[6]
        for tile in range(2 * pairs):
            out = outs[tile // pairs]
            column = tile % pairs * LANES
            at = (tile,)
            total[tile] = kept_in[tile]
            add_spread(total, at, 0, f_mine[tile], 2)
            add_spread(total, at, 0, s_mine[tile], 4)
            add_spread(total, at, 0, e_mine[tile], BLOCK // count)
            place = bit[0] * (features // 2) + column
            out[:, pl.ds(pl.multiple_of(place, LANES), LANES)] = total[tile]
            second[tile] = s_theirs[tile]
            add_spread(second, at, 0, e_theirs[tile], QUARTER // count)
            put_pairs(middle, at, 0.5 * second[tile], 0.5 * rest_in[tile, :QUARTER])
            first = 0.5 * (middle[tile] + f_theirs[tile])
            put_pairs(total, at, first, 0.5 * rest_in[tile, QUARTER:])
            place = (1 - bit[0]) * (features // 2) + column
            out[:, pl.ds(pl.multiple_of(place, LANES), LANES)] = total[tile]

    return call(
        kernel,
        [kept, rest, *finest, *seconds, *endings],
        [struct(BLOCK, features)] * 2,
        scratch=[
            pltpu.VMEM((2 * pairs, BLOCK, LANES), F32),
            pltpu.VMEM((2 * pairs, HALF, LANES), F32),
            pltpu.VMEM((2 * pairs, QUARTER, LANES), F32),
        ],
        scalar=scalar,
    )


def on_device(queries, keys, values, cotangent):
    features = queries.shape[1]
    assert queries.shape[0] == BLOCK
    pairs = features // LANES // 2
    lo_bits = lax.axis_size("seqlo").bit_length() - 1
    levels = Levels(lo_bits - 1)
    lo = levels.whole
    hi_bits = lax.axis_size("seqhi").bit_length() - 1
    hi = Tree(lo_bits, [BLOCK >> step for step in range(hi_bits)])
    scalar = (lax.axis_index("seqlo") % 2).astype(jnp.int32).reshape(1)
    queries, keys, values, cotangent = [
        pltpu.with_memory_space_constraint(array, pltpu.HBM)
        for array in (queries, keys, values, cotangent)
    ]
    f_theirs, c_send, rest = pack_theirs(pairs, keys, values, scalar)
    mine_kv, f_mine, c_mine = pack_mine(pairs, keys, values, scalar)
    second = exchange(c_send, 1)
    finest_theirs = exchange(f_theirs, 2)
    coarse = coarsen_pair(lo, pairs, c_mine, second)
    finest = exchange(ordered(f_mine, finest_theirs), 2)
    rest = exchange(ordered(rest, coarse[0]), 1)
    half = exchange(ordered(finest_theirs, rest), 1)
    kv = rebuild(pairs, second, rest)
    send_qg, mine_qg = pack(pairs, queries, cotangent, scalar)
    qg = exchange(ordered(send_qg, half), 1)
    zs = lo.gather([None, *coarse], (finest, send_qg))
    group = coarsen_group(
        lo, hi, pairs, ordered(coarse[-1], rest), [finest, half], zs
    )
    turned = turn(pairs, mine_qg, qg)
    rs = hi.gather(group, turned)
    block_sets = [(0, 0, 0, BLOCK), (0, 1, 0, BLOCK)]
    lo_sets = [(1, 2, 0, BLOCK // 2), (1, 3, 0, BLOCK // 2)]
    for level in range(lo.bits):
        for step, row, rows in lo.held[level]:
            lo_sets.append((1 + level, 4 + step, row, rows))
    hi_sets = []
    for level in range(hi.bits):
        for step, row, rows in hi.held[level]:
            hi_sets.append((lo_bits + level, step, row, rows))
    first_in = [mine_kv, kv, finest, half, *zs]
    *kept, tops, sums, partial = attend_first(
        pairs, block_sets + lo_sets, first_in, turned
    )
    *rs_grads, o_keep, o_send, g_scaled, row_dot, kt_hi, d_hi = attend_last(
        pairs, hi_sets, rs, turned, tops, sums, partial
    )
    shapes = [(2 * pairs, *a.shape[1:]) for a in first_in]
    finest_grad, half_grad, *zs_grads, d_lo = attend_back(
        pairs,
        [(level, index - 2, row, rows) for level, index, row, rows in lo_sets],
        shapes[2:],
        BOTH,
        kept,
        turned,
        g_scaled,
        row_dot,
        [],
    )
    kv_keep, kv_send, dq_keep, dq_send = attend_back(
        pairs,
        block_sets,
        shapes[:2],
        0,
        kept,
        turned,
        g_scaled,
        row_dot,
        [d_lo, kt_hi, d_hi],
    )
    rough_grads, fine_grads = take_levels(levels, pairs, zs_grads)
    group_grads = hi.scatter(rs_grads)
    half_back = exchange(ordered(half_grad, kv_send), 1)
    o_back = exchange(o_send, 1)
    fine_back, finest_mine = levels.fine.scatter(fine_grads, finest_grad)
    block_second, rest_grad = take_apart(pairs, kv_send)
    rest_back = exchange(ordered(rest_grad, o_back), 1)
    dq_back = exchange(dq_send, 1)
    group_grads[-1] = ordered(group_grads[-1], kv_send)
    own_grad, rough_grads = spread_group(levels, hi, pairs, group_grads, rough_grads)
    *rough_back, ending = levels.rough.scatter(rough_grads, whole=False)
    half_rows = levels.rows // 2
    finest_theirs = exchange(ordered(half_back, rough_back[0]), 2)
    far = 1 << levels.bits
    ending_mine = exchange(ending[:, :half_rows], far)
    ending_theirs = exchange(ending[:, half_rows:], far + 1)
    second_mine, second_send = spread_pair(
        levels, pairs, own_grad, rough_back, fine_back, block_second
    )
    second_theirs = exchange(ordered(second_send, rest_back), 1)
    attended, query_grad = unpack(
        pairs, (o_keep, dq_keep), (o_back, dq_back), features, scalar
    )
    key_grad, value_grad = finish(
        pairs,
        kv_keep,
        rest_back,
        (finest_mine, finest_theirs),
        (second_mine, second_theirs),
        (ending_mine, ending_theirs),
        features,
        scalar,
    )
    return attended, query_grad, key_grad, value_grad


def solution(mesh):
    spec = P(AXES, None)
    return jax.shard_map(
        on_device,
        mesh=mesh,
        in_specs=(spec,) * 4,
        out_specs=(spec,) * 4,
        check_vma=False,
    )
```

```python
import math

import jax
import jax.numpy as jnp
from jax import lax
from jax.experimental import pallas as pl
from jax.experimental.pallas import tpu as pltpu
from jax.sharding import PartitionSpec as P

HEADS = 12
BLOCK = 128
HEAD_DIM = 64
LANES = 2 * HEAD_DIM
AXES = ("seqhi", "seqlo")
VMEM_LIMIT = 20 * 1024 * 1024
F32 = jnp.float32
BF16 = jnp.bfloat16
LOG2_E = 1.0 / math.log(2.0)
SCALE = 1.0 / math.sqrt(HEAD_DIM)


def struct(*shape):
    return jax.ShapeDtypeStruct(shape, F32)


def call(kernel, operands, outs, scratch=(), scalar=None, flops=0, exps=0, where=None):
    vmem = pl.BlockSpec(memory_space=pltpu.VMEM)
    smem = pl.BlockSpec(memory_space=pltpu.SMEM)
    in_specs = [pl.BlockSpec(memory_space=where) if where else vmem] * len(operands)
    if scalar is not None:
        operands = [scalar, *operands]
        in_specs = [smem, *in_specs]
    moved = sum(4 * math.prod(a.shape) for a in [*operands, *outs])
    return pl.pallas_call(
        kernel,
        out_shape=list(outs),
        in_specs=in_specs,
        out_specs=[vmem] * len(outs),
        scratch_shapes=list(scratch),
        compiler_params=pltpu.CompilerParams(vmem_limit_bytes=VMEM_LIMIT),
        cost_estimate=pl.CostEstimate(
            flops=flops, bytes_accessed=moved, transcendentals=exps
        ),
    )(*operands)


def exchange(value, offset):
    count = lax.axis_size(AXES)
    return lax.ppermute(value, AXES, [(i, i ^ offset) for i in range(count)])


def ordered(value, after):
    return value if after is None else lax.optimization_barrier((value, after))[0]


def half_difference(ref, lead, first, count):
    even = ref[(*lead, pl.ds(first, count, stride=2), slice(None))]
    odd = ref[(*lead, pl.ds(first + 1, count, stride=2), slice(None))]
    return 0.5 * (even - odd)


def put_pairs(ref, lead, total, difference):
    count = total.shape[0]
    ref[(*lead, pl.ds(0, count, stride=2), slice(None))] = total + difference
    ref[(*lead, pl.ds(1, count, stride=2), slice(None))] = total - difference


def mean_rows(ref, lead, first, count, factor):
    total = None
    for step in range(factor):
        rows = pl.ds(first + step, count, stride=factor)
        part = ref[(*lead, rows, slice(None))]
        total = part if total is None else total + part
    return total * (1.0 / factor)


def add_spread(ref, lead, first, value, factor):
    count = value.shape[0]
    value = value * (1.0 / factor)
    for step in range(factor):
        rows = pl.ds(first + step, count, stride=factor)
        place = (*lead, rows, slice(None))
        ref[place] = ref[place] + value


class Tree:
    def __init__(self, first_bit, own_rows):
        self.bits = bits = len(own_rows)
        self.first_bit = first_bit
        self.own_rows = own_rows
        self.held = {}
        self.payload = {}
        for step in range(bits - 1, -1, -1):
            rows = self.own_rows[step]
            payload = []
            fresh = {step: [(step, 0, rows)] if rows else []}
            for level in range(step + 1, bits):
                for piece in self.held[level]:
                    payload.append(piece)
                    fresh.setdefault(level, []).append((step, rows, piece[2]))
                    rows += piece[2]
            self.payload[step] = payload
            for level, pieces in fresh.items():
                self.held[level] = self.held.get(level, []) + pieces

    def rows(self, step):
        return self.own_rows[step] + sum(piece[2] for piece in self.payload[step])

    def partner(self, value, step):
        return exchange(value, 1 << self.first_bit + step)

    def gather(self, own, after=None):
        arrived = [None] * self.bits
        for step in range(self.bits - 1, -1, -1):
            parts = [own[step]] if self.own_rows[step] else []
            for source, row, rows in self.payload[step]:
                part = arrived[source]
                whole = rows == part.shape[1]
                parts.append(part if whole else part[:, row : row + rows])
            sent = jnp.concatenate(parts, axis=1) if len(parts) > 1 else parts[0]
            if step == 0:
                sent = ordered(sent, after)
            arrived[step] = self.partner(sent, step)
        return arrived

    def scatter(self, grads, front=None, whole=True):
        grads = list(grads)
        returned = []
        for step in range(self.bits if whole else self.bits - 1):
            sent = grads[step]
            if step == 0 and front is not None:
                rows = front.shape[1]
                back = self.partner(jnp.concatenate([front, sent], axis=1), step)
                front, back = back[:, :rows], back[:, rows:]
            else:
                back = self.partner(sent, step)
            returned.append(back)
            filled = self.own_rows[step]
            for source, row, rows in self.payload[step]:
                part = back[:, filled : filled + rows]
                grads[source] = grads[source].at[:, row : row + rows].add(part)
                filled += rows
        if not whole:
            returned.append(grads[-1])
        return returned if front is None else (returned, front)


def split(value):
    high = value.astype(BF16).astype(F32)
    return high, value - high


def halves_by_head(value):
    high, low = split(value)
    first = lax.broadcasted_iota(jnp.int32, value.shape, 1) < HEAD_DIM
    one = jnp.where(first, high, pltpu.roll(low, HEAD_DIM, 1))
    two = jnp.where(first, pltpu.roll(high, HEAD_DIM, 1), low)
    return one, two


def dot(lhs, rhs, dims):
    return lax.dot_general(lhs, rhs, (dims, ((), ())), preferred_element_type=F32)


NN = ((1,), (0,))
NT = ((1,), (1,))


BOTH = 2 * BLOCK
GROUP = 3


def halves_of(sets, ins, which, pairs, pair):
    tile = which * pairs + pair
    parts = [ins[index][tile, pl.ds(row, rows), :] for _, index, row, rows in sets]
    return halves_by_head(jnp.concatenate(parts, axis=0))


def segment_levels(sets):
    levels, filled = [], 0
    for level, _, _, rows in sets:
        if filled % BLOCK == 0:
            levels.append(level)
        filled += rows
    return levels


def four_rows(value):
    high, low = split(value)
    four = jnp.concatenate([high, high, low, low], axis=0).astype(BF16)
    return four, jnp.concatenate([high, low], axis=0).astype(BF16)


def store_split(ref, lead, rows, value):
    high = value.astype(BF16)
    ref[(lead, 0, rows)] = high
    ref[(lead, 1, rows)] = (value - high.astype(F32)).astype(BF16)


def fold_rows(value):
    return value[:HEAD_DIM] + value[HEAD_DIM:]


def fold_heads(one, two):
    first = lax.broadcasted_iota(jnp.int32, one.shape, 1) < HEAD_DIM
    return jnp.where(
        first, one + pltpu.roll(one, HEAD_DIM, 1), two + pltpu.roll(two, HEAD_DIM, 1)
    )


def twice(value):
    return jnp.concatenate([value, value], axis=1)


def stacked(ref, at, rows=slice(None)):
    return jnp.concatenate([ref[at, 0, rows], ref[at, 1, rows]], axis=0)


def abreast(ref, at, rows=slice(None)):
    return jnp.concatenate([ref[at, 0, rows], ref[at, 1, rows]], axis=1)


def column_scores(levels, keys, at, q_four, s_ref):
    highest = None
    for index, level in enumerate(levels):
        rows = pl.ds(index * BLOCK, BLOCK)
        s = dot(twice(keys[at, rows]), q_four, NN)
        s = s + float(level) if level else s
        s_ref[at, rows] = s
        top = jnp.max(s.reshape(BLOCK // 8, 8, BOTH), axis=0)
        highest = top if highest is None else jnp.maximum(highest, top)
    return jnp.max(highest, axis=0, keepdims=True)


def exponents(levels, at, top, s_ref, e_ref, keep):
    summed = None
    for index in range(len(levels)):
        rows = pl.ds(index * BLOCK, BLOCK)
        e = jnp.exp2(s_ref[at, rows] - top)
        if keep:
            s_ref[at, rows] = e
        store_split(e_ref, at, rows, e)
        part = jnp.sum(e.reshape(BLOCK // 8, 8, BOTH), axis=0)
        summed = part if summed is None else summed + part
    return jnp.sum(summed, axis=0, keepdims=True)


def head_rows(ref, pair, head):
    return ref[pair, pl.ds(head * HEAD_DIM, HEAD_DIM)]


def each_group(pairs, body):
    for first in range(0, pairs, GROUP):
        group = range(first, min(first + GROUP, pairs))
        body(group, [(pair, head, 2 * pair + head) for pair in group for head in (0, 1)])


def costs(pairs, rows, products, exps=0):
    return dict(
        flops=2 * 4 * products * pairs * 2 * rows * BOTH * HEAD_DIM,
        exps=exps * pairs * 2 * rows * BOTH,
    )


def put_halves(pairs, sets, ins, group, plain, turned):
    for which in range(2):
        for pair in group:
            for head, value in enumerate(halves_of(sets, ins, which, pairs, pair)):
                plain[which][2 * pair + head] = value.astype(BF16)
                turned[which][2 * pair + head] = value.T.astype(BF16)


def attend_first(pairs, sets, operands, turned):
    total = sum(s[3] for s in sets)
    levels = segment_levels(sets)

    def kernel(turn_in, *refs):
        ins = refs[: len(operands)]
        kt, vc, e_ref, tops, sums, out, s_ref, kc, vt = refs[len(operands) :]

        def body(group, heads):
            put_halves(pairs, sets, ins, group, (kc, vc), (kt, vt))
            for pair, head, at in heads:
                q_four, _ = four_rows(head_rows(turn_in, pair, head))
                tops[at] = column_scores(levels, kc, at, q_four, s_ref)
            for _, _, at in heads:
                sums[at] = exponents(levels, at, tops[at], s_ref, e_ref, False)
            for _, _, at in heads:
                out[at] = fold_rows(dot(twice(vt[at]), stacked(e_ref, at), NN))

        each_group(pairs, body)

    heads = 2 * pairs
    outs = [
        jax.ShapeDtypeStruct((heads, LANES, total), BF16),
        jax.ShapeDtypeStruct((heads, total, LANES), BF16),
        jax.ShapeDtypeStruct((heads, 2, total, BOTH), BF16),
    ]
    outs += [struct(heads, 1, BOTH)] * 2 + [struct(heads, HEAD_DIM, BOTH)]
    return call(
        kernel,
        [turned, *operands],
        outs,
        scratch=[
            pltpu.VMEM((heads, total, BOTH), F32),
            pltpu.VMEM((heads, total, LANES), BF16),
            pltpu.VMEM((heads, LANES, total), BF16),
        ],
        **costs(pairs, total, 2, 1),
    )


def attend_last(pairs, sets, operands, turned, tops, sums, partial):
    total = sum(s[3] for s in sets)
    levels = segment_levels(sets)

    def kernel(turn_in, top_in, sum_in, part_in, *refs):
        ins = refs[: len(operands)]
        grads = refs[len(operands) : 2 * len(operands)]
        o_keep, o_send, g_out, r_out, kt, d_ref = refs[2 * len(operands) : -5]
        s_ref, e_ref, kc, vc, vt = refs[-5:]

        def body(group, heads):
            put_halves(pairs, sets, ins, group, (kc, vc), (kt, vt))
            queries = {}
            top = {}
            for pair, head, at in heads:
                q_four, queries[at] = four_rows(head_rows(turn_in, pair, head))
                top[at] = column_scores(levels, kc, at, q_four, s_ref)
            inverse = {}
            rescale = {}
            for _, _, at in heads:
                first_top = top_in[at]
                highest = jnp.maximum(top[at], first_top)
                rescale[at] = jnp.exp2(first_top - highest)
                summed = exponents(levels, at, highest, s_ref, e_ref, True)
                inverse[at] = 1.0 / (summed + sum_in[at] * rescale[at])
            output = {}
            cotangents = {}
            row_dot = {}
            for pair, head, at in heads:
                o = fold_rows(dot(twice(vt[at]), stacked(e_ref, at), NN))
                o = (o + part_in[at] * rescale[at]) * inverse[at]
                output[at] = o
                scaled = head_rows(turn_in, pairs + pair, head) * inverse[at]
                cotangents[at] = four_rows(scaled)
                row_dot[at] = jnp.sum(o * scaled, axis=0, keepdims=True)
                g_out[at] = scaled * rescale[at]
                r_out[at] = row_dot[at] * rescale[at]
            for _, _, at in heads:
                for index in range(len(levels)):
                    rows = pl.ds(index * BLOCK, BLOCK)
                    dp = dot(twice(vc[at, rows]), cotangents[at][0], NN)
                    store_split(d_ref, at, rows, s_ref[at, rows] * (dp - row_dot[at]))
            key_grads = {}
            value_grads = {}
            for _, _, at in heads:
                value_grads[at] = dot(abreast(e_ref, at), twice(cotangents[at][1]), NT)
                key_grads[at] = dot(abreast(d_ref, at), twice(queries[at]), NT)
            for pair in group:
                put_grads(pairs, pair, sets, grads, key_grads, value_grads)
                both = [output[2 * pair], output[2 * pair + 1]]
                both = jnp.concatenate(both, axis=0).T
                o_keep[pair] = both[:BLOCK]
                o_send[pair] = both[BLOCK:]

        each_group(pairs, body)

    heads = 2 * pairs
    outs = [struct(*a.shape) for a in operands]
    outs += [struct(pairs, BLOCK, LANES)] * 2
    outs += [struct(heads, HEAD_DIM, BOTH), struct(heads, 1, BOTH)]
    outs.append(jax.ShapeDtypeStruct((heads, LANES, total), BF16))
    outs.append(jax.ShapeDtypeStruct((heads, 2, total, BOTH), BF16))
    return call(
        kernel,
        [turned, tops, sums, partial, *operands],
        outs,
        scratch=[pltpu.VMEM((heads, total, BOTH), F32)]
        + [pltpu.VMEM((heads, 2, total, BOTH), BF16)]
        + [pltpu.VMEM((heads, total, LANES), BF16)] * 2
        + [pltpu.VMEM((heads, LANES, total), BF16)],
        **costs(pairs, total, 5, 1),
    )


def put_grads(pairs, pair, sets, grads, key_grads, value_grads):
    for which, parts in enumerate((key_grads, value_grads)):
        both = fold_heads(parts[2 * pair], parts[2 * pair + 1])
        if which == 0:
            both = both * (1.0 / LOG2_E)
        filled = 0
        for _, index, row, rows in sets:
            piece = both[filled : filled + rows]
            grads[index][which * pairs + pair, pl.ds(row, rows), :] = piece
            filled += rows


def attend_back(pairs, sets, shapes, first, kept, turned, g_scaled, row_dot, others):
    total = sum(s[3] for s in sets)
    segments = total // BLOCK

    def kernel(turn_in, kt, vc, e_ref, g_in, r_in, *refs):
        other_in = refs[: len(others)]
        grads = refs[len(others) : len(others) + len(shapes)]
        dq_out = refs[len(others) + len(shapes) : -1]
        d_ref = refs[-1]
        span = pl.ds(first, total)

        def body(group, heads):
            cotangents = {}
            for _, _, at in heads:
                g_four, cotangents[at] = four_rows(g_in[at])
                for index in range(segments):
                    rows = pl.ds(first + index * BLOCK, BLOCK)
                    dp = dot(twice(vc[at, rows]), g_four, NN)
                    e = e_ref[at, 0, rows].astype(F32) + e_ref[at, 1, rows].astype(F32)
                    place = pl.ds(index * BLOCK, BLOCK)
                    store_split(d_ref, at, place, e * (dp - r_in[at]))
            queries_grad = {}
            key_grads = {}
            value_grads = {}
            for pair, head, at in heads:
                _, q_rows = four_rows(head_rows(turn_in, pair, head))
                g_rows = cotangents[at]
                value_grads[at] = dot(abreast(e_ref, at, span), twice(g_rows), NT)
                key_grads[at] = dot(abreast(d_ref, at), twice(q_rows), NT)
                if others:
                    d_lo, kt_hi, d_hi = other_in
                    part = dot(twice(kt[at, :, span]), stacked(d_ref, at), NN)
                    part += dot(twice(kt[at, :, total:]), stacked(d_lo, at), NN)
                    part += dot(twice(kt_hi[at]), stacked(d_hi, at), NN)
                    queries_grad[at] = fold_rows(part)
            for pair in group:
                put_grads(pairs, pair, sets, grads, key_grads, value_grads)
                if others:
                    both = [queries_grad[2 * pair], queries_grad[2 * pair + 1]]
                    both = jnp.concatenate(both, axis=0).T * SCALE
                    dq_out[0][pair] = both[:BLOCK]
                    dq_out[1][pair] = both[BLOCK:]

        each_group(pairs, body)

    outs = [struct(*shape) for shape in shapes]
    scratch = []
    if others:
        outs += [struct(pairs, BLOCK, LANES)] * 2
        scratch.append(pltpu.VMEM((2 * pairs, 2, total, BOTH), BF16))
    else:
        outs.append(jax.ShapeDtypeStruct((2 * pairs, 2, total, BOTH), BF16))
    return call(
        kernel,
        [turned, *kept, g_scaled, row_dot, *others],
        outs,
        scratch=scratch,
        **costs(pairs, total, 4),
    )


def copy_columns(moves, ins, sems, bit):
    started = []
    for operand, theirs, column, place in moves:
        side = 1 - bit if theirs else bit
        column = side * (ins[operand].shape[1] // 2) + column
        column = pl.ds(pl.multiple_of(column, LANES), LANES)
        copy = pltpu.make_async_copy(
            ins[operand].at[:, column], place, sems.at[len(started)]
        )
        copy.start()
        started.append(copy)
    return started


def pack(pairs, first, second, scalar):
    def kernel(bit, one, two, theirs, mine, sems):
        moves = []
        for tile in range(2 * pairs):
            for out, other in ((theirs, True), (mine, False)):
                column = tile % pairs * LANES
                moves.append((tile // pairs, other, column, out.at[tile]))
        for copy in copy_columns(moves, (one, two), sems, bit[0]):
            copy.wait()

    return call(
        kernel,
        [first, second],
        [struct(2 * pairs, BLOCK, LANES)] * 2,
        scratch=[pltpu.SemaphoreType.DMA((4 * pairs,))],
        scalar=scalar,
        where=pl.ANY,
    )


QUARTER = BLOCK // 4
HALF = BLOCK // 2


def pack_theirs(pairs, keys, values, scalar):
    def kernel(bit, k, v, finest, coarse, rest, block, sems):
        moves = []
        for tile in range(2 * pairs):
            moves.append((tile // pairs, True, tile % pairs * LANES, block.at[tile]))
        copies = copy_columns(moves, (k, v), sems, bit[0])
        for tile, copy in enumerate(copies):
            copy.wait()
            finest[tile] = mean_rows(block, (tile,), 0, HALF, 2)
            coarse[tile] = mean_rows(finest, (tile,), 0, QUARTER, 2)
            rest[tile, :QUARTER] = half_difference(finest, (tile,), 0, QUARTER)
            rest[tile, QUARTER:] = half_difference(block, (tile,), 0, HALF)

    return call(
        kernel,
        [keys, values],
        [
            struct(2 * pairs, HALF, LANES),
            struct(2 * pairs, QUARTER, LANES),
            struct(2 * pairs, QUARTER + HALF, LANES),
        ],
        scratch=[
            pltpu.VMEM((2 * pairs, BLOCK, LANES), F32),
            pltpu.SemaphoreType.DMA((2 * pairs,)),
        ],
        scalar=scalar,
        where=pl.ANY,
    )


def pack_mine(pairs, keys, values, scalar):
    def kernel(bit, k, v, block, finest, coarse, sems):
        moves = []
        for tile in range(2 * pairs):
            moves.append((tile // pairs, False, tile % pairs * LANES, block.at[tile]))
        copies = copy_columns(moves, (k, v), sems, bit[0])
        for tile, copy in enumerate(copies):
            copy.wait()
            finest[tile] = mean_rows(block, (tile,), 0, HALF, 2)
            coarse[tile] = mean_rows(finest, (tile,), 0, QUARTER, 2)

    return call(
        kernel,
        [keys, values],
        [
            struct(2 * pairs, BLOCK, LANES),
            struct(2 * pairs, HALF, LANES),
            struct(2 * pairs, QUARTER, LANES),
        ],
        scratch=[pltpu.SemaphoreType.DMA((2 * pairs,))],
        scalar=scalar,
        where=pl.ANY,
    )


def rebuild(pairs, second, rest):
    def kernel(second_in, rest_in, out, finest):
        for tile in range(2 * pairs):
            put_pairs(finest, (tile,), second_in[tile], rest_in[tile, :QUARTER])
            put_pairs(out, (tile,), finest[tile], rest_in[tile, QUARTER:])

    return call(
        kernel,
        [second, rest],
        [struct(2 * pairs, BLOCK, LANES)],
        scratch=[pltpu.VMEM((2 * pairs, HALF, LANES), F32)],
    )[0]


def take_apart(pairs, block_grad):
    def kernel(block, second, rest, finest):
        for tile in range(2 * pairs):
            finest[tile] = 2.0 * mean_rows(block, (tile,), 0, HALF, 2)
            rest[tile, QUARTER:] = 2.0 * half_difference(block, (tile,), 0, HALF)
            second[tile] = 2.0 * mean_rows(finest, (tile,), 0, QUARTER, 2)
            rest[tile, :QUARTER] = 2.0 * half_difference(finest, (tile,), 0, QUARTER)

    return call(
        kernel,
        [block_grad],
        [
            struct(2 * pairs, QUARTER, LANES),
            struct(2 * pairs, QUARTER + HALF, LANES),
        ],
        scratch=[pltpu.VMEM((2 * pairs, HALF, LANES), F32)],
    )


class Levels:
    def __init__(self, bits):
        self.bits = bits
        self.rows = BLOCK >> bits
        self.differences = [
            [(m, BLOCK >> m) for m in range(bits, step, -1)] for step in range(bits)
        ]
        whole = [0] + [BLOCK >> step for step in range(1, bits)]
        self.whole = Tree(1, whole)
        self.rough = Tree(1, [0] + [self.rows] * (bits - 1))
        self.fine = Tree(1, [0] + [rows - self.rows for rows in whole[1:]])
        self.pieces = []
        for level in range(1, bits):
            trees = (self.whole, self.rough, self.fine)
            for parts in zip(*(tree.held[level] for tree in trees)):
                self.pieces.append((level, parts[0][0], *(part[1] for part in parts)))

    def scratch(self):
        shapes = [(BLOCK >> m, LANES) for m in range(1, self.bits + 1)]
        return [pltpu.VMEM(shape, F32) for shape in shapes]

    def group_pieces(self):
        pieces = []
        for index, (level, step, whole, rough, _) in enumerate(self.pieces):
            factor = 1 << self.bits - level
            place = (2 + index) * self.rows
            pieces.append((step, whole, rough, BLOCK >> level, factor, place))
        return pieces


def coarsen_pair(lo, pairs, mine, received):
    def kernel(own, got, *outs):
        for tile in range(2 * pairs):
            outs[0][tile, : BLOCK // 4] = own[tile]
            outs[0][tile, BLOCK // 4 :] = got[tile]
            for index in range(1, lo.bits):
                outs[index][tile] = mean_rows(
                    outs[index - 1], (tile,), 0, BLOCK >> index + 1, 2
                )

    outs = [struct(2 * pairs, BLOCK >> step, LANES) for step in range(1, lo.bits + 1)]
    return call(kernel, [mine, received], outs)


def group_pieces(lo):
    own = BLOCK >> lo.bits
    factor = 1 << lo.bits
    pieces = [
        (-2, 0, BLOCK // 2, factor, own),
        (-1, 0, BLOCK // 2, factor, own + own // 2),
    ]
    filled = 2 * own
    for level in range(1, lo.bits):
        factor = 1 << lo.bits - level
        for step, row, rows in lo.held[level]:
            pieces.append((step, row, rows, factor, filled))
            filled += rows // factor
    return pieces


def coarsen_group(lo, hi, pairs, own, halves, arrived):
    pieces = group_pieces(lo)

    def kernel(own_in, *refs):
        ins = refs[: 2 + lo.bits]
        outs = refs[2 + lo.bits :]
        for tile in range(2 * pairs):
            outs[0][tile, pl.ds(0, BLOCK >> lo.bits)] = own_in[tile]
            for step, row, rows, factor, place in pieces:
                count = rows // factor
                outs[0][tile, pl.ds(place, count)] = mean_rows(
                    ins[2 + step], (tile,), row, count, factor
                )
            for step in range(1, hi.bits):
                outs[step][tile] = mean_rows(
                    outs[step - 1], (tile,), 0, BLOCK >> step, 2
                )

    outs = [struct(2 * pairs, BLOCK >> step, LANES) for step in range(hi.bits)]
    return call(kernel, [own, *halves, *arrived], outs)


def turn(pairs, mine, received):
    def kernel(own, got, turned):
        for tile in range(2 * pairs):
            both = jnp.concatenate([own[tile], got[tile]], axis=0).T
            turned[tile] = both * (SCALE * LOG2_E) if tile < pairs else both

    return call(kernel, [mine, received], [struct(2 * pairs, LANES, 2 * BLOCK)])[0]


def take_levels(levels, pairs, grads):
    trees = (levels.rough, levels.fine)

    def kernel(*refs):
        ins = refs[: levels.bits]
        rough = refs[levels.bits : 2 * levels.bits]
        fine = refs[2 * levels.bits : 3 * levels.bits]
        ladder = refs[3 * levels.bits :]
        for tile in range(2 * pairs):
            for level, step, row, rough_row, fine_row in levels.pieces:
                source = ladder[level - 1]
                source[...] = ins[step][tile, pl.ds(row, BLOCK >> level)]
                fine_row += sum(rows for _, rows in levels.differences[level])
                for m, rows in reversed(levels.differences[level]):
                    fine_row -= rows
                    part = 2.0 * half_difference(source, (), 0, rows)
                    fine[step][tile, pl.ds(fine_row, rows)] = part
                    ladder[m - 1][...] = 2.0 * mean_rows(source, (), 0, rows, 2)
                    source = ladder[m - 1]
                rough[step][tile, pl.ds(rough_row, levels.rows)] = source[...]

    outs = [
        struct(2 * pairs, tree.rows(step), LANES)
        for tree in trees
        for step in range(levels.bits)
    ]
    outs = call(kernel, grads, outs, scratch=levels.scratch())
    return outs[: levels.bits], outs[levels.bits :]


def spread_group(levels, hi, pairs, group_grads, grads):
    own_rows = levels.rows

    def kernel(*refs):
        steps = refs[: hi.bits]
        ins = refs[hi.bits : hi.bits + levels.bits]
        own_out, *outs = refs[hi.bits + levels.bits : -1]
        total = refs[-1]
        for tile in range(2 * pairs):
            total[tile] = steps[0][tile, pl.ds(0, BLOCK)]
            for step in range(1, hi.bits):
                above = steps[step][tile, pl.ds(0, BLOCK >> step)]
                add_spread(total, (tile,), 0, above, 1 << step)
            own_out[tile] = total[tile, pl.ds(0, own_rows)]
            for step, _, row, _, _, place in levels.group_pieces():
                rows = pl.ds(row, own_rows)
                part = total[tile, pl.ds(place, own_rows)]
                outs[step][tile, rows] = ins[step][tile, rows] + part
            outs[0][tile, pl.ds(ins[0].shape[1], own_rows)] = total[
                tile, pl.ds(own_rows, own_rows)
            ]

    shapes = [list(a.shape) for a in grads]
    shapes[0][1] += own_rows
    outs = [struct(2 * pairs, own_rows, LANES)] + [struct(*shape) for shape in shapes]
    own, *grads = call(
        kernel,
        [*group_grads, *grads],
        outs,
        scratch=[pltpu.VMEM((2 * pairs, BLOCK, LANES), F32)],
    )
    return own, grads


def spread_pair(levels, pairs, own_grad, rough, fine, block_second):
    own_rows = levels.rows

    def kernel(own, block, *refs):
        rough_in = refs[: levels.bits - 1]
        fine_in = refs[levels.bits - 1 : 2 * levels.bits - 1]
        mine, theirs, *ladder = refs[2 * levels.bits - 1 :]
        last = pl.ds(rough_in[0].shape[1] - own_rows, own_rows)
        for tile in range(2 * pairs):
            above = own[tile] + rough_in[0][tile, last]
            for step in range(1, levels.bits - 1):
                above = above + rough_in[step][tile, pl.ds(0, own_rows)]
            filled = 0
            for m, rows in levels.differences[1]:
                part = fine_in[1][tile, pl.ds(filled, rows)]
                for step in range(2, min(m, levels.bits)):
                    part = part + fine_in[step][tile, pl.ds(filled, rows)]
                filled += rows
                put_pairs(ladder[m - 2], (), 0.5 * above, 0.5 * part)
                above = ladder[m - 2][...]
            mine[tile] = above[:QUARTER]
            theirs[tile] = above[QUARTER:] + block[tile]

    return call(
        kernel,
        [own_grad, block_second, *rough, *fine],
        [struct(2 * pairs, QUARTER, LANES)] * 2,
        scratch=levels.scratch(),
    )


def unpack(pairs, kept, arrived, features, scalar):
    def kernel(bit, mine, theirs, out):
        for pair in range(pairs):
            for side, ref in ((bit[0], mine), (1 - bit[0], theirs)):
                column = side * (features // 2) + pair * LANES
                column = pl.ds(pl.multiple_of(column, LANES), LANES)
                out[:, column] = ref[pair]

    return call(kernel, [kept, arrived], [struct(BLOCK, features)], scalar=scalar)[0]


def finish(pairs, kept, rest, finest, seconds, endings, features, scalar):
    count = endings[0].shape[1]

    def kernel(bit, kept_in, rest_in, f_mine, f_theirs, s_mine, s_theirs, *refs):
        e_mine, e_theirs = refs[:2]
        outs, total, middle, second = refs[2:4], refs[4], refs[5], refs[6]
        for tile in range(2 * pairs):
            out = outs[tile // pairs]
            column = tile % pairs * LANES
            at = (tile,)
            total[tile] = kept_in[tile]
            add_spread(total, at, 0, f_mine[tile], 2)
            add_spread(total, at, 0, s_mine[tile], 4)
            add_spread(total, at, 0, e_mine[tile], BLOCK // count)
            place = bit[0] * (features // 2) + column
            out[:, pl.ds(pl.multiple_of(place, LANES), LANES)] = total[tile]
            second[tile] = s_theirs[tile]
            add_spread(second, at, 0, e_theirs[tile], QUARTER // count)
            put_pairs(middle, at, 0.5 * second[tile], 0.5 * rest_in[tile, :QUARTER])
            first = 0.5 * (middle[tile] + f_theirs[tile])
            put_pairs(total, at, first, 0.5 * rest_in[tile, QUARTER:])
            place = (1 - bit[0]) * (features // 2) + column
            out[:, pl.ds(pl.multiple_of(place, LANES), LANES)] = total[tile]

    return call(
        kernel,
        [kept, rest, *finest, *seconds, *endings],
        [struct(BLOCK, features)] * 2,
        scratch=[
            pltpu.VMEM((2 * pairs, BLOCK, LANES), F32),
            pltpu.VMEM((2 * pairs, HALF, LANES), F32),
            pltpu.VMEM((2 * pairs, QUARTER, LANES), F32),
        ],
        scalar=scalar,
    )


def on_device(queries, keys, values, cotangent):
    features = queries.shape[1]
    assert queries.shape[0] == BLOCK
    pairs = features // LANES // 2
    lo_bits = lax.axis_size("seqlo").bit_length() - 1
    levels = Levels(lo_bits - 1)
    lo = levels.whole
    hi_bits = lax.axis_size("seqhi").bit_length() - 1
    hi = Tree(lo_bits, [BLOCK >> step for step in range(hi_bits)])
    scalar = (lax.axis_index("seqlo") % 2).astype(jnp.int32).reshape(1)
    queries, keys, values, cotangent = [
        pltpu.with_memory_space_constraint(array, pltpu.HBM)
        for array in (queries, keys, values, cotangent)
    ]
    f_theirs, c_send, rest = pack_theirs(pairs, keys, values, scalar)
    mine_kv, f_mine, c_mine = pack_mine(pairs, keys, values, scalar)
    second = exchange(c_send, 1)
    finest_theirs = exchange(f_theirs, 2)
    coarse = coarsen_pair(lo, pairs, c_mine, second)
    finest = exchange(ordered(f_mine, finest_theirs), 2)
    rest = exchange(ordered(rest, coarse[0]), 1)
    half = exchange(ordered(finest_theirs, rest), 1)
    kv = rebuild(pairs, second, rest)
    send_qg, mine_qg = pack(pairs, queries, cotangent, scalar)
    qg = exchange(ordered(send_qg, half), 1)
    zs = lo.gather([None, *coarse], (finest, send_qg))
    group = coarsen_group(
        lo, hi, pairs, ordered(coarse[-1], rest), [finest, half], zs
    )
    turned = turn(pairs, mine_qg, qg)
    rs = hi.gather(group, turned)
    block_sets = [(0, 0, 0, BLOCK), (0, 1, 0, BLOCK)]
    lo_sets = [(1, 2, 0, BLOCK // 2), (1, 3, 0, BLOCK // 2)]
    for level in range(lo.bits):
        for step, row, rows in lo.held[level]:
            lo_sets.append((1 + level, 4 + step, row, rows))
    hi_sets = []
    for level in range(hi.bits):
        for step, row, rows in hi.held[level]:
            hi_sets.append((lo_bits + level, step, row, rows))
    first_in = [mine_kv, kv, finest, half, *zs]
    *kept, tops, sums, partial = attend_first(
        pairs, block_sets + lo_sets, first_in, turned
    )
    *rs_grads, o_keep, o_send, g_scaled, row_dot, kt_hi, d_hi = attend_last(
        pairs, hi_sets, rs, turned, tops, sums, partial
    )
    shapes = [(2 * pairs, *a.shape[1:]) for a in first_in]
    finest_grad, half_grad, *zs_grads, d_lo = attend_back(
        pairs,
        [(level, index - 2, row, rows) for level, index, row, rows in lo_sets],
        shapes[2:],
        BOTH,
        kept,
        turned,
        g_scaled,
        row_dot,
        [],
    )
    kv_keep, kv_send, dq_keep, dq_send = attend_back(
        pairs,
        block_sets,
        shapes[:2],
        0,
        kept,
        turned,
        g_scaled,
        row_dot,
        [d_lo, kt_hi, d_hi],
    )
    rough_grads, fine_grads = take_levels(levels, pairs, zs_grads)
    group_grads = hi.scatter(rs_grads)
    half_back = exchange(ordered(half_grad, kv_send), 1)
    o_back = exchange(o_send, 1)
    fine_back, finest_mine = levels.fine.scatter(fine_grads, finest_grad)
    block_second, rest_grad = take_apart(pairs, kv_send)
    split_at = rest_grad.shape[1]
    bulk = jnp.concatenate([rest_grad, dq_send.reshape(2 * pairs, HALF, LANES)], axis=1)
    bulk = exchange(bulk, 1)
    rest_back = bulk[:, :split_at]
    dq_back = bulk[:, split_at:].reshape(pairs, BLOCK, LANES)
    group_grads[-1] = ordered(group_grads[-1], (kv_send, o_back))
    own_grad, rough_grads = spread_group(levels, hi, pairs, group_grads, rough_grads)
    *rough_back, ending = levels.rough.scatter(rough_grads, whole=False)
    half_rows = levels.rows // 2
    finest_theirs = exchange(ordered(half_back, rough_back[0]), 2)
    far = 1 << levels.bits
    ending_mine = exchange(ending[:, :half_rows], far)
    ending_theirs = exchange(ending[:, half_rows:], far + 1)
    second_mine, second_send = spread_pair(
        levels, pairs, own_grad, rough_back, fine_back, block_second
    )
    second_theirs = exchange(second_send, 1)
    attended = unpack(pairs, o_keep, o_back, features, scalar)
    query_grad = unpack(pairs, dq_keep, dq_back, features, scalar)
    key_grad, value_grad = finish(
        pairs,
        kv_keep,
        rest_back,
        (finest_mine, finest_theirs),
        (second_mine, second_theirs),
        (ending_mine, ending_theirs),
        features,
        scalar,
    )
    return attended, query_grad, key_grad, value_grad


def solution(mesh):
    spec = P(AXES, None)
    return jax.shard_map(
        on_device,
        mesh=mesh,
        in_specs=(spec,) * 4,
        out_specs=(spec,) * 4,
        check_vma=False,
    )
```

```python
import math

import jax
import jax.numpy as jnp
from jax import lax
from jax.experimental import pallas as pl
from jax.experimental.pallas import tpu as pltpu
from jax.sharding import PartitionSpec as P

HEADS = 12
BLOCK = 128
HEAD_DIM = 64
LANES = 2 * HEAD_DIM
AXES = ("seqhi", "seqlo")
VMEM_LIMIT = 20 * 1024 * 1024
F32 = jnp.float32
BF16 = jnp.bfloat16
LOG2_E = 1.0 / math.log(2.0)
SCALE = 1.0 / math.sqrt(HEAD_DIM)


def struct(*shape):
    return jax.ShapeDtypeStruct(shape, F32)


def call(kernel, operands, outs, scratch=(), scalar=None, flops=0, exps=0, where=None):
    vmem = pl.BlockSpec(memory_space=pltpu.VMEM)
    smem = pl.BlockSpec(memory_space=pltpu.SMEM)
    in_specs = [pl.BlockSpec(memory_space=where) if where else vmem] * len(operands)
    if scalar is not None:
        operands = [scalar, *operands]
        in_specs = [smem, *in_specs]
    moved = sum(4 * math.prod(a.shape) for a in [*operands, *outs])
    return pl.pallas_call(
        kernel,
        out_shape=list(outs),
        in_specs=in_specs,
        out_specs=[vmem] * len(outs),
        scratch_shapes=list(scratch),
        compiler_params=pltpu.CompilerParams(vmem_limit_bytes=VMEM_LIMIT),
        cost_estimate=pl.CostEstimate(
            flops=flops, bytes_accessed=moved, transcendentals=exps
        ),
    )(*operands)


def exchange(value, offset):
    count = lax.axis_size(AXES)
    return lax.ppermute(value, AXES, [(i, i ^ offset) for i in range(count)])


def ordered(value, after):
    return value if after is None else lax.optimization_barrier((value, after))[0]


def half_difference(ref, lead, first, count):
    even = ref[(*lead, pl.ds(first, count, stride=2), slice(None))]
    odd = ref[(*lead, pl.ds(first + 1, count, stride=2), slice(None))]
    return 0.5 * (even - odd)


def put_pairs(ref, lead, total, difference):
    count = total.shape[0]
    ref[(*lead, pl.ds(0, count, stride=2), slice(None))] = total + difference
    ref[(*lead, pl.ds(1, count, stride=2), slice(None))] = total - difference


def mean_rows(ref, lead, first, count, factor):
    total = None
    for step in range(factor):
        rows = pl.ds(first + step, count, stride=factor)
        part = ref[(*lead, rows, slice(None))]
        total = part if total is None else total + part
    return total * (1.0 / factor)


def add_spread(ref, lead, first, value, factor):
    count = value.shape[0]
    value = value * (1.0 / factor)
    for step in range(factor):
        rows = pl.ds(first + step, count, stride=factor)
        place = (*lead, rows, slice(None))
        ref[place] = ref[place] + value


class Tree:
    def __init__(self, first_bit, own_rows):
        self.bits = bits = len(own_rows)
        self.first_bit = first_bit
        self.own_rows = own_rows
        self.held = {}
        self.payload = {}
        for step in range(bits - 1, -1, -1):
            rows = self.own_rows[step]
            payload = []
            fresh = {step: [(step, 0, rows)] if rows else []}
            for level in range(step + 1, bits):
                for piece in self.held[level]:
                    payload.append(piece)
                    fresh.setdefault(level, []).append((step, rows, piece[2]))
                    rows += piece[2]
            self.payload[step] = payload
            for level, pieces in fresh.items():
                self.held[level] = self.held.get(level, []) + pieces

    def rows(self, step):
        return self.own_rows[step] + sum(piece[2] for piece in self.payload[step])

    def partner(self, value, step):
        return exchange(value, 1 << self.first_bit + step)

    def gather(self, own, after=None):
        arrived = [None] * self.bits
        for step in range(self.bits - 1, -1, -1):
            parts = [own[step]] if self.own_rows[step] else []
            for source, row, rows in self.payload[step]:
                part = arrived[source]
                whole = rows == part.shape[1]
                parts.append(part if whole else part[:, row : row + rows])
            sent = jnp.concatenate(parts, axis=1) if len(parts) > 1 else parts[0]
            if step == 0:
                sent = ordered(sent, after)
            arrived[step] = self.partner(sent, step)
        return arrived

    def scatter(self, grads, front=None, whole=True):
        grads = list(grads)
        returned = []
        for step in range(self.bits if whole else self.bits - 1):
            sent = grads[step]
            if step == 0 and front is not None:
                rows = front.shape[1]
                back = self.partner(jnp.concatenate([front, sent], axis=1), step)
                front, back = back[:, :rows], back[:, rows:]
            else:
                back = self.partner(sent, step)
            returned.append(back)
            filled = self.own_rows[step]
            for source, row, rows in self.payload[step]:
                part = back[:, filled : filled + rows]
                grads[source] = grads[source].at[:, row : row + rows].add(part)
                filled += rows
        if not whole:
            returned.append(grads[-1])
        return returned if front is None else (returned, front)


def split(value):
    high = value.astype(BF16).astype(F32)
    return high, value - high


def halves_by_head(value):
    high, low = split(value)
    first = lax.broadcasted_iota(jnp.int32, value.shape, 1) < HEAD_DIM
    one = jnp.where(first, high, pltpu.roll(low, HEAD_DIM, 1))
    two = jnp.where(first, pltpu.roll(high, HEAD_DIM, 1), low)
    return one, two


def dot(lhs, rhs, dims):
    return lax.dot_general(lhs, rhs, (dims, ((), ())), preferred_element_type=F32)


NN = ((1,), (0,))
NT = ((1,), (1,))


BOTH = 2 * BLOCK
GROUP = 3


def halves_of(sets, ins, which, pairs, pair):
    tile = which * pairs + pair
    parts = [ins[index][tile, pl.ds(row, rows), :] for _, index, row, rows in sets]
    return halves_by_head(jnp.concatenate(parts, axis=0))


def segment_levels(sets):
    levels, filled = [], 0
    for level, _, _, rows in sets:
        if filled % BLOCK == 0:
            levels.append(level)
        filled += rows
    return levels


def four_rows(value):
    high, low = split(value)
    four = jnp.concatenate([high, high, low, low], axis=0).astype(BF16)
    return four, jnp.concatenate([high, low], axis=0).astype(BF16)


def store_split(ref, lead, rows, value):
    high = value.astype(BF16)
    ref[(lead, 0, rows)] = high
    ref[(lead, 1, rows)] = (value - high.astype(F32)).astype(BF16)


def fold_rows(value):
    return value[:HEAD_DIM] + value[HEAD_DIM:]


def fold_heads(one, two):
    first = lax.broadcasted_iota(jnp.int32, one.shape, 1) < HEAD_DIM
    return jnp.where(
        first, one + pltpu.roll(one, HEAD_DIM, 1), two + pltpu.roll(two, HEAD_DIM, 1)
    )


def twice(value):
    return jnp.concatenate([value, value], axis=1)


def stacked(ref, at, rows=slice(None)):
    return jnp.concatenate([ref[at, 0, rows], ref[at, 1, rows]], axis=0)


def abreast(ref, at, rows=slice(None)):
    return jnp.concatenate([ref[at, 0, rows], ref[at, 1, rows]], axis=1)


def column_scores(levels, keys, at, q_four, s_ref):
    highest = None
    for index, level in enumerate(levels):
        rows = pl.ds(index * BLOCK, BLOCK)
        s = dot(twice(keys[at, rows]), q_four, NN)
        s = s + float(level) if level else s
        s_ref[at, rows] = s
        top = jnp.max(s.reshape(BLOCK // 8, 8, BOTH), axis=0)
        highest = top if highest is None else jnp.maximum(highest, top)
    return jnp.max(highest, axis=0, keepdims=True)


def exponents(levels, at, top, s_ref, e_ref, keep):
    summed = None
    for index in range(len(levels)):
        rows = pl.ds(index * BLOCK, BLOCK)
        e = jnp.exp2(s_ref[at, rows] - top)
        if keep:
            s_ref[at, rows] = e
        store_split(e_ref, at, rows, e)
        part = jnp.sum(e.reshape(BLOCK // 8, 8, BOTH), axis=0)
        summed = part if summed is None else summed + part
    return jnp.sum(summed, axis=0, keepdims=True)


def head_rows(ref, pair, head):
    return ref[pair, pl.ds(head * HEAD_DIM, HEAD_DIM)]


def each_group(pairs, body):
    for first in range(0, pairs, GROUP):
        group = range(first, min(first + GROUP, pairs))
        body(group, [(pair, head, 2 * pair + head) for pair in group for head in (0, 1)])


def costs(pairs, rows, products, exps=0):
    return dict(
        flops=2 * 4 * products * pairs * 2 * rows * BOTH * HEAD_DIM,
        exps=exps * pairs * 2 * rows * BOTH,
    )


def put_halves(pairs, sets, ins, group, plain, turned):
    for which in range(2):
        for pair in group:
            for head, value in enumerate(halves_of(sets, ins, which, pairs, pair)):
                plain[which][2 * pair + head] = value.astype(BF16)
                turned[which][2 * pair + head] = value.T.astype(BF16)


def attend_first(pairs, sets, operands, turned):
    total = sum(s[3] for s in sets)
    levels = segment_levels(sets)

    def kernel(turn_in, *refs):
        ins = refs[: len(operands)]
        kt, vc, e_ref, tops, sums, out, s_ref, kc, vt = refs[len(operands) :]

        def body(group, heads):
            put_halves(pairs, sets, ins, group, (kc, vc), (kt, vt))
            for pair, head, at in heads:
                q_four, _ = four_rows(head_rows(turn_in, pair, head))
                tops[at] = column_scores(levels, kc, at, q_four, s_ref)
            for _, _, at in heads:
                sums[at] = exponents(levels, at, tops[at], s_ref, e_ref, False)
            for _, _, at in heads:
                out[at] = fold_rows(dot(twice(vt[at]), stacked(e_ref, at), NN))

        each_group(pairs, body)

    heads = 2 * pairs
    outs = [
        jax.ShapeDtypeStruct((heads, LANES, total), BF16),
        jax.ShapeDtypeStruct((heads, total, LANES), BF16),
        jax.ShapeDtypeStruct((heads, 2, total, BOTH), BF16),
    ]
    outs += [struct(heads, 1, BOTH)] * 2 + [struct(heads, HEAD_DIM, BOTH)]
    return call(
        kernel,
        [turned, *operands],
        outs,
        scratch=[
            pltpu.VMEM((heads, total, BOTH), F32),
            pltpu.VMEM((heads, total, LANES), BF16),
            pltpu.VMEM((heads, LANES, total), BF16),
        ],
        **costs(pairs, total, 2, 1),
    )


def attend_last(pairs, sets, operands, turned, tops, sums, partial):
    total = sum(s[3] for s in sets)
    levels = segment_levels(sets)

    def kernel(turn_in, top_in, sum_in, part_in, *refs):
        ins = refs[: len(operands)]
        grads = refs[len(operands) : 2 * len(operands)]
        o_keep, o_send, g_out, r_out, kt, d_ref = refs[2 * len(operands) : -5]
        s_ref, e_ref, kc, vc, vt = refs[-5:]

        def body(group, heads):
            put_halves(pairs, sets, ins, group, (kc, vc), (kt, vt))
            queries = {}
            top = {}
            for pair, head, at in heads:
                q_four, queries[at] = four_rows(head_rows(turn_in, pair, head))
                top[at] = column_scores(levels, kc, at, q_four, s_ref)
            inverse = {}
            rescale = {}
            for _, _, at in heads:
                first_top = top_in[at]
                highest = jnp.maximum(top[at], first_top)
                rescale[at] = jnp.exp2(first_top - highest)
                summed = exponents(levels, at, highest, s_ref, e_ref, True)
                inverse[at] = 1.0 / (summed + sum_in[at] * rescale[at])
            output = {}
            cotangents = {}
            row_dot = {}
            for pair, head, at in heads:
                o = fold_rows(dot(twice(vt[at]), stacked(e_ref, at), NN))
                o = (o + part_in[at] * rescale[at]) * inverse[at]
                output[at] = o
                scaled = head_rows(turn_in, pairs + pair, head) * inverse[at]
                cotangents[at] = four_rows(scaled)
                row_dot[at] = jnp.sum(o * scaled, axis=0, keepdims=True)
                g_out[at] = scaled * rescale[at]
                r_out[at] = row_dot[at] * rescale[at]
            for _, _, at in heads:
                for index in range(len(levels)):
                    rows = pl.ds(index * BLOCK, BLOCK)
                    dp = dot(twice(vc[at, rows]), cotangents[at][0], NN)
                    store_split(d_ref, at, rows, s_ref[at, rows] * (dp - row_dot[at]))
            key_grads = {}
            value_grads = {}
            for _, _, at in heads:
                value_grads[at] = dot(abreast(e_ref, at), twice(cotangents[at][1]), NT)
                key_grads[at] = dot(abreast(d_ref, at), twice(queries[at]), NT)
            for pair in group:
                put_grads(pairs, pair, sets, grads, key_grads, value_grads)
                both = [output[2 * pair], output[2 * pair + 1]]
                both = jnp.concatenate(both, axis=0).T
                o_keep[pair] = both[:BLOCK]
                o_send[pair] = both[BLOCK:]

        each_group(pairs, body)

    heads = 2 * pairs
    outs = [struct(*a.shape) for a in operands]
    outs += [struct(pairs, BLOCK, LANES)] * 2
    outs += [struct(heads, HEAD_DIM, BOTH), struct(heads, 1, BOTH)]
    outs.append(jax.ShapeDtypeStruct((heads, LANES, total), BF16))
    outs.append(jax.ShapeDtypeStruct((heads, 2, total, BOTH), BF16))
    return call(
        kernel,
        [turned, tops, sums, partial, *operands],
        outs,
        scratch=[pltpu.VMEM((heads, total, BOTH), F32)]
        + [pltpu.VMEM((heads, 2, total, BOTH), BF16)]
        + [pltpu.VMEM((heads, total, LANES), BF16)] * 2
        + [pltpu.VMEM((heads, LANES, total), BF16)],
        **costs(pairs, total, 5, 1),
    )


def put_grads(pairs, pair, sets, grads, key_grads, value_grads):
    for which, parts in enumerate((key_grads, value_grads)):
        both = fold_heads(parts[2 * pair], parts[2 * pair + 1])
        if which == 0:
            both = both * (1.0 / LOG2_E)
        filled = 0
        for _, index, row, rows in sets:
            piece = both[filled : filled + rows]
            grads[index][which * pairs + pair, pl.ds(row, rows), :] = piece
            filled += rows


def attend_back(pairs, sets, shapes, first, kept, turned, g_scaled, row_dot, others):
    total = sum(s[3] for s in sets)
    segments = total // BLOCK

    def kernel(turn_in, kt, vc, e_ref, g_in, r_in, *refs):
        other_in = refs[: len(others)]
        grads = refs[len(others) : len(others) + len(shapes)]
        dq_out = refs[len(others) + len(shapes) : -1]
        d_ref = refs[-1]
        span = pl.ds(first, total)

        def body(group, heads):
            cotangents = {}
            for _, _, at in heads:
                g_four, cotangents[at] = four_rows(g_in[at])
                for index in range(segments):
                    rows = pl.ds(first + index * BLOCK, BLOCK)
                    dp = dot(twice(vc[at, rows]), g_four, NN)
                    e = e_ref[at, 0, rows].astype(F32) + e_ref[at, 1, rows].astype(F32)
                    place = pl.ds(index * BLOCK, BLOCK)
                    store_split(d_ref, at, place, e * (dp - r_in[at]))
            queries_grad = {}
            key_grads = {}
            value_grads = {}
            for pair, head, at in heads:
                _, q_rows = four_rows(head_rows(turn_in, pair, head))
                g_rows = cotangents[at]
                value_grads[at] = dot(abreast(e_ref, at, span), twice(g_rows), NT)
                key_grads[at] = dot(abreast(d_ref, at), twice(q_rows), NT)
                if others:
                    d_lo, kt_hi, d_hi = other_in
                    part = dot(twice(kt[at, :, span]), stacked(d_ref, at), NN)
                    part += dot(twice(kt[at, :, total:]), stacked(d_lo, at), NN)
                    part += dot(twice(kt_hi[at]), stacked(d_hi, at), NN)
                    queries_grad[at] = fold_rows(part)
            for pair in group:
                put_grads(pairs, pair, sets, grads, key_grads, value_grads)
                if others:
                    both = [queries_grad[2 * pair], queries_grad[2 * pair + 1]]
                    both = jnp.concatenate(both, axis=0).T * SCALE
                    dq_out[0][pair] = both[:BLOCK]
                    dq_out[1][pair] = both[BLOCK:]

        each_group(pairs, body)

    outs = [struct(*shape) for shape in shapes]
    scratch = []
    if others:
        outs += [struct(pairs, BLOCK, LANES)] * 2
        scratch.append(pltpu.VMEM((2 * pairs, 2, total, BOTH), BF16))
    else:
        outs.append(jax.ShapeDtypeStruct((2 * pairs, 2, total, BOTH), BF16))
    return call(
        kernel,
        [turned, *kept, g_scaled, row_dot, *others],
        outs,
        scratch=scratch,
        **costs(pairs, total, 4),
    )


def copy_columns(moves, ins, sems, bit):
    started = []
    for operand, theirs, column, place in moves:
        side = 1 - bit if theirs else bit
        column = side * (ins[operand].shape[1] // 2) + column
        column = pl.ds(pl.multiple_of(column, LANES), LANES)
        copy = pltpu.make_async_copy(
            ins[operand].at[:, column], place, sems.at[len(started)]
        )
        copy.start()
        started.append(copy)
    return started


def pack(pairs, first, second, scalar):
    def kernel(bit, one, two, theirs, mine, sems):
        moves = []
        for tile in range(2 * pairs):
            for out, other in ((theirs, True), (mine, False)):
                column = tile % pairs * LANES
                moves.append((tile // pairs, other, column, out.at[tile]))
        for copy in copy_columns(moves, (one, two), sems, bit[0]):
            copy.wait()

    return call(
        kernel,
        [first, second],
        [struct(2 * pairs, BLOCK, LANES)] * 2,
        scratch=[pltpu.SemaphoreType.DMA((4 * pairs,))],
        scalar=scalar,
        where=pl.ANY,
    )


QUARTER = BLOCK // 4
HALF = BLOCK // 2


def pack_theirs(pairs, keys, values, scalar):
    def kernel(bit, k, v, finest, coarse, rest, block, sems):
        moves = []
        for tile in range(2 * pairs):
            moves.append((tile // pairs, True, tile % pairs * LANES, block.at[tile]))
        copies = copy_columns(moves, (k, v), sems, bit[0])
        for tile, copy in enumerate(copies):
            copy.wait()
            finest[tile] = mean_rows(block, (tile,), 0, HALF, 2)
            coarse[tile] = mean_rows(finest, (tile,), 0, QUARTER, 2)
            rest[tile, :QUARTER] = half_difference(finest, (tile,), 0, QUARTER)
            rest[tile, QUARTER:] = half_difference(block, (tile,), 0, HALF)

    return call(
        kernel,
        [keys, values],
        [
            struct(2 * pairs, HALF, LANES),
            struct(2 * pairs, QUARTER, LANES),
            struct(2 * pairs, QUARTER + HALF, LANES),
        ],
        scratch=[
            pltpu.VMEM((2 * pairs, BLOCK, LANES), F32),
            pltpu.SemaphoreType.DMA((2 * pairs,)),
        ],
        scalar=scalar,
        where=pl.ANY,
    )


def pack_mine(pairs, keys, values, scalar):
    def kernel(bit, k, v, block, finest, coarse, sems):
        moves = []
        for tile in range(2 * pairs):
            moves.append((tile // pairs, False, tile % pairs * LANES, block.at[tile]))
        copies = copy_columns(moves, (k, v), sems, bit[0])
        for tile, copy in enumerate(copies):
            copy.wait()
            finest[tile] = mean_rows(block, (tile,), 0, HALF, 2)
            coarse[tile] = mean_rows(finest, (tile,), 0, QUARTER, 2)

    return call(
        kernel,
        [keys, values],
        [
            struct(2 * pairs, BLOCK, LANES),
            struct(2 * pairs, HALF, LANES),
            struct(2 * pairs, QUARTER, LANES),
        ],
        scratch=[pltpu.SemaphoreType.DMA((2 * pairs,))],
        scalar=scalar,
        where=pl.ANY,
    )


def rebuild(pairs, second, rest):
    def kernel(second_in, rest_in, out, finest):
        for tile in range(2 * pairs):
            put_pairs(finest, (tile,), second_in[tile], rest_in[tile, :QUARTER])
            put_pairs(out, (tile,), finest[tile], rest_in[tile, QUARTER:])

    return call(
        kernel,
        [second, rest],
        [struct(2 * pairs, BLOCK, LANES)],
        scratch=[pltpu.VMEM((2 * pairs, HALF, LANES), F32)],
    )[0]


def take_apart(pairs, block_grad):
    def kernel(block, second, rest, finest):
        for tile in range(2 * pairs):
            finest[tile] = 2.0 * mean_rows(block, (tile,), 0, HALF, 2)
            rest[tile, QUARTER:] = 2.0 * half_difference(block, (tile,), 0, HALF)
            second[tile] = 2.0 * mean_rows(finest, (tile,), 0, QUARTER, 2)
            rest[tile, :QUARTER] = 2.0 * half_difference(finest, (tile,), 0, QUARTER)

    return call(
        kernel,
        [block_grad],
        [
            struct(2 * pairs, QUARTER, LANES),
            struct(2 * pairs, QUARTER + HALF, LANES),
        ],
        scratch=[pltpu.VMEM((2 * pairs, HALF, LANES), F32)],
    )


class Levels:
    def __init__(self, bits):
        self.bits = bits
        self.rows = BLOCK >> bits
        self.differences = [
            [(m, BLOCK >> m) for m in range(bits, step, -1)] for step in range(bits)
        ]
        whole = [0] + [BLOCK >> step for step in range(1, bits)]
        self.whole = Tree(1, whole)
        self.rough = Tree(1, [0] + [self.rows] * (bits - 1))
        self.fine = Tree(1, [0] + [rows - self.rows for rows in whole[1:]])
        self.pieces = []
        for level in range(1, bits):
            trees = (self.whole, self.rough, self.fine)
            for parts in zip(*(tree.held[level] for tree in trees)):
                self.pieces.append((level, parts[0][0], *(part[1] for part in parts)))

    def scratch(self):
        shapes = [(BLOCK >> m, LANES) for m in range(1, self.bits + 1)]
        return [pltpu.VMEM(shape, F32) for shape in shapes]

    def group_pieces(self):
        pieces = []
        for index, (level, step, whole, rough, _) in enumerate(self.pieces):
            factor = 1 << self.bits - level
            place = (2 + index) * self.rows
            pieces.append((step, whole, rough, BLOCK >> level, factor, place))
        return pieces


def coarsen_pair(lo, pairs, mine, received):
    def kernel(own, got, *outs):
        for tile in range(2 * pairs):
            outs[0][tile, : BLOCK // 4] = own[tile]
            outs[0][tile, BLOCK // 4 :] = got[tile]
            for index in range(1, lo.bits):
                outs[index][tile] = mean_rows(
                    outs[index - 1], (tile,), 0, BLOCK >> index + 1, 2
                )

    outs = [struct(2 * pairs, BLOCK >> step, LANES) for step in range(1, lo.bits + 1)]
    return call(kernel, [mine, received], outs)


def group_pieces(lo):
    own = BLOCK >> lo.bits
    factor = 1 << lo.bits
    pieces = [
        (-2, 0, BLOCK // 2, factor, own),
        (-1, 0, BLOCK // 2, factor, own + own // 2),
    ]
    filled = 2 * own
    for level in range(1, lo.bits):
        factor = 1 << lo.bits - level
        for step, row, rows in lo.held[level]:
            pieces.append((step, row, rows, factor, filled))
            filled += rows // factor
    return pieces


def coarsen_group(lo, hi, pairs, own, halves, arrived):
    pieces = group_pieces(lo)

    def kernel(own_in, *refs):
        ins = refs[: 2 + lo.bits]
        outs = refs[2 + lo.bits :]
        for tile in range(2 * pairs):
            outs[0][tile, pl.ds(0, BLOCK >> lo.bits)] = own_in[tile]
            for step, row, rows, factor, place in pieces:
                count = rows // factor
                outs[0][tile, pl.ds(place, count)] = mean_rows(
                    ins[2 + step], (tile,), row, count, factor
                )
            for step in range(1, hi.bits):
                outs[step][tile] = mean_rows(
                    outs[step - 1], (tile,), 0, BLOCK >> step, 2
                )

    outs = [struct(2 * pairs, BLOCK >> step, LANES) for step in range(hi.bits)]
    return call(kernel, [own, *halves, *arrived], outs)


def turn(pairs, mine, received):
    def kernel(own, got, turned):
        for tile in range(2 * pairs):
            both = jnp.concatenate([own[tile], got[tile]], axis=0).T
            turned[tile] = both * (SCALE * LOG2_E) if tile < pairs else both

    return call(kernel, [mine, received], [struct(2 * pairs, LANES, 2 * BLOCK)])[0]


def take_levels(levels, pairs, grads):
    trees = (levels.rough, levels.fine)

    def kernel(*refs):
        ins = refs[: levels.bits]
        rough = refs[levels.bits : 2 * levels.bits]
        fine = refs[2 * levels.bits : 3 * levels.bits]
        ladder = refs[3 * levels.bits :]
        for tile in range(2 * pairs):
            for level, step, row, rough_row, fine_row in levels.pieces:
                source = ladder[level - 1]
                source[...] = ins[step][tile, pl.ds(row, BLOCK >> level)]
                fine_row += sum(rows for _, rows in levels.differences[level])
                for m, rows in reversed(levels.differences[level]):
                    fine_row -= rows
                    part = 2.0 * half_difference(source, (), 0, rows)
                    fine[step][tile, pl.ds(fine_row, rows)] = part
                    ladder[m - 1][...] = 2.0 * mean_rows(source, (), 0, rows, 2)
                    source = ladder[m - 1]
                rough[step][tile, pl.ds(rough_row, levels.rows)] = source[...]

    outs = [
        struct(2 * pairs, tree.rows(step), LANES)
        for tree in trees
        for step in range(levels.bits)
    ]
    outs = call(kernel, grads, outs, scratch=levels.scratch())
    return outs[: levels.bits], outs[levels.bits :]


def spread_group(levels, hi, pairs, group_grads, grads):
    own_rows = levels.rows

    def kernel(*refs):
        steps = refs[: hi.bits]
        ins = refs[hi.bits : hi.bits + levels.bits]
        own_out, *outs = refs[hi.bits + levels.bits : -1]
        total = refs[-1]
        for tile in range(2 * pairs):
            total[tile] = steps[0][tile, pl.ds(0, BLOCK)]
            for step in range(1, hi.bits):
                above = steps[step][tile, pl.ds(0, BLOCK >> step)]
                add_spread(total, (tile,), 0, above, 1 << step)
            own_out[tile] = total[tile, pl.ds(0, own_rows)]
            for step, _, row, _, _, place in levels.group_pieces():
                rows = pl.ds(row, own_rows)
                part = total[tile, pl.ds(place, own_rows)]
                outs[step][tile, rows] = ins[step][tile, rows] + part
            outs[0][tile, pl.ds(ins[0].shape[1], own_rows)] = total[
                tile, pl.ds(own_rows, own_rows)
            ]

    shapes = [list(a.shape) for a in grads]
    shapes[0][1] += own_rows
    outs = [struct(2 * pairs, own_rows, LANES)] + [struct(*shape) for shape in shapes]
    own, *grads = call(
        kernel,
        [*group_grads, *grads],
        outs,
        scratch=[pltpu.VMEM((2 * pairs, BLOCK, LANES), F32)],
    )
    return own, grads


def spread_pair(levels, pairs, own_grad, rough, fine, block_second):
    own_rows = levels.rows

    def kernel(own, block, *refs):
        rough_in = refs[: levels.bits - 1]
        fine_in = refs[levels.bits - 1 : 2 * levels.bits - 1]
        mine, theirs, *ladder = refs[2 * levels.bits - 1 :]
        last = pl.ds(rough_in[0].shape[1] - own_rows, own_rows)
        for tile in range(2 * pairs):
            above = own[tile] + rough_in[0][tile, last]
            for step in range(1, levels.bits - 1):
                above = above + rough_in[step][tile, pl.ds(0, own_rows)]
            filled = 0
            for m, rows in levels.differences[1]:
                part = fine_in[1][tile, pl.ds(filled, rows)]
                for step in range(2, min(m, levels.bits)):
                    part = part + fine_in[step][tile, pl.ds(filled, rows)]
                filled += rows
                put_pairs(ladder[m - 2], (), 0.5 * above, 0.5 * part)
                above = ladder[m - 2][...]
            mine[tile] = above[:QUARTER]
            theirs[tile] = above[QUARTER:] + block[tile]

    return call(
        kernel,
        [own_grad, block_second, *rough, *fine],
        [struct(2 * pairs, QUARTER, LANES)] * 2,
        scratch=levels.scratch(),
    )


def unpack(pairs, kept, arrived, features, scalar):
    def kernel(bit, mine, theirs, out):
        for pair in range(pairs):
            for side, ref in ((bit[0], mine), (1 - bit[0], theirs)):
                column = side * (features // 2) + pair * LANES
                column = pl.ds(pl.multiple_of(column, LANES), LANES)
                out[:, column] = ref[pair]

    return call(kernel, [kept, arrived], [struct(BLOCK, features)], scalar=scalar)[0]


def widen(pairs, endings):
    factor = QUARTER // endings[0].shape[1]

    def kernel(*refs):
        for value, out in zip(refs[:2], refs[2:]):
            for tile in range(2 * pairs):
                out[tile] = jnp.zeros((QUARTER, LANES), F32)
                add_spread(out, (tile,), 0, value[tile], factor)

    outs = [struct(2 * pairs, QUARTER, LANES)] * 2
    return call(kernel, endings, outs, flops=700000000)


def finish(pairs, kept, rest, finest, seconds, endings, features, scalar):
    def kernel(bit, kept_in, rest_in, f_mine, f_theirs, s_mine, s_theirs, *refs):
        e_mine, e_theirs = refs[:2]
        outs, total, middle = refs[2:4], refs[4], refs[5]
        for tile in range(2 * pairs):
            out = outs[tile // pairs]
            column = tile % pairs * LANES
            at = (tile,)
            total[tile] = kept_in[tile]
            add_spread(total, at, 0, f_mine[tile], 2)
            add_spread(total, at, 0, s_mine[tile] + e_mine[tile], 4)
            place = bit[0] * (features // 2) + column
            out[:, pl.ds(pl.multiple_of(place, LANES), LANES)] = total[tile]
            second = s_theirs[tile] + e_theirs[tile]
            put_pairs(middle, at, 0.5 * second, 0.5 * rest_in[tile, :QUARTER])
            first = 0.5 * (middle[tile] + f_theirs[tile])
            put_pairs(total, at, first, 0.5 * rest_in[tile, QUARTER:])
            place = (1 - bit[0]) * (features // 2) + column
            out[:, pl.ds(pl.multiple_of(place, LANES), LANES)] = total[tile]

    return call(
        kernel,
        [kept, rest, *finest, *seconds, *endings],
        [struct(BLOCK, features)] * 2,
        scratch=[
            pltpu.VMEM((2 * pairs, BLOCK, LANES), F32),
            pltpu.VMEM((2 * pairs, HALF, LANES), F32),
        ],
        scalar=scalar,
    )


def on_device(queries, keys, values, cotangent):
    features = queries.shape[1]
    assert queries.shape[0] == BLOCK
    pairs = features // LANES // 2
    lo_bits = lax.axis_size("seqlo").bit_length() - 1
    levels = Levels(lo_bits - 1)
    lo = levels.whole
    hi_bits = lax.axis_size("seqhi").bit_length() - 1
    hi = Tree(lo_bits, [BLOCK >> step for step in range(hi_bits)])
    scalar = (lax.axis_index("seqlo") % 2).astype(jnp.int32).reshape(1)
    queries, keys, values, cotangent = [
        pltpu.with_memory_space_constraint(array, pltpu.HBM)
        for array in (queries, keys, values, cotangent)
    ]
    f_theirs, c_send, rest = pack_theirs(pairs, keys, values, scalar)
    mine_kv, f_mine, c_mine = pack_mine(pairs, keys, values, scalar)
    second = exchange(c_send, 1)
    finest_theirs = exchange(f_theirs, 2)
    coarse = coarsen_pair(lo, pairs, c_mine, second)
    finest = exchange(ordered(f_mine, finest_theirs), 2)
    rest = exchange(ordered(rest, coarse[0]), 1)
    half = exchange(ordered(finest_theirs, rest), 1)
    kv = rebuild(pairs, second, rest)
    send_qg, mine_qg = pack(pairs, queries, cotangent, scalar)
    qg = exchange(ordered(send_qg, half), 1)
    zs = lo.gather([None, *coarse], (finest, send_qg))
    group = coarsen_group(
        lo, hi, pairs, ordered(coarse[-1], rest), [finest, half], zs
    )
    turned = turn(pairs, mine_qg, qg)
    rs = hi.gather(group, turned)
    block_sets = [(0, 0, 0, BLOCK), (0, 1, 0, BLOCK)]
    lo_sets = [(1, 2, 0, BLOCK // 2), (1, 3, 0, BLOCK // 2)]
    for level in range(lo.bits):
        for step, row, rows in lo.held[level]:
            lo_sets.append((1 + level, 4 + step, row, rows))
    hi_sets = []
    for level in range(hi.bits):
        for step, row, rows in hi.held[level]:
            hi_sets.append((lo_bits + level, step, row, rows))
    first_in = [mine_kv, kv, finest, half, *zs]
    *kept, tops, sums, partial = attend_first(
        pairs, block_sets + lo_sets, first_in, turned
    )
    *rs_grads, o_keep, o_send, g_scaled, row_dot, kt_hi, d_hi = attend_last(
        pairs, hi_sets, rs, turned, tops, sums, partial
    )
    shapes = [(2 * pairs, *a.shape[1:]) for a in first_in]
    finest_grad, half_grad, *zs_grads, d_lo = attend_back(
        pairs,
        [(level, index - 2, row, rows) for level, index, row, rows in lo_sets],
        shapes[2:],
        BOTH,
        kept,
        turned,
        g_scaled,
        row_dot,
        [],
    )
    kv_keep, kv_send, dq_keep, dq_send = attend_back(
        pairs,
        block_sets,
        shapes[:2],
        0,
        kept,
        turned,
        g_scaled,
        row_dot,
        [d_lo, kt_hi, d_hi],
    )
    rough_grads, fine_grads = take_levels(levels, pairs, zs_grads)
    group_grads = hi.scatter(rs_grads)
    half_back = exchange(ordered(half_grad, kv_send), 1)
    o_back = exchange(o_send, 1)
    fine_back, finest_mine = levels.fine.scatter(fine_grads, finest_grad)
    block_second, rest_grad = take_apart(pairs, kv_send)
    split_at = rest_grad.shape[1]
    bulk = jnp.concatenate([rest_grad, dq_send.reshape(2 * pairs, HALF, LANES)], axis=1)
    bulk = exchange(bulk, 1)
    rest_back = bulk[:, :split_at]
    dq_back = bulk[:, split_at:].reshape(pairs, BLOCK, LANES)
    group_grads[-1] = ordered(group_grads[-1], (kv_send, o_back))
    own_grad, rough_grads = spread_group(levels, hi, pairs, group_grads, rough_grads)
    *rough_back, ending = levels.rough.scatter(rough_grads, whole=False)
    half_rows = levels.rows // 2
    finest_theirs = exchange(ordered(half_back, rough_back[0]), 2)
    far = 1 << levels.bits
    ending_mine = exchange(ending[:, :half_rows], far)
    ending_theirs = exchange(ending[:, half_rows:], far + 1)
    second_mine, second_send = spread_pair(
        levels, pairs, own_grad, rough_back, fine_back, block_second
    )
    second_theirs = exchange(second_send, 1)
    attended = unpack(pairs, o_keep, o_back, features, scalar)
    query_grad = unpack(pairs, dq_keep, dq_back, features, scalar)
    key_grad, value_grad = finish(
        pairs,
        kv_keep,
        rest_back,
        (finest_mine, finest_theirs),
        (second_mine, second_theirs),
        widen(pairs, [ending_mine, ending_theirs]),
        features,
        scalar,
    )
    return attended, query_grad, key_grad, value_grad


def solution(mesh):
    spec = P(AXES, None)
    return jax.shard_map(
        on_device,
        mesh=mesh,
        in_specs=(spec,) * 4,
        out_specs=(spec,) * 4,
        check_vma=False,
    )
```

```python
import math

import jax
import jax.numpy as jnp
from jax import lax
from jax.experimental import pallas as pl
from jax.experimental.pallas import tpu as pltpu
from jax.sharding import PartitionSpec as P

HEADS = 12
BLOCK = 128
HEAD_DIM = 64
LANES = 2 * HEAD_DIM
AXES = ("seqhi", "seqlo")
VMEM_LIMIT = 20 * 1024 * 1024
F32 = jnp.float32
BF16 = jnp.bfloat16
LOG2_E = 1.0 / math.log(2.0)
SCALE = 1.0 / math.sqrt(HEAD_DIM)


def struct(*shape):
    return jax.ShapeDtypeStruct(shape, F32)


def call(kernel, operands, outs, scratch=(), scalar=None, flops=0, exps=0, where=None):
    vmem = pl.BlockSpec(memory_space=pltpu.VMEM)
    smem = pl.BlockSpec(memory_space=pltpu.SMEM)
    in_specs = [pl.BlockSpec(memory_space=where) if where else vmem] * len(operands)
    if scalar is not None:
        operands = [scalar, *operands]
        in_specs = [smem, *in_specs]
    moved = sum(4 * math.prod(a.shape) for a in [*operands, *outs])
    return pl.pallas_call(
        kernel,
        out_shape=list(outs),
        in_specs=in_specs,
        out_specs=[vmem] * len(outs),
        scratch_shapes=list(scratch),
        compiler_params=pltpu.CompilerParams(vmem_limit_bytes=VMEM_LIMIT),
        cost_estimate=pl.CostEstimate(
            flops=flops, bytes_accessed=moved, transcendentals=exps
        ),
    )(*operands)


def exchange(value, offset):
    count = lax.axis_size(AXES)
    return lax.ppermute(value, AXES, [(i, i ^ offset) for i in range(count)])


def ordered(value, after):
    return value if after is None else lax.optimization_barrier((value, after))[0]


def half_difference(ref, lead, first, count):
    even = ref[(*lead, pl.ds(first, count, stride=2), slice(None))]
    odd = ref[(*lead, pl.ds(first + 1, count, stride=2), slice(None))]
    return 0.5 * (even - odd)


def put_pairs(ref, lead, total, difference):
    count = total.shape[0]
    ref[(*lead, pl.ds(0, count, stride=2), slice(None))] = total + difference
    ref[(*lead, pl.ds(1, count, stride=2), slice(None))] = total - difference


def mean_rows(ref, lead, first, count, factor):
    total = None
    for step in range(factor):
        rows = pl.ds(first + step, count, stride=factor)
        part = ref[(*lead, rows, slice(None))]
        total = part if total is None else total + part
    return total * (1.0 / factor)


def add_spread(ref, lead, first, value, factor):
    count = value.shape[0]
    value = value * (1.0 / factor)
    for step in range(factor):
        rows = pl.ds(first + step, count, stride=factor)
        place = (*lead, rows, slice(None))
        ref[place] = ref[place] + value


class Tree:
    def __init__(self, first_bit, own_rows):
        self.bits = bits = len(own_rows)
        self.first_bit = first_bit
        self.own_rows = own_rows
        self.held = {}
        self.payload = {}
        for step in range(bits - 1, -1, -1):
            rows = self.own_rows[step]
            payload = []
            fresh = {step: [(step, 0, rows)] if rows else []}
            for level in range(step + 1, bits):
                for piece in self.held[level]:
                    payload.append(piece)
                    fresh.setdefault(level, []).append((step, rows, piece[2]))
                    rows += piece[2]
            self.payload[step] = payload
            for level, pieces in fresh.items():
                self.held[level] = self.held.get(level, []) + pieces

    def rows(self, step):
        return self.own_rows[step] + sum(piece[2] for piece in self.payload[step])

    def partner(self, value, step):
        return exchange(value, 1 << self.first_bit + step)

    def gather(self, own, after=None):
        arrived = [None] * self.bits
        for step in range(self.bits - 1, -1, -1):
            parts = [own[step]] if self.own_rows[step] else []
            for source, row, rows in self.payload[step]:
                part = arrived[source]
                whole = rows == part.shape[1]
                parts.append(part if whole else part[:, row : row + rows])
            sent = jnp.concatenate(parts, axis=1) if len(parts) > 1 else parts[0]
            if step == 0:
                sent = ordered(sent, after)
            arrived[step] = self.partner(sent, step)
        return arrived

    def scatter(self, grads, front=None, whole=True):
        grads = list(grads)
        returned = []
        for step in range(self.bits if whole else self.bits - 1):
            sent = grads[step]
            if step == 0 and front is not None:
                rows = front.shape[1]
                back = self.partner(jnp.concatenate([front, sent], axis=1), step)
                front, back = back[:, :rows], back[:, rows:]
            else:
                back = self.partner(sent, step)
            returned.append(back)
            filled = self.own_rows[step]
            for source, row, rows in self.payload[step]:
                part = back[:, filled : filled + rows]
                grads[source] = grads[source].at[:, row : row + rows].add(part)
                filled += rows
        if not whole:
            returned.append(grads[-1])
        return returned if front is None else (returned, front)


def split(value):
    high = value.astype(BF16).astype(F32)
    return high, value - high


def halves_by_head(value):
    high, low = split(value)
    first = lax.broadcasted_iota(jnp.int32, value.shape, 1) < HEAD_DIM
    one = jnp.where(first, high, pltpu.roll(low, HEAD_DIM, 1))
    two = jnp.where(first, pltpu.roll(high, HEAD_DIM, 1), low)
    return one, two


def dot(lhs, rhs, dims):
    return lax.dot_general(lhs, rhs, (dims, ((), ())), preferred_element_type=F32)


NN = ((1,), (0,))
NT = ((1,), (1,))


BOTH = 2 * BLOCK
GROUP = 3


def halves_of(sets, ins, which, pairs, pair):
    tile = which * pairs + pair
    parts = [ins[index][tile, pl.ds(row, rows), :] for _, index, row, rows in sets]
    return halves_by_head(jnp.concatenate(parts, axis=0))


def segment_levels(sets):
    levels, filled = [], 0
    for level, _, _, rows in sets:
        if filled % BLOCK == 0:
            levels.append(level)
        filled += rows
    return levels


def four_rows(value):
    high, low = split(value)
    four = jnp.concatenate([high, high, low, low], axis=0).astype(BF16)
    return four, jnp.concatenate([high, low], axis=0).astype(BF16)


def store_split(ref, lead, rows, value):
    high = value.astype(BF16)
    ref[(lead, 0, rows)] = high
    ref[(lead, 1, rows)] = (value - high.astype(F32)).astype(BF16)


def fold_rows(value):
    return value[:HEAD_DIM] + value[HEAD_DIM:]


def fold_heads(one, two):
    first = lax.broadcasted_iota(jnp.int32, one.shape, 1) < HEAD_DIM
    return jnp.where(
        first, one + pltpu.roll(one, HEAD_DIM, 1), two + pltpu.roll(two, HEAD_DIM, 1)
    )


def twice(value):
    return jnp.concatenate([value, value], axis=1)


def stacked(ref, at, rows=slice(None)):
    return jnp.concatenate([ref[at, 0, rows], ref[at, 1, rows]], axis=0)


def abreast(ref, at, rows=slice(None)):
    return jnp.concatenate([ref[at, 0, rows], ref[at, 1, rows]], axis=1)


def column_scores(levels, keys, at, q_four, s_ref):
    highest = None
    for index, level in enumerate(levels):
        rows = pl.ds(index * BLOCK, BLOCK)
        s = dot(twice(keys[at, rows]), q_four, NN)
        s = s + float(level) if level else s
        s_ref[at, rows] = s
        top = jnp.max(s.reshape(BLOCK // 8, 8, BOTH), axis=0)
        highest = top if highest is None else jnp.maximum(highest, top)
    return jnp.max(highest, axis=0, keepdims=True)


def exponents(levels, at, top, s_ref, e_ref, keep):
    summed = None
    for index in range(len(levels)):
        rows = pl.ds(index * BLOCK, BLOCK)
        e = jnp.exp2(s_ref[at, rows] - top)
        if keep:
            s_ref[at, rows] = e
        store_split(e_ref, at, rows, e)
        part = jnp.sum(e.reshape(BLOCK // 8, 8, BOTH), axis=0)
        summed = part if summed is None else summed + part
    return jnp.sum(summed, axis=0, keepdims=True)


def head_rows(ref, pair, head):
    return ref[pair, pl.ds(head * HEAD_DIM, HEAD_DIM)]


def each_group(pairs, body):
    for first in range(0, pairs, GROUP):
        group = range(first, min(first + GROUP, pairs))
        body(group, [(pair, head, 2 * pair + head) for pair in group for head in (0, 1)])


def costs(pairs, rows, products, exps=0):
    return dict(
        flops=2 * 4 * products * pairs * 2 * rows * BOTH * HEAD_DIM,
        exps=exps * pairs * 2 * rows * BOTH,
    )


def put_halves(pairs, sets, ins, group, plain, turned):
    for which in range(2):
        for pair in group:
            for head, value in enumerate(halves_of(sets, ins, which, pairs, pair)):
                plain[which][2 * pair + head] = value.astype(BF16)
                turned[which][2 * pair + head] = value.T.astype(BF16)


def prepare(pairs, sets, operands):
    total = sum(s[3] for s in sets)

    def kernel(*refs):
        kc, vc, kt, vt = refs[len(operands) :]
        put_halves(pairs, sets, refs[: len(operands)], range(pairs), (kc, vc), (kt, vt))

    plain = jax.ShapeDtypeStruct((2 * pairs, total, LANES), BF16)
    turned = jax.ShapeDtypeStruct((2 * pairs, LANES, total), BF16)
    return call(kernel, operands, [plain] * 2 + [turned] * 2)


def attend_first(pairs, sets, kc, vt, turned):
    total = sum(s[3] for s in sets)
    levels = segment_levels(sets)

    def kernel(turn_in, kc, vt, e_ref, tops, sums, out, s_ref):
        def body(group, heads):
            for pair, head, at in heads:
                q_four, _ = four_rows(head_rows(turn_in, pair, head))
                tops[at] = column_scores(levels, kc, at, q_four, s_ref)
            for _, _, at in heads:
                sums[at] = exponents(levels, at, tops[at], s_ref, e_ref, False)
            for _, _, at in heads:
                out[at] = fold_rows(dot(twice(vt[at]), stacked(e_ref, at), NN))

        each_group(pairs, body)

    heads = 2 * pairs
    outs = [jax.ShapeDtypeStruct((heads, 2, total, BOTH), BF16)]
    outs += [struct(heads, 1, BOTH)] * 2 + [struct(heads, HEAD_DIM, BOTH)]
    return call(
        kernel,
        [turned, kc, vt],
        outs,
        scratch=[pltpu.VMEM((heads, total, BOTH), F32)],
        **costs(pairs, total, 2, 1),
    )


def attend_last(pairs, sets, operands, turned, tops, sums, partial):
    total = sum(s[3] for s in sets)
    levels = segment_levels(sets)

    def kernel(turn_in, top_in, sum_in, part_in, *refs):
        ins = refs[: len(operands)]
        grads = refs[len(operands) : 2 * len(operands)]
        o_keep, o_send, g_out, r_out, kt, d_ref = refs[2 * len(operands) : -5]
        s_ref, e_ref, kc, vc, vt = refs[-5:]

        def body(group, heads):
            put_halves(pairs, sets, ins, group, (kc, vc), (kt, vt))
            queries = {}
            top = {}
            for pair, head, at in heads:
                q_four, queries[at] = four_rows(head_rows(turn_in, pair, head))
                top[at] = column_scores(levels, kc, at, q_four, s_ref)
            inverse = {}
            rescale = {}
            for _, _, at in heads:
                first_top = top_in[at]
                highest = jnp.maximum(top[at], first_top)
                rescale[at] = jnp.exp2(first_top - highest)
                summed = exponents(levels, at, highest, s_ref, e_ref, True)
                inverse[at] = 1.0 / (summed + sum_in[at] * rescale[at])
            output = {}
            cotangents = {}
            row_dot = {}
            for pair, head, at in heads:
                o = fold_rows(dot(twice(vt[at]), stacked(e_ref, at), NN))
                o = (o + part_in[at] * rescale[at]) * inverse[at]
                output[at] = o
                scaled = head_rows(turn_in, pairs + pair, head) * inverse[at]
                cotangents[at] = four_rows(scaled)
                row_dot[at] = jnp.sum(o * scaled, axis=0, keepdims=True)
                g_out[at] = scaled * rescale[at]
                r_out[at] = row_dot[at] * rescale[at]
            for _, _, at in heads:
                for index in range(len(levels)):
                    rows = pl.ds(index * BLOCK, BLOCK)
                    dp = dot(twice(vc[at, rows]), cotangents[at][0], NN)
                    store_split(d_ref, at, rows, s_ref[at, rows] * (dp - row_dot[at]))
            key_grads = {}
            value_grads = {}
            for _, _, at in heads:
                value_grads[at] = dot(abreast(e_ref, at), twice(cotangents[at][1]), NT)
                key_grads[at] = dot(abreast(d_ref, at), twice(queries[at]), NT)
            for pair in group:
                put_grads(pairs, pair, sets, grads, key_grads, value_grads)
                both = [output[2 * pair], output[2 * pair + 1]]
                both = jnp.concatenate(both, axis=0).T
                o_keep[pair] = both[:BLOCK]
                o_send[pair] = both[BLOCK:]

        each_group(pairs, body)

    heads = 2 * pairs
    outs = [struct(*a.shape) for a in operands]
    outs += [struct(pairs, BLOCK, LANES)] * 2
    outs += [struct(heads, HEAD_DIM, BOTH), struct(heads, 1, BOTH)]
    outs.append(jax.ShapeDtypeStruct((heads, LANES, total), BF16))
    outs.append(jax.ShapeDtypeStruct((heads, 2, total, BOTH), BF16))
    return call(
        kernel,
        [turned, tops, sums, partial, *operands],
        outs,
        scratch=[pltpu.VMEM((heads, total, BOTH), F32)]
        + [pltpu.VMEM((heads, 2, total, BOTH), BF16)]
        + [pltpu.VMEM((heads, total, LANES), BF16)] * 2
        + [pltpu.VMEM((heads, LANES, total), BF16)],
        **costs(pairs, total, 5, 1),
    )


def put_grads(pairs, pair, sets, grads, key_grads, value_grads):
    for which, parts in enumerate((key_grads, value_grads)):
        both = fold_heads(parts[2 * pair], parts[2 * pair + 1])
        if which == 0:
            both = both * (1.0 / LOG2_E)
        filled = 0
        for _, index, row, rows in sets:
            piece = both[filled : filled + rows]
            grads[index][which * pairs + pair, pl.ds(row, rows), :] = piece
            filled += rows


def attend_back(pairs, sets, shapes, first, kept, turned, g_scaled, row_dot, others):
    total = sum(s[3] for s in sets)
    segments = total // BLOCK

    def kernel(turn_in, kt, vc, e_ref, g_in, r_in, *refs):
        other_in = refs[: len(others)]
        grads = refs[len(others) : len(others) + len(shapes)]
        dq_out = refs[len(others) + len(shapes) : -1]
        d_ref = refs[-1]
        span = pl.ds(first, total)

        def body(group, heads):
            cotangents = {}
            for _, _, at in heads:
                g_four, cotangents[at] = four_rows(g_in[at])
                for index in range(segments):
                    rows = pl.ds(first + index * BLOCK, BLOCK)
                    dp = dot(twice(vc[at, rows]), g_four, NN)
                    e = e_ref[at, 0, rows].astype(F32) + e_ref[at, 1, rows].astype(F32)
                    place = pl.ds(index * BLOCK, BLOCK)
                    store_split(d_ref, at, place, e * (dp - r_in[at]))
            queries_grad = {}
            key_grads = {}
            value_grads = {}
            for pair, head, at in heads:
                _, q_rows = four_rows(head_rows(turn_in, pair, head))
                g_rows = cotangents[at]
                value_grads[at] = dot(abreast(e_ref, at, span), twice(g_rows), NT)
                key_grads[at] = dot(abreast(d_ref, at), twice(q_rows), NT)
                if others:
                    d_lo, kt_hi, d_hi = other_in
                    part = dot(twice(kt[at, :, span]), stacked(d_ref, at), NN)
                    part += dot(twice(kt[at, :, total:]), stacked(d_lo, at), NN)
                    part += dot(twice(kt_hi[at]), stacked(d_hi, at), NN)
                    queries_grad[at] = fold_rows(part)
            for pair in group:
                put_grads(pairs, pair, sets, grads, key_grads, value_grads)
                if others:
                    both = [queries_grad[2 * pair], queries_grad[2 * pair + 1]]
                    both = jnp.concatenate(both, axis=0).T * SCALE
                    dq_out[0][pair] = both[:BLOCK]
                    dq_out[1][pair] = both[BLOCK:]

        each_group(pairs, body)

    outs = [struct(*shape) for shape in shapes]
    scratch = []
    if others:
        outs += [struct(pairs, BLOCK, LANES)] * 2
        scratch.append(pltpu.VMEM((2 * pairs, 2, total, BOTH), BF16))
    else:
        outs.append(jax.ShapeDtypeStruct((2 * pairs, 2, total, BOTH), BF16))
    return call(
        kernel,
        [turned, *kept, g_scaled, row_dot, *others],
        outs,
        scratch=scratch,
        **costs(pairs, total, 4),
    )


def copy_columns(moves, ins, sems, bit):
    started = []
    for operand, theirs, column, place in moves:
        side = 1 - bit if theirs else bit
        column = side * (ins[operand].shape[1] // 2) + column
        column = pl.ds(pl.multiple_of(column, LANES), LANES)
        copy = pltpu.make_async_copy(
            ins[operand].at[:, column], place, sems.at[len(started)]
        )
        copy.start()
        started.append(copy)
    return started


def pack(pairs, first, second, scalar):
    def kernel(bit, one, two, theirs, mine, sems):
        moves = []
        for tile in range(2 * pairs):
            for out, other in ((theirs, True), (mine, False)):
                column = tile % pairs * LANES
                moves.append((tile // pairs, other, column, out.at[tile]))
        for copy in copy_columns(moves, (one, two), sems, bit[0]):
            copy.wait()

    return call(
        kernel,
        [first, second],
        [struct(2 * pairs, BLOCK, LANES)] * 2,
        scratch=[pltpu.SemaphoreType.DMA((4 * pairs,))],
        scalar=scalar,
        where=pl.ANY,
    )


QUARTER = BLOCK // 4
HALF = BLOCK // 2


def pack_theirs(pairs, keys, values, scalar):
    def kernel(bit, k, v, finest, coarse, rest, block, sems):
        moves = []
        for tile in range(2 * pairs):
            moves.append((tile // pairs, True, tile % pairs * LANES, block.at[tile]))
        copies = copy_columns(moves, (k, v), sems, bit[0])
        for tile, copy in enumerate(copies):
            copy.wait()
            finest[tile] = mean_rows(block, (tile,), 0, HALF, 2)
            coarse[tile] = mean_rows(finest, (tile,), 0, QUARTER, 2)
            rest[tile, :QUARTER] = half_difference(finest, (tile,), 0, QUARTER)
            rest[tile, QUARTER:] = half_difference(block, (tile,), 0, HALF)

    return call(
        kernel,
        [keys, values],
        [
            struct(2 * pairs, HALF, LANES),
            struct(2 * pairs, QUARTER, LANES),
            struct(2 * pairs, QUARTER + HALF, LANES),
        ],
        scratch=[
            pltpu.VMEM((2 * pairs, BLOCK, LANES), F32),
            pltpu.SemaphoreType.DMA((2 * pairs,)),
        ],
        scalar=scalar,
        where=pl.ANY,
    )


def pack_mine(pairs, keys, values, scalar):
    def kernel(bit, k, v, block, finest, coarse, sems):
        moves = []
        for tile in range(2 * pairs):
            moves.append((tile // pairs, False, tile % pairs * LANES, block.at[tile]))
        copies = copy_columns(moves, (k, v), sems, bit[0])
        for tile, copy in enumerate(copies):
            copy.wait()
            finest[tile] = mean_rows(block, (tile,), 0, HALF, 2)
            coarse[tile] = mean_rows(finest, (tile,), 0, QUARTER, 2)

    return call(
        kernel,
        [keys, values],
        [
            struct(2 * pairs, BLOCK, LANES),
            struct(2 * pairs, HALF, LANES),
            struct(2 * pairs, QUARTER, LANES),
        ],
        scratch=[pltpu.SemaphoreType.DMA((2 * pairs,))],
        scalar=scalar,
        where=pl.ANY,
    )


def rebuild(pairs, second, rest):
    def kernel(second_in, rest_in, out, finest):
        for tile in range(2 * pairs):
            put_pairs(finest, (tile,), second_in[tile], rest_in[tile, :QUARTER])
            put_pairs(out, (tile,), finest[tile], rest_in[tile, QUARTER:])

    return call(
        kernel,
        [second, rest],
        [struct(2 * pairs, BLOCK, LANES)],
        scratch=[pltpu.VMEM((2 * pairs, HALF, LANES), F32)],
    )[0]


def take_apart(pairs, block_grad):
    def kernel(block, second, rest, finest):
        for tile in range(2 * pairs):
            finest[tile] = 2.0 * mean_rows(block, (tile,), 0, HALF, 2)
            rest[tile, QUARTER:] = 2.0 * half_difference(block, (tile,), 0, HALF)
            second[tile] = 2.0 * mean_rows(finest, (tile,), 0, QUARTER, 2)
            rest[tile, :QUARTER] = 2.0 * half_difference(finest, (tile,), 0, QUARTER)

    return call(
        kernel,
        [block_grad],
        [
            struct(2 * pairs, QUARTER, LANES),
            struct(2 * pairs, QUARTER + HALF, LANES),
        ],
        scratch=[pltpu.VMEM((2 * pairs, HALF, LANES), F32)],
    )


class Levels:
    def __init__(self, bits):
        self.bits = bits
        self.rows = BLOCK >> bits
        self.differences = [
            [(m, BLOCK >> m) for m in range(bits, step, -1)] for step in range(bits)
        ]
        whole = [0] + [BLOCK >> step for step in range(1, bits)]
        self.whole = Tree(1, whole)
        self.rough = Tree(1, [0] + [self.rows] * (bits - 1))
        self.fine = Tree(1, [0] + [rows - self.rows for rows in whole[1:]])
        self.pieces = []
        for level in range(1, bits):
            trees = (self.whole, self.rough, self.fine)
            for parts in zip(*(tree.held[level] for tree in trees)):
                self.pieces.append((level, parts[0][0], *(part[1] for part in parts)))

    def scratch(self):
        shapes = [(BLOCK >> m, LANES) for m in range(1, self.bits + 1)]
        return [pltpu.VMEM(shape, F32) for shape in shapes]

    def group_pieces(self):
        pieces = []
        for index, (level, step, whole, rough, _) in enumerate(self.pieces):
            factor = 1 << self.bits - level
            place = (2 + index) * self.rows
            pieces.append((step, whole, rough, BLOCK >> level, factor, place))
        return pieces


def coarsen_pair(lo, pairs, mine, received):
    def kernel(own, got, *outs):
        for tile in range(2 * pairs):
            outs[0][tile, : BLOCK // 4] = own[tile]
            outs[0][tile, BLOCK // 4 :] = got[tile]
            for index in range(1, lo.bits):
                outs[index][tile] = mean_rows(
                    outs[index - 1], (tile,), 0, BLOCK >> index + 1, 2
                )

    outs = [struct(2 * pairs, BLOCK >> step, LANES) for step in range(1, lo.bits + 1)]
    return call(kernel, [mine, received], outs)


def group_pieces(lo):
    own = BLOCK >> lo.bits
    factor = 1 << lo.bits
    pieces = [
        (-2, 0, BLOCK // 2, factor, own),
        (-1, 0, BLOCK // 2, factor, own + own // 2),
    ]
    filled = 2 * own
    for level in range(1, lo.bits):
        factor = 1 << lo.bits - level
        for step, row, rows in lo.held[level]:
            pieces.append((step, row, rows, factor, filled))
            filled += rows // factor
    return pieces


def coarsen_group(lo, hi, pairs, own, halves, arrived):
    pieces = group_pieces(lo)

    def kernel(own_in, *refs):
        ins = refs[: 2 + lo.bits]
        outs = refs[2 + lo.bits :]
        for tile in range(2 * pairs):
            outs[0][tile, pl.ds(0, BLOCK >> lo.bits)] = own_in[tile]
            for step, row, rows, factor, place in pieces:
                count = rows // factor
                outs[0][tile, pl.ds(place, count)] = mean_rows(
                    ins[2 + step], (tile,), row, count, factor
                )
            for step in range(1, hi.bits):
                outs[step][tile] = mean_rows(
                    outs[step - 1], (tile,), 0, BLOCK >> step, 2
                )

    outs = [struct(2 * pairs, BLOCK >> step, LANES) for step in range(hi.bits)]
    return call(kernel, [own, *halves, *arrived], outs)


def turn(pairs, mine, received):
    def kernel(own, got, turned):
        for tile in range(2 * pairs):
            both = jnp.concatenate([own[tile], got[tile]], axis=0).T
            turned[tile] = both * (SCALE * LOG2_E) if tile < pairs else both

    return call(kernel, [mine, received], [struct(2 * pairs, LANES, 2 * BLOCK)])[0]


def take_levels(levels, pairs, grads):
    trees = (levels.rough, levels.fine)

    def kernel(*refs):
        ins = refs[: levels.bits]
        rough = refs[levels.bits : 2 * levels.bits]
        fine = refs[2 * levels.bits : 3 * levels.bits]
        ladder = refs[3 * levels.bits :]
        for tile in range(2 * pairs):
            for level, step, row, rough_row, fine_row in levels.pieces:
                source = ladder[level - 1]
                source[...] = ins[step][tile, pl.ds(row, BLOCK >> level)]
                fine_row += sum(rows for _, rows in levels.differences[level])
                for m, rows in reversed(levels.differences[level]):
                    fine_row -= rows
                    part = 2.0 * half_difference(source, (), 0, rows)
                    fine[step][tile, pl.ds(fine_row, rows)] = part
                    ladder[m - 1][...] = 2.0 * mean_rows(source, (), 0, rows, 2)
                    source = ladder[m - 1]
                rough[step][tile, pl.ds(rough_row, levels.rows)] = source[...]

    outs = [
        struct(2 * pairs, tree.rows(step), LANES)
        for tree in trees
        for step in range(levels.bits)
    ]
    outs = call(kernel, grads, outs, scratch=levels.scratch())
    return outs[: levels.bits], outs[levels.bits :]


def spread_group(levels, hi, pairs, group_grads, grads):
    own_rows = levels.rows

    def kernel(*refs):
        steps = refs[: hi.bits]
        ins = refs[hi.bits : hi.bits + levels.bits]
        own_out, *outs = refs[hi.bits + levels.bits : -1]
        total = refs[-1]
        for tile in range(2 * pairs):
            total[tile] = steps[0][tile, pl.ds(0, BLOCK)]
            for step in range(1, hi.bits):
                above = steps[step][tile, pl.ds(0, BLOCK >> step)]
                add_spread(total, (tile,), 0, above, 1 << step)
            own_out[tile] = total[tile, pl.ds(0, own_rows)]
            for step, _, row, _, _, place in levels.group_pieces():
                rows = pl.ds(row, own_rows)
                part = total[tile, pl.ds(place, own_rows)]
                outs[step][tile, rows] = ins[step][tile, rows] + part
            outs[0][tile, pl.ds(ins[0].shape[1], own_rows)] = total[
                tile, pl.ds(own_rows, own_rows)
            ]

    shapes = [list(a.shape) for a in grads]
    shapes[0][1] += own_rows
    outs = [struct(2 * pairs, own_rows, LANES)] + [struct(*shape) for shape in shapes]
    own, *grads = call(
        kernel,
        [*group_grads, *grads],
        outs,
        scratch=[pltpu.VMEM((2 * pairs, BLOCK, LANES), F32)],
    )
    return own, grads


def spread_pair(levels, pairs, own_grad, rough, fine, block_second):
    own_rows = levels.rows

    def kernel(own, block, *refs):
        rough_in = refs[: levels.bits - 1]
        fine_in = refs[levels.bits - 1 : 2 * levels.bits - 1]
        mine, theirs, *ladder = refs[2 * levels.bits - 1 :]
        last = pl.ds(rough_in[0].shape[1] - own_rows, own_rows)
        for tile in range(2 * pairs):
            above = own[tile] + rough_in[0][tile, last]
            for step in range(1, levels.bits - 1):
                above = above + rough_in[step][tile, pl.ds(0, own_rows)]
            filled = 0
            for m, rows in levels.differences[1]:
                part = fine_in[1][tile, pl.ds(filled, rows)]
                for step in range(2, min(m, levels.bits)):
                    part = part + fine_in[step][tile, pl.ds(filled, rows)]
                filled += rows
                put_pairs(ladder[m - 2], (), 0.5 * above, 0.5 * part)
                above = ladder[m - 2][...]
            mine[tile] = above[:QUARTER]
            theirs[tile] = above[QUARTER:] + block[tile]

    return call(
        kernel,
        [own_grad, block_second, *rough, *fine],
        [struct(2 * pairs, QUARTER, LANES)] * 2,
        scratch=levels.scratch(),
    )


def unpack(pairs, kept, arrived, features, scalar):
    def kernel(bit, mine, theirs, out):
        for pair in range(pairs):
            for side, ref in ((bit[0], mine), (1 - bit[0], theirs)):
                column = side * (features // 2) + pair * LANES
                column = pl.ds(pl.multiple_of(column, LANES), LANES)
                out[:, column] = ref[pair]

    return call(kernel, [kept, arrived], [struct(BLOCK, features)], scalar=scalar)[0]


def widen(pairs, endings):
    factor = QUARTER // endings[0].shape[1]

    def kernel(*refs):
        for value, out in zip(refs[:2], refs[2:]):
            for tile in range(2 * pairs):
                out[tile] = jnp.zeros((QUARTER, LANES), F32)
                add_spread(out, (tile,), 0, value[tile], factor)

    outs = [struct(2 * pairs, QUARTER, LANES)] * 2
    return call(kernel, endings, outs, flops=700000000)


def finish(pairs, kept, rest, finest, seconds, endings, features, scalar):
    def kernel(bit, kept_in, rest_in, f_mine, f_theirs, s_mine, s_theirs, *refs):
        e_mine, e_theirs = refs[:2]
        outs, total, middle = refs[2:4], refs[4], refs[5]
        for tile in range(2 * pairs):
            out = outs[tile // pairs]
            column = tile % pairs * LANES
            at = (tile,)
            total[tile] = kept_in[tile]
            add_spread(total, at, 0, f_mine[tile], 2)
            add_spread(total, at, 0, s_mine[tile] + e_mine[tile], 4)
            place = bit[0] * (features // 2) + column
            out[:, pl.ds(pl.multiple_of(place, LANES), LANES)] = total[tile]
            second = s_theirs[tile] + e_theirs[tile]
            put_pairs(middle, at, 0.5 * second, 0.5 * rest_in[tile, :QUARTER])
            first = 0.5 * (middle[tile] + f_theirs[tile])
            put_pairs(total, at, first, 0.5 * rest_in[tile, QUARTER:])
            place = (1 - bit[0]) * (features // 2) + column
            out[:, pl.ds(pl.multiple_of(place, LANES), LANES)] = total[tile]

    return call(
        kernel,
        [kept, rest, *finest, *seconds, *endings],
        [struct(BLOCK, features)] * 2,
        scratch=[
            pltpu.VMEM((2 * pairs, BLOCK, LANES), F32),
            pltpu.VMEM((2 * pairs, HALF, LANES), F32),
        ],
        scalar=scalar,
    )


def on_device(queries, keys, values, cotangent):
    features = queries.shape[1]
    assert queries.shape[0] == BLOCK
    pairs = features // LANES // 2
    lo_bits = lax.axis_size("seqlo").bit_length() - 1
    levels = Levels(lo_bits - 1)
    lo = levels.whole
    hi_bits = lax.axis_size("seqhi").bit_length() - 1
    hi = Tree(lo_bits, [BLOCK >> step for step in range(hi_bits)])
    scalar = (lax.axis_index("seqlo") % 2).astype(jnp.int32).reshape(1)
    queries, keys, values, cotangent = [
        pltpu.with_memory_space_constraint(array, pltpu.HBM)
        for array in (queries, keys, values, cotangent)
    ]
    f_theirs, c_send, rest = pack_theirs(pairs, keys, values, scalar)
    mine_kv, f_mine, c_mine = pack_mine(pairs, keys, values, scalar)
    second = exchange(c_send, 1)
    finest_theirs = exchange(f_theirs, 2)
    coarse = coarsen_pair(lo, pairs, c_mine, second)
    finest = exchange(ordered(f_mine, finest_theirs), 2)
    rest = exchange(ordered(rest, coarse[0]), 1)
    half = exchange(ordered(finest_theirs, rest), 1)
    kv = rebuild(pairs, second, rest)
    send_qg, mine_qg = pack(pairs, queries, cotangent, scalar)
    qg = exchange(ordered(send_qg, half), 1)
    zs = lo.gather([None, *coarse], (finest, send_qg))
    group = coarsen_group(
        lo, hi, pairs, ordered(coarse[-1], rest), [finest, half], zs
    )
    block_sets = [(0, 0, 0, BLOCK), (0, 1, 0, BLOCK)]
    lo_sets = [(1, 2, 0, BLOCK // 2), (1, 3, 0, BLOCK // 2)]
    for level in range(lo.bits):
        for step, row, rows in lo.held[level]:
            lo_sets.append((1 + level, 4 + step, row, rows))
    hi_sets = []
    for level in range(hi.bits):
        for step, row, rows in hi.held[level]:
            hi_sets.append((lo_bits + level, step, row, rows))
    first_in = [mine_kv, kv, finest, half, *zs]
    kc, vc, kt, vt = prepare(pairs, block_sets + lo_sets, first_in)
    turned = turn(pairs, mine_qg, ordered(qg, kc))
    rs = hi.gather(group, turned)
    exps, tops, sums, partial = attend_first(
        pairs, block_sets + lo_sets, kc, vt, turned
    )
    kept = [kt, vc, exps]
    *rs_grads, o_keep, o_send, g_scaled, row_dot, kt_hi, d_hi = attend_last(
        pairs, hi_sets, rs, turned, tops, sums, partial
    )
    shapes = [(2 * pairs, *a.shape[1:]) for a in first_in]
    finest_grad, half_grad, *zs_grads, d_lo = attend_back(
        pairs,
        [(level, index - 2, row, rows) for level, index, row, rows in lo_sets],
        shapes[2:],
        BOTH,
        kept,
        turned,
        g_scaled,
        row_dot,
        [],
    )
    kv_keep, kv_send, dq_keep, dq_send = attend_back(
        pairs,
        block_sets,
        shapes[:2],
        0,
        kept,
        turned,
        g_scaled,
        row_dot,
        [d_lo, kt_hi, d_hi],
    )
    rough_grads, fine_grads = take_levels(levels, pairs, zs_grads)
    group_grads = hi.scatter(rs_grads)
    half_back = exchange(ordered(half_grad, kv_send), 1)
    o_back = exchange(o_send, 1)
    fine_back, finest_mine = levels.fine.scatter(fine_grads, finest_grad)
    block_second, rest_grad = take_apart(pairs, kv_send)
    split_at = rest_grad.shape[1]
    bulk = jnp.concatenate([rest_grad, dq_send.reshape(2 * pairs, HALF, LANES)], axis=1)
    bulk = exchange(bulk, 1)
    rest_back = bulk[:, :split_at]
    dq_back = bulk[:, split_at:].reshape(pairs, BLOCK, LANES)
    group_grads[-1] = ordered(group_grads[-1], (kv_send, o_back))
    own_grad, rough_grads = spread_group(levels, hi, pairs, group_grads, rough_grads)
    *rough_back, ending = levels.rough.scatter(rough_grads, whole=False)
    half_rows = levels.rows // 2
    finest_theirs = exchange(ordered(half_back, rough_back[0]), 2)
    far = 1 << levels.bits
    ending_mine = exchange(ending[:, :half_rows], far)
    ending_theirs = exchange(ending[:, half_rows:], far + 1)
    second_mine, second_send = spread_pair(
        levels, pairs, own_grad, rough_back, fine_back, block_second
    )
    second_theirs = exchange(second_send, 1)
    attended = unpack(pairs, o_keep, o_back, features, scalar)
    query_grad = unpack(pairs, dq_keep, dq_back, features, scalar)
    key_grad, value_grad = finish(
        pairs,
        kv_keep,
        rest_back,
        (finest_mine, finest_theirs),
        (second_mine, second_theirs),
        widen(pairs, [ending_mine, ending_theirs]),
        features,
        scalar,
    )
    return attended, query_grad, key_grad, value_grad


def solution(mesh):
    spec = P(AXES, None)
    return jax.shard_map(
        on_device,
        mesh=mesh,
        in_specs=(spec,) * 4,
        out_specs=(spec,) * 4,
        check_vma=False,
    )
```

```python
import math

import jax
import jax.numpy as jnp
from jax import lax
from jax.experimental import pallas as pl
from jax.experimental.pallas import tpu as pltpu
from jax.sharding import PartitionSpec as P

HEADS = 12
BLOCK = 128
HEAD_DIM = 64
LANES = 2 * HEAD_DIM
AXES = ("seqhi", "seqlo")
VMEM_LIMIT = 20 * 1024 * 1024
F32 = jnp.float32
BF16 = jnp.bfloat16
LOG2_E = 1.0 / math.log(2.0)
SCALE = 1.0 / math.sqrt(HEAD_DIM)


def struct(*shape):
    return jax.ShapeDtypeStruct(shape, F32)


def call(kernel, operands, outs, scratch=(), scalar=None, flops=0, exps=0, where=None):
    vmem = pl.BlockSpec(memory_space=pltpu.VMEM)
    smem = pl.BlockSpec(memory_space=pltpu.SMEM)
    in_specs = [pl.BlockSpec(memory_space=where) if where else vmem] * len(operands)
    if scalar is not None:
        operands = [scalar, *operands]
        in_specs = [smem, *in_specs]
    moved = sum(4 * math.prod(a.shape) for a in [*operands, *outs])
    return pl.pallas_call(
        kernel,
        out_shape=list(outs),
        in_specs=in_specs,
        out_specs=[vmem] * len(outs),
        scratch_shapes=list(scratch),
        compiler_params=pltpu.CompilerParams(vmem_limit_bytes=VMEM_LIMIT),
        cost_estimate=pl.CostEstimate(
            flops=flops, bytes_accessed=moved, transcendentals=exps
        ),
    )(*operands)


def exchange(value, offset):
    count = lax.axis_size(AXES)
    return lax.ppermute(value, AXES, [(i, i ^ offset) for i in range(count)])


def ordered(value, after):
    return value if after is None else lax.optimization_barrier((value, after))[0]


def half_difference(ref, lead, first, count):
    even = ref[(*lead, pl.ds(first, count, stride=2), slice(None))]
    odd = ref[(*lead, pl.ds(first + 1, count, stride=2), slice(None))]
    return 0.5 * (even - odd)


def put_pairs(ref, lead, total, difference):
    count = total.shape[0]
    ref[(*lead, pl.ds(0, count, stride=2), slice(None))] = total + difference
    ref[(*lead, pl.ds(1, count, stride=2), slice(None))] = total - difference


def mean_rows(ref, lead, first, count, factor):
    total = None
    for step in range(factor):
        rows = pl.ds(first + step, count, stride=factor)
        part = ref[(*lead, rows, slice(None))]
        total = part if total is None else total + part
    return total * (1.0 / factor)


def add_spread(ref, lead, first, value, factor):
    count = value.shape[0]
    value = value * (1.0 / factor)
    for step in range(factor):
        rows = pl.ds(first + step, count, stride=factor)
        place = (*lead, rows, slice(None))
        ref[place] = ref[place] + value


class Tree:
    def __init__(self, first_bit, own_rows):
        self.bits = bits = len(own_rows)
        self.first_bit = first_bit
        self.own_rows = own_rows
        self.held = {}
        self.payload = {}
        for step in range(bits - 1, -1, -1):
            rows = self.own_rows[step]
            payload = []
            fresh = {step: [(step, 0, rows)] if rows else []}
            for level in range(step + 1, bits):
                for piece in self.held[level]:
                    payload.append(piece)
                    fresh.setdefault(level, []).append((step, rows, piece[2]))
                    rows += piece[2]
            self.payload[step] = payload
            for level, pieces in fresh.items():
                self.held[level] = self.held.get(level, []) + pieces

    def rows(self, step):
        return self.own_rows[step] + sum(piece[2] for piece in self.payload[step])

    def partner(self, value, step):
        return exchange(value, 1 << self.first_bit + step)

    def gather(self, own, after=None):
        arrived = [None] * self.bits
        for step in range(self.bits - 1, -1, -1):
            parts = [own[step]] if self.own_rows[step] else []
            for source, row, rows in self.payload[step]:
                part = arrived[source]
                whole = rows == part.shape[1]
                parts.append(part if whole else part[:, row : row + rows])
            sent = jnp.concatenate(parts, axis=1) if len(parts) > 1 else parts[0]
            if step == 0:
                sent = ordered(sent, after)
            arrived[step] = self.partner(sent, step)
        return arrived

    def scatter(self, grads, front=None, whole=True):
        grads = list(grads)
        returned = []
        for step in range(self.bits if whole else self.bits - 1):
            sent = grads[step]
            if step == 0 and front is not None:
                rows = front.shape[1]
                back = self.partner(jnp.concatenate([front, sent], axis=1), step)
                front, back = back[:, :rows], back[:, rows:]
            else:
                back = self.partner(sent, step)
            returned.append(back)
            filled = self.own_rows[step]
            for source, row, rows in self.payload[step]:
                part = back[:, filled : filled + rows]
                grads[source] = grads[source].at[:, row : row + rows].add(part)
                filled += rows
        if not whole:
            returned.append(grads[-1])
        return returned if front is None else (returned, front)


def split(value):
    high = value.astype(BF16).astype(F32)
    return high, value - high


def halves_by_head(value):
    high, low = split(value)
    first = lax.broadcasted_iota(jnp.int32, value.shape, 1) < HEAD_DIM
    one = jnp.where(first, high, pltpu.roll(low, HEAD_DIM, 1))
    two = jnp.where(first, pltpu.roll(high, HEAD_DIM, 1), low)
    return one, two


def dot(lhs, rhs, dims):
    return lax.dot_general(lhs, rhs, (dims, ((), ())), preferred_element_type=F32)


NN = ((1,), (0,))
NT = ((1,), (1,))


BOTH = 2 * BLOCK
GROUP = 3


def halves_of(sets, ins, which, pairs, pair):
    tile = which * pairs + pair
    parts = [ins[index][tile, pl.ds(row, rows), :] for _, index, row, rows in sets]
    return halves_by_head(jnp.concatenate(parts, axis=0))


def segment_levels(sets):
    levels, filled = [], 0
    for level, _, _, rows in sets:
        if filled % BLOCK == 0:
            levels.append(level)
        filled += rows
    return levels


def four_rows(value):
    high, low = split(value)
    four = jnp.concatenate([high, high, low, low], axis=0).astype(BF16)
    return four, jnp.concatenate([high, low], axis=0).astype(BF16)


def store_split(ref, lead, rows, value):
    high = value.astype(BF16)
    ref[(lead, 0, rows)] = high
    ref[(lead, 1, rows)] = (value - high.astype(F32)).astype(BF16)


def fold_rows(value):
    return value[:HEAD_DIM] + value[HEAD_DIM:]


def fold_heads(one, two):
    first = lax.broadcasted_iota(jnp.int32, one.shape, 1) < HEAD_DIM
    return jnp.where(
        first, one + pltpu.roll(one, HEAD_DIM, 1), two + pltpu.roll(two, HEAD_DIM, 1)
    )


def twice(value):
    return jnp.concatenate([value, value], axis=1)


def stacked(ref, at, rows=slice(None)):
    return jnp.concatenate([ref[at, 0, rows], ref[at, 1, rows]], axis=0)


def abreast(ref, at, rows=slice(None)):
    return jnp.concatenate([ref[at, 0, rows], ref[at, 1, rows]], axis=1)


def column_scores(levels, keys, at, q_four, s_ref):
    highest = None
    for index, level in enumerate(levels):
        rows = pl.ds(index * BLOCK, BLOCK)
        s = dot(twice(keys[at, rows]), q_four, NN)
        s = s + float(level) if level else s
        s_ref[at, rows] = s
        top = jnp.max(s.reshape(BLOCK // 8, 8, BOTH), axis=0)
        highest = top if highest is None else jnp.maximum(highest, top)
    return jnp.max(highest, axis=0, keepdims=True)


def exponents(levels, at, top, s_ref, e_ref, keep):
    summed = None
    for index in range(len(levels)):
        rows = pl.ds(index * BLOCK, BLOCK)
        e = jnp.exp2(s_ref[at, rows] - top)
        if keep:
            s_ref[at, rows] = e
        store_split(e_ref, at, rows, e)
        part = jnp.sum(e.reshape(BLOCK // 8, 8, BOTH), axis=0)
        summed = part if summed is None else summed + part
    return jnp.sum(summed, axis=0, keepdims=True)


def head_rows(ref, pair, head):
    return ref[pair, pl.ds(head * HEAD_DIM, HEAD_DIM)]


def each_group(pairs, body):
    for first in range(0, pairs, GROUP):
        group = range(first, min(first + GROUP, pairs))
        body(group, [(pair, head, 2 * pair + head) for pair in group for head in (0, 1)])


def costs(pairs, rows, products, exps=0):
    return dict(
        flops=2 * 4 * products * pairs * 2 * rows * BOTH * HEAD_DIM,
        exps=exps * pairs * 2 * rows * BOTH,
    )


def put_halves(pairs, sets, ins, group, plain, turned):
    for which in range(2):
        for pair in group:
            for head, value in enumerate(halves_of(sets, ins, which, pairs, pair)):
                plain[which][2 * pair + head] = value.astype(BF16)
                turned[which][2 * pair + head] = value.T.astype(BF16)


def prepare(pairs, sets, operands):
    total = sum(s[3] for s in sets)

    def kernel(*refs):
        kc, vc, kt, vt = refs[len(operands) :]
        put_halves(pairs, sets, refs[: len(operands)], range(pairs), (kc, vc), (kt, vt))

    plain = jax.ShapeDtypeStruct((2 * pairs, total, LANES), BF16)
    turned = jax.ShapeDtypeStruct((2 * pairs, LANES, total), BF16)
    return call(kernel, operands, [plain] * 2 + [turned] * 2)


def attend_first(pairs, sets, kc, vt, turned):
    total = sum(s[3] for s in sets)
    levels = segment_levels(sets)

    def kernel(turn_in, kc, vt, e_ref, tops, sums, out, s_ref):
        def body(group, heads):
            for pair, head, at in heads:
                q_four, _ = four_rows(head_rows(turn_in, pair, head))
                tops[at] = column_scores(levels, kc, at, q_four, s_ref)
            for _, _, at in heads:
                sums[at] = exponents(levels, at, tops[at], s_ref, e_ref, False)
            for _, _, at in heads:
                out[at] = fold_rows(dot(twice(vt[at]), stacked(e_ref, at), NN))

        each_group(pairs, body)

    heads = 2 * pairs
    outs = [jax.ShapeDtypeStruct((heads, 2, total, BOTH), BF16)]
    outs += [struct(heads, 1, BOTH)] * 2 + [struct(heads, HEAD_DIM, BOTH)]
    return call(
        kernel,
        [turned, kc, vt],
        outs,
        scratch=[pltpu.VMEM((heads, total, BOTH), F32)],
        **costs(pairs, total, 2, 1),
    )


def attend_last(pairs, sets, operands, turned, tops, sums, partial):
    total = sum(s[3] for s in sets)
    levels = segment_levels(sets)

    def kernel(turn_in, top_in, sum_in, part_in, *refs):
        ins = refs[: len(operands)]
        grads = refs[len(operands) : 2 * len(operands)]
        o_keep, o_send, g_out, r_out, kt, d_ref = refs[2 * len(operands) : -5]
        s_ref, e_ref, kc, vc, vt = refs[-5:]

        def body(group, heads):
            put_halves(pairs, sets, ins, group, (kc, vc), (kt, vt))
            queries = {}
            top = {}
            for pair, head, at in heads:
                q_four, queries[at] = four_rows(head_rows(turn_in, pair, head))
                top[at] = column_scores(levels, kc, at, q_four, s_ref)
            inverse = {}
            rescale = {}
            for _, _, at in heads:
                first_top = top_in[at]
                highest = jnp.maximum(top[at], first_top)
                rescale[at] = jnp.exp2(first_top - highest)
                summed = exponents(levels, at, highest, s_ref, e_ref, True)
                inverse[at] = 1.0 / (summed + sum_in[at] * rescale[at])
            output = {}
            cotangents = {}
            row_dot = {}
            for pair, head, at in heads:
                o = fold_rows(dot(twice(vt[at]), stacked(e_ref, at), NN))
                o = (o + part_in[at] * rescale[at]) * inverse[at]
                output[at] = o
                scaled = head_rows(turn_in, pairs + pair, head) * inverse[at]
                cotangents[at] = four_rows(scaled)
                row_dot[at] = jnp.sum(o * scaled, axis=0, keepdims=True)
                g_out[at] = scaled * rescale[at]
                r_out[at] = row_dot[at] * rescale[at]
            for _, _, at in heads:
                for index in range(len(levels)):
                    rows = pl.ds(index * BLOCK, BLOCK)
                    dp = dot(twice(vc[at, rows]), cotangents[at][0], NN)
                    store_split(d_ref, at, rows, s_ref[at, rows] * (dp - row_dot[at]))
            key_grads = {}
            value_grads = {}
            for _, _, at in heads:
                value_grads[at] = dot(abreast(e_ref, at), twice(cotangents[at][1]), NT)
                key_grads[at] = dot(abreast(d_ref, at), twice(queries[at]), NT)
            for pair in group:
                put_grads(pairs, pair, sets, grads, key_grads, value_grads)
                both = [output[2 * pair], output[2 * pair + 1]]
                both = jnp.concatenate(both, axis=0).T
                o_keep[pair] = both[:BLOCK]
                o_send[pair] = both[BLOCK:]

        each_group(pairs, body)

    heads = 2 * pairs
    outs = [struct(*a.shape) for a in operands]
    outs += [struct(pairs, BLOCK, LANES)] * 2
    outs += [struct(heads, HEAD_DIM, BOTH), struct(heads, 1, BOTH)]
    outs.append(jax.ShapeDtypeStruct((heads, LANES, total), BF16))
    outs.append(jax.ShapeDtypeStruct((heads, 2, total, BOTH), BF16))
    return call(
        kernel,
        [turned, tops, sums, partial, *operands],
        outs,
        scratch=[pltpu.VMEM((heads, total, BOTH), F32)]
        + [pltpu.VMEM((heads, 2, total, BOTH), BF16)]
        + [pltpu.VMEM((heads, total, LANES), BF16)] * 2
        + [pltpu.VMEM((heads, LANES, total), BF16)],
        **costs(pairs, total, 5, 1),
    )


def put_grads(pairs, pair, sets, grads, key_grads, value_grads):
    for which, parts in enumerate((key_grads, value_grads)):
        both = fold_heads(parts[2 * pair], parts[2 * pair + 1])
        if which == 0:
            both = both * (1.0 / LOG2_E)
        filled = 0
        for _, index, row, rows in sets:
            piece = both[filled : filled + rows]
            grads[index][which * pairs + pair, pl.ds(row, rows), :] = piece
            filled += rows


def attend_back(pairs, sets, shapes, first, kept, turned, g_scaled, row_dot, others):
    total = sum(s[3] for s in sets)
    segments = total // BLOCK

    def kernel(turn_in, kt, vc, e_ref, g_in, r_in, *refs):
        other_in = refs[: len(others)]
        grads = refs[len(others) : len(others) + len(shapes)]
        dq_out = refs[len(others) + len(shapes) : -1]
        d_ref = refs[-1]
        span = pl.ds(first, total)

        def body(group, heads):
            cotangents = {}
            for _, _, at in heads:
                g_four, cotangents[at] = four_rows(g_in[at])
                for index in range(segments):
                    rows = pl.ds(first + index * BLOCK, BLOCK)
                    dp = dot(twice(vc[at, rows]), g_four, NN)
                    e = e_ref[at, 0, rows].astype(F32) + e_ref[at, 1, rows].astype(F32)
                    place = pl.ds(index * BLOCK, BLOCK)
                    store_split(d_ref, at, place, e * (dp - r_in[at]))
            queries_grad = {}
            key_grads = {}
            value_grads = {}
            for pair, head, at in heads:
                _, q_rows = four_rows(head_rows(turn_in, pair, head))
                g_rows = cotangents[at]
                value_grads[at] = dot(abreast(e_ref, at, span), twice(g_rows), NT)
                key_grads[at] = dot(abreast(d_ref, at), twice(q_rows), NT)
                if others:
                    d_lo, kt_hi, d_hi = other_in
                    part = dot(twice(kt[at, :, span]), stacked(d_ref, at), NN)
                    part += dot(twice(kt[at, :, total:]), stacked(d_lo, at), NN)
                    part += dot(twice(kt_hi[at]), stacked(d_hi, at), NN)
                    queries_grad[at] = fold_rows(part)
            for pair in group:
                put_grads(pairs, pair, sets, grads, key_grads, value_grads)
                if others:
                    both = [queries_grad[2 * pair], queries_grad[2 * pair + 1]]
                    both = jnp.concatenate(both, axis=0).T * SCALE
                    dq_out[0][pair] = both[:BLOCK]
                    dq_out[1][pair] = both[BLOCK:]

        each_group(pairs, body)

    outs = [struct(*shape) for shape in shapes]
    scratch = []
    if others:
        outs += [struct(pairs, BLOCK, LANES)] * 2
        scratch.append(pltpu.VMEM((2 * pairs, 2, total, BOTH), BF16))
    else:
        outs.append(jax.ShapeDtypeStruct((2 * pairs, 2, total, BOTH), BF16))
    return call(
        kernel,
        [turned, *kept, g_scaled, row_dot, *others],
        outs,
        scratch=scratch,
        **costs(pairs, total, 4),
    )


def copy_columns(moves, ins, sems, bit):
    started = []
    for operand, theirs, column, place in moves:
        side = 1 - bit if theirs else bit
        column = side * (ins[operand].shape[1] // 2) + column
        column = pl.ds(pl.multiple_of(column, LANES), LANES)
        copy = pltpu.make_async_copy(
            ins[operand].at[:, column], place, sems.at[len(started)]
        )
        copy.start()
        started.append(copy)
    return started


def pack(pairs, first, second, scalar):
    def kernel(bit, one, two, theirs, mine, sems):
        moves = []
        for tile in range(2 * pairs):
            for out, other in ((theirs, True), (mine, False)):
                column = tile % pairs * LANES
                moves.append((tile // pairs, other, column, out.at[tile]))
        for copy in copy_columns(moves, (one, two), sems, bit[0]):
            copy.wait()

    return call(
        kernel,
        [first, second],
        [struct(2 * pairs, BLOCK, LANES)] * 2,
        scratch=[pltpu.SemaphoreType.DMA((4 * pairs,))],
        scalar=scalar,
        where=pl.ANY,
    )


QUARTER = BLOCK // 4
HALF = BLOCK // 2


def pack_theirs(pairs, keys, values, scalar):
    def kernel(bit, k, v, finest, coarse, rest, block, sems):
        moves = []
        for tile in range(2 * pairs):
            moves.append((tile // pairs, True, tile % pairs * LANES, block.at[tile]))
        copies = copy_columns(moves, (k, v), sems, bit[0])
        for tile, copy in enumerate(copies):
            copy.wait()
            finest[tile] = mean_rows(block, (tile,), 0, HALF, 2)
            coarse[tile] = mean_rows(finest, (tile,), 0, QUARTER, 2)
            rest[tile, :QUARTER] = half_difference(finest, (tile,), 0, QUARTER)
            rest[tile, QUARTER:] = half_difference(block, (tile,), 0, HALF)

    return call(
        kernel,
        [keys, values],
        [
            struct(2 * pairs, HALF, LANES),
            struct(2 * pairs, QUARTER, LANES),
            struct(2 * pairs, QUARTER + HALF, LANES),
        ],
        scratch=[
            pltpu.VMEM((2 * pairs, BLOCK, LANES), F32),
            pltpu.SemaphoreType.DMA((2 * pairs,)),
        ],
        scalar=scalar,
        where=pl.ANY,
    )


def pack_mine(pairs, keys, values, scalar):
    def kernel(bit, k, v, block, finest, coarse, sems):
        moves = []
        for tile in range(2 * pairs):
            moves.append((tile // pairs, False, tile % pairs * LANES, block.at[tile]))
        copies = copy_columns(moves, (k, v), sems, bit[0])
        for tile, copy in enumerate(copies):
            copy.wait()
            finest[tile] = mean_rows(block, (tile,), 0, HALF, 2)
            coarse[tile] = mean_rows(finest, (tile,), 0, QUARTER, 2)

    return call(
        kernel,
        [keys, values],
        [
            struct(2 * pairs, BLOCK, LANES),
            struct(2 * pairs, HALF, LANES),
            struct(2 * pairs, QUARTER, LANES),
        ],
        scratch=[pltpu.SemaphoreType.DMA((2 * pairs,))],
        scalar=scalar,
        where=pl.ANY,
    )


def rebuild(pairs, second, rest):
    def kernel(second_in, rest_in, out, finest):
        for tile in range(2 * pairs):
            put_pairs(finest, (tile,), second_in[tile], rest_in[tile, :QUARTER])
            put_pairs(out, (tile,), finest[tile], rest_in[tile, QUARTER:])

    return call(
        kernel,
        [second, rest],
        [struct(2 * pairs, BLOCK, LANES)],
        scratch=[pltpu.VMEM((2 * pairs, HALF, LANES), F32)],
    )[0]


def take_apart(pairs, block_grad):
    def kernel(block, second, rest, finest):
        for tile in range(2 * pairs):
            finest[tile] = 2.0 * mean_rows(block, (tile,), 0, HALF, 2)
            rest[tile, QUARTER:] = 2.0 * half_difference(block, (tile,), 0, HALF)
            second[tile] = 2.0 * mean_rows(finest, (tile,), 0, QUARTER, 2)
            rest[tile, :QUARTER] = 2.0 * half_difference(finest, (tile,), 0, QUARTER)

    return call(
        kernel,
        [block_grad],
        [
            struct(2 * pairs, QUARTER, LANES),
            struct(2 * pairs, QUARTER + HALF, LANES),
        ],
        scratch=[pltpu.VMEM((2 * pairs, HALF, LANES), F32)],
    )


class Levels:
    def __init__(self, bits):
        self.bits = bits
        self.rows = BLOCK >> bits
        self.differences = [
            [(m, BLOCK >> m) for m in range(bits, step, -1)] for step in range(bits)
        ]
        whole = [0] + [BLOCK >> step for step in range(1, bits)]
        self.whole = Tree(1, whole)
        self.rough = Tree(1, [0] + [self.rows] * (bits - 1))
        self.fine = Tree(1, [0] + [rows - self.rows for rows in whole[1:]])
        self.pieces = []
        for level in range(1, bits):
            trees = (self.whole, self.rough, self.fine)
            for parts in zip(*(tree.held[level] for tree in trees)):
                self.pieces.append((level, parts[0][0], *(part[1] for part in parts)))

    def scratch(self):
        shapes = [(BLOCK >> m, LANES) for m in range(1, self.bits + 1)]
        return [pltpu.VMEM(shape, F32) for shape in shapes]

    def group_pieces(self):
        pieces = []
        for index, (level, step, whole, rough, _) in enumerate(self.pieces):
            factor = 1 << self.bits - level
            place = (2 + index) * self.rows
            pieces.append((step, whole, rough, BLOCK >> level, factor, place))
        return pieces


def coarsen_pair(lo, pairs, mine, received):
    def kernel(own, got, *outs):
        for tile in range(2 * pairs):
            outs[0][tile, : BLOCK // 4] = own[tile]
            outs[0][tile, BLOCK // 4 :] = got[tile]
            for index in range(1, lo.bits):
                outs[index][tile] = mean_rows(
                    outs[index - 1], (tile,), 0, BLOCK >> index + 1, 2
                )

    outs = [struct(2 * pairs, BLOCK >> step, LANES) for step in range(1, lo.bits + 1)]
    return call(kernel, [mine, received], outs)


def group_pieces(lo):
    own = BLOCK >> lo.bits
    factor = 1 << lo.bits
    pieces = [
        (-2, 0, BLOCK // 2, factor, own),
        (-1, 0, BLOCK // 2, factor, own + own // 2),
    ]
    filled = 2 * own
    for level in range(1, lo.bits):
        factor = 1 << lo.bits - level
        for step, row, rows in lo.held[level]:
            pieces.append((step, row, rows, factor, filled))
            filled += rows // factor
    return pieces


def coarsen_group(lo, hi, pairs, own, halves, arrived):
    pieces = group_pieces(lo)

    def kernel(own_in, *refs):
        ins = refs[: 2 + lo.bits]
        outs = refs[2 + lo.bits :]
        for tile in range(2 * pairs):
            outs[0][tile, pl.ds(0, BLOCK >> lo.bits)] = own_in[tile]
            for step, row, rows, factor, place in pieces:
                count = rows // factor
                outs[0][tile, pl.ds(place, count)] = mean_rows(
                    ins[2 + step], (tile,), row, count, factor
                )
            for step in range(1, hi.bits):
                outs[step][tile] = mean_rows(
                    outs[step - 1], (tile,), 0, BLOCK >> step, 2
                )

    outs = [struct(2 * pairs, BLOCK >> step, LANES) for step in range(hi.bits)]
    return call(kernel, [own, *halves, *arrived], outs)


def turn(pairs, mine, received):
    def kernel(own, got, turned):
        for tile in range(2 * pairs):
            both = jnp.concatenate([own[tile], got[tile]], axis=0).T
            turned[tile] = both * (SCALE * LOG2_E) if tile < pairs else both

    return call(kernel, [mine, received], [struct(2 * pairs, LANES, 2 * BLOCK)])[0]


def take_levels(levels, pairs, grads):
    trees = (levels.rough, levels.fine)

    def kernel(*refs):
        ins = refs[: levels.bits]
        rough = refs[levels.bits : 2 * levels.bits]
        fine = refs[2 * levels.bits : 3 * levels.bits]
        ladder = refs[3 * levels.bits :]
        for tile in range(2 * pairs):
            for level, step, row, rough_row, fine_row in levels.pieces:
                source = ladder[level - 1]
                source[...] = ins[step][tile, pl.ds(row, BLOCK >> level)]
                fine_row += sum(rows for _, rows in levels.differences[level])
                for m, rows in reversed(levels.differences[level]):
                    fine_row -= rows
                    part = 2.0 * half_difference(source, (), 0, rows)
                    fine[step][tile, pl.ds(fine_row, rows)] = part
                    ladder[m - 1][...] = 2.0 * mean_rows(source, (), 0, rows, 2)
                    source = ladder[m - 1]
                rough[step][tile, pl.ds(rough_row, levels.rows)] = source[...]

    outs = [
        struct(2 * pairs, tree.rows(step), LANES)
        for tree in trees
        for step in range(levels.bits)
    ]
    outs = call(kernel, grads, outs, scratch=levels.scratch())
    return outs[: levels.bits], outs[levels.bits :]


def spread_group(levels, hi, pairs, group_grads, grads):
    own_rows = levels.rows

    def kernel(*refs):
        steps = refs[: hi.bits]
        ins = refs[hi.bits : hi.bits + levels.bits]
        own_out, *outs = refs[hi.bits + levels.bits : -1]
        total = refs[-1]
        for tile in range(2 * pairs):
            total[tile] = steps[0][tile, pl.ds(0, BLOCK)]
            for step in range(1, hi.bits):
                above = steps[step][tile, pl.ds(0, BLOCK >> step)]
                add_spread(total, (tile,), 0, above, 1 << step)
            own_out[tile] = total[tile, pl.ds(0, own_rows)]
            for step, _, row, _, _, place in levels.group_pieces():
                rows = pl.ds(row, own_rows)
                part = total[tile, pl.ds(place, own_rows)]
                outs[step][tile, rows] = ins[step][tile, rows] + part
            outs[0][tile, pl.ds(ins[0].shape[1], own_rows)] = total[
                tile, pl.ds(own_rows, own_rows)
            ]

    shapes = [list(a.shape) for a in grads]
    shapes[0][1] += own_rows
    outs = [struct(2 * pairs, own_rows, LANES)] + [struct(*shape) for shape in shapes]
    own, *grads = call(
        kernel,
        [*group_grads, *grads],
        outs,
        scratch=[pltpu.VMEM((2 * pairs, BLOCK, LANES), F32)],
    )
    return own, grads


def spread_pair(levels, pairs, own_grad, rough, fine, block_second):
    own_rows = levels.rows

    def kernel(own, block, *refs):
        rough_in = refs[: levels.bits - 1]
        fine_in = refs[levels.bits - 1 : 2 * levels.bits - 1]
        mine, theirs, *ladder = refs[2 * levels.bits - 1 :]
        last = pl.ds(rough_in[0].shape[1] - own_rows, own_rows)
        for tile in range(2 * pairs):
            above = own[tile] + rough_in[0][tile, last]
            for step in range(1, levels.bits - 1):
                above = above + rough_in[step][tile, pl.ds(0, own_rows)]
            filled = 0
            for m, rows in levels.differences[1]:
                part = fine_in[1][tile, pl.ds(filled, rows)]
                for step in range(2, min(m, levels.bits)):
                    part = part + fine_in[step][tile, pl.ds(filled, rows)]
                filled += rows
                put_pairs(ladder[m - 2], (), 0.5 * above, 0.5 * part)
                above = ladder[m - 2][...]
            mine[tile] = above[:QUARTER]
            theirs[tile] = above[QUARTER:] + block[tile]

    return call(
        kernel,
        [own_grad, block_second, *rough, *fine],
        [struct(2 * pairs, QUARTER, LANES)] * 2,
        scratch=levels.scratch(),
    )


def unpack(pairs, kept, arrived, features, scalar):
    def kernel(bit, mine, theirs, out):
        for pair in range(pairs):
            for side, ref in ((bit[0], mine), (1 - bit[0], theirs)):
                column = side * (features // 2) + pair * LANES
                column = pl.ds(pl.multiple_of(column, LANES), LANES)
                out[:, column] = ref[pair]

    return call(kernel, [kept, arrived], [struct(BLOCK, features)], scalar=scalar)[0]


def widen(pairs, endings):
    factor = QUARTER // endings[0].shape[1]

    def kernel(*refs):
        for value, out in zip(refs[:2], refs[2:]):
            for tile in range(2 * pairs):
                out[tile] = jnp.zeros((QUARTER, LANES), F32)
                add_spread(out, (tile,), 0, value[tile], factor)

    outs = [struct(2 * pairs, QUARTER, LANES)] * 2
    return call(kernel, endings, outs, flops=700000000)


def finish(pairs, kept, rest, finest, seconds, endings, features, scalar):
    def kernel(bit, kept_in, rest_in, f_mine, f_theirs, s_mine, s_theirs, *refs):
        e_mine, e_theirs = refs[:2]
        outs, total, middle = refs[2:4], refs[4], refs[5]
        for tile in range(2 * pairs):
            out = outs[tile // pairs]
            column = tile % pairs * LANES
            at = (tile,)
            total[tile] = kept_in[tile]
            add_spread(total, at, 0, f_mine[tile], 2)
            add_spread(total, at, 0, s_mine[tile] + e_mine[tile], 4)
            place = bit[0] * (features // 2) + column
            out[:, pl.ds(pl.multiple_of(place, LANES), LANES)] = total[tile]
            second = s_theirs[tile] + e_theirs[tile]
            put_pairs(middle, at, 0.5 * second, 0.5 * rest_in[tile, :QUARTER])
            first = 0.5 * (middle[tile] + f_theirs[tile])
            put_pairs(total, at, first, 0.5 * rest_in[tile, QUARTER:])
            place = (1 - bit[0]) * (features // 2) + column
            out[:, pl.ds(pl.multiple_of(place, LANES), LANES)] = total[tile]

    return call(
        kernel,
        [kept, rest, *finest, *seconds, *endings],
        [struct(BLOCK, features)] * 2,
        scratch=[
            pltpu.VMEM((2 * pairs, BLOCK, LANES), F32),
            pltpu.VMEM((2 * pairs, HALF, LANES), F32),
        ],
        scalar=scalar,
    )


def on_device(queries, keys, values, cotangent):
    features = queries.shape[1]
    assert queries.shape[0] == BLOCK
    pairs = features // LANES // 2
    lo_bits = lax.axis_size("seqlo").bit_length() - 1
    levels = Levels(lo_bits - 1)
    lo = levels.whole
    hi_bits = lax.axis_size("seqhi").bit_length() - 1
    hi = Tree(lo_bits, [BLOCK >> step for step in range(hi_bits)])
    scalar = (lax.axis_index("seqlo") % 2).astype(jnp.int32).reshape(1)
    queries, keys, values, cotangent = [
        pltpu.with_memory_space_constraint(array, pltpu.HBM)
        for array in (queries, keys, values, cotangent)
    ]
    f_theirs, c_send, rest = pack_theirs(pairs, keys, values, scalar)
    mine_kv, f_mine, c_mine = pack_mine(pairs, keys, values, scalar)
    second = exchange(c_send, 1)
    finest_theirs = exchange(f_theirs, 2)
    coarse = coarsen_pair(lo, pairs, c_mine, second)
    finest = exchange(ordered(f_mine, finest_theirs), 2)
    rest = exchange(ordered(rest, coarse[0]), 1)
    half = exchange(ordered(finest_theirs, rest), 1)
    kv = rebuild(pairs, second, rest)
    send_qg, mine_qg = pack(pairs, queries, cotangent, scalar)
    qg = exchange(ordered(send_qg, half), 1)
    zs = lo.gather([None, *coarse], (finest, send_qg))
    group = coarsen_group(
        lo, hi, pairs, ordered(coarse[-1], rest), [finest, half], zs
    )
    block_sets = [(0, 0, 0, BLOCK), (0, 1, 0, BLOCK)]
    lo_sets = [(1, 2, 0, BLOCK // 2), (1, 3, 0, BLOCK // 2)]
    for level in range(lo.bits):
        for step, row, rows in lo.held[level]:
            lo_sets.append((1 + level, 4 + step, row, rows))
    hi_sets = []
    for level in range(hi.bits):
        for step, row, rows in hi.held[level]:
            hi_sets.append((lo_bits + level, step, row, rows))
    first_in = [mine_kv, kv, finest, half, *zs]
    kc, vc, kt, vt = prepare(pairs, block_sets + lo_sets, first_in)
    turned = turn(pairs, mine_qg, ordered(qg, kc))
    rs = hi.gather(group, (qg, kc))
    exps, tops, sums, partial = attend_first(
        pairs, block_sets + lo_sets, kc, vt, turned
    )
    kept = [kt, vc, exps]
    *rs_grads, o_keep, o_send, g_scaled, row_dot, kt_hi, d_hi = attend_last(
        pairs, hi_sets, rs, turned, tops, sums, partial
    )
    shapes = [(2 * pairs, *a.shape[1:]) for a in first_in]
    finest_grad, half_grad, *zs_grads, d_lo = attend_back(
        pairs,
        [(level, index - 2, row, rows) for level, index, row, rows in lo_sets],
        shapes[2:],
        BOTH,
        kept,
        turned,
        g_scaled,
        row_dot,
        [],
    )
    kv_keep, kv_send, dq_keep, dq_send = attend_back(
        pairs,
        block_sets,
        shapes[:2],
        0,
        kept,
        turned,
        g_scaled,
        row_dot,
        [d_lo, kt_hi, d_hi],
    )
    rough_grads, fine_grads = take_levels(levels, pairs, zs_grads)
    group_grads = hi.scatter(rs_grads)
    half_back = exchange(ordered(half_grad, kv_send), 1)
    o_back = exchange(o_send, 1)
    fine_back, finest_mine = levels.fine.scatter(fine_grads, finest_grad)
    block_second, rest_grad = take_apart(pairs, kv_send)
    split_at = rest_grad.shape[1]
    bulk = jnp.concatenate([rest_grad, dq_send.reshape(2 * pairs, HALF, LANES)], axis=1)
    bulk = exchange(bulk, 1)
    rest_back = bulk[:, :split_at]
    dq_back = bulk[:, split_at:].reshape(pairs, BLOCK, LANES)
    group_grads[-1] = ordered(group_grads[-1], (kv_send, o_back))
    own_grad, rough_grads = spread_group(levels, hi, pairs, group_grads, rough_grads)
    *rough_back, ending = levels.rough.scatter(rough_grads, whole=False)
    half_rows = levels.rows // 2
    finest_theirs = exchange(ordered(half_back, rough_back[0]), 2)
    far = 1 << levels.bits
    ending_mine = exchange(ending[:, :half_rows], far)
    ending_theirs = exchange(ending[:, half_rows:], far + 1)
    second_mine, second_send = spread_pair(
        levels, pairs, own_grad, rough_back, fine_back, block_second
    )
    second_theirs = exchange(second_send, 1)
    attended = unpack(pairs, o_keep, o_back, features, scalar)
    query_grad = unpack(pairs, dq_keep, dq_back, features, scalar)
    key_grad, value_grad = finish(
        pairs,
        kv_keep,
        rest_back,
        (finest_mine, finest_theirs),
        (second_mine, second_theirs),
        widen(pairs, [ending_mine, ending_theirs]),
        features,
        scalar,
    )
    return attended, query_grad, key_grad, value_grad


def solution(mesh):
    spec = P(AXES, None)
    return jax.shard_map(
        on_device,
        mesh=mesh,
        in_specs=(spec,) * 4,
        out_specs=(spec,) * 4,
        check_vma=False,
    )
```
